32 devices in a mesh: fsdp: 2 (over x), ctx: 8 (over z, core), tp: 2 (over y).
Axes of the slice: x: 2, y: 2, z: 4, core: 2. Of those that a mesh axis runs over, the one named last changes fastest.
Arguments:
- tokens: bfloat16 [8192, 1024], P(('fsdp', 'ctx')), may hold values from -6 to 6
- cotangent: bfloat16 [8192, 1024], P(('fsdp', 'ctx')), may hold values from -6 to 6
- lengths: int32 [2, 4], P('fsdp'), may hold values from 512 to 2048, as said below
- order: int32 [2, 4], P('fsdp'), may hold values from 0 to 3, each once within a row
- qkv_weight: float32 [1024, 3, 1024], P('fsdp', None, 'tp'), may hold values from -0.1875 to 0.1875
- attn_weight: float32 [1024, 1024], P('tp', 'fsdp'), may hold values from -4 to 4
- wide_weight: float32 [1024, 2, 2624], P('fsdp', None, 'tp'), may hold values from -0.1875 to 0.1875
- down_weight: float32 [2624, 1024], P('tp', 'fsdp'), may hold values from -0.125 to 0.125
- norm_gains: float32 [2, 1024], P(None, 'fsdp'), may hold values from 0.5 to 1.5
- qkv_mean: float32 [1024, 3, 1024], P('fsdp', None, 'tp'), may hold values from -40 to 40
- attn_mean: float32 [1024, 1024], P('tp', 'fsdp'), may hold values from -4 to 4
- wide_mean: float32 [1024, 2, 2624], P('fsdp', None, 'tp'), may hold values from -16 to 16
- down_mean: float32 [2624, 1024], P('tp', 'fsdp'), may hold values from -32 to 32
- gains_mean: float32 [2, 1024], P(None, 'fsdp'), may hold values from -40 to 40
- qkv_square: float32 [1024, 3, 1024], P('fsdp', None, 'tp'), may hold values from 40.96 to 655.36
- attn_square: float32 [1024, 1024], P('tp', 'fsdp'), may hold values from 0.18 to 2.94
- wide_square: float32 [1024, 2, 2624], P('fsdp', None, 'tp'), may hold values from 7.3728 to 120.4224
- down_square: float32 [2624, 1024], P('tp', 'fsdp'), may hold values from 24.576 to 401.408
- gains_square: float32 [2, 1024], P(None, 'fsdp'), may hold values from 40.96 to 655.36
Outputs:
- output: bfloat16 [8192, 1024], P(('fsdp', 'ctx'))
- input_grad: bfloat16 [8192, 1024], P(('fsdp', 'ctx'))
- qkv_new: float32 [1024, 3, 1024], P('fsdp', None, 'tp')
- qkv_first: float32 [1024, 3, 1024], P('fsdp', None, 'tp')
- qkv_second: float32 [1024, 3, 1024], P('fsdp', None, 'tp')
- attn_new: float32 [1024, 1024], P('tp', 'fsdp')
- attn_first: float32 [1024, 1024], P('tp', 'fsdp')
- attn_second: float32 [1024, 1024], P('tp', 'fsdp')
- wide_new: float32 [1024, 2, 2624], P('fsdp', None, 'tp')
- wide_first: float32 [1024, 2, 2624], P('fsdp', None, 'tp')
- wide_second: float32 [1024, 2, 2624], P('fsdp', None, 'tp')
- down_new: float32 [2624, 1024], P('tp', 'fsdp')
- down_first: float32 [2624, 1024], P('tp', 'fsdp')
- down_second: float32 [2624, 1024], P('tp', 'fsdp')
- gains_new: float32 [2, 1024], P(None, 'fsdp')
- gains_first: float32 [2, 1024], P(None, 'fsdp')
- gains_second: float32 [2, 1024], P(None, 'fsdp')
The draws below stay inside these ranges and needn't reach their ends.
Inputs may be any that keep to these rules, and one draw needn't show every extreme that they name: Each row lists the lengths of one group's 4 sequences; they sum to 4096, and the largest is exactly 2048.
All inputs are finite; a program needn't handle non-finite values.
Results may differ from the reference program's by a relative error of at most 0.03.
Values may be sent and summed in bfloat16 or wider, within the bound.
A program may use at most 192 MiB of HBM per device.

```python
import math
import jax
import jax.numpy as jnp
from jax import lax

D = 1024
HEADS = 16
HD = 64
FF = 2624
TOK_DEV = 512
SEQS = 4
STEP = 10
GROUP = 4096
TOKENS = 8192
BLOCK = 64
LMAX = 2048
LMIN = 512
N_FSDP = 2
N_CTX = 8


def draw_lengths(key, part):
    key = jax.random.fold_in(key, 11)
    cut_key, roll_key = jax.random.split(key)
    spare_rows = GROUP // 8
    cut_points = jnp.sort(jax.random.randint(cut_key, (N_FSDP, 2), 0, spare_rows + 1), axis=1)
    pieces = jnp.stack([cut_points[:, 0], cut_points[:, 1] - cut_points[:, 0], spare_rows - cut_points[:, 1]], axis=1)
    filled = jnp.concatenate([jnp.full((N_FSDP, 1), LMAX, jnp.int32), LMIN + pieces.astype(jnp.int32)], axis=1)
    rotation = jax.random.randint(roll_key, (N_FSDP, 1), 0, SEQS)
    gather_index = (jnp.arange(SEQS, dtype=jnp.int32)[None, :] + rotation) % SEQS
    return jnp.take_along_axis(filled, gather_index, axis=1).astype(jnp.int32)


def steps_of(stream_key, shape, cuts, smallest, top_value):
    def one(dim, shards_of):
        draws = jax.random.uniform(jax.random.fold_in(jax.random.fold_in(stream_key, 6), dim), (shards_of,), jnp.float32, smallest / len(cuts), top_value / len(cuts))
        return jnp.repeat(jnp.exp(draws), shape[dim] // shards_of).reshape((-1,) + (1,) * (len(shape) - dim - 1))

    gain = one(*cuts[0])
    for cut in cuts[1:]:
        gain = gain * one(*cut)
    return gain


def noise(key, extent, scale, limit, cuts=(), kind=jnp.bfloat16):
    gain = steps_of(key, extent, cuts, -0.22, 0.18) if cuts else 1.0
    values = jax.random.normal(key, extent, jnp.float32) * scale * gain
    return jnp.minimum(jnp.maximum(values, -limit), limit).astype(kind)


def setup_inputs(seed: int = 0) -> dict:
    arg_keys = jax.random.split(jax.random.key(seed), 20)
    return {
        "tokens": noise(arg_keys[0], (TOKENS, D), 1.0, 6.0, ((0, 16),)),
        "cotangent": noise(arg_keys[1], (TOKENS, D), 1.0, 6.0, ((0, 16),)),
        "lengths": draw_lengths(jax.random.fold_in(arg_keys[19], 71), 0),
        "order": jax.vmap(lambda own: jax.random.permutation(own, SEQS))(jax.random.split(arg_keys[3], N_FSDP)).reshape((N_FSDP, SEQS)).astype(jnp.int32),
        "qkv_weight": noise(arg_keys[4], (D, 3, D), D ** -0.5, 0.1875, ((0, 2), (2, 2)), jnp.float32),
        "attn_weight": noise(arg_keys[5], (D, D), (max(1, D * 8 // GROUP)) ** -0.5, 4.0, ((0, 2), (1, 2)), jnp.float32),
        "wide_weight": noise(arg_keys[6], (D, 2, FF), D ** -0.5, 0.1875, ((0, 2), (2, 2)), jnp.float32),
        "down_weight": noise(arg_keys[7], (FF, D), FF ** -0.5, 0.125, ((0, 2), (1, 2)), jnp.float32),
        "norm_gains": jnp.clip(1.0 + 0.1 * jax.random.normal(arg_keys[8], (2, D), jnp.float32), 0.5, 1.5),
        "qkv_mean": noise(arg_keys[9], (D, 3, D), (0.078 * TOKENS ** 0.5), 40.0, ((0, 2), (2, 2)), jnp.float32),
        "attn_mean": noise(arg_keys[10], (D, D), (0.33 * N_FSDP ** 0.5), 4.0, ((0, 2), (1, 2)), jnp.float32),
        "wide_mean": noise(arg_keys[11], (D, 2, FF), (0.033 * TOKENS ** 0.5), 16.0, ((0, 2), (2, 2)), jnp.float32),
        "down_mean": noise(arg_keys[12], (FF, D), (0.061 * TOKENS ** 0.5), 32.0, ((0, 2), (1, 2)), jnp.float32),
        "gains_mean": noise(arg_keys[13], (2, D), (0.078 * TOKENS ** 0.5), 40.0, ((1, 2),), jnp.float32),
        "qkv_square": jnp.clip(jnp.exp(math.log(655.36) - 2.7725887 * jax.random.uniform(arg_keys[14], (D, 3, D), jnp.float32) ** steps_of(arg_keys[14], (D, 3, D), ((0, 2), (2, 2)), -0.2, 0.2)), 40.96, 655.36),
        "attn_square": jnp.clip(jnp.exp(math.log(2.94) - 2.793208 * jax.random.uniform(arg_keys[15], (D, D), jnp.float32) ** steps_of(arg_keys[15], (D, D), ((0, 2), (1, 2)), -0.2, 0.2)), 0.18, 2.94),
        "wide_square": jnp.clip(jnp.exp(math.log(120.4224) - 2.79320804 * jax.random.uniform(arg_keys[16], (D, 2, FF), jnp.float32) ** steps_of(arg_keys[16], (D, 2, FF), ((0, 2), (2, 2)), -0.2, 0.2)), 7.3728, 120.4224),
        "down_square": jnp.clip(jnp.exp(math.log(401.408) - 2.793208 * jax.random.uniform(arg_keys[17], (FF, D), jnp.float32) ** steps_of(arg_keys[17], (FF, D), ((0, 2), (1, 2)), -0.2, 0.2)), 24.576, 401.408),
        "gains_square": jnp.clip(jnp.exp(math.log(655.36) - 2.7725887 * jax.random.uniform(arg_keys[18], (2, D), jnp.float32) ** steps_of(arg_keys[18], (2, D), ((1, 2),), -0.2, 0.2)), 40.96, 655.36),
    }


@jax.custom_vjp
def low(v):
    return lax.optimization_barrier(v.astype(jnp.bfloat16)).astype(jnp.float32)

@jax.custom_vjp
def low_back(v):
    return v

def low_keep(v):
    return (low(v), None)

def low_pass(kept, grad):
    return (grad,)

def back_keep(v):
    return (v, None)

def back_low(kept, grad):
    return (low(grad),)
low.defvjp(low_keep, low_pass)
low_back.defvjp(back_keep, back_low)
NORM_EPS = 1e-05
ROPE_BASE = 160000.0
BETA_FIRST = 0.9
BETA_SECOND = 0.98
ADAM_EPS = 1e-06
DECAY = 0.01
RATE_ATTN = 0.5
RATE_GAIN = 0.8
MASKED = -1e+30

def normalize(values):
    centered = values - lax.optimization_barrier(jnp.mean(values, axis=1, keepdims=True))
    scaling = lax.rsqrt(lax.optimization_barrier(jnp.mean(centered * centered, axis=1, keepdims=True)) + NORM_EPS)
    return centered * scaling

def packed_place(local_row, device, devices, block_size):
    return (local_row // block_size * devices + device) * block_size + local_row % block_size

def sequence_of(lengths_row, order_row, places):
    count_seqs = lengths_row.shape[0]
    chosen = (order_row[:, None] == jnp.arange(count_seqs, dtype=jnp.int32)[None, :]).astype(jnp.int32)
    in_order = lax.optimization_barrier(jnp.sum(chosen * lengths_row[None, :], axis=1))
    endings = jnp.cumsum(in_order)
    passed = (endings[None, :] <= places[:, None]).astype(jnp.int32)
    segment = lax.optimization_barrier(jnp.sum(passed, axis=1))
    offset = lax.optimization_barrier(jnp.sum(passed * in_order[None, :], axis=1))
    return (segment, places - offset)

def rope_tables(position, half_size):
    frequency = ROPE_BASE ** (-(2.0 * jnp.arange(half_size, dtype=jnp.float32)) / (2.0 * half_size))
    angles = position.astype(jnp.float32)[:, None] * frequency[None, :]
    return (jnp.cos(angles), jnp.sin(angles))

def rotate(values, cosine, sines):
    half_size = values.shape[-1] // 2
    first_half = values[..., :half_size]
    second_half = values[..., half_size:]
    cos_wide = cosine[:, None, :]
    sin_wide = sines[:, None, :]
    return jnp.concatenate([first_half * cos_wide - second_half * sin_wide, second_half * cos_wide + first_half * sin_wide], axis=-1)

def highest(pattern, left_side, right_side):
    return jnp.einsum(pattern, left_side, right_side, precision=lax.Precision.HIGHEST)

def attend(queries, keys, values, segments):
    query_rows = min(512, GROUP)
    block_count = GROUP // query_rows
    scaling = HD ** (-0.5)

    def one_group(group_args):
        group_query, group_key, group_value, group_seg = group_args

        def one_block(block_args):
            block_query, block_seg = block_args
            scores = highest('qhd,khd->hqk', block_query, group_key) * scaling
            allowed = (block_seg[:, None] == group_seg[None, :])[None]
            scores = low_back(jnp.where(allowed, scores, MASKED))
            weights = jax.nn.softmax(scores, axis=-1)
            return highest('hqk,khd->qhd', low(weights), group_value)
        blocks = lax.map(jax.checkpoint(one_block), (group_query.reshape(block_count, query_rows, HEADS, HD), group_seg.reshape(block_count, query_rows)))
        return blocks.reshape(GROUP, HEADS, HD)
    attended = lax.map(one_group, (queries.reshape(N_FSDP, GROUP, HEADS, HD), keys.reshape(N_FSDP, GROUP, HEADS, HD), values.reshape(N_FSDP, GROUP, HEADS, HD), segments.reshape(N_FSDP, GROUP)))
    return attended.reshape(TOKENS, HEADS, HD)

def forward(inputs, qkv_weight, attn_weight, wide_weight, down_weight, norm_gains, segments, cosine, sines):
    gains = low(norm_gains)
    entry_one = low(normalize(inputs) * gains[0][None, :])
    projected = low_back(highest('td,dkf->tkf', entry_one, low(qkv_weight)))
    shaped = projected.reshape(TOKENS, 3, HEADS, HD)
    queries = low(rotate(shaped[:, 0], cosine, sines))
    keys = low(rotate(shaped[:, 1], cosine, sines))
    values = low(shaped[:, 2])
    attended = attend(queries, keys, values, segments).reshape(TOKENS, D)
    attended = low(low_back(attended))
    mixed_sum = low_back(highest('tf,fd->td', attended, low(attn_weight)))
    middle = inputs + mixed_sum
    entry_two = low(normalize(middle) * gains[1][None, :])
    gate_up = low_back(highest('td,dkf->tkf', entry_two, low(wide_weight)))
    hidden = low(jax.nn.gelu(gate_up[:, 0], approximate=False) * gate_up[:, 1])
    return middle + highest('tf,fd->td', hidden, low(down_weight))

def adam_step(weight, gradient, moment, squared, rate_now):
    first = BETA_FIRST * moment + (1.0 - BETA_FIRST) * gradient
    second = BETA_SECOND * squared + (1.0 - BETA_SECOND) * gradient * gradient
    corrected = first / (1.0 - BETA_FIRST ** STEP)
    spread = jnp.sqrt(second / (1.0 - BETA_SECOND ** STEP))
    return (weight - rate_now * (corrected / (spread + ADAM_EPS) + DECAY * weight), first, second)

def reference(tokens, cotangent, lengths, order, qkv_weight, attn_weight, wide_weight, down_weight, norm_gains, qkv_mean, attn_mean, wide_mean, down_mean, gains_mean, qkv_square, attn_square, wide_square, down_square, gains_square):
    row_ids = jnp.arange(TOKENS, dtype=jnp.int32)
    within = row_ids % GROUP
    places = packed_place(within % TOK_DEV, within // TOK_DEV, N_CTX, BLOCK)
    segments, position = jax.vmap(sequence_of)(lengths, order, places.reshape(N_FSDP, GROUP))
    cosine, sines = rope_tables(position.reshape(TOKENS), HD // 2)
    flat_segments = segments.reshape(TOKENS)

    def layer_run(inputs, qkv_w, attn_w, wide_w, down_w, gains):
        return forward(inputs, qkv_w, attn_w, wide_w, down_w, gains, flat_segments, cosine, sines)
    result, pullback = jax.vjp(layer_run, tokens.astype(jnp.float32), qkv_weight, attn_weight, wide_weight, down_weight, norm_gains)
    gradients = pullback(cotangent.astype(jnp.float32))
    qkv_out = adam_step(qkv_weight, gradients[1], qkv_mean, qkv_square, D ** (-0.5))
    attn_out = adam_step(attn_weight, gradients[2], attn_mean, attn_square, RATE_ATTN)
    wide_out = adam_step(wide_weight, gradients[3], wide_mean, wide_square, D ** (-0.5))
    down_out = adam_step(down_weight, gradients[4], down_mean, down_square, FF ** (-0.5))
    gains_out = adam_step(norm_gains, gradients[5], gains_mean, gains_square, RATE_GAIN)
    return (result.astype(jnp.bfloat16), gradients[0].astype(jnp.bfloat16), qkv_out[0], qkv_out[1], qkv_out[2], attn_out[0], attn_out[1], attn_out[2], wide_out[0], wide_out[1], wide_out[2], down_out[0], down_out[1], down_out[2], gains_out[0], gains_out[1], gains_out[2])
```

```python
import functools

import jax
import jax.numpy as jnp
from jax import lax
from jax.experimental import pallas as pl
from jax.experimental.pallas import tpu as pltpu
from jax.sharding import PartitionSpec as P

D = 1024
HD = 64
FF = 2624
STEP = 10


NORM_EPS = 1e-05
ROPE_BASE = 160000.0
BETA_FIRST = 0.9
BETA_SECOND = 0.98
ADAM_EPS = 1e-06
DECAY = 0.01
RATE_ATTN = 0.5
RATE_GAIN = 0.8
MASKED = -1e30

MESH = pl.DeviceIdType.MESH
BF16 = jnp.bfloat16
F32 = jnp.float32
VMEM_BYTES = 60 * 2**20


class Sizes:
    def __init__(self, fsdp, ctx, rows, width, head_width, units):
        self.fsdp = fsdp
        self.ctx = ctx
        self.chips = ctx // 2
        self.rows = rows
        self.block = rows // 8
        self.group = rows * ctx
        self.width = width
        self.shard = width // fsdp
        self.heads = head_width // HD
        self.head_width = head_width
        self.units = units
        self.share = max(1, ctx // self.heads)
        self.chip_heads = max(1, self.heads // self.chips)
        self.chunk = self.chip_heads * 3 * HD


def remote(src, dst, send, recv, device):
    return pltpu.make_async_remote_copy(
        src_ref=src,
        dst_ref=dst,
        send_sem=send,
        recv_sem=recv,
        device_id=device,
        device_id_type=MESH,
    )


def greet(devices):
    barrier = pltpu.get_barrier_semaphore()
    for device in devices:
        pl.semaphore_signal(barrier, inc=1, device_id=device, device_id_type=MESH)
    pl.semaphore_wait(barrier, len(devices))


def vmem():
    return pl.BlockSpec(memory_space=pltpu.VMEM)


def anywhere():
    return pl.BlockSpec(memory_space=pl.ANY)


def normalize(values):
    centered = values - jnp.mean(values, axis=1, keepdims=True)
    scaling = lax.rsqrt(jnp.mean(centered * centered, axis=1, keepdims=True) + NORM_EPS)
    return (centered * scaling, scaling)


def norm_back(grad_hat, normed, scaling):
    return scaling * (
        grad_hat
        - jnp.mean(grad_hat, axis=1, keepdims=True)
        - normed * jnp.mean(grad_hat * normed, axis=1, keepdims=True)
    )


def swap_halves(values):
    lane = lax.broadcasted_iota(jnp.int32, values.shape, 1)
    return jnp.where(
        lane % HD < HD // 2, pltpu.roll(values, 2 * HD - HD // 2, 1), pltpu.roll(values, HD // 2, 1)
    )


def packed_place(local_row, device, devices, block_size):
    return (local_row // block_size * devices + device) * block_size + local_row % block_size


def sequence_ends(lengths_row, order_row):
    count_seqs = lengths_row.shape[0]
    chosen = (order_row[:, None] == jnp.arange(count_seqs, dtype=jnp.int32)[None, :]).astype(
        jnp.int32
    )
    in_order = jnp.sum(chosen * lengths_row[None, :], axis=1)
    return (in_order, jnp.cumsum(in_order))


def positions(in_order, endings, places):
    passed = (endings[None, :] <= places[:, None]).astype(jnp.int32)
    return places - jnp.sum(passed * in_order[None, :], axis=1)


def rope_tables(position):
    half_size = HD // 2
    frequency = ROPE_BASE ** (-(2.0 * jnp.arange(half_size, dtype=jnp.float32)) / (2.0 * half_size))
    angles = position.astype(jnp.float32)[:, None] * frequency[None, :]
    cosine, sines = jnp.cos(angles), jnp.sin(angles)
    return (
        jnp.concatenate([cosine] * 4, axis=1),
        jnp.concatenate([-sines, sines, -sines, sines], axis=1),
    )


def project_kernel(
    z_,
    tok_ref,
    gain_ref,
    cos_ref,
    sin_ref,
    wq_ref,
    wo_ref,
    wi_ref,
    packed_ref,
    wq_out,
    wo_out,
    wi_out,
    gain_out,
    entry_s,
    wq_s,
    send_s,
    gain_s,
    gain_send,
    gain_recv,
    wq_send,
    wq_recv,
    wq_fsend,
    wq_frecv,
    w_send,
    w_recv,
    w_fsend,
    w_frecv,
    a_send,
    a_recv,
    local_sem,
):
    f, c, t = lax.axis_index("fsdp"), lax.axis_index("ctx"), lax.axis_index("tp")
    core = lax.rem(c, 2)
    chip = c // 2
    mate = (f, c + 1 - 2 * core, t)
    others = range(1, z_.fsdp)

    def ahead(k):
        return lax.rem(f + k, z_.fsdp)

    def behind(k):
        return lax.rem(f + z_.fsdp - k, z_.fsdp)

    def chip_of(s):
        return lax.rem(chip + 1 + s, z_.chips)

    greet(
        [(ahead(k), c, t) for k in others]
        + [(f, lax.rem(c + j, z_.ctx), t) for j in range(1, z_.ctx)]
    )

    half = z_.shard // 2

    def gain_copy(k, owner):
        return remote(
            gain_ref, gain_s.at[owner], gain_send.at[k - 1], gain_recv.at[k - 1], (ahead(k), c, t)
        )

    def wq_copy(s, k, owner):
        p = chip_of(s)
        rows = pl.ds(pl.multiple_of(core * half, half), half)
        return remote(
            wq_ref.at[p, rows],
            wq_s.at[p, owner, rows],
            wq_send.at[s, k - 1],
            wq_recv.at[s, k - 1],
            (ahead(k), c, t),
        )

    def wq_pass(s, k, side):
        p = chip_of(s)
        rows = pl.ds(pl.multiple_of(side * half, half), half)
        place = wq_s.at[p, behind(k), rows]
        return remote(place, place, wq_fsend.at[s, k - 1], wq_frecv.at[s, k - 1], mate)

    attn_half = z_.head_width // 2

    def wo_copy(k, owner):
        rows = pl.ds(pl.multiple_of(core * attn_half, attn_half), attn_half)
        return remote(
            wo_ref.at[rows],
            wo_out.at[owner, rows],
            w_send.at[0, k - 1],
            w_recv.at[0, k - 1],
            (ahead(k), c, t),
        )

    def wo_pass(k, side):
        rows = pl.ds(pl.multiple_of(side * attn_half, attn_half), attn_half)
        place = wo_out.at[behind(k), rows]
        return remote(place, place, w_fsend.at[0, k - 1], w_frecv.at[0, k - 1], mate)

    def wi_copy(k, owner):
        return remote(
            wi_ref.at[core],
            wi_out.at[core, owner],
            w_send.at[1, k - 1],
            w_recv.at[1, k - 1],
            (ahead(k), c, t),
        )

    def wi_pass(k, side):
        place = wi_out.at[side, behind(k)]
        return remote(place, place, w_fsend.at[1, k - 1], w_frecv.at[1, k - 1], mate)

    def head_copy(s, side, source):
        p = chip_of(s)
        return remote(
            send_s.at[s, side % z_.chip_heads],
            packed_ref.at[:, source],
            a_send.at[s, side],
            a_recv.at[s, core],
            (f, 2 * p + side, t),
        )

    def head_arrival(s, side):
        source = 2 * lax.rem(chip + 2 * z_.chips - 1 - s, z_.chips) + side
        return remote(
            send_s.at[s, 0], packed_ref.at[:, source], a_send.at[s, 0], a_recv.at[s, side], mate
        )

    for k in others:
        gain_copy(k, f).start()
    for k in others:
        wq_copy(0, k, f).start()
    own_wq = pltpu.make_async_copy(wq_ref, wq_s.at[:, f], local_sem.at[0])
    own_wo = pltpu.make_async_copy(wo_ref, wo_out.at[f], local_sem.at[1])
    own_wi = pltpu.make_async_copy(wi_ref, wi_out.at[:, f], local_sem.at[2])
    own_wq.start()
    own_wo.start()
    own_wi.start()
    gain_s[f] = gain_ref[...]
    for k in others:
        wq_copy(1, k, f).start()
    for k in others:
        gain_copy(k, behind(k)).wait()

    gain_out[...] = gain_s[...]
    tile = min(128, z_.rows)

    def norm_tile(i, carried):
        rows = pl.ds(pl.multiple_of(i * tile, tile), tile)
        normed, nothing = normalize(tok_ref[rows, :].astype(F32))
        for g in range(z_.fsdp):
            columns = slice(g * z_.shard, (g + 1) * z_.shard)
            entry_s[g, rows, :] = (normed[:, columns] * gain_s[g, 0:1, :]).astype(BF16)
        return carried

    lax.fori_loop(0, z_.rows // tile, norm_tile, 0)
    own_wq.wait()

    def chunk_step(s, carried):
        for k in others:

            @pl.when(s + 2 < z_.chips)
            def more():
                wq_copy(s + 2, k, f).start()

            @pl.when(s + 2 == z_.chips)
            def attn_part():
                wo_copy(k, f).start()

            @pl.when(s + 1 == z_.chips)
            def wide_part():
                wi_copy(k, f).start()

            arrived = wq_copy(s, k, behind(k))
            arrived.wait_recv()
            wq_pass(s, k, core).start()
        for k in others:
            wq_pass(s, k, 1 - core).wait_recv()
        p = chip_of(s)
        total = jnp.zeros((z_.rows, z_.chunk), F32)
        for g in range(z_.fsdp):
            total = total + jnp.dot(entry_s[g], wq_s[p, g], preferred_element_type=F32)
        for i in range(z_.chip_heads):
            pair = total[:, 2 * HD * i : 2 * HD * (i + 1)]
            pair = pair * cos_ref[...] + swap_halves(pair) * sin_ref[...]
            send_s[s, i, 0:8] = pair.astype(BF16).reshape(8, z_.block, 2 * HD)
            start = z_.chip_heads * 2 * HD + HD * i
            value = total[:, start : start + HD]
            value = jnp.concatenate([value[: z_.rows // 2], value[z_.rows // 2 :]], axis=1)
            send_s[s, i, 8:12] = value.astype(BF16).reshape(4, z_.block, 2 * HD)

        @pl.when(s < z_.chips - 1)
        def away():
            for side in range(2):
                head_copy(s, side, c).start()

        return carried

    lax.fori_loop(0, z_.chips, chunk_step, 0)
    last = z_.chips - 1
    kept = pltpu.make_async_copy(
        send_s.at[last, lax.rem(core, z_.chip_heads)], packed_ref.at[:, c], local_sem.at[3]
    )
    kept.start()
    crossed = remote(
        send_s.at[last, lax.rem(1 - core, z_.chip_heads)],
        packed_ref.at[:, c],
        a_send.at[last, 0],
        a_recv.at[last, 0],
        mate,
    )
    crossed.start()
    keep_wq = pltpu.make_async_copy(wq_s, wq_out, local_sem.at[4])
    keep_wq.start()
    for k in others:
        wo_copy(k, behind(k)).wait_recv()
        wo_pass(k, core).start()
    for k in others:
        wi_copy(k, behind(k)).wait_recv()
        wi_pass(k, core).start()
    for s in range(z_.chips - 1):
        for side in range(2):
            head_arrival(s, side).wait_recv()
            head_copy(s, side, c).wait_send()
    crossed_in = remote(
        send_s.at[last, 0],
        packed_ref.at[:, c + 1 - 2 * core],
        a_send.at[last, 0],
        a_recv.at[last, 0],
        mate,
    )
    crossed_in.wait_recv()
    crossed.wait_send()
    for k in others:
        for s in range(z_.chips):
            wq_copy(s, k, f).wait_send()
            wq_pass(s, k, core).wait_send()
        wo_copy(k, f).wait_send()
        wi_copy(k, f).wait_send()
        wo_pass(k, core).wait_send()
        wi_pass(k, core).wait_send()
        wo_pass(k, 1 - core).wait_recv()
        wi_pass(k, 1 - core).wait_recv()
    kept.wait()
    keep_wq.wait()
    own_wo.wait()
    own_wi.wait()


def project(z_, tokens, gains, cosine, sines, wq, wo, wi):
    peers = max(1, z_.fsdp - 1)
    dma = pltpu.SemaphoreType.DMA
    return pl.pallas_call(
        functools.partial(project_kernel, z_),
        out_shape=(
            jax.ShapeDtypeStruct((12, z_.ctx, z_.block, 2 * HD), BF16),
            jax.ShapeDtypeStruct((z_.chips, z_.fsdp, z_.shard, z_.chunk), BF16),
            jax.ShapeDtypeStruct((z_.fsdp, z_.head_width, z_.shard), BF16),
            jax.ShapeDtypeStruct((2, z_.fsdp, z_.shard, z_.units), BF16),
            jax.ShapeDtypeStruct((z_.fsdp, 8, z_.shard), F32),
        ),
        in_specs=[vmem()] * 5 + [anywhere()] * 2,
        out_specs=(anywhere(), anywhere(), anywhere(), anywhere(), vmem()),
        scratch_shapes=[
            pltpu.VMEM((z_.fsdp, z_.rows, z_.shard), BF16),
            pltpu.VMEM((z_.chips, z_.fsdp, z_.shard, z_.chunk), BF16),
            pltpu.VMEM((z_.chips, z_.chip_heads, 12, z_.block, 2 * HD), BF16),
            pltpu.VMEM((z_.fsdp, 8, z_.shard), F32),
            dma((peers,)),
            dma((peers,)),
            dma((z_.chips, peers)),
            dma((z_.chips, peers)),
            dma((z_.chips, peers)),
            dma((z_.chips, peers)),
            dma((2, peers)),
            dma((2, peers)),
            dma((2, peers)),
            dma((2, peers)),
            dma((z_.chips, 2)),
            dma((z_.chips, 2)),
            dma((5,)),
        ],
        compiler_params=pltpu.CompilerParams(
            collective_id=0, has_side_effects=True, vmem_limit_bytes=VMEM_BYTES
        ),
        name="project",
    )(tokens, gains, cosine, sines, wq, wo, wi)


def sequence_at(ends_ref, place):
    start, end = jnp.int32(0), ends_ref[0]
    for k in range(ends_ref.shape[0] - 1):
        past = ends_ref[k] <= place
        start = jnp.where(past, ends_ref[k], start)
        end = jnp.where(past, ends_ref[k + 1], end)
    return (start, end)


def segments_of(ends_ref, places):
    segment = jnp.zeros(places.shape, jnp.int32)
    for k in range(ends_ref.shape[0]):
        segment = segment + (ends_ref[k] <= places).astype(jnp.int32)
    return segment


def attend_kernel(
    z_,
    q_tile,
    k_tile,
    ends_ref,
    packed_ref,
    out_ref,
    outt_ref,
    lse_ref,
    query_s,
    value_s,
    top_s,
    total_s,
):
    group = z_.group
    half = group // 2
    piece = min(512, half)
    scaling = HD ** (-0.5)
    sums = 16
    query_s[0:HD, :] = jnp.zeros((HD, group), BF16)
    value_s[HD : HD + sums, :] = jnp.ones((sums, group), BF16)

    def prepare(i, carried):
        rows = pl.ds(pl.multiple_of(i * piece, piece), piece)
        turned = packed_ref[rows, :].astype(F32).T
        query_s[HD : 2 * HD, rows] = (turned[0:HD] * scaling).astype(BF16)

        @pl.when(i < half // piece)
        def values():
            turned_value = (
                packed_ref[pl.ds(pl.multiple_of(group + i * piece, piece), piece), :].astype(F32).T
            ).astype(BF16)
            value_s[0:HD, rows] = turned_value[0:HD]
            value_s[0:HD, pl.ds(pl.multiple_of(half + i * piece, piece), piece)] = turned_value[
                HD : 2 * HD
            ]

        return carried

    lax.fori_loop(0, group // piece, prepare, 0)

    def one_tile(i, carried):
        first = pl.multiple_of(i * q_tile, q_tile)
        columns = pl.ds(first, q_tile)
        low, low_end = sequence_at(ends_ref, first)
        high_start, high = sequence_at(ends_ref, first + q_tile - 1)
        single = low == high_start
        top_s[...] = jnp.full(top_s.shape, MASKED, F32)
        total_s[...] = jnp.zeros(total_s.shape, F32)

        def one_step(j, masked):
            start = pl.multiple_of(j * k_tile, k_tile)
            rows = pl.ds(start, k_tile)
            scores = jnp.dot(packed_ref[rows, :], query_s[:, columns], preferred_element_type=F32)
            if masked:
                key_seg = segments_of(
                    ends_ref, start + lax.broadcasted_iota(jnp.int32, (k_tile, 1), 0)
                )
                query_seg = segments_of(
                    ends_ref, first + lax.broadcasted_iota(jnp.int32, (1, q_tile), 1)
                )
                scores = jnp.where(key_seg == query_seg, scores, MASKED)
            before = top_s[0:1, :]
            after = jnp.maximum(before, jnp.max(scores, axis=0, keepdims=True))
            weights = jnp.exp(scores - after).astype(BF16)
            top_s[0:1, :] = after
            total_s[...] = total_s[...] * jnp.exp(before - after) + jnp.dot(
                value_s[:, rows], weights, preferred_element_type=F32
            )

        def step(j, inner):
            start = j * k_tile
            whole = single & (start >= low) & (start + k_tile <= high)

            @pl.when(whole)
            def plain():
                one_step(j, False)

            @pl.when(jnp.logical_not(whole))
            def partial():
                one_step(j, True)

            return inner

        lax.fori_loop(low // k_tile, (high + k_tile - 1) // k_tile, step, 0)
        summed = total_s[HD : HD + 1, :]
        lse_ref[:, columns] = jnp.broadcast_to(top_s[0:1, :] + jnp.log(summed), (8, q_tile))
        outt_ref[:, columns] = total_s[0:HD, :] / summed
        return carried

    lax.fori_loop(0, group // q_tile, one_tile, 0)

    def finish(i, carried):
        rows = pl.ds(pl.multiple_of(i * piece, piece), piece)
        later = pl.ds(pl.multiple_of(half + i * piece, piece), piece)
        both = jnp.concatenate([outt_ref[:, rows], outt_ref[:, later]], axis=0)
        out_ref[rows, :] = both.T.astype(BF16)
        return carried

    lax.fori_loop(0, half // piece, finish, 0)


def attend(z_, ends, packed):
    q_tile, k_tile = 512, 512
    group = z_.group
    return pl.pallas_call(
        functools.partial(attend_kernel, z_, q_tile, k_tile),
        out_shape=(
            jax.ShapeDtypeStruct((group // 2, 2 * HD), BF16),
            jax.ShapeDtypeStruct((HD, group), F32),
            jax.ShapeDtypeStruct((8, group), F32),
        ),
        in_specs=[pl.BlockSpec(memory_space=pltpu.SMEM), vmem()],
        out_specs=(vmem(), vmem(), vmem()),
        scratch_shapes=[
            pltpu.VMEM((2 * HD, group), BF16),
            pltpu.VMEM((HD + 16, group), BF16),
            pltpu.VMEM((8, q_tile), F32),
            pltpu.VMEM((HD + 16, q_tile), F32),
        ],
        compiler_params=pltpu.CompilerParams(vmem_limit_bytes=VMEM_BYTES),
        name="attend",
    )(ends, packed)


def attend_back_kernel(
    z_,
    q_tile,
    k_tile,
    ends_ref,
    packed_ref,
    grad_ref,
    outt_ref,
    lse_ref,
    out_ref,
    query_s,
    key_s,
    swapped_s,
    grad_s,
    gradt_s,
    delta_s,
    query_grad_s,
    key_acc,
    value_acc,
):
    group = z_.group
    half = group // 2
    piece = min(512, half)
    scaling = HD ** (-0.5)
    query_s[0:HD, :] = jnp.zeros((HD, group), BF16)
    gradt_s[0:HD, :] = jnp.zeros((HD, group), BF16)
    gradt_s[2 * HD : 3 * HD, :] = jnp.zeros((HD, group), BF16)

    def prepare(i, carried):
        rows = pl.ds(pl.multiple_of(i * piece, piece), piece)
        pair = packed_ref[rows, :].astype(F32)
        turned = pair.T
        query_s[HD : 2 * HD, rows] = (turned[0:HD] * scaling).astype(BF16)
        key_s[:, rows] = turned[HD : 2 * HD].astype(BF16)
        swapped_s[rows, :] = pltpu.roll(pair, HD, 1).astype(BF16)
        query_grad_s[:, rows] = jnp.zeros((HD, piece), F32)

        @pl.when(i < half // piece)
        def grads():
            later = pl.ds(pl.multiple_of(half + i * piece, piece), piece)
            both = grad_ref[rows, :].astype(F32)
            turned_grad = both.T
            grad_s[rows, :] = both.astype(BF16)
            grad_s[later, :] = pltpu.roll(both, HD, 1).astype(BF16)
            for place, part in ((rows, turned_grad[0:HD]), (later, turned_grad[HD : 2 * HD])):
                gradt_s[HD : 2 * HD, place] = part.astype(BF16)
                delta = jnp.sum(part * outt_ref[:, place], axis=0, keepdims=True)
                delta_s[:, place] = jnp.broadcast_to(delta, (8, piece))

        return carried

    lax.fori_loop(0, group // piece, prepare, 0)

    def one_tile(j, carried):
        start = pl.multiple_of(j * k_tile, k_tile)
        rows = pl.ds(start, k_tile)
        upper = (start >= half).astype(jnp.int32)
        value_rows = pl.ds(pl.multiple_of(group + start - upper * half, k_tile), k_tile)
        turned_rows = pl.ds(pl.multiple_of(HD - upper * HD, HD), 2 * HD)
        low, low_end = sequence_at(ends_ref, start)
        high_start, high = sequence_at(ends_ref, start + k_tile - 1)
        single = low == high_start
        key_acc[...] = jnp.zeros(key_acc.shape, F32)
        value_acc[...] = jnp.zeros(value_acc.shape, F32)

        def one_step(i, masked):
            first = pl.multiple_of(i * q_tile, q_tile)
            columns = pl.ds(first, q_tile)
            scores = jnp.dot(packed_ref[rows, :], query_s[:, columns], preferred_element_type=F32)
            chances = jnp.exp(scores - lse_ref[0:1, columns])
            if masked:
                key_seg = segments_of(
                    ends_ref, start + lax.broadcasted_iota(jnp.int32, (k_tile, 1), 0)
                )
                query_seg = segments_of(
                    ends_ref, first + lax.broadcasted_iota(jnp.int32, (1, q_tile), 1)
                )
                chances = jnp.where(key_seg == query_seg, chances, 0.0)
            chance_grad = jnp.dot(
                packed_ref[value_rows, :],
                gradt_s[turned_rows, columns],
                preferred_element_type=F32,
            )
            score_grad = (chances * (chance_grad - delta_s[0:1, columns])).astype(BF16)
            value_acc[...] += jnp.dot(
                chances.astype(BF16), grad_s[columns, :], preferred_element_type=F32
            )
            key_acc[...] += jnp.dot(
                score_grad, swapped_s[columns, :], preferred_element_type=F32
            )
            query_grad_s[:, columns] += jnp.dot(
                key_s[:, rows], score_grad, preferred_element_type=F32
            )

        def step(i, inner):
            first = i * q_tile
            whole = single & (first >= low) & (first + q_tile <= high)

            @pl.when(whole)
            def plain():
                one_step(i, False)

            @pl.when(jnp.logical_not(whole))
            def partial():
                one_step(i, True)

            return inner

        lax.fori_loop(low // q_tile, (high + q_tile - 1) // q_tile, step, 0)
        out_ref[rows, HD : 2 * HD] = (key_acc[:, HD : 2 * HD] * scaling).astype(BF16)

        @pl.when(upper == 0)
        def lower_values():
            out_ref[pl.ds(pl.multiple_of(group + start, k_tile), k_tile), 0:HD] = value_acc[
                :, 0:HD
            ].astype(BF16)

        @pl.when(upper == 1)
        def upper_values():
            out_ref[
                pl.ds(pl.multiple_of(group + start - half, k_tile), k_tile), HD : 2 * HD
            ] = pltpu.roll(value_acc[...], HD, 1)[:, HD : 2 * HD].astype(BF16)

        return carried

    lax.fori_loop(0, group // k_tile, one_tile, 0)

    def finish(i, carried):
        rows = pl.ds(pl.multiple_of(i * piece, piece), piece)
        turned = query_grad_s[:, rows] * scaling
        out_ref[rows, 0:HD] = (
            jnp.concatenate([turned, jnp.zeros((HD, piece), F32)], axis=0).T[:, 0:HD].astype(BF16)
        )
        return carried

    lax.fori_loop(0, group // piece, finish, 0)


def attend_back(z_, ends, packed, grads, outt, lse):
    q_tile, k_tile = 512, 512
    group = z_.group
    return pl.pallas_call(
        functools.partial(attend_back_kernel, z_, q_tile, k_tile),
        out_shape=jax.ShapeDtypeStruct((group + group // 2, 2 * HD), BF16),
        in_specs=[pl.BlockSpec(memory_space=pltpu.SMEM)] + [vmem()] * 4,
        out_specs=vmem(),
        scratch_shapes=[
            pltpu.VMEM((2 * HD, group), BF16),
            pltpu.VMEM((HD, group), BF16),
            pltpu.VMEM((group, 2 * HD), BF16),
            pltpu.VMEM((group, 2 * HD), BF16),
            pltpu.VMEM((3 * HD, group), BF16),
            pltpu.VMEM((8, group), F32),
            pltpu.VMEM((HD, group), F32),
            pltpu.VMEM((k_tile, 2 * HD), F32),
            pltpu.VMEM((k_tile, 2 * HD), F32),
        ],
        compiler_params=pltpu.CompilerParams(vmem_limit_bytes=VMEM_BYTES),
        name="attend_back",
    )(ends, packed, grads, outt, lse)


def adam_step(weight, gradient, moment, squared, rate_now):
    first = BETA_FIRST * moment + (1.0 - BETA_FIRST) * gradient
    second = BETA_SECOND * squared + (1.0 - BETA_SECOND) * gradient * gradient
    corrected = first / (1.0 - BETA_FIRST**STEP)
    spread = jnp.sqrt(second / (1.0 - BETA_SECOND**STEP))
    return (weight - rate_now * (corrected / (spread + ADAM_EPS) + DECAY * weight), first, second)


def update_all(weights, gradients, moments, squares, rates):
    results = []
    for weight, gradient, moment, squared, rate_now in zip(
        weights, gradients, moments, squares, rates
    ):
        results.extend(adam_step(weight, gradient, moment, squared, rate_now))
    return results


def exact_gelu(values):
    return jax.nn.gelu(values, approximate=False)


def by_chip(z_, weight):
    rows = weight.shape[0]
    split = weight.reshape(rows, 3, z_.chips, z_.chip_heads, HD)
    pairs = split[:, 0:2].transpose(2, 0, 3, 1, 4).reshape(z_.chips, rows, -1)
    values = split[:, 2].transpose(1, 0, 2, 3).reshape(z_.chips, rows, -1)
    return jnp.concatenate([pairs, values], axis=2)


def from_chips(z_, chunked):
    rows = chunked.shape[1]
    cut = z_.chip_heads * 2 * HD
    pairs = chunked[:, :, :cut].reshape(z_.chips, rows, z_.chip_heads, 2, HD)
    pairs = pairs.transpose(1, 3, 0, 2, 4).reshape(rows, 2, z_.head_width)
    values = chunked[:, :, cut:].reshape(z_.chips, rows, z_.chip_heads, HD)
    values = values.transpose(1, 0, 2, 3).reshape(rows, 1, z_.head_width)
    return jnp.concatenate([pairs, values], axis=1)


def heads_to_tokens(z_, packed):
    parts = packed.shape[0]
    moved = lax.all_to_all(packed, "ctx", split_axis=1, concat_axis=1, tiled=True)
    moved = moved.reshape(parts, z_.heads, z_.share, z_.block, 2 * HD)
    return lax.dynamic_index_in_dim(moved, lax.axis_index("ctx") % z_.share, 2, keepdims=False)


def tokens_to_heads(z_, packed):
    return lax.all_to_all(
        jnp.repeat(packed, z_.share, axis=1), "ctx", split_axis=1, concat_axis=1, tiled=True
    )


def unpack_values(z_, packed):
    split = packed.reshape(4, z_.heads, z_.block, 2, HD)
    return split.transpose(3, 0, 2, 1, 4).reshape(z_.rows, z_.heads, HD)


def pack_values(z_, values):
    split = values.reshape(2, 4, z_.block, z_.heads, HD)
    return split.transpose(1, 3, 2, 0, 4).reshape(4, z_.heads, z_.block, 2 * HD)


def on_device(
    tokens,
    cotangent,
    lengths,
    order,
    qkv_weight,
    attn_weight,
    wide_weight,
    down_weight,
    norm_gains,
    qkv_mean,
    attn_mean,
    wide_mean,
    down_mean,
    gains_mean,
    qkv_square,
    attn_square,
    wide_square,
    down_square,
    gains_square,
):
    z_ = Sizes(
        lax.axis_size("fsdp"),
        lax.axis_size("ctx"),
        tokens.shape[0],
        tokens.shape[1],
        qkv_weight.shape[2],
        wide_weight.shape[2],
    )
    ctx_index = lax.axis_index("ctx")
    in_order, endings = sequence_ends(lengths[0], order[0])
    local_ids = jnp.arange(z_.rows, dtype=jnp.int32)
    cosine, sines = rope_tables(
        positions(in_order, endings, packed_place(local_ids, ctx_index, z_.ctx, z_.block))
    )
    gain_rows = jnp.pad(norm_gains.astype(BF16).astype(F32), ((0, 6), (0, 0)))
    packed, wq_full, wo_full, wi_full, gains_full = project(
        z_,
        tokens,
        gain_rows,
        cosine,
        sines,
        by_chip(z_, qkv_weight.astype(BF16)),
        attn_weight.astype(BF16),
        wide_weight.astype(BF16).transpose(1, 0, 2),
    )
    down_low = lax.all_gather(down_weight.astype(BF16), "fsdp", axis=1, tiled=True)
    attn_low = wo_full.transpose(1, 0, 2).reshape(z_.head_width, z_.width)
    wide_low = wi_full.reshape(2, z_.width, z_.units)
    gains = gains_full.transpose(1, 0, 2).reshape(8, z_.width)
    inputs = tokens.astype(F32)
    normed_one, scaling_one = normalize(inputs)
    entry_one = (normed_one * gains[0][None, :]).astype(BF16)
    packed = packed.reshape(12 * z_.ctx * z_.block, 2 * HD)
    attended_packed, attended_turned, lse = attend(z_, endings, packed)
    attended_low = unpack_values(
        z_, heads_to_tokens(z_, attended_packed.reshape(4, z_.ctx, z_.block, 2 * HD))
    ).reshape(z_.rows, z_.head_width)
    mixed_sum = lax.psum(
        jnp.dot(attended_low, attn_low, preferred_element_type=F32).astype(BF16), "tp"
    ).astype(F32)
    middle = inputs + mixed_sum
    normed_two, scaling_two = normalize(middle)
    entry_two = (normed_two * gains[1][None, :]).astype(BF16)
    gate_up = jnp.einsum("td,kdf->tkf", entry_two, wide_low, preferred_element_type=F32)
    activated, gelu_pull = jax.vjp(exact_gelu, gate_up[:, 0])
    hidden_low = (activated * gate_up[:, 1]).astype(BF16)
    branch = lax.psum(
        jnp.dot(hidden_low, down_low, preferred_element_type=F32).astype(BF16), "tp"
    ).astype(F32)
    output = (middle + branch).astype(BF16)
    grad_out = cotangent.astype(F32)
    down_grad = jnp.einsum("tf,td->fd", hidden_low, cotangent, preferred_element_type=F32)
    hidden_grad = jnp.einsum("td,fd->tf", cotangent, down_low, preferred_element_type=F32)
    act_grad = gelu_pull(hidden_grad * gate_up[:, 1])[0]
    gate_grad = hidden_grad * activated
    gated_grad = jnp.stack([act_grad, gate_grad], axis=1).astype(BF16)
    wide_grad = jnp.einsum("td,tkf->dkf", entry_two, gated_grad, preferred_element_type=F32)
    back_two = lax.psum(
        jnp.einsum("tkf,kdf->td", gated_grad, wide_low, preferred_element_type=F32).astype(BF16),
        "tp",
    ).astype(F32)
    gain_second = jnp.sum(back_two * normed_two, axis=0)
    middle_grad = grad_out + norm_back(back_two * gains[1][None, :], normed_two, scaling_two)
    middle_low = middle_grad.astype(BF16)
    attn_grad = jnp.einsum("tf,td->fd", attended_low, middle_low, preferred_element_type=F32)
    attended_grad = (
        jnp.einsum("td,fd->tf", middle_low, attn_low, preferred_element_type=F32)
        .astype(BF16)
        .reshape(z_.rows, z_.heads, HD)
    )
    grads_packed = tokens_to_heads(z_, pack_values(z_, attended_grad))
    head_grads = attend_back(
        z_,
        endings,
        packed,
        grads_packed.reshape(z_.group // 2, 2 * HD),
        attended_turned,
        lse,
    )
    token_grads = heads_to_tokens(z_, head_grads.reshape(12, z_.ctx, z_.block, 2 * HD))
    pair_grad = token_grads[0:8].transpose(0, 2, 1, 3).reshape(z_.rows * z_.heads, 2 * HD)
    pair_grad = pair_grad.astype(F32)
    lane = jnp.arange(2 * HD)
    swapped = jnp.where(
        lane % HD < HD // 2,
        jnp.roll(pair_grad, -(HD // 2), axis=1),
        jnp.roll(pair_grad, HD // 2, axis=1),
    )
    wide_cos = jnp.repeat(cosine, z_.heads, axis=0)
    wide_sin = jnp.repeat(sines, z_.heads, axis=0)
    pair_grad = (pair_grad * wide_cos - swapped * wide_sin).astype(BF16)
    pair_grad = pair_grad.reshape(z_.rows, z_.chips, z_.chip_heads * 2 * HD)
    value_grad = unpack_values(z_, token_grads[8:12]).reshape(
        z_.rows, z_.chips, z_.chip_heads * HD
    )
    projected_grad = jnp.concatenate([pair_grad, value_grad], axis=2)
    wq_flat = wq_full.reshape(z_.chips, z_.width, z_.chunk)
    qkv_grad = jnp.einsum("td,tpc->pdc", entry_one, projected_grad, preferred_element_type=F32)
    back_one = lax.psum(
        jnp.einsum("tpc,pdc->td", projected_grad, wq_flat, preferred_element_type=F32).astype(BF16),
        "tp",
    ).astype(F32)
    gain_first = jnp.sum(back_one * normed_one, axis=0)
    input_grad = (
        middle_grad + norm_back(back_one * gains[0][None, :], normed_one, scaling_one)
    ).astype(BF16)
    gains_grad = jnp.stack([gain_first, gain_second])
    rates = (D ** (-0.5), RATE_ATTN, D ** (-0.5), FF ** (-0.5), RATE_GAIN)
    shards = [
        lax.psum_scatter(g.astype(BF16), "fsdp", scatter_dimension=axis, tiled=True)
        for g, axis in (
            (qkv_grad, 1),
            (attn_grad, 1),
            (wide_grad, 0),
            (down_grad, 1),
            (gains_grad, 1),
        )
    ]
    shards = [lax.psum(g, "ctx").astype(F32) for g in shards]
    shards[0] = from_chips(z_, shards[0])
    final = update_all(
        (qkv_weight, attn_weight, wide_weight, down_weight, norm_gains),
        shards,
        (qkv_mean, attn_mean, wide_mean, down_mean, gains_mean),
        (qkv_square, attn_square, wide_square, down_square, gains_square),
        rates,
    )
    return (output, input_grad) + tuple(final)


def solution(mesh):
    return jax.shard_map(
        on_device,
        mesh=mesh,
        in_specs=(
            P(("fsdp", "ctx"), None),
            P(("fsdp", "ctx"), None),
            P("fsdp", None),
            P("fsdp", None),
            P("fsdp", None, "tp"),
            P("tp", "fsdp"),
            P("fsdp", None, "tp"),
            P("tp", "fsdp"),
            P(None, "fsdp"),
            P("fsdp", None, "tp"),
            P("tp", "fsdp"),
            P("fsdp", None, "tp"),
            P("tp", "fsdp"),
            P(None, "fsdp"),
            P("fsdp", None, "tp"),
            P("tp", "fsdp"),
            P("fsdp", None, "tp"),
            P("tp", "fsdp"),
            P(None, "fsdp"),
        ),
        out_specs=(
            P(("fsdp", "ctx"), None),
            P(("fsdp", "ctx"), None),
            P("fsdp", None, "tp"),
            P("fsdp", None, "tp"),
            P("fsdp", None, "tp"),
            P("tp", "fsdp"),
            P("tp", "fsdp"),
            P("tp", "fsdp"),
            P("fsdp", None, "tp"),
            P("fsdp", None, "tp"),
            P("fsdp", None, "tp"),
            P("tp", "fsdp"),
            P("tp", "fsdp"),
            P("tp", "fsdp"),
            P(None, "fsdp"),
            P(None, "fsdp"),
            P(None, "fsdp"),
        ),
        check_vma=False,
    )
```

```python
import functools

import jax
import jax.numpy as jnp
from jax import lax
from jax.experimental import pallas as pl
from jax.experimental.pallas import tpu as pltpu
from jax.sharding import PartitionSpec as P

D = 1024
HD = 64
FF = 2624
STEP = 10


NORM_EPS = 1e-05
ROPE_BASE = 160000.0
BETA_FIRST = 0.9
BETA_SECOND = 0.98
ADAM_EPS = 1e-06
DECAY = 0.01
RATE_ATTN = 0.5
RATE_GAIN = 0.8
MASKED = -1e30

MESH = pl.DeviceIdType.MESH
BF16 = jnp.bfloat16
F32 = jnp.float32
VMEM_BYTES = 60 * 2**20


class Sizes:
    def __init__(self, fsdp, ctx, rows, width, head_width, units):
        self.fsdp = fsdp
        self.ctx = ctx
        self.chips = ctx // 2
        self.rows = rows
        self.block = rows // 8
        self.group = rows * ctx
        self.width = width
        self.shard = width // fsdp
        self.heads = head_width // HD
        self.head_width = head_width
        self.units = units
        self.share = max(1, ctx // self.heads)
        self.chip_heads = max(1, self.heads // self.chips)
        self.chunk = self.chip_heads * 3 * HD


def remote(src, dst, send, recv, device):
    return pltpu.make_async_remote_copy(
        src_ref=src,
        dst_ref=dst,
        send_sem=send,
        recv_sem=recv,
        device_id=device,
        device_id_type=MESH,
    )


def greet(devices):
    barrier = pltpu.get_barrier_semaphore()
    for device in devices:
        pl.semaphore_signal(barrier, inc=1, device_id=device, device_id_type=MESH)
    pl.semaphore_wait(barrier, len(devices))


def vmem():
    return pl.BlockSpec(memory_space=pltpu.VMEM)


def anywhere():
    return pl.BlockSpec(memory_space=pl.ANY)


def normalize(values):
    centered = values - jnp.mean(values, axis=1, keepdims=True)
    scaling = lax.rsqrt(jnp.mean(centered * centered, axis=1, keepdims=True) + NORM_EPS)
    return (centered * scaling, scaling)


def norm_back(grad_hat, normed, scaling):
    return scaling * (
        grad_hat
        - jnp.mean(grad_hat, axis=1, keepdims=True)
        - normed * jnp.mean(grad_hat * normed, axis=1, keepdims=True)
    )


def swap_halves(values):
    lane = lax.broadcasted_iota(jnp.int32, values.shape, 1)
    return jnp.where(
        lane % HD < HD // 2, pltpu.roll(values, 2 * HD - HD // 2, 1), pltpu.roll(values, HD // 2, 1)
    )


def packed_place(local_row, device, devices, block_size):
    return (local_row // block_size * devices + device) * block_size + local_row % block_size


def sequence_ends(lengths_row, order_row):
    count_seqs = lengths_row.shape[0]
    chosen = (order_row[:, None] == jnp.arange(count_seqs, dtype=jnp.int32)[None, :]).astype(
        jnp.int32
    )
    in_order = jnp.sum(chosen * lengths_row[None, :], axis=1)
    return (in_order, jnp.cumsum(in_order))


def positions(in_order, endings, places):
    passed = (endings[None, :] <= places[:, None]).astype(jnp.int32)
    return places - jnp.sum(passed * in_order[None, :], axis=1)


def rope_tables(position):
    half_size = HD // 2
    frequency = ROPE_BASE ** (-(2.0 * jnp.arange(half_size, dtype=jnp.float32)) / (2.0 * half_size))
    angles = position.astype(jnp.float32)[:, None] * frequency[None, :]
    cosine, sines = jnp.cos(angles), jnp.sin(angles)
    return (
        jnp.concatenate([cosine] * 4, axis=1),
        jnp.concatenate([-sines, sines, -sines, sines], axis=1),
    )


def project_kernel(
    z_,
    tok_ref,
    gain_ref,
    cos_ref,
    sin_ref,
    wq_ref,
    wo_ref,
    wi_ref,
    packed_ref,
    wq_out,
    wo_out,
    wi_out,
    gain_out,
    entry_s,
    wq_s,
    send_s,
    gain_s,
    gain_send,
    gain_recv,
    wq_send,
    wq_recv,
    wq_fsend,
    wq_frecv,
    w_send,
    w_recv,
    w_fsend,
    w_frecv,
    a_send,
    a_recv,
    local_sem,
):
    f, c, t = lax.axis_index("fsdp"), lax.axis_index("ctx"), lax.axis_index("tp")
    core = lax.rem(c, 2)
    chip = c // 2
    mate = (f, c + 1 - 2 * core, t)
    others = range(1, z_.fsdp)

    def ahead(k):
        return lax.rem(f + k, z_.fsdp)

    def behind(k):
        return lax.rem(f + z_.fsdp - k, z_.fsdp)

    def chip_of(s):
        return lax.rem(chip + 1 + s, z_.chips)

    greet(
        [(ahead(k), c, t) for k in others]
        + [(f, lax.rem(c + j, z_.ctx), t) for j in range(1, z_.ctx)]
    )

    half = z_.shard // 2

    def gain_copy(k, owner):
        return remote(
            gain_ref, gain_s.at[owner], gain_send.at[k - 1], gain_recv.at[k - 1], (ahead(k), c, t)
        )

    def wq_copy(s, k, owner):
        p = chip_of(s)
        rows = pl.ds(pl.multiple_of(core * half, half), half)
        return remote(
            wq_ref.at[p, rows],
            wq_s.at[p, owner, rows],
            wq_send.at[s, k - 1],
            wq_recv.at[s, k - 1],
            (ahead(k), c, t),
        )

    def wq_pass(s, k, side):
        p = chip_of(s)
        rows = pl.ds(pl.multiple_of(side * half, half), half)
        place = wq_s.at[p, behind(k), rows]
        return remote(place, place, wq_fsend.at[s, k - 1], wq_frecv.at[s, k - 1], mate)

    attn_half = z_.head_width // 2

    def wo_copy(k, owner):
        rows = pl.ds(pl.multiple_of(core * attn_half, attn_half), attn_half)
        return remote(
            wo_ref.at[rows],
            wo_out.at[owner, rows],
            w_send.at[0, k - 1],
            w_recv.at[0, k - 1],
            (ahead(k), c, t),
        )

    def wo_pass(k, side):
        rows = pl.ds(pl.multiple_of(side * attn_half, attn_half), attn_half)
        place = wo_out.at[behind(k), rows]
        return remote(place, place, w_fsend.at[0, k - 1], w_frecv.at[0, k - 1], mate)

    def wi_copy(k, owner):
        return remote(
            wi_ref.at[core],
            wi_out.at[core, owner],
            w_send.at[1, k - 1],
            w_recv.at[1, k - 1],
            (ahead(k), c, t),
        )

    def wi_pass(k, side):
        place = wi_out.at[side, behind(k)]
        return remote(place, place, w_fsend.at[1, k - 1], w_frecv.at[1, k - 1], mate)

    def head_copy(s, side, source):
        p = chip_of(s)
        return remote(
            send_s.at[s, side % z_.chip_heads],
            packed_ref.at[:, source],
            a_send.at[s, side],
            a_recv.at[s, core],
            (f, 2 * p + side, t),
        )

    def head_arrival(s, side):
        source = 2 * lax.rem(chip + 2 * z_.chips - 1 - s, z_.chips) + side
        return remote(
            send_s.at[s, 0], packed_ref.at[:, source], a_send.at[s, 0], a_recv.at[s, side], mate
        )

    for k in others:
        gain_copy(k, f).start()
    for k in others:
        wq_copy(0, k, f).start()
    own_wq = pltpu.make_async_copy(wq_ref, wq_s.at[:, f], local_sem.at[0])
    own_wo = pltpu.make_async_copy(wo_ref, wo_out.at[f], local_sem.at[1])
    own_wi = pltpu.make_async_copy(wi_ref, wi_out.at[:, f], local_sem.at[2])
    own_wq.start()
    own_wo.start()
    own_wi.start()
    gain_s[f] = gain_ref[...]
    for k in others:
        wq_copy(1, k, f).start()
    for k in others:
        gain_copy(k, behind(k)).wait()

    gain_out[...] = gain_s[...]
    tile = min(128, z_.rows)

    def norm_tile(i, carried):
        rows = pl.ds(pl.multiple_of(i * tile, tile), tile)
        normed, nothing = normalize(tok_ref[rows, :].astype(F32))
        for g in range(z_.fsdp):
            columns = slice(g * z_.shard, (g + 1) * z_.shard)
            entry_s[g, rows, :] = (normed[:, columns] * gain_s[g, 0:1, :]).astype(BF16)
        return carried

    lax.fori_loop(0, z_.rows // tile, norm_tile, 0)
    own_wq.wait()

    def chunk_step(s, carried):
        for k in others:

            @pl.when(s + 2 < z_.chips)
            def more():
                wq_copy(s + 2, k, f).start()

            @pl.when(s + 2 == z_.chips)
            def attn_part():
                wo_copy(k, f).start()

            @pl.when(s + 1 == z_.chips)
            def wide_part():
                wi_copy(k, f).start()

            arrived = wq_copy(s, k, behind(k))
            arrived.wait_recv()
            wq_pass(s, k, core).start()
        for k in others:
            wq_pass(s, k, 1 - core).wait_recv()
        p = chip_of(s)
        total = jnp.zeros((z_.rows, z_.chunk), F32)
        for g in range(z_.fsdp):
            total = total + jnp.dot(entry_s[g], wq_s[p, g], preferred_element_type=F32)
        for i in range(z_.chip_heads):
            pair = total[:, 2 * HD * i : 2 * HD * (i + 1)]
            pair = pair * cos_ref[...] + swap_halves(pair) * sin_ref[...]
            send_s[s, i, 0:8] = pair.astype(BF16).reshape(8, z_.block, 2 * HD)
            start = z_.chip_heads * 2 * HD + HD * i
            value = total[:, start : start + HD]
            value = jnp.concatenate([value[: z_.rows // 2], value[z_.rows // 2 :]], axis=1)
            send_s[s, i, 8:12] = value.astype(BF16).reshape(4, z_.block, 2 * HD)

        @pl.when(s < z_.chips - 1)
        def away():
            for side in range(2):
                head_copy(s, side, c).start()

        return carried

    lax.fori_loop(0, z_.chips, chunk_step, 0)
    last = z_.chips - 1
    kept = pltpu.make_async_copy(
        send_s.at[last, lax.rem(core, z_.chip_heads)], packed_ref.at[:, c], local_sem.at[3]
    )
    kept.start()
    crossed = remote(
        send_s.at[last, lax.rem(1 - core, z_.chip_heads)],
        packed_ref.at[:, c],
        a_send.at[last, 0],
        a_recv.at[last, 0],
        mate,
    )
    crossed.start()
    keep_wq = pltpu.make_async_copy(wq_s, wq_out, local_sem.at[4])
    keep_wq.start()
    for k in others:
        wo_copy(k, behind(k)).wait_recv()
        wo_pass(k, core).start()
    for k in others:
        wi_copy(k, behind(k)).wait_recv()
        wi_pass(k, core).start()
    for s in range(z_.chips - 1):
        for side in range(2):
            head_arrival(s, side).wait_recv()
            head_copy(s, side, c).wait_send()
    crossed_in = remote(
        send_s.at[last, 0],
        packed_ref.at[:, c + 1 - 2 * core],
        a_send.at[last, 0],
        a_recv.at[last, 0],
        mate,
    )
    crossed_in.wait_recv()
    crossed.wait_send()
    for k in others:
        for s in range(z_.chips):
            wq_copy(s, k, f).wait_send()
            wq_pass(s, k, core).wait_send()
        wo_copy(k, f).wait_send()
        wi_copy(k, f).wait_send()
        wo_pass(k, core).wait_send()
        wi_pass(k, core).wait_send()
        wo_pass(k, 1 - core).wait_recv()
        wi_pass(k, 1 - core).wait_recv()
    kept.wait()
    keep_wq.wait()
    own_wo.wait()
    own_wi.wait()


def project(z_, tokens, gains, cosine, sines, wq, wo, wi):
    peers = max(1, z_.fsdp - 1)
    dma = pltpu.SemaphoreType.DMA
    return pl.pallas_call(
        functools.partial(project_kernel, z_),
        out_shape=(
            jax.ShapeDtypeStruct((12, z_.ctx, z_.block, 2 * HD), BF16),
            jax.ShapeDtypeStruct((z_.chips, z_.fsdp, z_.shard, z_.chunk), BF16),
            jax.ShapeDtypeStruct((z_.fsdp, z_.head_width, z_.shard), BF16),
            jax.ShapeDtypeStruct((2, z_.fsdp, z_.shard, z_.units), BF16),
            jax.ShapeDtypeStruct((z_.fsdp, 8, z_.shard), F32),
        ),
        in_specs=[vmem()] * 5 + [anywhere()] * 2,
        out_specs=(anywhere(), anywhere(), anywhere(), anywhere(), vmem()),
        scratch_shapes=[
            pltpu.VMEM((z_.fsdp, z_.rows, z_.shard), BF16),
            pltpu.VMEM((z_.chips, z_.fsdp, z_.shard, z_.chunk), BF16),
            pltpu.VMEM((z_.chips, z_.chip_heads, 12, z_.block, 2 * HD), BF16),
            pltpu.VMEM((z_.fsdp, 8, z_.shard), F32),
            dma((peers,)),
            dma((peers,)),
            dma((z_.chips, peers)),
            dma((z_.chips, peers)),
            dma((z_.chips, peers)),
            dma((z_.chips, peers)),
            dma((2, peers)),
            dma((2, peers)),
            dma((2, peers)),
            dma((2, peers)),
            dma((z_.chips, 2)),
            dma((z_.chips, 2)),
            dma((5,)),
        ],
        compiler_params=pltpu.CompilerParams(
            collective_id=0, has_side_effects=True, vmem_limit_bytes=VMEM_BYTES
        ),
        name="project",
    )(tokens, gains, cosine, sines, wq, wo, wi)


def sequence_at(ends_ref, place):
    start, end = jnp.int32(0), ends_ref[0]
    for k in range(ends_ref.shape[0] - 1):
        past = ends_ref[k] <= place
        start = jnp.where(past, ends_ref[k], start)
        end = jnp.where(past, ends_ref[k + 1], end)
    return (start, end)


def segments_of(ends_ref, places):
    segment = jnp.zeros(places.shape, jnp.int32)
    for k in range(ends_ref.shape[0]):
        segment = segment + (ends_ref[k] <= places).astype(jnp.int32)
    return segment


def attend_kernel(
    z_,
    q_tile,
    k_tile,
    ends_ref,
    packed_ref,
    out_ref,
    outt_ref,
    lse_ref,
    query_s,
    value_s,
    top_s,
    total_s,
):
    group = z_.group
    half = group // 2
    piece = min(512, half)
    scaling = HD ** (-0.5)
    sums = 16
    packed_ref = packed_ref.reshape(group + half, 2 * HD)
    out_ref = out_ref.reshape(half, 2 * HD)
    query_s[0:HD, :] = jnp.zeros((HD, group), BF16)
    value_s[HD : HD + sums, :] = jnp.ones((sums, group), BF16)

    def prepare(i, carried):
        rows = pl.ds(pl.multiple_of(i * piece, piece), piece)
        turned = packed_ref[rows, :].astype(F32).T
        query_s[HD : 2 * HD, rows] = (turned[0:HD] * scaling).astype(BF16)

        @pl.when(i < half // piece)
        def values():
            turned_value = (
                packed_ref[pl.ds(pl.multiple_of(group + i * piece, piece), piece), :].astype(F32).T
            ).astype(BF16)
            value_s[0:HD, rows] = turned_value[0:HD]
            value_s[0:HD, pl.ds(pl.multiple_of(half + i * piece, piece), piece)] = turned_value[
                HD : 2 * HD
            ]

        return carried

    lax.fori_loop(0, group // piece, prepare, 0)

    def one_tile(i, carried):
        first = pl.multiple_of(i * q_tile, q_tile)
        columns = pl.ds(first, q_tile)
        low, low_end = sequence_at(ends_ref, first)
        high_start, high = sequence_at(ends_ref, first + q_tile - 1)
        single = low == high_start
        top_s[...] = jnp.full(top_s.shape, MASKED, F32)
        total_s[...] = jnp.zeros(total_s.shape, F32)

        def one_step(j, masked):
            start = pl.multiple_of(j * k_tile, k_tile)
            rows = pl.ds(start, k_tile)
            scores = jnp.dot(packed_ref[rows, :], query_s[:, columns], preferred_element_type=F32)
            if masked:
                key_seg = segments_of(
                    ends_ref, start + lax.broadcasted_iota(jnp.int32, (k_tile, 1), 0)
                )
                query_seg = segments_of(
                    ends_ref, first + lax.broadcasted_iota(jnp.int32, (1, q_tile), 1)
                )
                scores = jnp.where(key_seg == query_seg, scores, MASKED)
            before = top_s[0:1, :]
            after = jnp.maximum(before, jnp.max(scores, axis=0, keepdims=True))
            weights = jnp.exp(scores - after).astype(BF16)
            top_s[0:1, :] = after
            total_s[...] = total_s[...] * jnp.exp(before - after) + jnp.dot(
                value_s[:, rows], weights, preferred_element_type=F32
            )

        def step(j, inner):
            start = j * k_tile
            whole = single & (start >= low) & (start + k_tile <= high)

            @pl.when(whole)
            def plain():
                one_step(j, False)

            @pl.when(jnp.logical_not(whole))
            def partial():
                one_step(j, True)

            return inner

        lax.fori_loop(low // k_tile, (high + k_tile - 1) // k_tile, step, 0)
        summed = total_s[HD : HD + 1, :]
        lse_ref[:, columns] = jnp.broadcast_to(top_s[0:1, :] + jnp.log(summed), (8, q_tile))
        outt_ref[:, columns] = total_s[0:HD, :] / summed
        return carried

    lax.fori_loop(0, group // q_tile, one_tile, 0)

    def finish(i, carried):
        rows = pl.ds(pl.multiple_of(i * piece, piece), piece)
        later = pl.ds(pl.multiple_of(half + i * piece, piece), piece)
        both = jnp.concatenate([outt_ref[:, rows], outt_ref[:, later]], axis=0)
        out_ref[rows, :] = both.T.astype(BF16)
        return carried

    lax.fori_loop(0, half // piece, finish, 0)


def attend(z_, ends, packed):
    q_tile, k_tile = 512, 512
    group = z_.group
    return pl.pallas_call(
        functools.partial(attend_kernel, z_, q_tile, k_tile),
        out_shape=(
            jax.ShapeDtypeStruct((4, z_.ctx, z_.block, 2 * HD), BF16),
            jax.ShapeDtypeStruct((HD, group), F32),
            jax.ShapeDtypeStruct((8, group), F32),
        ),
        in_specs=[pl.BlockSpec(memory_space=pltpu.SMEM), vmem()],
        out_specs=(vmem(), vmem(), vmem()),
        scratch_shapes=[
            pltpu.VMEM((2 * HD, group), BF16),
            pltpu.VMEM((HD + 16, group), BF16),
            pltpu.VMEM((8, q_tile), F32),
            pltpu.VMEM((HD + 16, q_tile), F32),
        ],
        compiler_params=pltpu.CompilerParams(vmem_limit_bytes=VMEM_BYTES),
        name="attend",
    )(ends, packed)


def attend_back_kernel(
    z_,
    q_tile,
    k_tile,
    ends_ref,
    packed_ref,
    grad_ref,
    outt_ref,
    lse_ref,
    out_ref,
    query_s,
    key_s,
    swapped_s,
    grad_s,
    gradt_s,
    delta_s,
    query_grad_s,
    key_acc,
    value_acc,
):
    group = z_.group
    half = group // 2
    piece = min(512, half)
    scaling = HD ** (-0.5)
    packed_ref = packed_ref.reshape(group + half, 2 * HD)
    grad_ref = grad_ref.reshape(half, 2 * HD)
    out_ref = out_ref.reshape(group + half, 2 * HD)
    query_s[0:HD, :] = jnp.zeros((HD, group), BF16)
    gradt_s[0:HD, :] = jnp.zeros((HD, group), BF16)
    gradt_s[2 * HD : 3 * HD, :] = jnp.zeros((HD, group), BF16)

    def prepare(i, carried):
        rows = pl.ds(pl.multiple_of(i * piece, piece), piece)
        pair = packed_ref[rows, :].astype(F32)
        turned = pair.T
        query_s[HD : 2 * HD, rows] = (turned[0:HD] * scaling).astype(BF16)
        key_s[:, rows] = turned[HD : 2 * HD].astype(BF16)
        swapped_s[rows, :] = pltpu.roll(pair, HD, 1).astype(BF16)
        query_grad_s[:, rows] = jnp.zeros((HD, piece), F32)

        @pl.when(i < half // piece)
        def grads():
            later = pl.ds(pl.multiple_of(half + i * piece, piece), piece)
            both = grad_ref[rows, :].astype(F32)
            turned_grad = both.T
            grad_s[rows, :] = both.astype(BF16)
            grad_s[later, :] = pltpu.roll(both, HD, 1).astype(BF16)
            for place, part in ((rows, turned_grad[0:HD]), (later, turned_grad[HD : 2 * HD])):
                gradt_s[HD : 2 * HD, place] = part.astype(BF16)
                delta = jnp.sum(part * outt_ref[:, place], axis=0, keepdims=True)
                delta_s[:, place] = jnp.broadcast_to(delta, (8, piece))

        return carried

    lax.fori_loop(0, group // piece, prepare, 0)

    def one_tile(j, carried):
        start = pl.multiple_of(j * k_tile, k_tile)
        rows = pl.ds(start, k_tile)
        upper = (start >= half).astype(jnp.int32)
        value_rows = pl.ds(pl.multiple_of(group + start - upper * half, k_tile), k_tile)
        turned_rows = pl.ds(pl.multiple_of(HD - upper * HD, HD), 2 * HD)
        low, low_end = sequence_at(ends_ref, start)
        high_start, high = sequence_at(ends_ref, start + k_tile - 1)
        single = low == high_start
        key_acc[...] = jnp.zeros(key_acc.shape, F32)
        value_acc[...] = jnp.zeros(value_acc.shape, F32)

        def one_step(i, masked):
            first = pl.multiple_of(i * q_tile, q_tile)
            columns = pl.ds(first, q_tile)
            scores = jnp.dot(packed_ref[rows, :], query_s[:, columns], preferred_element_type=F32)
            chances = jnp.exp(scores - lse_ref[0:1, columns])
            if masked:
                key_seg = segments_of(
                    ends_ref, start + lax.broadcasted_iota(jnp.int32, (k_tile, 1), 0)
                )
                query_seg = segments_of(
                    ends_ref, first + lax.broadcasted_iota(jnp.int32, (1, q_tile), 1)
                )
                chances = jnp.where(key_seg == query_seg, chances, 0.0)
            chance_grad = jnp.dot(
                packed_ref[value_rows, :],
                gradt_s[turned_rows, columns],
                preferred_element_type=F32,
            )
            score_grad = (chances * (chance_grad - delta_s[0:1, columns])).astype(BF16)
            value_acc[...] += jnp.dot(
                chances.astype(BF16), grad_s[columns, :], preferred_element_type=F32
            )
            key_acc[...] += jnp.dot(
                score_grad, swapped_s[columns, :], preferred_element_type=F32
            )
            query_grad_s[:, columns] += jnp.dot(
                key_s[:, rows], score_grad, preferred_element_type=F32
            )

        def step(i, inner):
            first = i * q_tile
            whole = single & (first >= low) & (first + q_tile <= high)

            @pl.when(whole)
            def plain():
                one_step(i, False)

            @pl.when(jnp.logical_not(whole))
            def partial():
                one_step(i, True)

            return inner

        lax.fori_loop(low // q_tile, (high + q_tile - 1) // q_tile, step, 0)
        out_ref[rows, HD : 2 * HD] = (key_acc[:, HD : 2 * HD] * scaling).astype(BF16)

        @pl.when(upper == 0)
        def lower_values():
            out_ref[pl.ds(pl.multiple_of(group + start, k_tile), k_tile), 0:HD] = value_acc[
                :, 0:HD
            ].astype(BF16)

        @pl.when(upper == 1)
        def upper_values():
            out_ref[
                pl.ds(pl.multiple_of(group + start - half, k_tile), k_tile), HD : 2 * HD
            ] = pltpu.roll(value_acc[...], HD, 1)[:, HD : 2 * HD].astype(BF16)

        return carried

    lax.fori_loop(0, group // k_tile, one_tile, 0)

    def finish(i, carried):
        rows = pl.ds(pl.multiple_of(i * piece, piece), piece)
        turned = query_grad_s[:, rows] * scaling
        out_ref[rows, 0:HD] = (
            jnp.concatenate([turned, jnp.zeros((HD, piece), F32)], axis=0).T[:, 0:HD].astype(BF16)
        )
        return carried

    lax.fori_loop(0, group // piece, finish, 0)


def attend_back(z_, ends, packed, grads, outt, lse):
    q_tile, k_tile = 512, 512
    group = z_.group
    return pl.pallas_call(
        functools.partial(attend_back_kernel, z_, q_tile, k_tile),
        out_shape=jax.ShapeDtypeStruct((12, z_.ctx, z_.block, 2 * HD), BF16),
        in_specs=[pl.BlockSpec(memory_space=pltpu.SMEM)] + [vmem()] * 4,
        out_specs=vmem(),
        scratch_shapes=[
            pltpu.VMEM((2 * HD, group), BF16),
            pltpu.VMEM((HD, group), BF16),
            pltpu.VMEM((group, 2 * HD), BF16),
            pltpu.VMEM((group, 2 * HD), BF16),
            pltpu.VMEM((3 * HD, group), BF16),
            pltpu.VMEM((8, group), F32),
            pltpu.VMEM((HD, group), F32),
            pltpu.VMEM((k_tile, 2 * HD), F32),
            pltpu.VMEM((k_tile, 2 * HD), F32),
        ],
        compiler_params=pltpu.CompilerParams(vmem_limit_bytes=VMEM_BYTES),
        name="attend_back",
    )(ends, packed, grads, outt, lse)


def cuts_of(rows, count):
    unit = rows // 16
    marks = [16 * (unit * i // count) for i in range(count + 1)]
    return [(a, b - a) for a, b in zip(marks, marks[1:]) if b > a]


def over_rows(start, rows, step, body):
    whole = rows // step

    def turn(i, carried):
        body(pl.multiple_of(start + i * step, 16), step)
        return carried

    if whole > 1:
        lax.fori_loop(0, whole, turn, 0)
    elif whole == 1:
        body(start, step)
    if rows % step:
        body(start + whole * step, rows % step)


class Item:
    def __init__(self, number, rows, columns, cuts):
        self.number = number
        self.rows = rows
        self.columns = columns
        self.cuts = cuts_of(rows, cuts)


class Reducer:
    def __init__(self, z_, items, refs, sems):
        self.z_ = z_
        self.items = items
        self.refs = refs
        self.sems = sems
        f, c, t = lax.axis_index("fsdp"), lax.axis_index("ctx"), lax.axis_index("tp")
        self.f, self.c, self.t = f, c, t
        self.core = lax.rem(c, 2)
        self.chip = c // 2
        self.mate = (f, c + 1 - 2 * self.core, t)
        middle = z_.chips // 2
        low = self.chip < middle
        self.is_mid = (self.chip == middle - 1) | (self.chip == middle)
        self.has_outer = (self.chip > 0) & (self.chip < z_.chips - 1)
        towards = jnp.where(low, 2, -2)
        self.inner = (f, c + towards, t)
        self.outer = (f, c - towards, t)
        self.numbers = {}
        for item in items:
            for cut in range(len(item.cuts)):
                self.numbers[(item.number, cut)] = len(self.numbers)

    def ahead(self, k):
        return lax.rem(self.f + k, self.z_.fsdp)

    def behind(self, k):
        return lax.rem(self.f + self.z_.fsdp - k, self.z_.fsdp)


    def core_copy(self, item):
        source, own, mate_in = self.refs[item.number][:3]
        n = item.number
        return remote(
            source.at[:, 1 - self.core],
            mate_in,
            self.sems["core_send"].at[n],
            self.sems["core_recv"].at[n],
            self.mate,
        )

    def own_copy(self, item):
        source, own = self.refs[item.number][:2]
        return pltpu.make_async_copy(
            source.at[:, self.core], own, self.sems["own"].at[item.number]
        )

    def core_sum(self, item):
        own, mate_in = self.refs[item.number][1:3]
        self.core_copy(item).wait_recv()
        for g in range(self.z_.fsdp):

            def add(first, rows, g=g):
                place = pl.ds(first, rows)
                own[g, place, :] = (
                    own[g, place, :].astype(F32) + mate_in[g, place, :].astype(F32)
                ).astype(BF16)

            over_rows(0, item.rows, 128, add)


    def peer_copy(self, item, k, owner):
        own, peer_in = self.refs[item.number][1], self.refs[item.number][3]
        return remote(
            own.at[owner],
            peer_in.at[k - 1],
            self.sems["peer_send"].at[item.number, k - 1],
            self.sems["peer_recv"].at[item.number, k - 1],
            (self.ahead(k), self.c, self.t),
        )

    def peer_start(self, item):
        for k in range(1, self.z_.fsdp):
            self.peer_copy(item, k, self.ahead(k)).start()

    def peer_sum(self, item):
        own, peer_in = self.refs[item.number][1], self.refs[item.number][3]
        for k in range(1, self.z_.fsdp):
            self.peer_copy(item, k, self.ahead(k)).wait_recv()

        def add(first, rows):
            place = pl.ds(first, rows)
            total = own[self.f, place, :].astype(F32)
            for k in range(1, self.z_.fsdp):
                total = total + peer_in[k - 1, place, :].astype(F32)
            own[self.f, place, :] = total.astype(BF16)

        over_rows(0, item.rows, 128, add)


    def in_copy(self, item, cut, middle):
        own, peer_in, outer_in, inner_in = self.refs[item.number][1:2] + self.refs[item.number][3:6]
        rows = pl.ds(*item.cuts[cut])
        n = self.numbers[(item.number, cut)]
        if middle:
            target, name = inner_in, "inner_recv"
        else:
            target, name = outer_in, "outer_recv"
        return remote(
            own.at[self.f, rows],
            target.at[rows],
            self.sems["in_send"].at[n],
            self.sems[name].at[n],
            self.inner,
        )

    def out_copy(self, item, cut):
        inner_in = self.refs[item.number][5]
        rows = pl.ds(*item.cuts[cut])
        n = self.numbers[(item.number, cut)]
        return remote(
            inner_in.at[rows],
            inner_in.at[rows],
            self.sems["out_send"].at[n],
            self.sems["inner_recv"].at[n],
            self.outer,
        )

    def done_copy(self, item, cut):
        inner_in, out = self.refs[item.number][5:7]
        rows = pl.ds(*item.cuts[cut])
        n = self.numbers[(item.number, cut)]
        return remote(
            inner_in.at[rows],
            out.at[self.core, rows],
            self.sems["done_send"].at[n],
            self.sems["done_recv"].at[n],
            self.mate,
        )

    def keep_copy(self, item, cut):
        inner_in, out = self.refs[item.number][5:7]
        rows = pl.ds(*item.cuts[cut])
        n = self.numbers[(item.number, cut)]
        return pltpu.make_async_copy(
            inner_in.at[rows], out.at[self.core, rows], self.sems["keep"].at[n]
        )

    def outermost_start(self, item):
        @pl.when(jnp.logical_not(self.has_outer))
        def first():
            for cut in range(len(item.cuts)):
                self.inward_start(item, cut)

    def inward_start(self, item, cut):
        @pl.when(self.is_mid)
        def cross():
            self.in_copy(item, cut, True).start()

        @pl.when(jnp.logical_not(self.is_mid))
        def along():
            self.in_copy(item, cut, False).start()

    def inward(self, item, cut):
        own, outer_in = self.refs[item.number][1], self.refs[item.number][4]
        first, rows = item.cuts[cut]

        @pl.when(self.has_outer)
        def passed():
            self.in_copy(item, cut, False).wait_recv()

            def add(start, count):
                place = pl.ds(start, count)
                own[self.f, place, :] = (
                    own[self.f, place, :].astype(F32) + outer_in[place, :].astype(F32)
                ).astype(BF16)

            over_rows(first, rows, 128, add)
            self.inward_start(item, cut)

    def outward(self, item, cut):
        own, inner_in = self.refs[item.number][1], self.refs[item.number][5]
        first, rows = item.cuts[cut]
        self.out_copy(item, cut).wait_recv()

        @pl.when(self.is_mid)
        def total():
            def add(start, count):
                place = pl.ds(start, count)
                inner_in[place, :] = (
                    own[self.f, place, :].astype(F32) + inner_in[place, :].astype(F32)
                ).astype(BF16)

            over_rows(first, rows, 128, add)

        @pl.when(self.has_outer)
        def onward():
            self.out_copy(item, cut).start()

        self.done_copy(item, cut).start()
        self.keep_copy(item, cut).start()

    def line(self, parts):
        for i, (item, cut) in enumerate(parts):
            self.inward(item, cut)
            if i:
                self.outward(*parts[i - 1])
        self.outward(*parts[-1])

    def settle(self):
        for item in self.items:
            self.core_copy(item).wait_send()
            for k in range(1, self.z_.fsdp):
                self.peer_copy(item, k, self.ahead(k)).wait_send()
            for cut in range(len(item.cuts)):
                self.in_copy(item, cut, False).wait_send()

                @pl.when(self.has_outer)
                def outwards(item=item, cut=cut):
                    self.out_copy(item, cut).wait_send()

                self.done_copy(item, cut).wait()
                self.keep_copy(item, cut).wait()


def reduce_kernel(
    z_,
    items,
    tok_ref,
    gain_ref,
    cos_ref,
    sin_ref,
    branch_ref,
    middle_ref,
    mgrad_ref,
    gain2_ref,
    heads_ref,
    wq_ref,
    g_down,
    g_wide,
    g_attn,
    out_ref,
    igrad_ref,
    o_down,
    o_wide,
    o_attn,
    o_qkv,
    o_gain,
    *scratch,
):
    down, wide, attn, qkv, gain = items
    scratch = list(scratch)

    def take(count):
        taken = scratch[:count]
        del scratch[:count]
        return taken

    heads_s, wq_s, entry_s, grads_s, branch_s, back_s, back_in = take(7)
    g_qkv, g_gain, gain_acc = take(3)
    groups = [take(5) for item in items]
    (a_send, a_recv, y_send, y_recv, local_sem) = take(5)
    names = (
        "core_send",
        "core_recv",
        "own",
        "peer_send",
        "peer_recv",
        "in_send",
        "outer_recv",
        "inner_recv",
        "out_send",
        "done_send",
        "done_recv",
        "keep",
    )
    sems = dict(zip(names, take(len(names))))
    sources = (g_down, g_wide, g_attn, g_qkv, g_gain)
    outs = (o_down, o_wide, o_attn, o_qkv, o_gain)
    refs = [
        (source, *group, out) for source, group, out in zip(sources, groups, outs)
    ]
    red = Reducer(z_, items, refs, sems)
    f, c, t = red.f, red.c, red.t
    other = (f, c, 1 - t)
    count = z_.ctx // z_.share

    def to_token(j):
        return lax.rem(c + z_.share * j, z_.ctx)

    def from_head(j):
        return lax.rem(c + z_.ctx - z_.share * j, z_.ctx)

    def heads_copy(j):
        return remote(
            heads_ref.at[:, to_token(j)],
            heads_s.at[c // z_.share],
            a_send.at[j],
            a_recv.at[j],
            (f, to_token(j), t),
        )

    def branch_copy():
        return remote(branch_ref, branch_s, y_send.at[0], y_recv.at[0], other)

    def back_copy():
        return remote(back_s, back_in, y_send.at[1], y_recv.at[1], other)

    greet(
        [(red.ahead(k), c, t) for k in range(1, z_.fsdp)]
        + [(f, lax.rem(c + j, z_.ctx), t) for j in range(1, z_.ctx)]
        + [other]
    )
    for j in range(1, count):
        heads_copy(j).start()
    branch_copy().start()
    own_heads = pltpu.make_async_copy(heads_ref.at[:, c], heads_s.at[c // z_.share], local_sem.at[0])
    own_heads.start()
    for item in (down, wide, attn):
        red.core_copy(item).start()
        red.own_copy(item).start()
    load_wq = pltpu.make_async_copy(wq_ref, wq_s, local_sem.at[1])
    load_wq.start()

    for item in (down, wide, attn):
        red.own_copy(item).wait()
        red.core_sum(item)
        red.peer_start(item)

    tile = min(128, z_.rows)

    def entry_tile(i, carried):
        rows = pl.ds(pl.multiple_of(i * tile, tile), tile)
        normed, nothing = normalize(tok_ref[rows, :].astype(F32))
        for g in range(z_.fsdp):
            columns = slice(g * z_.shard, (g + 1) * z_.shard)
            entry_s[g, :, rows] = (normed[:, columns] * gain_ref[g, 0:1, :]).T.astype(BF16)
        return carried

    lax.fori_loop(0, z_.rows // tile, entry_tile, 0)

    red.peer_sum(down)
    red.outermost_start(down)

    branch_copy().wait_recv()

    def output_tile(i, carried):
        rows = pl.ds(pl.multiple_of(i * tile, tile), tile)
        branch = branch_ref[rows, :].astype(F32) + branch_s[rows, :].astype(F32)
        out_ref[rows, :] = (middle_ref[rows, :] + branch).astype(BF16)
        return carried

    lax.fori_loop(0, z_.rows // tile, output_tile, 0)

    own_heads.wait()
    for j in range(1, count):
        remote(
            heads_ref.at[:, c],
            heads_s.at[from_head(j) // z_.share],
            a_send.at[j],
            a_recv.at[j],
            red.mate,
        ).wait_recv()
    load_wq.wait()

    def chunk_grads(p, carried):
        for i in range(z_.chip_heads):
            h = p * z_.chip_heads + i
            pair = heads_s[h, 0:8].reshape(z_.rows, 2 * HD).astype(F32)
            pair = pair * cos_ref[...] - swap_halves(pair) * sin_ref[...]
            grads_s[p, :, 2 * HD * i : 2 * HD * (i + 1)] = pair.astype(BF16)
            value = heads_s[h, 8:12].reshape(z_.rows // 2, 2 * HD).astype(F32)
            start = z_.chip_heads * 2 * HD + HD * i
            grads_s[p, 0 : z_.rows // 2, start : start + HD] = value[:, 0:HD].astype(BF16)
            grads_s[p, z_.rows // 2 :, start : start + HD] = value[:, HD : 2 * HD].astype(BF16)
        return carried

    lax.fori_loop(0, z_.chips, chunk_grads, 0)

    for g in range(z_.fsdp):
        columns = slice(g * z_.shard, (g + 1) * z_.shard)

        def back_tile(i, carried):
            rows = pl.ds(pl.multiple_of(i * tile, tile), tile)
            total = jnp.zeros((tile, z_.shard), F32)
            for p in range(z_.chips):
                total = total + lax.dot_general(
                    grads_s[p, rows, :],
                    wq_s[p, g],
                    (((1,), (1,)), ((), ())),
                    preferred_element_type=F32,
                )
            back_s[rows, columns] = total.astype(BF16)
            return carried

        lax.fori_loop(0, z_.rows // tile, back_tile, 0)
    back_copy().start()

    half = z_.shard // 2

    def qkv_tile(p, carried):
        for g in range(z_.fsdp):
            for side in range(2):
                grad = jnp.dot(
                    entry_s[g, side * half : (side + 1) * half, :],
                    grads_s[p],
                    preferred_element_type=F32,
                )
                rows = pl.ds(pl.multiple_of(p * half, half), half)
                g_qkv[g, side, rows, :] = grad.astype(BF16)
        return carried

    lax.fori_loop(0, z_.chips, qkv_tile, 0)
    red.core_copy(qkv).start()
    red.own_copy(qkv).start()
    red.peer_sum(wide)
    red.outermost_start(wide)
    red.own_copy(qkv).wait()
    red.core_sum(qkv)
    red.peer_start(qkv)
    red.peer_sum(attn)
    red.outermost_start(attn)

    parts = [(item, cut) for item in (down, wide, attn) for cut in range(len(item.cuts))]
    early = len(parts) - 2
    red.line(parts[:early])

    back_copy().wait_recv()
    gain_acc[...] = jnp.zeros(gain_acc.shape, F32)

    def input_tile(i, carried):
        rows = pl.ds(pl.multiple_of(i * tile, tile), tile)
        normed, scaling = normalize(tok_ref[rows, :].astype(F32))
        back = back_s[rows, :].astype(F32) + back_in[rows, :].astype(F32)
        gain_acc[0:1, :] += jnp.sum(back * normed, axis=0, keepdims=True)
        gains = jnp.concatenate([gain_ref[g, 0:1, :] for g in range(z_.fsdp)], axis=1)
        igrad_ref[rows, :] = (
            mgrad_ref[rows, :] + norm_back(back * gains, normed, scaling)
        ).astype(BF16)
        return carried

    lax.fori_loop(0, z_.rows // tile, input_tile, 0)
    top = lax.broadcasted_iota(jnp.int32, (16, z_.shard), 0) == 0
    for g in range(z_.fsdp):
        columns = slice(g * z_.shard, (g + 1) * z_.shard)
        for side, row in ((0, gain_acc[0:1, columns]), (1, gain2_ref[0:1, columns])):
            g_gain[g, side] = jnp.where(top, row, 0.0).astype(BF16)
    red.core_copy(gain).start()
    red.own_copy(gain).start()
    red.peer_sum(qkv)
    red.outermost_start(qkv)
    red.own_copy(gain).wait()
    red.core_sum(gain)
    red.peer_start(gain)
    rest = parts[early:] + [(qkv, cut) for cut in range(len(qkv.cuts))]
    red.line(rest[:2])
    red.peer_sum(gain)
    red.outermost_start(gain)
    red.line(rest[2:] + [(gain, 0)])

    own_sends = [heads_copy(j) for j in range(1, count)] + [branch_copy(), back_copy()]
    for copy in own_sends:
        copy.wait_send()
    red.settle()


def reduce_all(
    z_, tokens, gains, cosine, sines, branch, middle, middle_grad, gain2, heads, wq, g_down, g_wide, g_attn
):
    items = (
        Item(0, z_.units // 2, z_.shard, 2),
        Item(1, z_.shard, z_.units, 4),
        Item(2, z_.head_width // 2, z_.shard, 1),
        Item(3, z_.chips * (z_.shard // 2), z_.chunk, 4),
        Item(4, 16, z_.shard, 1),
    )
    dma = pltpu.SemaphoreType.DMA
    peers = max(1, z_.fsdp - 1)
    pieces = sum(len(item.cuts) for item in items)
    groups = []
    for item in items:
        groups += [
            pltpu.VMEM((z_.fsdp, item.rows, item.columns), BF16),
            pltpu.VMEM((z_.fsdp, item.rows, item.columns), BF16),
            pltpu.VMEM((peers, item.rows, item.columns), BF16),
            pltpu.VMEM((item.rows, item.columns), BF16),
            pltpu.VMEM((item.rows, item.columns), BF16),
        ]
    count = z_.ctx // z_.share
    number = len(items)
    return pl.pallas_call(
        functools.partial(reduce_kernel, z_, items),
        out_shape=(
            jax.ShapeDtypeStruct((z_.rows, z_.width), BF16),
            jax.ShapeDtypeStruct((z_.rows, z_.width), BF16),
        )
        + tuple(jax.ShapeDtypeStruct((2, item.rows, item.columns), BF16) for item in items),
        in_specs=[vmem()] * 8 + [anywhere()] * 5,
        out_specs=tuple([vmem()] * 2 + [anywhere()] * 5),
        scratch_shapes=[
            pltpu.VMEM((z_.heads, 12, z_.block, 2 * HD), BF16),
            pltpu.VMEM((z_.chips, z_.fsdp, z_.shard, z_.chunk), BF16),
            pltpu.VMEM((z_.fsdp, z_.shard, z_.rows), BF16),
            pltpu.VMEM((z_.chips, z_.rows, z_.chunk), BF16),
            pltpu.VMEM((z_.rows, z_.width), BF16),
            pltpu.VMEM((z_.rows, z_.width), BF16),
            pltpu.VMEM((z_.rows, z_.width), BF16),
            pltpu.VMEM((z_.fsdp, 2, items[3].rows, items[3].columns), BF16),
            pltpu.VMEM((z_.fsdp, 2, 16, z_.shard), BF16),
            pltpu.VMEM((8, z_.width), F32),
        ]
        + groups
        + [dma((count,)), dma((count,)), dma((2,)), dma((2,)), dma((2,))]
        + [
            dma((number,)),
            dma((number,)),
            dma((number,)),
            dma((number, peers)),
            dma((number, peers)),
        ]
        + [dma((pieces,))] * 7,
        compiler_params=pltpu.CompilerParams(
            collective_id=1, has_side_effects=True, vmem_limit_bytes=VMEM_BYTES
        ),
        name="reduce",
    )(tokens, gains, cosine, sines, branch, middle, middle_grad, gain2, heads, wq, g_down, g_wide, g_attn)


def adam_step(weight, gradient, moment, squared, rate_now):
    first = BETA_FIRST * moment + (1.0 - BETA_FIRST) * gradient
    second = BETA_SECOND * squared + (1.0 - BETA_SECOND) * gradient * gradient
    corrected = first / (1.0 - BETA_FIRST**STEP)
    spread = jnp.sqrt(second / (1.0 - BETA_SECOND**STEP))
    return (weight - rate_now * (corrected / (spread + ADAM_EPS) + DECAY * weight), first, second)


def update_all(weights, gradients, moments, squares, rates):
    results = []
    for weight, gradient, moment, squared, rate_now in zip(
        weights, gradients, moments, squares, rates
    ):
        results.extend(adam_step(weight, gradient, moment, squared, rate_now))
    return results


def exact_gelu(values):
    return jax.nn.gelu(values, approximate=False)


def by_chip(z_, weight):
    rows = weight.shape[0]
    split = weight.reshape(rows, 3, z_.chips, z_.chip_heads, HD)
    pairs = split[:, 0:2].transpose(2, 0, 3, 1, 4).reshape(z_.chips, rows, -1)
    values = split[:, 2].transpose(1, 0, 2, 3).reshape(z_.chips, rows, -1)
    return jnp.concatenate([pairs, values], axis=2)


def from_chips(z_, chunked):
    rows = chunked.shape[1]
    cut = z_.chip_heads * 2 * HD
    pairs = chunked[:, :, :cut].reshape(z_.chips, rows, z_.chip_heads, 2, HD)
    pairs = pairs.transpose(1, 3, 0, 2, 4).reshape(rows, 2, z_.head_width)
    values = chunked[:, :, cut:].reshape(z_.chips, rows, z_.chip_heads, HD)
    values = values.transpose(1, 0, 2, 3).reshape(rows, 1, z_.head_width)
    return jnp.concatenate([pairs, values], axis=1)


def heads_to_tokens(z_, packed):
    parts = packed.shape[0]
    moved = lax.all_to_all(packed, "ctx", split_axis=1, concat_axis=1, tiled=True)
    moved = moved.reshape(parts, z_.heads, z_.share, z_.block, 2 * HD)
    return lax.dynamic_index_in_dim(moved, lax.axis_index("ctx") % z_.share, 2, keepdims=False)


def tokens_to_heads(z_, packed):
    return lax.all_to_all(
        jnp.repeat(packed, z_.share, axis=1), "ctx", split_axis=1, concat_axis=1, tiled=True
    )


def unpack_values(z_, packed):
    split = packed.reshape(4, z_.heads, z_.block, 2, HD)
    return split.transpose(3, 0, 2, 1, 4).reshape(z_.rows, z_.heads, HD)


def pack_values(z_, values):
    split = values.reshape(2, 4, z_.block, z_.heads, HD)
    return split.transpose(1, 3, 2, 0, 4).reshape(4, z_.heads, z_.block, 2 * HD)


def on_device(
    tokens,
    cotangent,
    lengths,
    order,
    qkv_weight,
    attn_weight,
    wide_weight,
    down_weight,
    norm_gains,
    qkv_mean,
    attn_mean,
    wide_mean,
    down_mean,
    gains_mean,
    qkv_square,
    attn_square,
    wide_square,
    down_square,
    gains_square,
):
    z_ = Sizes(
        lax.axis_size("fsdp"),
        lax.axis_size("ctx"),
        tokens.shape[0],
        tokens.shape[1],
        qkv_weight.shape[2],
        wide_weight.shape[2],
    )
    ctx_index = lax.axis_index("ctx")
    in_order, endings = sequence_ends(lengths[0], order[0])
    local_ids = jnp.arange(z_.rows, dtype=jnp.int32)
    cosine, sines = rope_tables(
        positions(in_order, endings, packed_place(local_ids, ctx_index, z_.ctx, z_.block))
    )
    gain_rows = jnp.pad(norm_gains.astype(BF16).astype(F32), ((0, 6), (0, 0)))
    packed, wq_full, wo_full, wi_full, gains_full = project(
        z_,
        tokens,
        gain_rows,
        cosine,
        sines,
        by_chip(z_, qkv_weight.astype(BF16)),
        attn_weight.astype(BF16),
        wide_weight.astype(BF16).transpose(1, 0, 2),
    )
    down_low = lax.all_gather(down_weight.astype(BF16), "fsdp", axis=1, tiled=True)
    attn_low = wo_full.transpose(1, 0, 2).reshape(z_.head_width, z_.width)
    wide_low = wi_full.reshape(2, z_.width, z_.units)
    gains = gains_full.transpose(1, 0, 2).reshape(8, z_.width)
    inputs = tokens.astype(F32)
    attended_packed, attended_turned, lse = attend(z_, endings, packed)
    attended_low = unpack_values(
        z_, heads_to_tokens(z_, attended_packed)
    ).reshape(z_.rows, z_.head_width)
    mixed_sum = lax.psum(
        jnp.dot(attended_low, attn_low, preferred_element_type=F32).astype(BF16), "tp"
    ).astype(F32)
    middle = inputs + mixed_sum
    normed_two, scaling_two = normalize(middle)
    entry_two = (normed_two * gains[1][None, :]).astype(BF16)
    gate_up = jnp.einsum("td,kdf->tkf", entry_two, wide_low, preferred_element_type=F32)
    activated, gelu_pull = jax.vjp(exact_gelu, gate_up[:, 0])
    hidden_low = (activated * gate_up[:, 1]).astype(BF16)
    grad_out = cotangent.astype(F32)
    down_grad = jnp.einsum("tf,td->fd", hidden_low, cotangent, preferred_element_type=F32)
    hidden_grad = jnp.einsum("td,fd->tf", cotangent, down_low, preferred_element_type=F32)
    act_grad = gelu_pull(hidden_grad * gate_up[:, 1])[0]
    gate_grad = hidden_grad * activated
    gated_grad = jnp.stack([act_grad, gate_grad], axis=1).astype(BF16)
    wide_grad = jnp.einsum("td,tkf->kdf", entry_two, gated_grad, preferred_element_type=F32)
    back_two = lax.psum(
        jnp.einsum("tkf,kdf->td", gated_grad, wide_low, preferred_element_type=F32).astype(BF16),
        "tp",
    ).astype(F32)
    gain_second = jnp.sum(back_two * normed_two, axis=0)
    middle_grad = grad_out + norm_back(back_two * gains[1][None, :], normed_two, scaling_two)
    middle_low = middle_grad.astype(BF16)
    attn_grad = jnp.einsum("tf,td->fd", attended_low, middle_low, preferred_element_type=F32)
    attended_grad = (
        jnp.einsum("td,fd->tf", middle_low, attn_low, preferred_element_type=F32)
        .astype(BF16)
        .reshape(z_.rows, z_.heads, HD)
    )
    grads_packed = tokens_to_heads(z_, pack_values(z_, attended_grad))
    head_grads = attend_back(
        z_,
        endings,
        packed,
        grads_packed,
        attended_turned,
        lse,
    )
    branch_low = jnp.dot(hidden_low, down_low, preferred_element_type=F32).astype(BF16)
    by_half = (z_.fsdp, 2)
    output, input_grad, down_sum, wide_sum, attn_sum, qkv_sum, gain_sum = reduce_all(
        z_,
        tokens,
        gains_full,
        cosine,
        sines,
        branch_low,
        middle,
        middle_grad,
        jnp.broadcast_to(gain_second[None, :], (8, z_.width)),
        head_grads,
        wq_full,
        down_grad.astype(BF16)
        .reshape(2, z_.units // 2, z_.fsdp, z_.shard)
        .transpose(2, 0, 1, 3),
        wide_grad.astype(BF16).reshape(2, z_.fsdp, z_.shard, z_.units).transpose(1, 0, 2, 3),
        attn_grad.astype(BF16)
        .reshape(2, z_.head_width // 2, z_.fsdp, z_.shard)
        .transpose(2, 0, 1, 3),
    )
    qkv_sum = qkv_sum.reshape(2, z_.chips, z_.shard // 2, z_.chunk).transpose(1, 0, 2, 3)
    shards = (
        from_chips(z_, qkv_sum.reshape(z_.chips, z_.shard, z_.chunk)).astype(F32),
        attn_sum.reshape(z_.head_width, z_.shard).astype(F32),
        wide_sum.transpose(1, 0, 2).astype(F32),
        down_sum.reshape(z_.units, z_.shard).astype(F32),
        gain_sum[:, 0, :].astype(F32),
    )
    rates = (D ** (-0.5), RATE_ATTN, D ** (-0.5), FF ** (-0.5), RATE_GAIN)
    final = update_all(
        (qkv_weight, attn_weight, wide_weight, down_weight, norm_gains),
        shards,
        (qkv_mean, attn_mean, wide_mean, down_mean, gains_mean),
        (qkv_square, attn_square, wide_square, down_square, gains_square),
        rates,
    )
    return (output, input_grad) + tuple(final)


def solution(mesh):
    return jax.shard_map(
        on_device,
        mesh=mesh,
        in_specs=(
            P(("fsdp", "ctx"), None),
            P(("fsdp", "ctx"), None),
            P("fsdp", None),
            P("fsdp", None),
            P("fsdp", None, "tp"),
            P("tp", "fsdp"),
            P("fsdp", None, "tp"),
            P("tp", "fsdp"),
            P(None, "fsdp"),
            P("fsdp", None, "tp"),
            P("tp", "fsdp"),
            P("fsdp", None, "tp"),
            P("tp", "fsdp"),
            P(None, "fsdp"),
            P("fsdp", None, "tp"),
            P("tp", "fsdp"),
            P("fsdp", None, "tp"),
            P("tp", "fsdp"),
            P(None, "fsdp"),
        ),
        out_specs=(
            P(("fsdp", "ctx"), None),
            P(("fsdp", "ctx"), None),
            P("fsdp", None, "tp"),
            P("fsdp", None, "tp"),
            P("fsdp", None, "tp"),
            P("tp", "fsdp"),
            P("tp", "fsdp"),
            P("tp", "fsdp"),
            P("fsdp", None, "tp"),
            P("fsdp", None, "tp"),
            P("fsdp", None, "tp"),
            P("tp", "fsdp"),
            P("tp", "fsdp"),
            P("tp", "fsdp"),
            P(None, "fsdp"),
            P(None, "fsdp"),
            P(None, "fsdp"),
        ),
        check_vma=False,
    )
```

```python
import functools

import jax
import jax.numpy as jnp
from jax import lax
from jax.experimental import pallas as pl
from jax.experimental.pallas import tpu as pltpu
from jax.sharding import PartitionSpec as P

D = 1024
HD = 64
FF = 2624
STEP = 10


NORM_EPS = 1e-05
ROPE_BASE = 160000.0
BETA_FIRST = 0.9
BETA_SECOND = 0.98
ADAM_EPS = 1e-06
DECAY = 0.01
RATE_ATTN = 0.5
RATE_GAIN = 0.8
MASKED = -1e30

MESH = pl.DeviceIdType.MESH
BF16 = jnp.bfloat16
F32 = jnp.float32
VMEM_BYTES = 60 * 2**20


class Sizes:
    def __init__(self, fsdp, ctx, rows, width, head_width, units):
        self.fsdp = fsdp
        self.ctx = ctx
        self.chips = ctx // 2
        self.rows = rows
        self.block = rows // 8
        self.group = rows * ctx
        self.width = width
        self.shard = width // fsdp
        self.heads = head_width // HD
        self.head_width = head_width
        self.units = units
        self.share = max(1, ctx // self.heads)
        self.chip_heads = max(1, self.heads // self.chips)
        self.chunk = self.chip_heads * 3 * HD


def remote(src, dst, send, recv, device):
    return pltpu.make_async_remote_copy(
        src_ref=src,
        dst_ref=dst,
        send_sem=send,
        recv_sem=recv,
        device_id=device,
        device_id_type=MESH,
    )


def greet(devices):
    barrier = pltpu.get_barrier_semaphore()
    for device in devices:
        pl.semaphore_signal(barrier, inc=1, device_id=device, device_id_type=MESH)
    pl.semaphore_wait(barrier, len(devices))


def vmem():
    return pl.BlockSpec(memory_space=pltpu.VMEM)


def anywhere():
    return pl.BlockSpec(memory_space=pl.ANY)


def normalize(values):
    centered = values - jnp.mean(values, axis=1, keepdims=True)
    scaling = lax.rsqrt(jnp.mean(centered * centered, axis=1, keepdims=True) + NORM_EPS)
    return (centered * scaling, scaling)


def norm_back(grad_hat, normed, scaling):
    return scaling * (
        grad_hat
        - jnp.mean(grad_hat, axis=1, keepdims=True)
        - normed * jnp.mean(grad_hat * normed, axis=1, keepdims=True)
    )


def swap_halves(values):
    lane = lax.broadcasted_iota(jnp.int32, values.shape, 1)
    return jnp.where(
        lane % HD < HD // 2, pltpu.roll(values, 2 * HD - HD // 2, 1), pltpu.roll(values, HD // 2, 1)
    )


def packed_place(local_row, device, devices, block_size):
    return (local_row // block_size * devices + device) * block_size + local_row % block_size


def sequence_ends(lengths_row, order_row):
    count_seqs = lengths_row.shape[0]
    chosen = (order_row[:, None] == jnp.arange(count_seqs, dtype=jnp.int32)[None, :]).astype(
        jnp.int32
    )
    in_order = jnp.sum(chosen * lengths_row[None, :], axis=1)
    return (in_order, jnp.cumsum(in_order))


def positions(in_order, endings, places):
    passed = (endings[None, :] <= places[:, None]).astype(jnp.int32)
    return places - jnp.sum(passed * in_order[None, :], axis=1)


def rope_tables(position):
    half_size = HD // 2
    frequency = ROPE_BASE ** (-(2.0 * jnp.arange(half_size, dtype=jnp.float32)) / (2.0 * half_size))
    angles = position.astype(jnp.float32)[:, None] * frequency[None, :]
    cosine, sines = jnp.cos(angles), jnp.sin(angles)
    return (
        jnp.concatenate([cosine] * 4, axis=1),
        jnp.concatenate([-sines, sines, -sines, sines], axis=1),
    )


def project_kernel(
    z_,
    tok_ref,
    gain_ref,
    cos_ref,
    sin_ref,
    wq_ref,
    wo_ref,
    wi_ref,
    packed_ref,
    wq_out,
    wo_out,
    wi_out,
    gain_out,
    entry_s,
    wq_s,
    send_s,
    gain_s,
    gain_send,
    gain_recv,
    wq_send,
    wq_recv,
    wq_fsend,
    wq_frecv,
    w_send,
    w_recv,
    w_fsend,
    w_frecv,
    a_send,
    a_recv,
    local_sem,
):
    f, c, t = lax.axis_index("fsdp"), lax.axis_index("ctx"), lax.axis_index("tp")
    core = lax.rem(c, 2)
    chip = c // 2
    mate = (f, c + 1 - 2 * core, t)
    others = range(1, z_.fsdp)

    def ahead(k):
        return lax.rem(f + k, z_.fsdp)

    def behind(k):
        return lax.rem(f + z_.fsdp - k, z_.fsdp)

    def chip_of(s):
        return lax.rem(chip + 1 + s, z_.chips)

    greet(
        [(ahead(k), c, t) for k in others]
        + [(f, lax.rem(c + j, z_.ctx), t) for j in range(1, z_.ctx)]
    )

    half = z_.shard // 2

    def gain_copy(k, owner):
        return remote(
            gain_ref, gain_s.at[owner], gain_send.at[k - 1], gain_recv.at[k - 1], (ahead(k), c, t)
        )

    def wq_copy(s, k, owner):
        p = chip_of(s)
        rows = pl.ds(pl.multiple_of(core * half, half), half)
        return remote(
            wq_ref.at[p, rows],
            wq_s.at[p, owner, rows],
            wq_send.at[s, k - 1],
            wq_recv.at[s, k - 1],
            (ahead(k), c, t),
        )

    def wq_pass(s, k, side):
        p = chip_of(s)
        rows = pl.ds(pl.multiple_of(side * half, half), half)
        place = wq_s.at[p, behind(k), rows]
        return remote(place, place, wq_fsend.at[s, k - 1], wq_frecv.at[s, k - 1], mate)

    attn_half = z_.head_width // 2

    def wo_copy(k, owner):
        rows = pl.ds(pl.multiple_of(core * attn_half, attn_half), attn_half)
        return remote(
            wo_ref.at[rows],
            wo_out.at[owner, rows],
            w_send.at[0, k - 1],
            w_recv.at[0, k - 1],
            (ahead(k), c, t),
        )

    def wo_pass(k, side):
        rows = pl.ds(pl.multiple_of(side * attn_half, attn_half), attn_half)
        place = wo_out.at[behind(k), rows]
        return remote(place, place, w_fsend.at[0, k - 1], w_frecv.at[0, k - 1], mate)

    def wi_copy(k, owner):
        return remote(
            wi_ref.at[core],
            wi_out.at[core, owner],
            w_send.at[1, k - 1],
            w_recv.at[1, k - 1],
            (ahead(k), c, t),
        )

    def wi_pass(k, side):
        place = wi_out.at[side, behind(k)]
        return remote(place, place, w_fsend.at[1, k - 1], w_frecv.at[1, k - 1], mate)

    def head_copy(s, side, source):
        p = chip_of(s)
        return remote(
            send_s.at[s, side % z_.chip_heads],
            packed_ref.at[:, source],
            a_send.at[s, side],
            a_recv.at[s, core],
            (f, 2 * p + side, t),
        )

    def head_arrival(s, side):
        source = 2 * lax.rem(chip + 2 * z_.chips - 1 - s, z_.chips) + side
        return remote(
            send_s.at[s, 0], packed_ref.at[:, source], a_send.at[s, 0], a_recv.at[s, side], mate
        )

    for k in others:
        gain_copy(k, f).start()
    for k in others:
        wq_copy(0, k, f).start()
    own_wq = pltpu.make_async_copy(wq_ref, wq_s.at[:, f], local_sem.at[0])
    own_wo = pltpu.make_async_copy(wo_ref, wo_out.at[f], local_sem.at[1])
    own_wi = pltpu.make_async_copy(wi_ref, wi_out.at[:, f], local_sem.at[2])
    own_wq.start()
    own_wo.start()
    own_wi.start()
    gain_s[f] = gain_ref[...]
    for k in others:
        wq_copy(1, k, f).start()
    for k in others:
        gain_copy(k, behind(k)).wait()

    gain_out[...] = gain_s[...]
    tile = min(128, z_.rows)

    def norm_tile(i, carried):
        rows = pl.ds(pl.multiple_of(i * tile, tile), tile)
        normed, nothing = normalize(tok_ref[rows, :].astype(F32))
        for g in range(z_.fsdp):
            columns = slice(g * z_.shard, (g + 1) * z_.shard)
            entry_s[g, rows, :] = (normed[:, columns] * gain_s[g, 0:1, :]).astype(BF16)
        return carried

    lax.fori_loop(0, z_.rows // tile, norm_tile, 0)
    own_wq.wait()

    def chunk_step(s, carried):
        for k in others:

            @pl.when(s + 2 < z_.chips)
            def more():
                wq_copy(s + 2, k, f).start()

            @pl.when(s + 2 == z_.chips)
            def attn_part():
                wo_copy(k, f).start()

            @pl.when(s + 1 == z_.chips)
            def wide_part():
                wi_copy(k, f).start()

            arrived = wq_copy(s, k, behind(k))
            arrived.wait_recv()
            wq_pass(s, k, core).start()
        for k in others:
            wq_pass(s, k, 1 - core).wait_recv()
        p = chip_of(s)
        total = jnp.zeros((z_.rows, z_.chunk), F32)
        for g in range(z_.fsdp):
            total = total + jnp.dot(entry_s[g], wq_s[p, g], preferred_element_type=F32)
        for i in range(z_.chip_heads):
            pair = total[:, 2 * HD * i : 2 * HD * (i + 1)]
            pair = pair * cos_ref[...] + swap_halves(pair) * sin_ref[...]
            send_s[s, i, 0:8] = pair.astype(BF16).reshape(8, z_.block, 2 * HD)
            start = z_.chip_heads * 2 * HD + HD * i
            value = total[:, start : start + HD]
            value = jnp.concatenate([value[: z_.rows // 2], value[z_.rows // 2 :]], axis=1)
            send_s[s, i, 8:12] = value.astype(BF16).reshape(4, z_.block, 2 * HD)

        @pl.when(s < z_.chips - 1)
        def away():
            for side in range(2):
                head_copy(s, side, c).start()

        return carried

    lax.fori_loop(0, z_.chips, chunk_step, 0)
    last = z_.chips - 1
    kept = pltpu.make_async_copy(
        send_s.at[last, lax.rem(core, z_.chip_heads)], packed_ref.at[:, c], local_sem.at[3]
    )
    kept.start()
    crossed = remote(
        send_s.at[last, lax.rem(1 - core, z_.chip_heads)],
        packed_ref.at[:, c],
        a_send.at[last, 0],
        a_recv.at[last, 0],
        mate,
    )
    crossed.start()
    keep_wq = pltpu.make_async_copy(wq_s, wq_out, local_sem.at[4])
    keep_wq.start()
    for k in others:
        wo_copy(k, behind(k)).wait_recv()
        wo_pass(k, core).start()
    for k in others:
        wi_copy(k, behind(k)).wait_recv()
        wi_pass(k, core).start()
    for s in range(z_.chips - 1):
        for side in range(2):
            head_arrival(s, side).wait_recv()
            head_copy(s, side, c).wait_send()
    crossed_in = remote(
        send_s.at[last, 0],
        packed_ref.at[:, c + 1 - 2 * core],
        a_send.at[last, 0],
        a_recv.at[last, 0],
        mate,
    )
    crossed_in.wait_recv()
    crossed.wait_send()
    for k in others:
        for s in range(z_.chips):
            wq_copy(s, k, f).wait_send()
            wq_pass(s, k, core).wait_send()
        wo_copy(k, f).wait_send()
        wi_copy(k, f).wait_send()
        wo_pass(k, core).wait_send()
        wi_pass(k, core).wait_send()
        wo_pass(k, 1 - core).wait_recv()
        wi_pass(k, 1 - core).wait_recv()
    kept.wait()
    keep_wq.wait()
    own_wo.wait()
    own_wi.wait()


def project(z_, tokens, gains, cosine, sines, wq, wo, wi):
    peers = max(1, z_.fsdp - 1)
    dma = pltpu.SemaphoreType.DMA
    return pl.pallas_call(
        functools.partial(project_kernel, z_),
        out_shape=(
            jax.ShapeDtypeStruct((12, z_.ctx, z_.block, 2 * HD), BF16),
            jax.ShapeDtypeStruct((z_.chips, z_.fsdp, z_.shard, z_.chunk), BF16),
            jax.ShapeDtypeStruct((z_.fsdp, z_.head_width, z_.shard), BF16),
            jax.ShapeDtypeStruct((2, z_.fsdp, z_.shard, z_.units), BF16),
            jax.ShapeDtypeStruct((z_.fsdp, 8, z_.shard), F32),
        ),
        in_specs=[vmem()] * 5 + [anywhere()] * 2,
        out_specs=(anywhere(), anywhere(), anywhere(), anywhere(), vmem()),
        scratch_shapes=[
            pltpu.VMEM((z_.fsdp, z_.rows, z_.shard), BF16),
            pltpu.VMEM((z_.chips, z_.fsdp, z_.shard, z_.chunk), BF16),
            pltpu.VMEM((z_.chips, z_.chip_heads, 12, z_.block, 2 * HD), BF16),
            pltpu.VMEM((z_.fsdp, 8, z_.shard), F32),
            dma((peers,)),
            dma((peers,)),
            dma((z_.chips, peers)),
            dma((z_.chips, peers)),
            dma((z_.chips, peers)),
            dma((z_.chips, peers)),
            dma((2, peers)),
            dma((2, peers)),
            dma((2, peers)),
            dma((2, peers)),
            dma((z_.chips, 2)),
            dma((z_.chips, 2)),
            dma((5,)),
        ],
        compiler_params=pltpu.CompilerParams(
            collective_id=0, has_side_effects=True, vmem_limit_bytes=VMEM_BYTES
        ),
        name="project",
    )(tokens, gains, cosine, sines, wq, wo, wi)


def sequence_at(ends_ref, place):
    start, end = jnp.int32(0), ends_ref[0]
    for k in range(ends_ref.shape[0] - 1):
        past = ends_ref[k] <= place
        start = jnp.where(past, ends_ref[k], start)
        end = jnp.where(past, ends_ref[k + 1], end)
    return (start, end)


def segments_of(ends_ref, places):
    segment = jnp.zeros(places.shape, jnp.int32)
    for k in range(ends_ref.shape[0]):
        segment = segment + (ends_ref[k] <= places).astype(jnp.int32)
    return segment


def attend_kernel(
    z_,
    q_tile,
    k_tile,
    ends_ref,
    packed_ref,
    out_ref,
    outt_ref,
    lse_ref,
    query_s,
    value_s,
    top_s,
    total_s,
):
    group = z_.group
    half = group // 2
    piece = min(512, half)
    scaling = HD ** (-0.5)
    sums = 16
    packed_ref = packed_ref.reshape(group + half, 2 * HD)
    out_ref = out_ref.reshape(half, 2 * HD)
    query_s[0:HD, :] = jnp.zeros((HD, group), BF16)
    value_s[HD : HD + sums, :] = jnp.ones((sums, group), BF16)

    def prepare(i, carried):
        rows = pl.ds(pl.multiple_of(i * piece, piece), piece)
        turned = packed_ref[rows, :].astype(F32).T
        query_s[HD : 2 * HD, rows] = (turned[0:HD] * scaling).astype(BF16)

        @pl.when(i < half // piece)
        def values():
            turned_value = (
                packed_ref[pl.ds(pl.multiple_of(group + i * piece, piece), piece), :].astype(F32).T
            ).astype(BF16)
            value_s[0:HD, rows] = turned_value[0:HD]
            value_s[0:HD, pl.ds(pl.multiple_of(half + i * piece, piece), piece)] = turned_value[
                HD : 2 * HD
            ]

        return carried

    lax.fori_loop(0, group // piece, prepare, 0)

    def one_tile(i, carried):
        first = pl.multiple_of(i * q_tile, q_tile)
        columns = pl.ds(first, q_tile)
        low, low_end = sequence_at(ends_ref, first)
        high_start, high = sequence_at(ends_ref, first + q_tile - 1)
        single = low == high_start
        top_s[...] = jnp.full(top_s.shape, MASKED, F32)
        total_s[...] = jnp.zeros(total_s.shape, F32)

        def one_step(j, masked):
            start = pl.multiple_of(j * k_tile, k_tile)
            rows = pl.ds(start, k_tile)
            scores = jnp.dot(packed_ref[rows, :], query_s[:, columns], preferred_element_type=F32)
            if masked:
                key_seg = segments_of(
                    ends_ref, start + lax.broadcasted_iota(jnp.int32, (k_tile, 1), 0)
                )
                query_seg = segments_of(
                    ends_ref, first + lax.broadcasted_iota(jnp.int32, (1, q_tile), 1)
                )
                scores = jnp.where(key_seg == query_seg, scores, MASKED)
            before = top_s[0:1, :]
            after = jnp.maximum(before, jnp.max(scores, axis=0, keepdims=True))
            weights = jnp.exp(scores - after).astype(BF16)
            top_s[0:1, :] = after
            total_s[...] = total_s[...] * jnp.exp(before - after) + jnp.dot(
                value_s[:, rows], weights, preferred_element_type=F32
            )

        def step(j, inner):
            start = j * k_tile
            whole = single & (start >= low) & (start + k_tile <= high)

            @pl.when(whole)
            def plain():
                one_step(j, False)

            @pl.when(jnp.logical_not(whole))
            def partial():
                one_step(j, True)

            return inner

        lax.fori_loop(low // k_tile, (high + k_tile - 1) // k_tile, step, 0)
        summed = total_s[HD : HD + 1, :]
        lse_ref[:, columns] = jnp.broadcast_to(top_s[0:1, :] + jnp.log(summed), (8, q_tile))
        outt_ref[:, columns] = total_s[0:HD, :] / summed
        return carried

    lax.fori_loop(0, group // q_tile, one_tile, 0)

    def finish(i, carried):
        rows = pl.ds(pl.multiple_of(i * piece, piece), piece)
        later = pl.ds(pl.multiple_of(half + i * piece, piece), piece)
        both = jnp.concatenate([outt_ref[:, rows], outt_ref[:, later]], axis=0)
        out_ref[rows, :] = both.T.astype(BF16)
        return carried

    lax.fori_loop(0, half // piece, finish, 0)


def attend(z_, ends, packed):
    q_tile, k_tile = 512, 512
    group = z_.group
    return pl.pallas_call(
        functools.partial(attend_kernel, z_, q_tile, k_tile),
        out_shape=(
            jax.ShapeDtypeStruct((4, z_.ctx, z_.block, 2 * HD), BF16),
            jax.ShapeDtypeStruct((HD, group), F32),
            jax.ShapeDtypeStruct((8, group), F32),
        ),
        in_specs=[pl.BlockSpec(memory_space=pltpu.SMEM), vmem()],
        out_specs=(vmem(), vmem(), vmem()),
        scratch_shapes=[
            pltpu.VMEM((2 * HD, group), BF16),
            pltpu.VMEM((HD + 16, group), BF16),
            pltpu.VMEM((8, q_tile), F32),
            pltpu.VMEM((HD + 16, q_tile), F32),
        ],
        compiler_params=pltpu.CompilerParams(vmem_limit_bytes=VMEM_BYTES),
        name="attend",
    )(ends, packed)


def attend_back_kernel(
    z_,
    q_tile,
    k_tile,
    ends_ref,
    packed_ref,
    grad_ref,
    outt_ref,
    lse_ref,
    out_ref,
    query_s,
    key_s,
    swapped_s,
    grad_s,
    gradt_s,
    delta_s,
    query_grad_s,
    key_acc,
    value_acc,
):
    group = z_.group
    half = group // 2
    piece = min(512, half)
    scaling = HD ** (-0.5)
    packed_ref = packed_ref.reshape(group + half, 2 * HD)
    grad_ref = grad_ref.reshape(half, 2 * HD)
    out_ref = out_ref.reshape(group + half, 2 * HD)
    query_s[0:HD, :] = jnp.zeros((HD, group), BF16)
    gradt_s[0:HD, :] = jnp.zeros((HD, group), BF16)
    gradt_s[2 * HD : 3 * HD, :] = jnp.zeros((HD, group), BF16)

    def prepare(i, carried):
        rows = pl.ds(pl.multiple_of(i * piece, piece), piece)
        pair = packed_ref[rows, :].astype(F32)
        turned = pair.T
        query_s[HD : 2 * HD, rows] = (turned[0:HD] * scaling).astype(BF16)
        key_s[:, rows] = turned[HD : 2 * HD].astype(BF16)
        swapped_s[rows, :] = pltpu.roll(pair, HD, 1).astype(BF16)
        query_grad_s[:, rows] = jnp.zeros((HD, piece), F32)

        @pl.when(i < half // piece)
        def grads():
            later = pl.ds(pl.multiple_of(half + i * piece, piece), piece)
            both = grad_ref[rows, :].astype(F32)
            turned_grad = both.T
            grad_s[rows, :] = both.astype(BF16)
            grad_s[later, :] = pltpu.roll(both, HD, 1).astype(BF16)
            for place, part in ((rows, turned_grad[0:HD]), (later, turned_grad[HD : 2 * HD])):
                gradt_s[HD : 2 * HD, place] = part.astype(BF16)
                delta = jnp.sum(part * outt_ref[:, place], axis=0, keepdims=True)
                delta_s[:, place] = jnp.broadcast_to(delta, (8, piece))

        return carried

    lax.fori_loop(0, group // piece, prepare, 0)

    def one_tile(j, carried):
        start = pl.multiple_of(j * k_tile, k_tile)
        rows = pl.ds(start, k_tile)
        upper = (start >= half).astype(jnp.int32)
        value_rows = pl.ds(pl.multiple_of(group + start - upper * half, k_tile), k_tile)
        turned_rows = pl.ds(pl.multiple_of(HD - upper * HD, HD), 2 * HD)
        low, low_end = sequence_at(ends_ref, start)
        high_start, high = sequence_at(ends_ref, start + k_tile - 1)
        single = low == high_start
        key_acc[...] = jnp.zeros(key_acc.shape, F32)
        value_acc[...] = jnp.zeros(value_acc.shape, F32)

        def one_step(i, masked):
            first = pl.multiple_of(i * q_tile, q_tile)
            columns = pl.ds(first, q_tile)
            scores = jnp.dot(packed_ref[rows, :], query_s[:, columns], preferred_element_type=F32)
            chances = jnp.exp(scores - lse_ref[0:1, columns])
            if masked:
                key_seg = segments_of(
                    ends_ref, start + lax.broadcasted_iota(jnp.int32, (k_tile, 1), 0)
                )
                query_seg = segments_of(
                    ends_ref, first + lax.broadcasted_iota(jnp.int32, (1, q_tile), 1)
                )
                chances = jnp.where(key_seg == query_seg, chances, 0.0)
            chance_grad = jnp.dot(
                packed_ref[value_rows, :],
                gradt_s[turned_rows, columns],
                preferred_element_type=F32,
            )
            score_grad = (chances * (chance_grad - delta_s[0:1, columns])).astype(BF16)
            value_acc[...] += jnp.dot(
                chances.astype(BF16), grad_s[columns, :], preferred_element_type=F32
            )
            key_acc[...] += jnp.dot(
                score_grad, swapped_s[columns, :], preferred_element_type=F32
            )
            query_grad_s[:, columns] += jnp.dot(
                key_s[:, rows], score_grad, preferred_element_type=F32
            )

        def step(i, inner):
            first = i * q_tile
            whole = single & (first >= low) & (first + q_tile <= high)

            @pl.when(whole)
            def plain():
                one_step(i, False)

            @pl.when(jnp.logical_not(whole))
            def partial():
                one_step(i, True)

            return inner

        lax.fori_loop(low // q_tile, (high + q_tile - 1) // q_tile, step, 0)
        out_ref[rows, HD : 2 * HD] = (key_acc[:, HD : 2 * HD] * scaling).astype(BF16)

        @pl.when(upper == 0)
        def lower_values():
            out_ref[pl.ds(pl.multiple_of(group + start, k_tile), k_tile), 0:HD] = value_acc[
                :, 0:HD
            ].astype(BF16)

        @pl.when(upper == 1)
        def upper_values():
            out_ref[
                pl.ds(pl.multiple_of(group + start - half, k_tile), k_tile), HD : 2 * HD
            ] = pltpu.roll(value_acc[...], HD, 1)[:, HD : 2 * HD].astype(BF16)

        return carried

    lax.fori_loop(0, group // k_tile, one_tile, 0)

    def finish(i, carried):
        rows = pl.ds(pl.multiple_of(i * piece, piece), piece)
        turned = query_grad_s[:, rows] * scaling
        out_ref[rows, 0:HD] = (
            jnp.concatenate([turned, jnp.zeros((HD, piece), F32)], axis=0).T[:, 0:HD].astype(BF16)
        )
        return carried

    lax.fori_loop(0, group // piece, finish, 0)


def attend_back(z_, ends, packed, grads, outt, lse):
    q_tile, k_tile = 512, 512
    group = z_.group
    return pl.pallas_call(
        functools.partial(attend_back_kernel, z_, q_tile, k_tile),
        out_shape=jax.ShapeDtypeStruct((12, z_.ctx, z_.block, 2 * HD), BF16),
        in_specs=[pl.BlockSpec(memory_space=pltpu.SMEM)] + [vmem()] * 4,
        out_specs=vmem(),
        scratch_shapes=[
            pltpu.VMEM((2 * HD, group), BF16),
            pltpu.VMEM((HD, group), BF16),
            pltpu.VMEM((group, 2 * HD), BF16),
            pltpu.VMEM((group, 2 * HD), BF16),
            pltpu.VMEM((3 * HD, group), BF16),
            pltpu.VMEM((8, group), F32),
            pltpu.VMEM((HD, group), F32),
            pltpu.VMEM((k_tile, 2 * HD), F32),
            pltpu.VMEM((k_tile, 2 * HD), F32),
        ],
        compiler_params=pltpu.CompilerParams(vmem_limit_bytes=VMEM_BYTES),
        name="attend_back",
    )(ends, packed, grads, outt, lse)


def middle_kernel(
    z_,
    tok_ref,
    cot_ref,
    gain_ref,
    heads_ref,
    wo_ref,
    wi_ref,
    wm_ref,
    branch_ref,
    middle_ref,
    mgrad_ref,
    gain2_ref,
    grads_ref,
    g_down,
    g_wide,
    g_attn,
    heads_s,
    wo_s,
    wi_s,
    wm_s,
    mixed_s,
    mixed_t,
    sum_s,
    sum_in,
    back_s,
    back_in,
    entry_s,
    entry_t,
    normed_s,
    scale_s,
    gate_s,
    hgrad_s,
    hidden_s,
    hidden_t,
    gated_s,
    mgrad_s,
    dsend_s,
    down_s,
    wide_s,
    attn_s,
    a_send,
    a_recv,
    d_send,
    d_recv,
    y_send,
    y_recv,
    w_send,
    w_recv,
    f_send,
    f_recv,
    local_sem,
):
    f, c, t = lax.axis_index("fsdp"), lax.axis_index("ctx"), lax.axis_index("tp")
    core = lax.rem(c, 2)
    mate = (f, c + 1 - 2 * core, t)
    other = (f, c, 1 - t)
    count = z_.ctx // z_.share
    others = range(1, z_.fsdp)
    half = z_.rows // 2

    def ahead(k):
        return lax.rem(f + k, z_.fsdp)

    def behind(k):
        return lax.rem(f + z_.fsdp - k, z_.fsdp)

    def to_token(j):
        return lax.rem(c + z_.share * j, z_.ctx)

    def from_head(j):
        return lax.rem(c + z_.ctx - z_.share * j, z_.ctx)

    def heads_copy(j):
        return remote(
            heads_ref.at[:, to_token(j)],
            heads_s.at[c // z_.share],
            a_send.at[j],
            a_recv.at[j],
            (f, to_token(j), t),
        )

    def heads_arrival(j):
        return remote(
            heads_ref.at[:, c],
            heads_s.at[from_head(j) // z_.share],
            a_send.at[j],
            a_recv.at[j],
            mate,
        )

    def grads_copy(j):
        rank = lax.rem(c + j, z_.ctx)
        return remote(
            dsend_s.at[rank // z_.share],
            grads_ref.at[:, c],
            d_send.at[j],
            d_recv.at[j],
            (f, rank, t),
        )

    def grads_arrival(j):
        source = lax.rem(c + z_.ctx - j, z_.ctx)
        return remote(
            dsend_s.at[0], grads_ref.at[:, source], d_send.at[j], d_recv.at[j], mate
        )

    units_half = z_.units // 2

    def down_copy(k):
        rows = pl.ds(pl.multiple_of(core * units_half, 16), units_half)
        return remote(
            wm_ref.at[rows],
            wm_s.at[f, rows],
            w_send.at[k - 1],
            w_recv.at[k - 1],
            (ahead(k), c, t),
        )

    def down_pass(k, side):
        rows = pl.ds(pl.multiple_of(side * units_half, 16), units_half)
        place = wm_s.at[behind(k), rows]
        return remote(place, place, f_send.at[k - 1], f_recv.at[k - 1], mate)

    def sum_copy(r):
        rows = pl.ds(r * half, half)
        return remote(sum_s.at[rows], sum_in.at[rows], y_send.at[r], y_recv.at[r], other)

    def back_copy(r):
        rows = pl.ds(r * half, half)
        return remote(
            back_s.at[rows], back_in.at[rows], y_send.at[2 + r], y_recv.at[2 + r], other
        )

    greet(
        [(ahead(k), c, t) for k in others]
        + [(f, lax.rem(c + j, z_.ctx), t) for j in range(1, z_.ctx)]
        + [other]
    )
    for j in range(1, count):
        heads_copy(j).start()
    for k in others:
        down_copy(k).start()
    own_heads = pltpu.make_async_copy(
        heads_ref.at[:, c], heads_s.at[c // z_.share], local_sem.at[0]
    )
    load_wo = pltpu.make_async_copy(wo_ref, wo_s, local_sem.at[1])
    load_wi = pltpu.make_async_copy(wi_ref, wi_s, local_sem.at[2])
    own_wm = pltpu.make_async_copy(wm_ref, wm_s.at[f], local_sem.at[3])
    for copy in (own_heads, load_wo, own_wm, load_wi):
        copy.start()
    load_wo.wait()
    own_heads.wait()
    for j in range(1, count):
        heads_arrival(j).wait_recv()

    low_lane = lax.broadcasted_iota(jnp.int32, (half, 2 * HD), 1) < HD
    for h in range(0, z_.heads, 2):
        columns = slice(h * HD, (h + 2) * HD)
        one = heads_s[h].reshape(half, 2 * HD).astype(F32)
        two = heads_s[h + 1].reshape(half, 2 * HD).astype(F32)
        early = jnp.where(low_lane, one, pltpu.roll(two, HD, 1))
        late = jnp.where(low_lane, pltpu.roll(one, HD, 1), two)
        mixed_s[0:half, columns] = early.astype(BF16)
        mixed_s[half:, columns] = late.astype(BF16)
        mixed_t[columns, 0:half] = early.T.astype(BF16)
        mixed_t[columns, half:] = late.T.astype(BF16)

    for r in range(2):
        rows = slice(r * half, (r + 1) * half)
        for g in range(z_.fsdp):
            sum_s[rows, g * z_.shard : (g + 1) * z_.shard] = jnp.dot(
                mixed_s[rows, :], wo_s[g], preferred_element_type=F32
            ).astype(BF16)
        sum_copy(r).start()

    for k in others:
        down_copy(k).wait_recv()
        down_pass(k, core).start()
    own_wm.wait()
    for k in others:
        down_pass(k, 1 - core).wait_recv()

    tile = min(128, half)

    def hidden_grad(i, carried):
        rows = pl.ds(pl.multiple_of(i * tile, tile), tile)
        total = jnp.zeros((tile, z_.units), F32)
        for g in range(z_.fsdp):
            total = total + lax.dot_general(
                cot_ref[rows, g * z_.shard : (g + 1) * z_.shard],
                wm_s[g],
                (((1,), (1,)), ((), ())),
                preferred_element_type=F32,
            )
        hgrad_s[rows, :] = total
        return carried

    lax.fori_loop(0, z_.rows // tile, hidden_grad, 0)
    load_wi.wait()
    full = z_.units // 128 * 128

    for r in range(2):
        sum_copy(r).wait_recv()

        def middle_tile(i, carried):
            rows = pl.ds(pl.multiple_of(r * half + i * tile, tile), tile)
            middle = tok_ref[rows, :].astype(F32) + (
                sum_s[rows, :].astype(F32) + sum_in[rows, :].astype(F32)
            )
            middle_ref[rows, :] = middle
            normed, scaling = normalize(middle)
            normed_s[rows, :] = normed
            scale_s[rows, :] = jnp.broadcast_to(scaling, (tile, 128))
            gains = jnp.concatenate([gain_ref[g, 1:2, :] for g in range(z_.fsdp)], axis=1)
            entry = normed * gains
            entry_s[rows, :] = entry.astype(BF16)
            entry_t[:, rows] = entry.T.astype(BF16)
            return carried

        lax.fori_loop(0, half // tile, middle_tile, 0)
        rows = pl.ds(r * half, half)

        def gate(k, carried):
            gate_s[k] = jnp.dot(entry_s[rows, :], wi_s[k], preferred_element_type=F32)
            return carried

        lax.fori_loop(0, 2, gate, 0)

        def activate(i, carried):
            inner = pl.ds(pl.multiple_of(i * 16, 16), 16)
            outer = pl.ds(pl.multiple_of(r * half + i * 16, 16), 16)
            up, side = gate_s[0, inner, :], gate_s[1, inner, :]
            grad = hgrad_s[outer, :]
            chance = 0.5 + 0.5 * lax.erf(up * (0.5**0.5))
            slope = chance + up * (jnp.exp(-0.5 * up * up) * 0.3989422804014327)
            active = up * chance
            hidden_s[outer, :] = (active * side).astype(BF16)
            gated_s[0, outer, :] = (grad * side * slope).astype(BF16)
            gated_s[1, outer, :] = (grad * active).astype(BF16)
            return carried

        lax.fori_loop(0, half // 16, activate, 0)

        for g in range(z_.fsdp):
            place = slice(g * z_.shard, (g + 1) * z_.shard)
            total = jnp.zeros((half, z_.shard), F32)
            for k in range(2):
                total = total + lax.dot_general(
                    gated_s[k, rows, :],
                    wi_s[k, place, :],
                    (((1,), (1,)), ((), ())),
                    preferred_element_type=F32,
                )
            back_s[rows, place] = total.astype(BF16)
        back_copy(r).start()

    def turn(i, carried):
        rows = pl.ds(pl.multiple_of(i * tile, tile), tile)
        for first in range(0, full, 128):
            block = hidden_s[rows, first : first + 128].astype(F32)
            hidden_t[first : first + 128, rows] = block.T.astype(BF16)
        if full < z_.units:
            rest = z_.units - full
            block = hidden_s[rows, full : z_.units].astype(F32)
            block = jnp.concatenate([block, jnp.zeros((tile, 128 - rest), F32)], axis=1)
            hidden_t[full : z_.units, rows] = block.T[0:rest].astype(BF16)
        return carried

    lax.fori_loop(0, z_.rows // tile, turn, 0)
    for g in range(z_.fsdp):
        place = slice(g * z_.shard, (g + 1) * z_.shard)
        for side in range(2):
            rows = slice(side * units_half, (side + 1) * units_half)
            down_s[g, side] = jnp.dot(
                hidden_t[rows, :], cot_ref[:, place], preferred_element_type=F32
            ).astype(BF16)
    keep_down = pltpu.make_async_copy(down_s, g_down, local_sem.at[4])
    keep_down.start()

    def wide_grad(k, carried):
        for g in range(z_.fsdp):
            wide_s[g, k] = jnp.dot(
                entry_t[g * z_.shard : (g + 1) * z_.shard, :],
                gated_s[k],
                preferred_element_type=F32,
            ).astype(BF16)
        return carried

    lax.fori_loop(0, 2, wide_grad, 0)
    keep_wide = pltpu.make_async_copy(wide_s, g_wide, local_sem.at[5])
    keep_wide.start()
    for g in range(z_.fsdp):
        place = slice(g * z_.shard, (g + 1) * z_.shard)
        branch_ref[:, place] = jnp.dot(
            hidden_s[...], wm_s[g], preferred_element_type=F32
        ).astype(BF16)

    gain2_ref[...] = jnp.zeros(gain2_ref.shape, F32)
    for r in range(2):
        back_copy(r).wait_recv()

        def back_tile(i, carried):
            rows = pl.ds(pl.multiple_of(r * half + i * tile, tile), tile)
            back = back_s[rows, :].astype(F32) + back_in[rows, :].astype(F32)
            normed = normed_s[rows, :]
            gain2_ref[0:1, :] += jnp.sum(back * normed, axis=0, keepdims=True)
            gains = jnp.concatenate([gain_ref[g, 1:2, :] for g in range(z_.fsdp)], axis=1)
            grad = cot_ref[rows, :].astype(F32) + norm_back(
                back * gains, normed, scale_s[rows, 0:1]
            )
            mgrad_ref[rows, :] = grad
            mgrad_s[rows, :] = grad.astype(BF16)
            return carried

        lax.fori_loop(0, half // tile, back_tile, 0)

    def heads_grad(rows):
        total = jnp.zeros((half, z_.head_width), F32)
        for g in range(z_.fsdp):
            total = total + lax.dot_general(
                mgrad_s[rows, g * z_.shard : (g + 1) * z_.shard],
                wo_s[g],
                (((1,), (1,)), ((), ())),
                preferred_element_type=F32,
            )
        return total

    early = heads_grad(slice(0, half))
    late = heads_grad(slice(half, z_.rows))
    for h in range(0, z_.heads, 2):
        columns = slice(h * HD, (h + 2) * HD)
        one = jnp.where(low_lane, early[:, columns], pltpu.roll(late[:, columns], HD, 1))
        two = jnp.where(low_lane, pltpu.roll(early[:, columns], HD, 1), late[:, columns])
        dsend_s[h] = one.astype(BF16).reshape(4, z_.block, 2 * HD)
        dsend_s[h + 1] = two.astype(BF16).reshape(4, z_.block, 2 * HD)
    for j in range(1, z_.ctx):
        grads_copy(j).start()
    own_grads = pltpu.make_async_copy(
        dsend_s.at[c // z_.share], grads_ref.at[:, c], local_sem.at[6]
    )
    own_grads.start()
    attn_half = z_.head_width // 2
    for g in range(z_.fsdp):
        for side in range(2):
            attn_s[g, side] = jnp.dot(
                mixed_t[side * attn_half : (side + 1) * attn_half, :],
                mgrad_s[:, g * z_.shard : (g + 1) * z_.shard],
                preferred_element_type=F32,
            ).astype(BF16)
    keep_attn = pltpu.make_async_copy(attn_s, g_attn, local_sem.at[7])
    keep_attn.start()

    own_grads.wait()
    for j in range(1, z_.ctx):
        grads_arrival(j).wait_recv()
        grads_copy(j).wait_send()
    for j in range(1, count):
        heads_copy(j).wait_send()
    for k in others:
        down_copy(k).wait_send()
        down_pass(k, core).wait_send()
    for r in range(2):
        sum_copy(r).wait_send()
        back_copy(r).wait_send()
    keep_down.wait()
    keep_wide.wait()
    keep_attn.wait()


def middle_part(z_, tokens, cotangent, gains, heads, wo, wi, wm):
    dma = pltpu.SemaphoreType.DMA
    peers = max(1, z_.fsdp - 1)
    count = z_.ctx // z_.share
    rows, width, units = z_.rows, z_.width, z_.units
    down = (z_.fsdp, 2, units // 2, z_.shard)
    wide = (z_.fsdp, 2, z_.shard, units)
    attn = (z_.fsdp, 2, z_.head_width // 2, z_.shard)
    return pl.pallas_call(
        functools.partial(middle_kernel, z_),
        out_shape=(
            jax.ShapeDtypeStruct((rows, width), BF16),
            jax.ShapeDtypeStruct((rows, width), F32),
            jax.ShapeDtypeStruct((rows, width), F32),
            jax.ShapeDtypeStruct((8, width), F32),
            jax.ShapeDtypeStruct((4, z_.ctx, z_.block, 2 * HD), BF16),
            jax.ShapeDtypeStruct(down, BF16),
            jax.ShapeDtypeStruct(wide, BF16),
            jax.ShapeDtypeStruct(attn, BF16),
        ),
        in_specs=[vmem()] * 3 + [anywhere()] * 4,
        out_specs=tuple([vmem()] * 4 + [anywhere()] * 4),
        scratch_shapes=[
            pltpu.VMEM((z_.heads, 4, z_.block, 2 * HD), BF16),
            pltpu.VMEM((z_.fsdp, z_.head_width, z_.shard), BF16),
            pltpu.VMEM((2, width, units), BF16),
            pltpu.VMEM((z_.fsdp, units, z_.shard), BF16),
            pltpu.VMEM((rows, z_.head_width), BF16),
            pltpu.VMEM((z_.head_width, rows), BF16),
            pltpu.VMEM((rows, width), BF16),
            pltpu.VMEM((rows, width), BF16),
            pltpu.VMEM((rows, width), BF16),
            pltpu.VMEM((rows, width), BF16),
            pltpu.VMEM((rows, width), BF16),
            pltpu.VMEM((width, rows), BF16),
            pltpu.VMEM((rows, width), F32),
            pltpu.VMEM((rows, 128), F32),
            pltpu.VMEM((2, rows // 2, units), F32),
            pltpu.VMEM((rows, units), F32),
            pltpu.VMEM((rows, units), BF16),
            pltpu.VMEM((units, rows), BF16),
            pltpu.VMEM((2, rows, units), BF16),
            pltpu.VMEM((rows, width), BF16),
            pltpu.VMEM((z_.heads, 4, z_.block, 2 * HD), BF16),
            pltpu.VMEM(down, BF16),
            pltpu.VMEM(wide, BF16),
            pltpu.VMEM(attn, BF16),
            dma((count,)),
            dma((count,)),
            dma((z_.ctx,)),
            dma((z_.ctx,)),
            dma((4,)),
            dma((4,)),
            dma((peers,)),
            dma((peers,)),
            dma((peers,)),
            dma((peers,)),
            dma((8,)),
        ],
        compiler_params=pltpu.CompilerParams(
            collective_id=2, has_side_effects=True, vmem_limit_bytes=VMEM_BYTES
        ),
        name="middle",
    )(tokens, cotangent, gains, heads, wo, wi, wm)


def cuts_of(rows, count):
    unit = rows // 16
    marks = [16 * (unit * i // count) for i in range(count + 1)]
    return [(a, b - a) for a, b in zip(marks, marks[1:]) if b > a]


def over_rows(start, rows, step, body):
    whole = rows // step

    def turn(i, carried):
        body(pl.multiple_of(start + i * step, 16), step)
        return carried

    if whole > 1:
        lax.fori_loop(0, whole, turn, 0)
    elif whole == 1:
        body(start, step)
    if rows % step:
        body(start + whole * step, rows % step)


class Item:
    def __init__(self, number, rows, columns, cuts):
        self.number = number
        self.rows = rows
        self.columns = columns
        self.cuts = cuts_of(rows, cuts)


class Reducer:
    def __init__(self, z_, items, refs, sems):
        self.z_ = z_
        self.items = items
        self.refs = refs
        self.sems = sems
        f, c, t = lax.axis_index("fsdp"), lax.axis_index("ctx"), lax.axis_index("tp")
        self.f, self.c, self.t = f, c, t
        self.core = lax.rem(c, 2)
        self.chip = c // 2
        self.mate = (f, c + 1 - 2 * self.core, t)
        middle = z_.chips // 2
        low = self.chip < middle
        self.is_mid = (self.chip == middle - 1) | (self.chip == middle)
        self.has_outer = (self.chip > 0) & (self.chip < z_.chips - 1)
        towards = jnp.where(low, 2, -2)
        self.inner = (f, c + towards, t)
        self.outer = (f, c - towards, t)
        self.numbers = {}
        for item in items:
            for cut in range(len(item.cuts)):
                self.numbers[(item.number, cut)] = len(self.numbers)

    def ahead(self, k):
        return lax.rem(self.f + k, self.z_.fsdp)

    def behind(self, k):
        return lax.rem(self.f + self.z_.fsdp - k, self.z_.fsdp)


    def core_copy(self, item):
        source, own, mate_in = self.refs[item.number][:3]
        n = item.number
        return remote(
            source.at[:, 1 - self.core],
            mate_in,
            self.sems["core_send"].at[n],
            self.sems["core_recv"].at[n],
            self.mate,
        )

    def own_copy(self, item):
        source, own = self.refs[item.number][:2]
        return pltpu.make_async_copy(
            source.at[:, self.core], own, self.sems["own"].at[item.number]
        )

    def core_sum(self, item):
        own, mate_in = self.refs[item.number][1:3]
        self.core_copy(item).wait_recv()
        for g in range(self.z_.fsdp):

            def add(first, rows, g=g):
                place = pl.ds(first, rows)
                own[g, place, :] = (
                    own[g, place, :].astype(F32) + mate_in[g, place, :].astype(F32)
                ).astype(BF16)

            over_rows(0, item.rows, 128, add)


    def peer_copy(self, item, k, owner):
        own, peer_in = self.refs[item.number][1], self.refs[item.number][3]
        return remote(
            own.at[owner],
            peer_in.at[k - 1],
            self.sems["peer_send"].at[item.number, k - 1],
            self.sems["peer_recv"].at[item.number, k - 1],
            (self.ahead(k), self.c, self.t),
        )

    def peer_start(self, item):
        for k in range(1, self.z_.fsdp):
            self.peer_copy(item, k, self.ahead(k)).start()

    def peer_sum(self, item):
        own, peer_in = self.refs[item.number][1], self.refs[item.number][3]
        for k in range(1, self.z_.fsdp):
            self.peer_copy(item, k, self.ahead(k)).wait_recv()

        def add(first, rows):
            place = pl.ds(first, rows)
            total = own[self.f, place, :].astype(F32)
            for k in range(1, self.z_.fsdp):
                total = total + peer_in[k - 1, place, :].astype(F32)
            own[self.f, place, :] = total.astype(BF16)

        over_rows(0, item.rows, 128, add)


    def in_copy(self, item, cut, middle):
        own, peer_in, outer_in, inner_in = self.refs[item.number][1:2] + self.refs[item.number][3:6]
        rows = pl.ds(*item.cuts[cut])
        n = self.numbers[(item.number, cut)]
        if middle:
            target, name = inner_in, "inner_recv"
        else:
            target, name = outer_in, "outer_recv"
        return remote(
            own.at[self.f, rows],
            target.at[rows],
            self.sems["in_send"].at[n],
            self.sems[name].at[n],
            self.inner,
        )

    def out_copy(self, item, cut):
        inner_in = self.refs[item.number][5]
        rows = pl.ds(*item.cuts[cut])
        n = self.numbers[(item.number, cut)]
        return remote(
            inner_in.at[rows],
            inner_in.at[rows],
            self.sems["out_send"].at[n],
            self.sems["inner_recv"].at[n],
            self.outer,
        )

    def done_copy(self, item, cut):
        inner_in, out = self.refs[item.number][5:7]
        rows = pl.ds(*item.cuts[cut])
        n = self.numbers[(item.number, cut)]
        return remote(
            inner_in.at[rows],
            out.at[self.core, rows],
            self.sems["done_send"].at[n],
            self.sems["done_recv"].at[n],
            self.mate,
        )

    def keep_copy(self, item, cut):
        inner_in, out = self.refs[item.number][5:7]
        rows = pl.ds(*item.cuts[cut])
        n = self.numbers[(item.number, cut)]
        return pltpu.make_async_copy(
            inner_in.at[rows], out.at[self.core, rows], self.sems["keep"].at[n]
        )

    def outermost_start(self, item):
        @pl.when(jnp.logical_not(self.has_outer))
        def first():
            for cut in range(len(item.cuts)):
                self.inward_start(item, cut)

    def inward_start(self, item, cut):
        @pl.when(self.is_mid)
        def cross():
            self.in_copy(item, cut, True).start()

        @pl.when(jnp.logical_not(self.is_mid))
        def along():
            self.in_copy(item, cut, False).start()

    def inward(self, item, cut):
        own, outer_in = self.refs[item.number][1], self.refs[item.number][4]
        first, rows = item.cuts[cut]

        @pl.when(self.has_outer)
        def passed():
            self.in_copy(item, cut, False).wait_recv()

            def add(start, count):
                place = pl.ds(start, count)
                own[self.f, place, :] = (
                    own[self.f, place, :].astype(F32) + outer_in[place, :].astype(F32)
                ).astype(BF16)

            over_rows(first, rows, 128, add)
            self.inward_start(item, cut)

    def outward(self, item, cut):
        own, inner_in = self.refs[item.number][1], self.refs[item.number][5]
        first, rows = item.cuts[cut]
        self.out_copy(item, cut).wait_recv()

        @pl.when(self.is_mid)
        def total():
            def add(start, count):
                place = pl.ds(start, count)
                inner_in[place, :] = (
                    own[self.f, place, :].astype(F32) + inner_in[place, :].astype(F32)
                ).astype(BF16)

            over_rows(first, rows, 128, add)

        @pl.when(self.has_outer)
        def onward():
            self.out_copy(item, cut).start()

        self.done_copy(item, cut).start()
        self.keep_copy(item, cut).start()

    def line(self, parts):
        for i, (item, cut) in enumerate(parts):
            self.inward(item, cut)
            if i:
                self.outward(*parts[i - 1])
        self.outward(*parts[-1])

    def settle(self):
        for item in self.items:
            self.core_copy(item).wait_send()
            for k in range(1, self.z_.fsdp):
                self.peer_copy(item, k, self.ahead(k)).wait_send()
            for cut in range(len(item.cuts)):
                self.in_copy(item, cut, False).wait_send()

                @pl.when(self.has_outer)
                def outwards(item=item, cut=cut):
                    self.out_copy(item, cut).wait_send()

                self.done_copy(item, cut).wait()
                self.keep_copy(item, cut).wait()


def reduce_kernel(
    z_,
    items,
    tok_ref,
    gain_ref,
    cos_ref,
    sin_ref,
    branch_ref,
    middle_ref,
    mgrad_ref,
    gain2_ref,
    heads_ref,
    wq_ref,
    g_down,
    g_wide,
    g_attn,
    out_ref,
    igrad_ref,
    o_down,
    o_wide,
    o_attn,
    o_qkv,
    o_gain,
    *scratch,
):
    down, wide, attn, qkv, gain = items
    scratch = list(scratch)

    def take(count):
        taken = scratch[:count]
        del scratch[:count]
        return taken

    heads_s, wq_s, entry_s, grads_s, branch_s, back_s, back_in = take(7)
    g_qkv, g_gain, gain_acc = take(3)
    groups = [take(5) for item in items]
    (a_send, a_recv, y_send, y_recv, local_sem) = take(5)
    names = (
        "core_send",
        "core_recv",
        "own",
        "peer_send",
        "peer_recv",
        "in_send",
        "outer_recv",
        "inner_recv",
        "out_send",
        "done_send",
        "done_recv",
        "keep",
    )
    sems = dict(zip(names, take(len(names))))
    sources = (g_down, g_wide, g_attn, g_qkv, g_gain)
    outs = (o_down, o_wide, o_attn, o_qkv, o_gain)
    refs = [
        (source, *group, out) for source, group, out in zip(sources, groups, outs)
    ]
    red = Reducer(z_, items, refs, sems)
    f, c, t = red.f, red.c, red.t
    other = (f, c, 1 - t)
    count = z_.ctx // z_.share

    def to_token(j):
        return lax.rem(c + z_.share * j, z_.ctx)

    def from_head(j):
        return lax.rem(c + z_.ctx - z_.share * j, z_.ctx)

    def heads_copy(j):
        return remote(
            heads_ref.at[:, to_token(j)],
            heads_s.at[c // z_.share],
            a_send.at[j],
            a_recv.at[j],
            (f, to_token(j), t),
        )

    def branch_copy():
        return remote(branch_ref, branch_s, y_send.at[0], y_recv.at[0], other)

    def back_copy():
        return remote(back_s, back_in, y_send.at[1], y_recv.at[1], other)

    greet(
        [(red.ahead(k), c, t) for k in range(1, z_.fsdp)]
        + [(f, lax.rem(c + j, z_.ctx), t) for j in range(1, z_.ctx)]
        + [other]
    )
    for j in range(1, count):
        heads_copy(j).start()
    branch_copy().start()
    own_heads = pltpu.make_async_copy(heads_ref.at[:, c], heads_s.at[c // z_.share], local_sem.at[0])
    own_heads.start()
    for item in (down, wide, attn):
        red.core_copy(item).start()
        red.own_copy(item).start()
    load_wq = pltpu.make_async_copy(wq_ref, wq_s, local_sem.at[1])
    load_wq.start()

    for item in (down, wide, attn):
        red.own_copy(item).wait()
        red.core_sum(item)
        red.peer_start(item)

    tile = min(128, z_.rows)

    def entry_tile(i, carried):
        rows = pl.ds(pl.multiple_of(i * tile, tile), tile)
        normed, nothing = normalize(tok_ref[rows, :].astype(F32))
        for g in range(z_.fsdp):
            columns = slice(g * z_.shard, (g + 1) * z_.shard)
            entry_s[g, :, rows] = (normed[:, columns] * gain_ref[g, 0:1, :]).T.astype(BF16)
        return carried

    lax.fori_loop(0, z_.rows // tile, entry_tile, 0)

    red.peer_sum(down)
    red.outermost_start(down)

    branch_copy().wait_recv()

    def output_tile(i, carried):
        rows = pl.ds(pl.multiple_of(i * tile, tile), tile)
        branch = branch_ref[rows, :].astype(F32) + branch_s[rows, :].astype(F32)
        out_ref[rows, :] = (middle_ref[rows, :] + branch).astype(BF16)
        return carried

    lax.fori_loop(0, z_.rows // tile, output_tile, 0)

    own_heads.wait()
    for j in range(1, count):
        remote(
            heads_ref.at[:, c],
            heads_s.at[from_head(j) // z_.share],
            a_send.at[j],
            a_recv.at[j],
            red.mate,
        ).wait_recv()
    load_wq.wait()

    def chunk_grads(p, carried):
        for i in range(z_.chip_heads):
            h = p * z_.chip_heads + i
            pair = heads_s[h, 0:8].reshape(z_.rows, 2 * HD).astype(F32)
            pair = pair * cos_ref[...] - swap_halves(pair) * sin_ref[...]
            grads_s[p, :, 2 * HD * i : 2 * HD * (i + 1)] = pair.astype(BF16)
            value = heads_s[h, 8:12].reshape(z_.rows // 2, 2 * HD).astype(F32)
            start = z_.chip_heads * 2 * HD + HD * i
            grads_s[p, 0 : z_.rows // 2, start : start + HD] = value[:, 0:HD].astype(BF16)
            grads_s[p, z_.rows // 2 :, start : start + HD] = value[:, HD : 2 * HD].astype(BF16)
        return carried

    lax.fori_loop(0, z_.chips, chunk_grads, 0)

    for g in range(z_.fsdp):
        columns = slice(g * z_.shard, (g + 1) * z_.shard)

        def back_tile(i, carried):
            rows = pl.ds(pl.multiple_of(i * tile, tile), tile)
            total = jnp.zeros((tile, z_.shard), F32)
            for p in range(z_.chips):
                total = total + lax.dot_general(
                    grads_s[p, rows, :],
                    wq_s[p, g],
                    (((1,), (1,)), ((), ())),
                    preferred_element_type=F32,
                )
            back_s[rows, columns] = total.astype(BF16)
            return carried

        lax.fori_loop(0, z_.rows // tile, back_tile, 0)
    back_copy().start()

    half = z_.shard // 2

    def qkv_tile(p, carried):
        for g in range(z_.fsdp):
            for side in range(2):
                grad = jnp.dot(
                    entry_s[g, side * half : (side + 1) * half, :],
                    grads_s[p],
                    preferred_element_type=F32,
                )
                rows = pl.ds(pl.multiple_of(p * half, half), half)
                g_qkv[g, side, rows, :] = grad.astype(BF16)
        return carried

    lax.fori_loop(0, z_.chips, qkv_tile, 0)
    red.core_copy(qkv).start()
    red.own_copy(qkv).start()
    red.peer_sum(wide)
    red.outermost_start(wide)
    red.own_copy(qkv).wait()
    red.core_sum(qkv)
    red.peer_start(qkv)
    red.peer_sum(attn)
    red.outermost_start(attn)

    parts = [(item, cut) for item in (down, wide, attn) for cut in range(len(item.cuts))]
    early = len(parts) - 2
    red.line(parts[:early])

    back_copy().wait_recv()
    gain_acc[...] = jnp.zeros(gain_acc.shape, F32)

    def input_tile(i, carried):
        rows = pl.ds(pl.multiple_of(i * tile, tile), tile)
        normed, scaling = normalize(tok_ref[rows, :].astype(F32))
        back = back_s[rows, :].astype(F32) + back_in[rows, :].astype(F32)
        gain_acc[0:1, :] += jnp.sum(back * normed, axis=0, keepdims=True)
        gains = jnp.concatenate([gain_ref[g, 0:1, :] for g in range(z_.fsdp)], axis=1)
        igrad_ref[rows, :] = (
            mgrad_ref[rows, :] + norm_back(back * gains, normed, scaling)
        ).astype(BF16)
        return carried

    lax.fori_loop(0, z_.rows // tile, input_tile, 0)
    top = lax.broadcasted_iota(jnp.int32, (16, z_.shard), 0) == 0
    for g in range(z_.fsdp):
        columns = slice(g * z_.shard, (g + 1) * z_.shard)
        for side, row in ((0, gain_acc[0:1, columns]), (1, gain2_ref[0:1, columns])):
            g_gain[g, side] = jnp.where(top, row, 0.0).astype(BF16)
    red.core_copy(gain).start()
    red.own_copy(gain).start()
    red.peer_sum(qkv)
    red.outermost_start(qkv)
    red.own_copy(gain).wait()
    red.core_sum(gain)
    red.peer_start(gain)
    rest = parts[early:] + [(qkv, cut) for cut in range(len(qkv.cuts))]
    red.line(rest[:2])
    red.peer_sum(gain)
    red.outermost_start(gain)
    red.line(rest[2:] + [(gain, 0)])

    own_sends = [heads_copy(j) for j in range(1, count)] + [branch_copy(), back_copy()]
    for copy in own_sends:
        copy.wait_send()
    red.settle()


def reduce_all(
    z_, tokens, gains, cosine, sines, branch, middle, middle_grad, gain2, heads, wq, g_down, g_wide, g_attn
):
    items = (
        Item(0, z_.units // 2, z_.shard, 2),
        Item(1, z_.shard, z_.units, 4),
        Item(2, z_.head_width // 2, z_.shard, 1),
        Item(3, z_.chips * (z_.shard // 2), z_.chunk, 4),
        Item(4, 16, z_.shard, 1),
    )
    dma = pltpu.SemaphoreType.DMA
    peers = max(1, z_.fsdp - 1)
    pieces = sum(len(item.cuts) for item in items)
    groups = []
    for item in items:
        groups += [
            pltpu.VMEM((z_.fsdp, item.rows, item.columns), BF16),
            pltpu.VMEM((z_.fsdp, item.rows, item.columns), BF16),
            pltpu.VMEM((peers, item.rows, item.columns), BF16),
            pltpu.VMEM((item.rows, item.columns), BF16),
            pltpu.VMEM((item.rows, item.columns), BF16),
        ]
    count = z_.ctx // z_.share
    number = len(items)
    return pl.pallas_call(
        functools.partial(reduce_kernel, z_, items),
        out_shape=(
            jax.ShapeDtypeStruct((z_.rows, z_.width), BF16),
            jax.ShapeDtypeStruct((z_.rows, z_.width), BF16),
        )
        + tuple(jax.ShapeDtypeStruct((2, item.rows, item.columns), BF16) for item in items),
        in_specs=[vmem()] * 8 + [anywhere()] * 5,
        out_specs=tuple([vmem()] * 2 + [anywhere()] * 5),
        scratch_shapes=[
            pltpu.VMEM((z_.heads, 12, z_.block, 2 * HD), BF16),
            pltpu.VMEM((z_.chips, z_.fsdp, z_.shard, z_.chunk), BF16),
            pltpu.VMEM((z_.fsdp, z_.shard, z_.rows), BF16),
            pltpu.VMEM((z_.chips, z_.rows, z_.chunk), BF16),
            pltpu.VMEM((z_.rows, z_.width), BF16),
            pltpu.VMEM((z_.rows, z_.width), BF16),
            pltpu.VMEM((z_.rows, z_.width), BF16),
            pltpu.VMEM((z_.fsdp, 2, items[3].rows, items[3].columns), BF16),
            pltpu.VMEM((z_.fsdp, 2, 16, z_.shard), BF16),
            pltpu.VMEM((8, z_.width), F32),
        ]
        + groups
        + [dma((count,)), dma((count,)), dma((2,)), dma((2,)), dma((2,))]
        + [
            dma((number,)),
            dma((number,)),
            dma((number,)),
            dma((number, peers)),
            dma((number, peers)),
        ]
        + [dma((pieces,))] * 7,
        compiler_params=pltpu.CompilerParams(
            collective_id=1, has_side_effects=True, vmem_limit_bytes=VMEM_BYTES
        ),
        name="reduce",
    )(tokens, gains, cosine, sines, branch, middle, middle_grad, gain2, heads, wq, g_down, g_wide, g_attn)


def adam_step(weight, gradient, moment, squared, rate_now):
    first = BETA_FIRST * moment + (1.0 - BETA_FIRST) * gradient
    second = BETA_SECOND * squared + (1.0 - BETA_SECOND) * gradient * gradient
    corrected = first / (1.0 - BETA_FIRST**STEP)
    spread = jnp.sqrt(second / (1.0 - BETA_SECOND**STEP))
    return (weight - rate_now * (corrected / (spread + ADAM_EPS) + DECAY * weight), first, second)


def update_all(weights, gradients, moments, squares, rates):
    results = []
    for weight, gradient, moment, squared, rate_now in zip(
        weights, gradients, moments, squares, rates
    ):
        results.extend(adam_step(weight, gradient, moment, squared, rate_now))
    return results


def by_chip(z_, weight):
    rows = weight.shape[0]
    split = weight.reshape(rows, 3, z_.chips, z_.chip_heads, HD)
    pairs = split[:, 0:2].transpose(2, 0, 3, 1, 4).reshape(z_.chips, rows, -1)
    values = split[:, 2].transpose(1, 0, 2, 3).reshape(z_.chips, rows, -1)
    return jnp.concatenate([pairs, values], axis=2)


def from_chips(z_, chunked):
    rows = chunked.shape[1]
    cut = z_.chip_heads * 2 * HD
    pairs = chunked[:, :, :cut].reshape(z_.chips, rows, z_.chip_heads, 2, HD)
    pairs = pairs.transpose(1, 3, 0, 2, 4).reshape(rows, 2, z_.head_width)
    values = chunked[:, :, cut:].reshape(z_.chips, rows, z_.chip_heads, HD)
    values = values.transpose(1, 0, 2, 3).reshape(rows, 1, z_.head_width)
    return jnp.concatenate([pairs, values], axis=1)


def on_device(
    tokens,
    cotangent,
    lengths,
    order,
    qkv_weight,
    attn_weight,
    wide_weight,
    down_weight,
    norm_gains,
    qkv_mean,
    attn_mean,
    wide_mean,
    down_mean,
    gains_mean,
    qkv_square,
    attn_square,
    wide_square,
    down_square,
    gains_square,
):
    z_ = Sizes(
        lax.axis_size("fsdp"),
        lax.axis_size("ctx"),
        tokens.shape[0],
        tokens.shape[1],
        qkv_weight.shape[2],
        wide_weight.shape[2],
    )
    ctx_index = lax.axis_index("ctx")
    in_order, endings = sequence_ends(lengths[0], order[0])
    local_ids = jnp.arange(z_.rows, dtype=jnp.int32)
    cosine, sines = rope_tables(
        positions(in_order, endings, packed_place(local_ids, ctx_index, z_.ctx, z_.block))
    )
    gain_rows = jnp.pad(norm_gains.astype(BF16).astype(F32), ((0, 6), (0, 0)))
    packed, wq_full, wo_full, wi_full, gains_full = project(
        z_,
        tokens,
        gain_rows,
        cosine,
        sines,
        by_chip(z_, qkv_weight.astype(BF16)),
        attn_weight.astype(BF16),
        wide_weight.astype(BF16).transpose(1, 0, 2),
    )
    attended_packed, attended_turned, lse = attend(z_, endings, packed)
    branch_low, middle, middle_grad, gain_second, grads_packed, down_grad, wide_grad, attn_grad = (
        middle_part(
            z_,
            tokens,
            cotangent,
            gains_full,
            attended_packed,
            wo_full,
            wi_full.reshape(2, z_.width, z_.units),
            down_weight.astype(BF16),
        )
    )
    head_grads = attend_back(
        z_,
        endings,
        packed,
        grads_packed,
        attended_turned,
        lse,
    )
    output, input_grad, down_sum, wide_sum, attn_sum, qkv_sum, gain_sum = reduce_all(
        z_,
        tokens,
        gains_full,
        cosine,
        sines,
        branch_low,
        middle,
        middle_grad,
        gain_second,
        head_grads,
        wq_full,
        down_grad,
        wide_grad,
        attn_grad,
    )
    qkv_sum = qkv_sum.reshape(2, z_.chips, z_.shard // 2, z_.chunk).transpose(1, 0, 2, 3)
    shards = (
        from_chips(z_, qkv_sum.reshape(z_.chips, z_.shard, z_.chunk)).astype(F32),
        attn_sum.reshape(z_.head_width, z_.shard).astype(F32),
        wide_sum.transpose(1, 0, 2).astype(F32),
        down_sum.reshape(z_.units, z_.shard).astype(F32),
        gain_sum[:, 0, :].astype(F32),
    )
    rates = (D ** (-0.5), RATE_ATTN, D ** (-0.5), FF ** (-0.5), RATE_GAIN)
    final = update_all(
        (qkv_weight, attn_weight, wide_weight, down_weight, norm_gains),
        shards,
        (qkv_mean, attn_mean, wide_mean, down_mean, gains_mean),
        (qkv_square, attn_square, wide_square, down_square, gains_square),
        rates,
    )
    return (output, input_grad) + tuple(final)


def solution(mesh):
    return jax.shard_map(
        on_device,
        mesh=mesh,
        in_specs=(
            P(("fsdp", "ctx"), None),
            P(("fsdp", "ctx"), None),
            P("fsdp", None),
            P("fsdp", None),
            P("fsdp", None, "tp"),
            P("tp", "fsdp"),
            P("fsdp", None, "tp"),
            P("tp", "fsdp"),
            P(None, "fsdp"),
            P("fsdp", None, "tp"),
            P("tp", "fsdp"),
            P("fsdp", None, "tp"),
            P("tp", "fsdp"),
            P(None, "fsdp"),
            P("fsdp", None, "tp"),
            P("tp", "fsdp"),
            P("fsdp", None, "tp"),
            P("tp", "fsdp"),
            P(None, "fsdp"),
        ),
        out_specs=(
            P(("fsdp", "ctx"), None),
            P(("fsdp", "ctx"), None),
            P("fsdp", None, "tp"),
            P("fsdp", None, "tp"),
            P("fsdp", None, "tp"),
            P("tp", "fsdp"),
            P("tp", "fsdp"),
            P("tp", "fsdp"),
            P("fsdp", None, "tp"),
            P("fsdp", None, "tp"),
            P("fsdp", None, "tp"),
            P("tp", "fsdp"),
            P("tp", "fsdp"),
            P("tp", "fsdp"),
            P(None, "fsdp"),
            P(None, "fsdp"),
            P(None, "fsdp"),
        ),
        check_vma=False,
    )
```

```python
import functools

import jax
import jax.numpy as jnp
from jax import lax
from jax.experimental import pallas as pl
from jax.experimental.pallas import tpu as pltpu
from jax.sharding import PartitionSpec as P

D = 1024
HD = 64
FF = 2624
STEP = 10


NORM_EPS = 1e-05
ROPE_BASE = 160000.0
BETA_FIRST = 0.9
BETA_SECOND = 0.98
ADAM_EPS = 1e-06
DECAY = 0.01
RATE_ATTN = 0.5
RATE_GAIN = 0.8
MASKED = -1e30

MESH = pl.DeviceIdType.MESH
BF16 = jnp.bfloat16
F32 = jnp.float32
VMEM_BYTES = 60 * 2**20


class Sizes:
    def __init__(self, fsdp, ctx, rows, width, head_width, units):
        self.fsdp = fsdp
        self.ctx = ctx
        self.chips = ctx // 2
        self.rows = rows
        self.block = rows // 8
        self.group = rows * ctx
        self.width = width
        self.shard = width // fsdp
        self.heads = head_width // HD
        self.head_width = head_width
        self.units = units
        self.share = max(1, ctx // self.heads)
        self.pairs = self.heads // 2
        self.ranks = ctx // self.pairs


def remote(src, dst, send, recv, device):
    return pltpu.make_async_remote_copy(
        src_ref=src,
        dst_ref=dst,
        send_sem=send,
        recv_sem=recv,
        device_id=device,
        device_id_type=MESH,
    )


def greet(devices):
    barrier = pltpu.get_barrier_semaphore()
    for device in devices:
        pl.semaphore_signal(barrier, inc=1, device_id=device, device_id_type=MESH)
    pl.semaphore_wait(barrier, len(devices))


def vmem():
    return pl.BlockSpec(memory_space=pltpu.VMEM)


def anywhere():
    return pl.BlockSpec(memory_space=pl.ANY)


def normalize(values):
    centered = values - jnp.mean(values, axis=1, keepdims=True)
    scaling = lax.rsqrt(jnp.mean(centered * centered, axis=1, keepdims=True) + NORM_EPS)
    return (centered * scaling, scaling)


def norm_back(grad_hat, normed, scaling):
    return scaling * (
        grad_hat
        - jnp.mean(grad_hat, axis=1, keepdims=True)
        - normed * jnp.mean(grad_hat * normed, axis=1, keepdims=True)
    )


def swap_halves(values):
    lane = lax.broadcasted_iota(jnp.int32, values.shape, 1)
    return jnp.where(
        lane % HD < HD // 2, pltpu.roll(values, 2 * HD - HD // 2, 1), pltpu.roll(values, HD // 2, 1)
    )


def packed_place(local_row, device, devices, block_size):
    return (local_row // block_size * devices + device) * block_size + local_row % block_size


def sequence_ends(lengths_row, order_row):
    count_seqs = lengths_row.shape[0]
    chosen = (order_row[:, None] == jnp.arange(count_seqs, dtype=jnp.int32)[None, :]).astype(
        jnp.int32
    )
    in_order = jnp.sum(chosen * lengths_row[None, :], axis=1)
    return (in_order, jnp.cumsum(in_order))


def positions(in_order, endings, places):
    passed = (endings[None, :] <= places[:, None]).astype(jnp.int32)
    return places - jnp.sum(passed * in_order[None, :], axis=1)


def rope_tables(position):
    half_size = HD // 2
    frequency = ROPE_BASE ** (-(2.0 * jnp.arange(half_size, dtype=jnp.float32)) / (2.0 * half_size))
    angles = position.astype(jnp.float32)[:, None] * frequency[None, :]
    cosine, sines = jnp.cos(angles), jnp.sin(angles)
    return (
        jnp.concatenate([cosine] * 4, axis=1),
        jnp.concatenate([-sines, sines, -sines, sines], axis=1),
    )


def cuts_of(rows, count):
    unit = rows // 16
    marks = [16 * (unit * i // count) for i in range(count + 1)]
    return [(a, b - a) for a, b in zip(marks, marks[1:]) if b > a]


def over_rows(start, rows, step, body):
    whole = rows // step

    def turn(i, carried):
        body(pl.multiple_of(start + i * step, 16), step)
        return carried

    if whole > 1:
        lax.fori_loop(0, whole, turn, 0)
    elif whole == 1:
        body(start, step)
    if rows % step:
        body(start + whole * step, rows % step)


def project_kernel(
    z_,
    tok_ref,
    gain_ref,
    cos_ref,
    sin_ref,
    wq_ref,
    wo_ref,
    wi_ref,
    packed_ref,
    wq_out,
    wo_out,
    wi_out,
    gain_out,
    entry_s,
    wq_f,
    wo_f,
    wi_f,
    wq_s,
    wo_s,
    wi_s,
    send_s,
    gain_s,
    gain_send,
    gain_recv,
    wq_send,
    wq_recv,
    wq_fsend,
    wq_frecv,
    w_send,
    w_recv,
    w_fsend,
    w_frecv,
    a_send,
    a_recv,
    local_sem,
):
    f, c, t = lax.axis_index("fsdp"), lax.axis_index("ctx"), lax.axis_index("tp")
    core = lax.rem(c, 2)
    mate = (f, c + 1 - 2 * core, t)
    others = range(1, z_.fsdp)
    mine = c // z_.ranks
    place_in = lax.rem(c, z_.ranks)
    last = z_.pairs - 1
    unit_half = z_.units // 2

    def ahead(k):
        return lax.rem(f + k, z_.fsdp)

    def behind(k):
        return lax.rem(f + z_.fsdp - k, z_.fsdp)

    def pair_of(s):
        return lax.rem(mine + 1 + s, z_.pairs)

    load_wq = pltpu.make_async_copy(wq_ref, wq_f, local_sem.at[0])
    load_wo = pltpu.make_async_copy(wo_ref, wo_f, local_sem.at[1])
    load_wi = pltpu.make_async_copy(wi_ref.at[:, 0:unit_half], wi_f, local_sem.at[2])
    load_wq.start()
    load_wo.start()
    load_wi.start()
    greet(
        [(ahead(k), c, t) for k in others]
        + [(f, lax.rem(c + j, z_.ctx), t) for j in range(1, z_.ctx)]
    )

    half = z_.shard // 2
    own_half = pl.ds(pl.multiple_of(core * half, half), half)
    mate_half = pl.ds(pl.multiple_of((1 - core) * half, half), half)

    def gain_copy(k, owner):
        return remote(
            gain_ref, gain_s.at[owner], gain_send.at[k - 1], gain_recv.at[k - 1], (ahead(k), c, t)
        )

    def wq_copy(s, k, owner):
        place = wq_s.at[pair_of(s), owner, own_half]
        return remote(
            place, place, wq_send.at[s, k - 1], wq_recv.at[s, k - 1], (ahead(k), c, t)
        )

    def wq_pass(s, k, rows):
        place = wq_s.at[pair_of(s), behind(k), rows]
        return remote(place, place, wq_fsend.at[s, k - 1], wq_frecv.at[s, k - 1], mate)

    attn_half = z_.head_width // 2

    def weight_places(side, owner):
        rows = pl.ds(pl.multiple_of(side * attn_half, attn_half), attn_half)
        return (
            (wo_s.at[rows], wo_out.at[owner, rows]),
            (wi_s.at[side], wi_out.at[side, owner]),
        )

    pieces = 2

    def w_copy(n, k, owner):
        source, place = weight_places(core, owner)[n]
        return remote(source, place, w_send.at[n, k - 1], w_recv.at[n, k - 1], (ahead(k), c, t))

    def w_pass(n, k, side):
        place = weight_places(side, behind(k))[n][1]
        return remote(place, place, w_fsend.at[n, k - 1], w_frecv.at[n, k - 1], mate)

    def head_copy(s, i):
        return remote(
            send_s.at[s, i // z_.share],
            packed_ref.at[:, c],
            a_send.at[s, i],
            a_recv.at[s, place_in],
            (f, pair_of(s) * z_.ranks + i, t),
        )

    def head_arrival(s, i):
        source = lax.rem(mine + 2 * z_.pairs - 1 - s, z_.pairs) * z_.ranks + i
        return remote(
            send_s.at[s, 0], packed_ref.at[:, source], a_send.at[s, 0], a_recv.at[s, i], mate
        )

    def near_copy(j):
        i = lax.rem(place_in + j, z_.ranks)
        return remote(
            send_s.at[last, i // z_.share],
            packed_ref.at[:, c],
            a_send.at[last, j],
            a_recv.at[last, j],
            (f, mine * z_.ranks + i, t),
        )

    def near_arrival(j):
        source = mine * z_.ranks + lax.rem(place_in + z_.ranks - j, z_.ranks)
        return remote(
            send_s.at[last, 0], packed_ref.at[:, source], a_send.at[last, j], a_recv.at[last, j], mate
        )

    for k in others:
        gain_copy(k, f).start()
    load_wq.wait()

    def round_pair(s):
        p = pair_of(s)
        columns = pl.ds(pl.multiple_of(p * 2 * HD, 2 * HD), 2 * HD)
        for kind in range(3):
            wq_s[p, f, :, kind * 2 * HD : (kind + 1) * 2 * HD] = wq_f[kind, :, columns].astype(BF16)

    for s in range(2):
        round_pair(s)
        for k in others:
            wq_copy(s, k, f).start()
    gain_s[f] = gain_ref[...]
    for k in others:
        gain_copy(k, behind(k)).wait()

    gain_out[...] = gain_s[...]
    tile = min(128, z_.rows)

    def norm_tile(i, carried):
        rows = pl.ds(pl.multiple_of(i * tile, tile), tile)
        normed, nothing = normalize(tok_ref[rows, :].astype(F32))
        for g in range(z_.fsdp):
            columns = slice(g * z_.shard, (g + 1) * z_.shard)
            entry_s[g, rows, :] = (normed[:, columns] * gain_s[g, 0:1, :]).astype(BF16)
        return carried

    lax.fori_loop(0, z_.rows // tile, norm_tile, 0)
    load_wo.wait()
    wo_s[...] = wo_f[...].astype(BF16)
    own_wo = pltpu.make_async_copy(wo_s, wo_out.at[f], local_sem.at[1])
    own_wo.start()
    load_wi.wait()
    own_wi = pltpu.make_async_copy(wi_s, wi_out.at[:, f], local_sem.at[2])

    def round_wide(side):
        def turn(first, rows):
            place = pl.ds(first, rows)
            wi_s[side, place, :] = wi_f[side, place, :].astype(BF16)

        over_rows(0, unit_half, 128, turn)

    lane = lax.broadcasted_iota(jnp.int32, (z_.rows, 2 * HD), 1) < HD
    lane_half = lax.broadcasted_iota(jnp.int32, (z_.rows // 2, 2 * HD), 1) < HD

    def chunk_step(s, carried):
        @pl.when(s + 2 < z_.pairs)
        def more():
            round_pair(s + 2)
            for k in others:
                wq_copy(s + 2, k, f).start()

        @pl.when(s + 2 == z_.pairs)
        def attn_part():
            for k in others:
                w_copy(0, k, f).start()
            round_wide(core)

        @pl.when(s + 1 == z_.pairs)
        def wide_part():
            for k in others:
                w_copy(1, k, f).start()

        for k in others:
            wq_copy(s, k, behind(k)).wait_recv()
            wq_pass(s, k, own_half).start()
        for k in others:
            wq_pass(s, k, mate_half).wait_recv()
        p = pair_of(s)
        total = jnp.zeros((z_.rows, 6 * HD), F32)
        for g in range(z_.fsdp):
            total = total + jnp.dot(entry_s[g], wq_s[p, g], preferred_element_type=F32)
        turned = []
        for kind in range(2):
            part = total[:, kind * 2 * HD : (kind + 1) * 2 * HD]
            turned.append(part * cos_ref[...] + swap_halves(part) * sin_ref[...])
        query, key = turned
        value = total[:, 4 * HD : 6 * HD]
        early, late = value[: z_.rows // 2], value[z_.rows // 2 :]
        both = (
            (
                jnp.where(lane, query, pltpu.roll(key, HD, 1)),
                jnp.where(lane_half, early, pltpu.roll(late, HD, 1)),
            ),
            (
                jnp.where(lane, pltpu.roll(query, HD, 1), key),
                jnp.where(lane_half, pltpu.roll(early, HD, 1), late),
            ),
        )
        for i in range(2):
            send_s[s, i, 0:8] = both[i][0].astype(BF16).reshape(8, z_.block, 2 * HD)
            send_s[s, i, 8:12] = both[i][1].astype(BF16).reshape(4, z_.block, 2 * HD)

        @pl.when(s < last)
        def away():
            for i in range(z_.ranks):
                head_copy(s, i).start()

        return carried

    lax.fori_loop(0, z_.pairs, chunk_step, 0)
    kept = pltpu.make_async_copy(
        send_s.at[last, place_in // z_.share], packed_ref.at[:, c], local_sem.at[3]
    )
    kept.start()
    for j in range(1, z_.ranks):
        near_copy(j).start()
    keep_wq = pltpu.make_async_copy(wq_s, wq_out, local_sem.at[4])
    keep_wq.start()
    round_wide(1 - core)
    own_wi.start()
    for n in range(pieces):
        for k in others:
            w_copy(n, k, behind(k)).wait_recv()
            w_pass(n, k, core).start()
    for s in range(last):
        for i in range(z_.ranks):
            head_arrival(s, i).wait_recv()
            head_copy(s, i).wait_send()
    for j in range(1, z_.ranks):
        near_arrival(j).wait_recv()
        near_copy(j).wait_send()
    for k in others:
        for s in range(z_.pairs):
            wq_copy(s, k, f).wait_send()
            wq_pass(s, k, own_half).wait_send()
        for n in range(pieces):
            w_copy(n, k, f).wait_send()
            w_pass(n, k, core).wait_send()
            w_pass(n, k, 1 - core).wait_recv()
    kept.wait()
    keep_wq.wait()
    own_wo.wait()
    own_wi.wait()


def project(z_, tokens, gains, cosine, sines, wq, wo, wi):
    peers = max(1, z_.fsdp - 1)
    dma = pltpu.SemaphoreType.DMA
    return pl.pallas_call(
        functools.partial(project_kernel, z_),
        out_shape=(
            jax.ShapeDtypeStruct((12, z_.ctx, z_.block, 2 * HD), BF16),
            jax.ShapeDtypeStruct((z_.pairs, z_.fsdp, z_.shard, 6 * HD), BF16),
            jax.ShapeDtypeStruct((z_.fsdp, z_.head_width, z_.shard), BF16),
            jax.ShapeDtypeStruct((2, z_.fsdp, z_.units // 2, z_.shard), BF16),
            jax.ShapeDtypeStruct((z_.fsdp, 8, z_.shard), F32),
        ),
        in_specs=[vmem()] * 4 + [anywhere()] * 3,
        out_specs=(anywhere(), anywhere(), anywhere(), anywhere(), vmem()),
        scratch_shapes=[
            pltpu.VMEM((z_.fsdp, z_.rows, z_.shard), BF16),
            pltpu.VMEM((3, z_.shard, z_.head_width), F32),
            pltpu.VMEM((z_.head_width, z_.shard), F32),
            pltpu.VMEM((2, z_.units // 2, z_.shard), F32),
            pltpu.VMEM((z_.pairs, z_.fsdp, z_.shard, 6 * HD), BF16),
            pltpu.VMEM((z_.head_width, z_.shard), BF16),
            pltpu.VMEM((2, z_.units // 2, z_.shard), BF16),
            pltpu.VMEM((z_.pairs, 2, 12, z_.block, 2 * HD), BF16),
            pltpu.VMEM((z_.fsdp, 8, z_.shard), F32),
            dma((peers,)),
            dma((peers,)),
            dma((z_.pairs, peers)),
            dma((z_.pairs, peers)),
            dma((z_.pairs, peers)),
            dma((z_.pairs, peers)),
            dma((2, peers)),
            dma((2, peers)),
            dma((2, peers)),
            dma((2, peers)),
            dma((z_.pairs, z_.ranks)),
            dma((z_.pairs, z_.ranks)),
            dma((5,)),
        ],
        compiler_params=pltpu.CompilerParams(
            collective_id=0, has_side_effects=True, vmem_limit_bytes=VMEM_BYTES
        ),
        name="project",
    )(tokens, gains, cosine, sines, wq, wo, wi)


def sequence_at(ends_ref, place):
    start, end = jnp.int32(0), ends_ref[0]
    for k in range(ends_ref.shape[0] - 1):
        past = ends_ref[k] <= place
        start = jnp.where(past, ends_ref[k], start)
        end = jnp.where(past, ends_ref[k + 1], end)
    return (start, end)


def segments_of(ends_ref, places):
    segment = jnp.zeros(places.shape, jnp.int32)
    for k in range(ends_ref.shape[0]):
        segment = segment + (ends_ref[k] <= places).astype(jnp.int32)
    return segment


def attend_kernel(
    z_,
    q_tile,
    k_tile,
    ends_ref,
    packed_ref,
    out_ref,
    outt_ref,
    lse_ref,
    query_s,
    value_s,
    top_s,
    total_s,
):
    group = z_.group
    half = group // 2
    piece = min(512, half)
    scaling = HD ** (-0.5)
    sums = 16
    packed_ref = packed_ref.reshape(group + half, 2 * HD)
    out_ref = out_ref.reshape(half, 2 * HD)
    query_s[0:HD, :] = jnp.zeros((HD, group), BF16)
    value_s[HD : HD + sums, :] = jnp.ones((sums, group), BF16)

    def prepare(i, carried):
        rows = pl.ds(pl.multiple_of(i * piece, piece), piece)
        turned = packed_ref[rows, :].astype(F32).T
        query_s[HD : 2 * HD, rows] = (turned[0:HD] * scaling).astype(BF16)

        @pl.when(i < half // piece)
        def values():
            turned_value = (
                packed_ref[pl.ds(pl.multiple_of(group + i * piece, piece), piece), :].astype(F32).T
            ).astype(BF16)
            value_s[0:HD, rows] = turned_value[0:HD]
            value_s[0:HD, pl.ds(pl.multiple_of(half + i * piece, piece), piece)] = turned_value[
                HD : 2 * HD
            ]

        return carried

    lax.fori_loop(0, group // piece, prepare, 0)

    def one_tile(i, carried):
        first = pl.multiple_of(i * q_tile, q_tile)
        columns = pl.ds(first, q_tile)
        low, low_end = sequence_at(ends_ref, first)
        high_start, high = sequence_at(ends_ref, first + q_tile - 1)
        single = low == high_start
        top_s[...] = jnp.full(top_s.shape, MASKED, F32)
        total_s[...] = jnp.zeros(total_s.shape, F32)

        def one_step(j, masked):
            start = pl.multiple_of(j * k_tile, k_tile)
            rows = pl.ds(start, k_tile)
            scores = jnp.dot(packed_ref[rows, :], query_s[:, columns], preferred_element_type=F32)
            if masked:
                key_seg = segments_of(
                    ends_ref, start + lax.broadcasted_iota(jnp.int32, (k_tile, 1), 0)
                )
                query_seg = segments_of(
                    ends_ref, first + lax.broadcasted_iota(jnp.int32, (1, q_tile), 1)
                )
                scores = jnp.where(key_seg == query_seg, scores, MASKED)
            before = top_s[0:1, :]
            after = jnp.maximum(before, jnp.max(scores, axis=0, keepdims=True))
            weights = jnp.exp(scores - after).astype(BF16)
            top_s[0:1, :] = after
            total_s[...] = total_s[...] * jnp.exp(before - after) + jnp.dot(
                value_s[:, rows], weights, preferred_element_type=F32
            )

        def step(j, inner):
            start = j * k_tile
            whole = single & (start >= low) & (start + k_tile <= high)

            @pl.when(whole)
            def plain():
                one_step(j, False)

            @pl.when(jnp.logical_not(whole))
            def partial():
                one_step(j, True)

            return inner

        lax.fori_loop(low // k_tile, (high + k_tile - 1) // k_tile, step, 0)
        summed = total_s[HD : HD + 1, :]
        lse_ref[:, columns] = jnp.broadcast_to(top_s[0:1, :] + jnp.log(summed), (8, q_tile))
        outt_ref[:, columns] = total_s[0:HD, :] / summed
        return carried

    lax.fori_loop(0, group // q_tile, one_tile, 0)

    def finish(i, carried):
        rows = pl.ds(pl.multiple_of(i * piece, piece), piece)
        later = pl.ds(pl.multiple_of(half + i * piece, piece), piece)
        both = jnp.concatenate([outt_ref[:, rows], outt_ref[:, later]], axis=0)
        out_ref[rows, :] = both.T.astype(BF16)
        return carried

    lax.fori_loop(0, half // piece, finish, 0)


def attend(z_, ends, packed):
    q_tile, k_tile = 512, 512
    group = z_.group
    return pl.pallas_call(
        functools.partial(attend_kernel, z_, q_tile, k_tile),
        out_shape=(
            jax.ShapeDtypeStruct((4, z_.ctx, z_.block, 2 * HD), BF16),
            jax.ShapeDtypeStruct((HD, group), F32),
            jax.ShapeDtypeStruct((8, group), F32),
        ),
        in_specs=[pl.BlockSpec(memory_space=pltpu.SMEM), vmem()],
        out_specs=(vmem(), vmem(), vmem()),
        scratch_shapes=[
            pltpu.VMEM((2 * HD, group), BF16),
            pltpu.VMEM((HD + 16, group), BF16),
            pltpu.VMEM((8, q_tile), F32),
            pltpu.VMEM((HD + 16, q_tile), F32),
        ],
        compiler_params=pltpu.CompilerParams(vmem_limit_bytes=VMEM_BYTES),
        name="attend",
    )(ends, packed)


def attend_back_kernel(
    z_,
    q_tile,
    k_tile,
    ends_ref,
    packed_ref,
    grad_ref,
    outt_ref,
    lse_ref,
    out_ref,
    query_s,
    key_s,
    swapped_s,
    grad_s,
    gradt_s,
    delta_s,
    query_grad_s,
    key_acc,
    value_acc,
):
    group = z_.group
    half = group // 2
    piece = min(512, half)
    scaling = HD ** (-0.5)
    packed_ref = packed_ref.reshape(group + half, 2 * HD)
    grad_ref = grad_ref.reshape(half, 2 * HD)
    out_ref = out_ref.reshape(group + half, 2 * HD)
    query_s[0:HD, :] = jnp.zeros((HD, group), BF16)
    gradt_s[0:HD, :] = jnp.zeros((HD, group), BF16)
    gradt_s[2 * HD : 3 * HD, :] = jnp.zeros((HD, group), BF16)

    def prepare(i, carried):
        rows = pl.ds(pl.multiple_of(i * piece, piece), piece)
        pair = packed_ref[rows, :].astype(F32)
        turned = pair.T
        query_s[HD : 2 * HD, rows] = (turned[0:HD] * scaling).astype(BF16)
        key_s[:, rows] = turned[HD : 2 * HD].astype(BF16)
        swapped_s[rows, :] = pltpu.roll(pair, HD, 1).astype(BF16)
        query_grad_s[:, rows] = jnp.zeros((HD, piece), F32)

        @pl.when(i < half // piece)
        def grads():
            later = pl.ds(pl.multiple_of(half + i * piece, piece), piece)
            both = grad_ref[rows, :].astype(F32)
            turned_grad = both.T
            grad_s[rows, :] = both.astype(BF16)
            grad_s[later, :] = pltpu.roll(both, HD, 1).astype(BF16)
            for place, part in ((rows, turned_grad[0:HD]), (later, turned_grad[HD : 2 * HD])):
                gradt_s[HD : 2 * HD, place] = part.astype(BF16)
                delta = jnp.sum(part * outt_ref[:, place], axis=0, keepdims=True)
                delta_s[:, place] = jnp.broadcast_to(delta, (8, piece))

        return carried

    lax.fori_loop(0, group // piece, prepare, 0)

    def one_tile(j, carried):
        start = pl.multiple_of(j * k_tile, k_tile)
        rows = pl.ds(start, k_tile)
        upper = (start >= half).astype(jnp.int32)
        value_rows = pl.ds(pl.multiple_of(group + start - upper * half, k_tile), k_tile)
        turned_rows = pl.ds(pl.multiple_of(HD - upper * HD, HD), 2 * HD)
        low, low_end = sequence_at(ends_ref, start)
        high_start, high = sequence_at(ends_ref, start + k_tile - 1)
        single = low == high_start
        key_acc[...] = jnp.zeros(key_acc.shape, F32)
        value_acc[...] = jnp.zeros(value_acc.shape, F32)

        def one_step(i, masked):
            first = pl.multiple_of(i * q_tile, q_tile)
            columns = pl.ds(first, q_tile)
            scores = jnp.dot(packed_ref[rows, :], query_s[:, columns], preferred_element_type=F32)
            chances = jnp.exp(scores - lse_ref[0:1, columns])
            if masked:
                key_seg = segments_of(
                    ends_ref, start + lax.broadcasted_iota(jnp.int32, (k_tile, 1), 0)
                )
                query_seg = segments_of(
                    ends_ref, first + lax.broadcasted_iota(jnp.int32, (1, q_tile), 1)
                )
                chances = jnp.where(key_seg == query_seg, chances, 0.0)
            chance_grad = jnp.dot(
                packed_ref[value_rows, :],
                gradt_s[turned_rows, columns],
                preferred_element_type=F32,
            )
            score_grad = (chances * (chance_grad - delta_s[0:1, columns])).astype(BF16)
            value_acc[...] += jnp.dot(
                chances.astype(BF16), grad_s[columns, :], preferred_element_type=F32
            )
            key_acc[...] += jnp.dot(
                score_grad, swapped_s[columns, :], preferred_element_type=F32
            )
            query_grad_s[:, columns] += jnp.dot(
                key_s[:, rows], score_grad, preferred_element_type=F32
            )

        def step(i, inner):
            first = i * q_tile
            whole = single & (first >= low) & (first + q_tile <= high)

            @pl.when(whole)
            def plain():
                one_step(i, False)

            @pl.when(jnp.logical_not(whole))
            def partial():
                one_step(i, True)

            return inner

        lax.fori_loop(low // q_tile, (high + q_tile - 1) // q_tile, step, 0)
        out_ref[rows, HD : 2 * HD] = (key_acc[:, HD : 2 * HD] * scaling).astype(BF16)

        @pl.when(upper == 0)
        def lower_values():
            out_ref[pl.ds(pl.multiple_of(group + start, k_tile), k_tile), 0:HD] = value_acc[
                :, 0:HD
            ].astype(BF16)

        @pl.when(upper == 1)
        def upper_values():
            out_ref[
                pl.ds(pl.multiple_of(group + start - half, k_tile), k_tile), HD : 2 * HD
            ] = pltpu.roll(value_acc[...], HD, 1)[:, HD : 2 * HD].astype(BF16)

        return carried

    lax.fori_loop(0, group // k_tile, one_tile, 0)

    def finish(i, carried):
        rows = pl.ds(pl.multiple_of(i * piece, piece), piece)
        turned = query_grad_s[:, rows] * scaling
        out_ref[rows, 0:HD] = (
            jnp.concatenate([turned, jnp.zeros((HD, piece), F32)], axis=0).T[:, 0:HD].astype(BF16)
        )
        return carried

    lax.fori_loop(0, group // piece, finish, 0)


def attend_back(z_, ends, packed, grads, outt, lse):
    q_tile, k_tile = 512, 512
    group = z_.group
    return pl.pallas_call(
        functools.partial(attend_back_kernel, z_, q_tile, k_tile),
        out_shape=jax.ShapeDtypeStruct((12, z_.ctx, z_.block, 2 * HD), BF16),
        in_specs=[pl.BlockSpec(memory_space=pltpu.SMEM)] + [vmem()] * 4,
        out_specs=vmem(),
        scratch_shapes=[
            pltpu.VMEM((2 * HD, group), BF16),
            pltpu.VMEM((HD, group), BF16),
            pltpu.VMEM((group, 2 * HD), BF16),
            pltpu.VMEM((group, 2 * HD), BF16),
            pltpu.VMEM((3 * HD, group), BF16),
            pltpu.VMEM((8, group), F32),
            pltpu.VMEM((HD, group), F32),
            pltpu.VMEM((k_tile, 2 * HD), F32),
            pltpu.VMEM((k_tile, 2 * HD), F32),
        ],
        compiler_params=pltpu.CompilerParams(vmem_limit_bytes=VMEM_BYTES),
        name="attend_back",
    )(ends, packed, grads, outt, lse)


def middle_kernel(
    z_,
    tok_ref,
    cot_ref,
    gain_ref,
    heads_ref,
    wo_ref,
    wi_ref,
    wide_ref,
    down_ref,
    branch_ref,
    middle_ref,
    mgrad_ref,
    gain2_ref,
    grads_ref,
    g_down,
    g_wide,
    g_attn,
    heads_s,
    wo_s,
    wi_s,
    wide_f,
    down_f,
    wm_s,
    mixed_s,
    mixed_t,
    sum_s,
    sum_in,
    back_s,
    back_in,
    entry_s,
    branch_s,
    middle_s,
    grad_f,
    normed_s,
    scale_s,
    gate_s,
    hgrad_s,
    hidden_s,
    hidden_t,
    gated_s,
    gated_t,
    mgrad_s,
    dsend_s,
    down_s,
    wide_s,
    attn_s,
    a_send,
    a_recv,
    d_send,
    d_recv,
    y_send,
    y_recv,
    w_send,
    w_recv,
    f_send,
    f_recv,
    local_sem,
):
    f, c, t = lax.axis_index("fsdp"), lax.axis_index("ctx"), lax.axis_index("tp")
    core = lax.rem(c, 2)
    mate = (f, c + 1 - 2 * core, t)
    other = (f, c, 1 - t)
    count = z_.ctx // z_.share
    others = range(1, z_.fsdp)
    half = z_.rows // 2

    def ahead(k):
        return lax.rem(f + k, z_.fsdp)

    def behind(k):
        return lax.rem(f + z_.fsdp - k, z_.fsdp)

    def to_token(j):
        return lax.rem(c + z_.share * j, z_.ctx)

    def from_head(j):
        return lax.rem(c + z_.ctx - z_.share * j, z_.ctx)

    def heads_copy(j):
        return remote(
            heads_ref.at[:, to_token(j)],
            heads_s.at[c // z_.share],
            a_send.at[j],
            a_recv.at[j],
            (f, to_token(j), t),
        )

    def heads_arrival(j):
        return remote(
            heads_ref.at[:, c],
            heads_s.at[from_head(j) // z_.share],
            a_send.at[j],
            a_recv.at[j],
            mate,
        )

    def grads_copy(j):
        rank = lax.rem(c + j, z_.ctx)
        return remote(
            dsend_s.at[rank // z_.share],
            grads_ref.at[:, c],
            d_send.at[j],
            d_recv.at[j],
            (f, rank, t),
        )

    def grads_arrival(j):
        source = lax.rem(c + z_.ctx - j, z_.ctx)
        return remote(
            dsend_s.at[0], grads_ref.at[:, source], d_send.at[j], d_recv.at[j], mate
        )

    units_half = z_.units // 2

    def weight_place(n, side, owner):
        if n == 0:
            rows = pl.ds(pl.multiple_of(side * units_half, 16), units_half)
            return wm_s.at[owner, rows]
        return wi_s.at[side, owner, units_half : z_.units]

    def w_copy(n, k, owner):
        place = weight_place(n, core, owner)
        return remote(place, place, w_send.at[n, k - 1], w_recv.at[n, k - 1], (ahead(k), c, t))

    def w_pass(n, k, side):
        place = weight_place(n, side, behind(k))
        return remote(place, place, f_send.at[n, k - 1], f_recv.at[n, k - 1], mate)

    def sum_copy(r):
        rows = pl.ds(r * half, half)
        return remote(sum_s.at[rows], sum_in.at[rows], y_send.at[r], y_recv.at[r], other)

    def back_copy(r):
        rows = pl.ds(r * half, half)
        return remote(
            back_s.at[rows], back_in.at[rows], y_send.at[2 + r], y_recv.at[2 + r], other
        )

    load_down = pltpu.make_async_copy(down_ref, down_f, local_sem.at[3])
    load_down.start()
    load_wide = pltpu.make_async_copy(
        wide_ref.at[:, units_half : z_.units], wide_f, local_sem.at[8]
    )
    load_wide.start()
    load_wo = pltpu.make_async_copy(wo_ref, wo_s, local_sem.at[1])
    load_wi = pltpu.make_async_copy(
        wi_ref, wi_s.at[:, :, 0:units_half], local_sem.at[2]
    )
    load_wo.start()
    load_wi.start()
    greet(
        [(ahead(k), c, t) for k in others]
        + [(f, lax.rem(c + j, z_.ctx), t) for j in range(1, z_.ctx)]
        + [other]
    )
    for j in range(1, count):
        heads_copy(j).start()
    own_heads = pltpu.make_async_copy(
        heads_ref.at[:, c], heads_s.at[c // z_.share], local_sem.at[0]
    )
    own_heads.start()
    load_down.wait()

    def round_down(first, rows):
        place = pl.ds(first, rows)
        wm_s[f, place, :] = down_f[place, :].astype(BF16)

    over_rows(0, z_.units, 128, round_down)
    for k in others:
        w_copy(0, k, f).start()
    load_wide.wait()
    for side in range(2):

        def round_wide(first, rows, side=side):
            wi_s[side, f, pl.ds(units_half + first, rows), :] = wide_f[
                side, pl.ds(first, rows), :
            ].astype(BF16)

        over_rows(0, units_half, 128, round_wide)
    for k in others:
        w_copy(1, k, f).start()
    load_wo.wait()
    own_heads.wait()
    for j in range(1, count):
        heads_arrival(j).wait_recv()

    low_lane = lax.broadcasted_iota(jnp.int32, (half, 2 * HD), 1) < HD
    for h in range(0, z_.heads, 2):
        columns = slice(h * HD, (h + 2) * HD)
        one = heads_s[h].reshape(half, 2 * HD).astype(F32)
        two = heads_s[h + 1].reshape(half, 2 * HD).astype(F32)
        early = jnp.where(low_lane, one, pltpu.roll(two, HD, 1))
        late = jnp.where(low_lane, pltpu.roll(one, HD, 1), two)
        mixed_s[0:half, columns] = early.astype(BF16)
        mixed_s[half:, columns] = late.astype(BF16)
        mixed_t[columns, 0:half] = early.T.astype(BF16)
        mixed_t[columns, half:] = late.T.astype(BF16)

    for r in range(2):
        rows = slice(r * half, (r + 1) * half)
        for g in range(z_.fsdp):
            sum_s[rows, g * z_.shard : (g + 1) * z_.shard] = jnp.dot(
                mixed_s[rows, :], wo_s[g], preferred_element_type=F32
            ).astype(BF16)
        sum_copy(r).start()

    for k in others:
        w_copy(0, k, behind(k)).wait_recv()
        w_pass(0, k, core).start()
    for k in others:
        w_pass(0, k, 1 - core).wait_recv()

    tile = min(128, half)

    def hidden_grad(i, carried):
        rows = pl.ds(pl.multiple_of(i * tile, tile), tile)
        total = jnp.zeros((tile, z_.units), F32)
        for g in range(z_.fsdp):
            total = total + lax.dot_general(
                cot_ref[rows, g * z_.shard : (g + 1) * z_.shard],
                wm_s[g],
                (((1,), (1,)), ((), ())),
                preferred_element_type=F32,
            )
        hgrad_s[rows, :] = total
        return carried

    lax.fori_loop(0, z_.rows // tile, hidden_grad, 0)
    load_wi.wait()
    for k in others:
        w_copy(1, k, behind(k)).wait_recv()
        w_pass(1, k, core).start()
    for k in others:
        w_pass(1, k, 1 - core).wait_recv()
    full = z_.units // 128 * 128

    for r in range(2):
        sum_copy(r).wait_recv()

        def middle_tile(i, carried):
            rows = pl.ds(pl.multiple_of(r * half + i * tile, tile), tile)
            middle = tok_ref[rows, :].astype(F32) + (
                sum_s[rows, :].astype(F32) + sum_in[rows, :].astype(F32)
            )
            middle_s[rows, :] = middle
            normed, scaling = normalize(middle)
            normed_s[rows, :] = normed
            scale_s[rows, :] = jnp.broadcast_to(scaling, (tile, 128))
            gains = jnp.concatenate([gain_ref[g, 1:2, :] for g in range(z_.fsdp)], axis=1)
            entry_s[rows, :] = (normed * gains).astype(BF16)
            return carried

        lax.fori_loop(0, half // tile, middle_tile, 0)
        rows = pl.ds(r * half, half)

        def gate(k, carried):
            total = jnp.zeros((half, z_.units), F32)
            for g in range(z_.fsdp):
                total = total + lax.dot_general(
                    entry_s[rows, g * z_.shard : (g + 1) * z_.shard],
                    wi_s[k, g],
                    (((1,), (1,)), ((), ())),
                    preferred_element_type=F32,
                )
            gate_s[k] = total
            return carried

        lax.fori_loop(0, 2, gate, 0)

        def activate(i, carried):
            inner = pl.ds(pl.multiple_of(i * 16, 16), 16)
            outer = pl.ds(pl.multiple_of(r * half + i * 16, 16), 16)
            up, side = gate_s[0, inner, :], gate_s[1, inner, :]
            grad = hgrad_s[outer, :]
            chance = 0.5 + 0.5 * lax.erf(up * (0.5**0.5))
            slope = chance + up * (jnp.exp(-0.5 * up * up) * 0.3989422804014327)
            active = up * chance
            hidden_s[outer, :] = (active * side).astype(BF16)
            gated_s[0, outer, :] = (grad * side * slope).astype(BF16)
            gated_s[1, outer, :] = (grad * active).astype(BF16)
            return carried

        lax.fori_loop(0, half // 16, activate, 0)

        for g in range(z_.fsdp):
            place = slice(g * z_.shard, (g + 1) * z_.shard)
            total = jnp.zeros((half, z_.shard), F32)
            for k in range(2):
                total = total + jnp.dot(
                    gated_s[k, rows, :], wi_s[k, g], preferred_element_type=F32
                )
            back_s[rows, place] = total.astype(BF16)
        back_copy(r).start()

    keep_middle = pltpu.make_async_copy(middle_s, middle_ref, local_sem.at[9])
    keep_middle.start()

    def turn(source, target):
        def turn_tile(i, carried):
            rows = pl.ds(pl.multiple_of(i * tile, tile), tile)
            for first in range(0, full, 128):
                block = source[rows, first : first + 128].astype(F32)
                target[first : first + 128, rows] = block.T.astype(BF16)
            if full < z_.units:
                rest = z_.units - full
                block = source[rows, full : z_.units].astype(F32)
                block = jnp.concatenate([block, jnp.zeros((tile, 128 - rest), F32)], axis=1)
                target[full : z_.units, rows] = block.T[0:rest].astype(BF16)
            return carried

        lax.fori_loop(0, z_.rows // tile, turn_tile, 0)

    turn(hidden_s, hidden_t)
    for g in range(z_.fsdp):
        place = slice(g * z_.shard, (g + 1) * z_.shard)
        for side in range(2):
            rows = slice(side * units_half, (side + 1) * units_half)
            down_s[g, side] = jnp.dot(
                hidden_t[rows, :], cot_ref[:, place], preferred_element_type=F32
            ).astype(BF16)
    keep_down = pltpu.make_async_copy(down_s, g_down, local_sem.at[4])
    keep_down.start()

    for k in range(2):
        turn(gated_s.at[k], gated_t.at[k])
        for g in range(z_.fsdp):
            wide_s[g, k] = jnp.dot(
                gated_t[k],
                entry_s[:, g * z_.shard : (g + 1) * z_.shard],
                preferred_element_type=F32,
            ).astype(BF16)
    keep_wide = pltpu.make_async_copy(wide_s, g_wide, local_sem.at[5])
    keep_wide.start()
    for g in range(z_.fsdp):
        place = slice(g * z_.shard, (g + 1) * z_.shard)
        branch_s[:, place] = jnp.dot(
            hidden_s[...], wm_s[g], preferred_element_type=F32
        ).astype(BF16)
    keep_branch = pltpu.make_async_copy(branch_s, branch_ref, local_sem.at[10])
    keep_branch.start()

    gain2_ref[...] = jnp.zeros(gain2_ref.shape, F32)
    for r in range(2):
        back_copy(r).wait_recv()

        def back_tile(i, carried):
            rows = pl.ds(pl.multiple_of(r * half + i * tile, tile), tile)
            back = back_s[rows, :].astype(F32) + back_in[rows, :].astype(F32)
            normed = normed_s[rows, :]
            gain2_ref[0:1, :] += jnp.sum(back * normed, axis=0, keepdims=True)
            gains = jnp.concatenate([gain_ref[g, 1:2, :] for g in range(z_.fsdp)], axis=1)
            grad = cot_ref[rows, :].astype(F32) + norm_back(
                back * gains, normed, scale_s[rows, 0:1]
            )
            grad_f[rows, :] = grad
            mgrad_s[rows, :] = grad.astype(BF16)
            return carried

        lax.fori_loop(0, half // tile, back_tile, 0)

    keep_grad = pltpu.make_async_copy(grad_f, mgrad_ref, local_sem.at[11])
    keep_grad.start()

    def heads_grad(rows):
        total = jnp.zeros((half, z_.head_width), F32)
        for g in range(z_.fsdp):
            total = total + lax.dot_general(
                mgrad_s[rows, g * z_.shard : (g + 1) * z_.shard],
                wo_s[g],
                (((1,), (1,)), ((), ())),
                preferred_element_type=F32,
            )
        return total

    early = heads_grad(slice(0, half))
    late = heads_grad(slice(half, z_.rows))
    for h in range(0, z_.heads, 2):
        columns = slice(h * HD, (h + 2) * HD)
        one = jnp.where(low_lane, early[:, columns], pltpu.roll(late[:, columns], HD, 1))
        two = jnp.where(low_lane, pltpu.roll(early[:, columns], HD, 1), late[:, columns])
        dsend_s[h] = one.astype(BF16).reshape(4, z_.block, 2 * HD)
        dsend_s[h + 1] = two.astype(BF16).reshape(4, z_.block, 2 * HD)
    for j in range(1, z_.ctx):
        grads_copy(j).start()
    own_grads = pltpu.make_async_copy(
        dsend_s.at[c // z_.share], grads_ref.at[:, c], local_sem.at[6]
    )
    own_grads.start()
    attn_half = z_.head_width // 2
    for g in range(z_.fsdp):
        for side in range(2):
            attn_s[g, side] = jnp.dot(
                mixed_t[side * attn_half : (side + 1) * attn_half, :],
                mgrad_s[:, g * z_.shard : (g + 1) * z_.shard],
                preferred_element_type=F32,
            ).astype(BF16)
    keep_attn = pltpu.make_async_copy(attn_s, g_attn, local_sem.at[7])
    keep_attn.start()

    own_grads.wait()
    for j in range(1, z_.ctx):
        grads_arrival(j).wait_recv()
        grads_copy(j).wait_send()
    for j in range(1, count):
        heads_copy(j).wait_send()
    for k in others:
        for n in range(2):
            w_copy(n, k, f).wait_send()
            w_pass(n, k, core).wait_send()
    for r in range(2):
        sum_copy(r).wait_send()
        back_copy(r).wait_send()
    keep_down.wait()
    keep_wide.wait()
    keep_attn.wait()
    keep_middle.wait()
    keep_branch.wait()
    keep_grad.wait()


def middle_part(z_, tokens, cotangent, gains, heads, wo, wi, wide_weight, down_weight):
    dma = pltpu.SemaphoreType.DMA
    peers = max(1, z_.fsdp - 1)
    count = z_.ctx // z_.share
    rows, width, units = z_.rows, z_.width, z_.units
    down = (z_.fsdp, 2, units // 2, z_.shard)
    wide = (z_.fsdp, 2, units, z_.shard)
    attn = (z_.fsdp, 2, z_.head_width // 2, z_.shard)
    return pl.pallas_call(
        functools.partial(middle_kernel, z_),
        out_shape=(
            jax.ShapeDtypeStruct((rows, width), BF16),
            jax.ShapeDtypeStruct((rows, width), F32),
            jax.ShapeDtypeStruct((rows, width), F32),
            jax.ShapeDtypeStruct((8, width), F32),
            jax.ShapeDtypeStruct((4, z_.ctx, z_.block, 2 * HD), BF16),
            jax.ShapeDtypeStruct(down, BF16),
            jax.ShapeDtypeStruct(wide, BF16),
            jax.ShapeDtypeStruct(attn, BF16),
        ),
        in_specs=[vmem()] * 3 + [anywhere()] * 5,
        out_specs=tuple([anywhere()] * 3 + [vmem()] + [anywhere()] * 4),
        scratch_shapes=[
            pltpu.VMEM((z_.heads, 4, z_.block, 2 * HD), BF16),
            pltpu.VMEM((z_.fsdp, z_.head_width, z_.shard), BF16),
            pltpu.VMEM((2, z_.fsdp, units, z_.shard), BF16),
            pltpu.VMEM((2, units // 2, z_.shard), F32),
            pltpu.VMEM((units, z_.shard), F32),
            pltpu.VMEM((z_.fsdp, units, z_.shard), BF16),
            pltpu.VMEM((rows, z_.head_width), BF16),
            pltpu.VMEM((z_.head_width, rows), BF16),
            pltpu.VMEM((rows, width), BF16),
            pltpu.VMEM((rows, width), BF16),
            pltpu.VMEM((rows, width), BF16),
            pltpu.VMEM((rows, width), BF16),
            pltpu.VMEM((rows, width), BF16),
            pltpu.VMEM((rows, width), BF16),
            pltpu.VMEM((rows, width), F32),
            pltpu.VMEM((rows, width), F32),
            pltpu.VMEM((rows, width), F32),
            pltpu.VMEM((rows, 128), F32),
            pltpu.VMEM((2, rows // 2, units), F32),
            pltpu.VMEM((rows, units), F32),
            pltpu.VMEM((rows, units), BF16),
            pltpu.VMEM((units, rows), BF16),
            pltpu.VMEM((2, rows, units), BF16),
            pltpu.VMEM((2, units, rows), BF16),
            pltpu.VMEM((rows, width), BF16),
            pltpu.VMEM((z_.heads, 4, z_.block, 2 * HD), BF16),
            pltpu.VMEM(down, BF16),
            pltpu.VMEM(wide, BF16),
            pltpu.VMEM(attn, BF16),
            dma((count,)),
            dma((count,)),
            dma((z_.ctx,)),
            dma((z_.ctx,)),
            dma((4,)),
            dma((4,)),
            dma((2, peers)),
            dma((2, peers)),
            dma((2, peers)),
            dma((2, peers)),
            dma((12,)),
        ],
        compiler_params=pltpu.CompilerParams(
            collective_id=2, has_side_effects=True, vmem_limit_bytes=VMEM_BYTES
        ),
        name="middle",
    )(tokens, cotangent, gains, heads, wo, wi, wide_weight, down_weight)


class Item:
    def __init__(self, number, rows, columns, cuts):
        self.number = number
        self.rows = rows
        self.columns = columns
        self.cuts = cuts_of(rows, cuts)


class Reducer:
    def __init__(self, z_, items, refs, sems):
        self.z_ = z_
        self.items = items
        self.refs = refs
        self.sems = sems
        f, c, t = lax.axis_index("fsdp"), lax.axis_index("ctx"), lax.axis_index("tp")
        self.f, self.c, self.t = f, c, t
        self.core = lax.rem(c, 2)
        self.chip = c // 2
        self.mate = (f, c + 1 - 2 * self.core, t)
        middle = z_.chips // 2
        low = self.chip < middle
        self.is_mid = (self.chip == middle - 1) | (self.chip == middle)
        self.has_outer = (self.chip > 0) & (self.chip < z_.chips - 1)
        towards = jnp.where(low, 2, -2)
        self.inner = (f, c + towards, t)
        self.outer = (f, c - towards, t)
        self.numbers = {}
        for item in items:
            for cut in range(len(item.cuts)):
                self.numbers[(item.number, cut)] = len(self.numbers)

    def ahead(self, k):
        return lax.rem(self.f + k, self.z_.fsdp)

    def behind(self, k):
        return lax.rem(self.f + self.z_.fsdp - k, self.z_.fsdp)


    def core_copy(self, item):
        source, own, mate_in = self.refs[item.number][:3]
        n = item.number
        return remote(
            source.at[:, 1 - self.core],
            mate_in,
            self.sems["core_send"].at[n],
            self.sems["core_recv"].at[n],
            self.mate,
        )

    def own_copy(self, item):
        source, own = self.refs[item.number][:2]
        return pltpu.make_async_copy(
            source.at[:, self.core], own, self.sems["own"].at[item.number]
        )

    def core_sum(self, item):
        own, mate_in = self.refs[item.number][1:3]
        self.core_copy(item).wait_recv()
        for g in range(self.z_.fsdp):

            def add(first, rows, g=g):
                place = pl.ds(first, rows)
                own[g, place, :] = (
                    own[g, place, :].astype(F32) + mate_in[g, place, :].astype(F32)
                ).astype(BF16)

            over_rows(0, item.rows, 128, add)


    def peer_copy(self, item, k, owner):
        own, peer_in = self.refs[item.number][1], self.refs[item.number][3]
        return remote(
            own.at[owner],
            peer_in.at[k - 1],
            self.sems["peer_send"].at[item.number, k - 1],
            self.sems["peer_recv"].at[item.number, k - 1],
            (self.ahead(k), self.c, self.t),
        )

    def peer_start(self, item):
        for k in range(1, self.z_.fsdp):
            self.peer_copy(item, k, self.ahead(k)).start()

    def peer_sum(self, item):
        own, peer_in = self.refs[item.number][1], self.refs[item.number][3]
        for k in range(1, self.z_.fsdp):
            self.peer_copy(item, k, self.ahead(k)).wait_recv()

        def add(first, rows):
            place = pl.ds(first, rows)
            total = own[self.f, place, :].astype(F32)
            for k in range(1, self.z_.fsdp):
                total = total + peer_in[k - 1, place, :].astype(F32)
            own[self.f, place, :] = total.astype(BF16)

        over_rows(0, item.rows, 128, add)


    def in_copy(self, item, cut, middle):
        own, peer_in, outer_in, inner_in = self.refs[item.number][1:2] + self.refs[item.number][3:6]
        rows = pl.ds(*item.cuts[cut])
        n = self.numbers[(item.number, cut)]
        if middle:
            target, name = inner_in, "inner_recv"
        else:
            target, name = outer_in, "outer_recv"
        return remote(
            own.at[self.f, rows],
            target.at[rows],
            self.sems["in_send"].at[n],
            self.sems[name].at[n],
            self.inner,
        )

    def out_copy(self, item, cut):
        inner_in = self.refs[item.number][5]
        rows = pl.ds(*item.cuts[cut])
        n = self.numbers[(item.number, cut)]
        return remote(
            inner_in.at[rows],
            inner_in.at[rows],
            self.sems["out_send"].at[n],
            self.sems["inner_recv"].at[n],
            self.outer,
        )

    def done_copy(self, item, cut):
        inner_in, mate_out = self.refs[item.number][5:7]
        rows = pl.ds(*item.cuts[cut])
        n = self.numbers[(item.number, cut)]
        return remote(
            inner_in.at[rows],
            mate_out.at[rows],
            self.sems["done_send"].at[n],
            self.sems["done_recv"].at[n],
            self.mate,
        )

    def outermost_start(self, item):
        @pl.when(jnp.logical_not(self.has_outer))
        def first():
            for cut in range(len(item.cuts)):
                self.inward_start(item, cut)

    def inward_start(self, item, cut):
        @pl.when(self.is_mid)
        def cross():
            self.in_copy(item, cut, True).start()

        @pl.when(jnp.logical_not(self.is_mid))
        def along():
            self.in_copy(item, cut, False).start()

    def inward(self, item, cut):
        own, outer_in = self.refs[item.number][1], self.refs[item.number][4]
        first, rows = item.cuts[cut]

        @pl.when(self.has_outer)
        def passed():
            self.in_copy(item, cut, False).wait_recv()

            def add(start, count):
                place = pl.ds(start, count)
                own[self.f, place, :] = (
                    own[self.f, place, :].astype(F32) + outer_in[place, :].astype(F32)
                ).astype(BF16)

            over_rows(first, rows, 128, add)
            self.inward_start(item, cut)

    def outward(self, item, cut):
        own, inner_in = self.refs[item.number][1], self.refs[item.number][5]
        first, rows = item.cuts[cut]
        self.out_copy(item, cut).wait_recv()

        @pl.when(self.is_mid)
        def total():
            def add(start, count):
                place = pl.ds(start, count)
                inner_in[place, :] = (
                    own[self.f, place, :].astype(F32) + inner_in[place, :].astype(F32)
                ).astype(BF16)

            over_rows(first, rows, 128, add)

        @pl.when(self.has_outer)
        def onward():
            self.out_copy(item, cut).start()

        self.done_copy(item, cut).start()

    def line(self, parts, finish, before):
        for i, (item, cut) in enumerate(parts):
            if i in before:
                before[i]()
            if i >= 2:
                finish.load(*parts[i - 2])
            self.inward(item, cut)
            if i >= 1:
                self.outward(*parts[i - 1])
            if i >= 2:
                finish.update(*parts[i - 2])
        for i in (len(parts) - 2, len(parts) - 1):
            if i >= 0:
                finish.load(*parts[i])
                if i == len(parts) - 1:
                    self.outward(*parts[i])
                finish.update(*parts[i])

    def settle(self):
        for item in self.items:
            self.core_copy(item).wait_send()
            for k in range(1, self.z_.fsdp):
                self.peer_copy(item, k, self.ahead(k)).wait_send()
            for cut in range(len(item.cuts)):
                self.in_copy(item, cut, False).wait_send()

                @pl.when(self.has_outer)
                def outwards(item=item, cut=cut):
                    self.out_copy(item, cut).wait_send()

                self.done_copy(item, cut).wait_send()


def adam_step(weight, gradient, moment, squared, rate_now):
    first = BETA_FIRST * moment + (1.0 - BETA_FIRST) * gradient
    second = BETA_SECOND * squared + (1.0 - BETA_SECOND) * gradient * gradient
    corrected = first / (1.0 - BETA_FIRST**STEP)
    spread = jnp.sqrt(second / (1.0 - BETA_SECOND**STEP))
    return (weight - rate_now * (corrected / (spread + ADAM_EPS) + DECAY * weight), first, second)


class Finisher:
    def __init__(self, z_, reducer, states, results, rates, plain_s, pair_s, load_sem, store_sem):
        self.z_ = z_
        self.red = reducer
        self.states = states
        self.results = results
        self.rates = rates
        self.plain_s = plain_s
        self.pair_s = pair_s
        self.load_sem = load_sem
        self.store_sem = store_sem
        self.stored = None

    def places(self, refs, item, cut, side):
        first, rows = item.cuts[cut]
        number = item.number
        half = self.z_.shard // 2
        found = []
        for n in range(3):
            if number == 3:
                place = refs[number][n].at[
                    :,
                    pl.ds(pl.multiple_of(side * half, half), half),
                    2 * HD * cut : 2 * HD * (cut + 1),
                ]
                slot = self.pair_s
            else:
                slot = self.plain_s
                if number == 1:
                    place = refs[number][n].at[side, first : first + rows]
                else:
                    place = refs[number][n].at[
                        pl.ds(pl.multiple_of(side * item.rows + first, 16), rows)
                    ]
            found.append((n, place, slot, rows))
        return found

    def slot_view(self, slot, which, n, rows):
        if slot is self.pair_s:
            return slot.at[which, n]
        return slot.at[which, n, 0:rows]

    def copies(self, refs, item, cut, sems, outwards):
        made = []
        for which in range(2):
            side = self.red.core if which == 0 else 1 - self.red.core
            for n, place, slot, rows in self.places(refs, item, cut, side):
                view = self.slot_view(slot, which, n, rows)
                ends = (view, place) if outwards else (place, view)
                made.append(pltpu.make_async_copy(*ends, sems.at[which, n]))
        return made

    def settle(self):
        if self.stored is not None:
            for copy in self.copies(self.results, *self.stored, self.store_sem, True):
                copy.wait()
        self.stored = None

    def load(self, item, cut):
        if item.number == 4:
            return
        self.settle()
        for copy in self.copies(self.states, item, cut, self.load_sem, False):
            copy.start()

    def update(self, item, cut):
        if item.number == 4:
            self.gain_update()
            return
        for copy in self.copies(self.states, item, cut, self.load_sem, False):
            copy.wait()
        first, rows = item.cuts[cut]
        inner_in, mate_out = self.red.refs[item.number][5:7]
        rate = self.rates[item.number]
        for which, sums in ((0, inner_in), (1, mate_out)):
            if which == 1:
                self.red.done_copy(item, cut).wait_recv()

            def step(start, count, which=which, sums=sums):
                place = pl.ds(start, count)
                gradient = sums[pl.ds(first + start, count), :].astype(F32)
                if item.number == 3:
                    for kind in range(3):
                        got = adam_step(
                            self.pair_s[which, 0, kind, place, :],
                            gradient[:, 2 * HD * kind : 2 * HD * (kind + 1)],
                            self.pair_s[which, 1, kind, place, :],
                            self.pair_s[which, 2, kind, place, :],
                            rate,
                        )
                        for n in range(3):
                            self.pair_s[which, n, kind, place, :] = got[n]
                else:
                    got = adam_step(
                        self.plain_s[which, 0, place, :],
                        gradient,
                        self.plain_s[which, 1, place, :],
                        self.plain_s[which, 2, place, :],
                        rate,
                    )
                    for n in range(3):
                        self.plain_s[which, n, place, :] = got[n]

            over_rows(0, rows, 64, step)
        for copy in self.copies(self.results, item, cut, self.store_sem, True):
            copy.start()
        self.stored = (item, cut)


def reduce_kernel(
    z_,
    items,
    tok_ref,
    gain_ref,
    cos_ref,
    sin_ref,
    branch_ref,
    middle_ref,
    mgrad_ref,
    gain2_ref,
    gw_ref,
    gm_ref,
    gv_ref,
    heads_ref,
    wq_ref,
    g_down,
    g_wide,
    g_attn,
    *others,
):
    down, wide, attn, qkv, gain = items
    scratch = list(others)

    def take(count):
        taken = scratch[:count]
        del scratch[:count]
        return taken

    states = [take(3) for n in range(4)]
    out_ref, igrad_ref = take(2)
    results = [take(3) for n in range(4)]
    gain_results = take(3)
    heads_s, wq_s, entry_s, grads_s, branch_own, branch_s, back_s, back_in = take(8)
    middle_s, mgrad_s = take(2)
    g_qkv, g_gain, gain_acc, plain_s, pair_s = take(5)
    groups = [take(6) for item in items]
    (a_send, a_recv, y_send, y_recv, local_sem, load_sem, store_sem) = take(7)
    names = (
        "core_send",
        "core_recv",
        "own",
        "peer_send",
        "peer_recv",
        "in_send",
        "outer_recv",
        "inner_recv",
        "out_send",
        "done_send",
        "done_recv",
    )
    sems = dict(zip(names, take(len(names))))
    sources = (g_down, g_wide, g_attn, g_qkv, g_gain)
    refs = [(source, *group) for source, group in zip(sources, groups)]
    red = Reducer(z_, items, refs, sems)
    rates = (FF ** (-0.5), D ** (-0.5), RATE_ATTN, D ** (-0.5))
    finish = Finisher(z_, red, states, results, rates, plain_s, pair_s, load_sem, store_sem)
    f, c, t = red.f, red.c, red.t
    other = (f, c, 1 - t)
    count = z_.ctx // z_.share

    def to_token(j):
        return lax.rem(c + z_.share * j, z_.ctx)

    def from_head(j):
        return lax.rem(c + z_.ctx - z_.share * j, z_.ctx)

    def heads_copy(j):
        return remote(
            heads_ref.at[:, to_token(j)],
            heads_s.at[c // z_.share],
            a_send.at[j],
            a_recv.at[j],
            (f, to_token(j), t),
        )

    def branch_copy():
        return remote(branch_ref, branch_s, y_send.at[0], y_recv.at[0], other)

    def back_copy():
        return remote(back_s, back_in, y_send.at[1], y_recv.at[1], other)

    load_wq = pltpu.make_async_copy(wq_ref, wq_s, local_sem.at[1])
    load_branch = pltpu.make_async_copy(branch_ref, branch_own, local_sem.at[2])
    load_middle = pltpu.make_async_copy(middle_ref, middle_s, local_sem.at[3])
    load_mgrad = pltpu.make_async_copy(mgrad_ref, mgrad_s, local_sem.at[4])
    for item in (down, wide, attn):
        red.own_copy(item).start()
    load_wq.start()
    load_branch.start()
    load_middle.start()
    load_mgrad.start()
    greet(
        [(red.ahead(k), c, t) for k in range(1, z_.fsdp)]
        + [(f, lax.rem(c + j, z_.ctx), t) for j in range(1, z_.ctx)]
        + [other]
    )
    for j in range(1, count):
        heads_copy(j).start()
    branch_copy().start()
    own_heads = pltpu.make_async_copy(heads_ref.at[:, c], heads_s.at[c // z_.share], local_sem.at[0])
    own_heads.start()
    for item in (down, wide, attn):
        red.core_copy(item).start()

    for item in (down, wide, attn):
        red.own_copy(item).wait()
        red.core_sum(item)
        red.peer_start(item)

    tile = min(128, z_.rows)

    def entry_tile(i, carried):
        rows = pl.ds(pl.multiple_of(i * tile, tile), tile)
        normed, nothing = normalize(tok_ref[rows, :].astype(F32))
        for g in range(z_.fsdp):
            columns = slice(g * z_.shard, (g + 1) * z_.shard)
            entry_s[g, :, rows] = (normed[:, columns] * gain_ref[g, 0:1, :]).T.astype(BF16)
        return carried

    lax.fori_loop(0, z_.rows // tile, entry_tile, 0)

    red.peer_sum(down)
    red.outermost_start(down)

    branch_copy().wait_recv()
    load_branch.wait()
    load_middle.wait()

    def output_tile(i, carried):
        rows = pl.ds(pl.multiple_of(i * tile, tile), tile)
        branch = branch_own[rows, :].astype(F32) + branch_s[rows, :].astype(F32)
        out_ref[rows, :] = (middle_s[rows, :] + branch).astype(BF16)
        return carried

    lax.fori_loop(0, z_.rows // tile, output_tile, 0)

    own_heads.wait()
    for j in range(1, count):
        remote(
            heads_ref.at[:, c],
            heads_s.at[from_head(j) // z_.share],
            a_send.at[j],
            a_recv.at[j],
            red.mate,
        ).wait_recv()
    load_wq.wait()

    lane = lax.broadcasted_iota(jnp.int32, (z_.rows, 2 * HD), 1) < HD
    lane_half = lax.broadcasted_iota(jnp.int32, (z_.rows // 2, 2 * HD), 1) < HD
    mid_row = z_.rows // 2

    def chunk_grads(p, carried):
        pair = [
            heads_s[2 * p + i, 0:8].reshape(z_.rows, 2 * HD).astype(F32) for i in range(2)
        ]
        query = jnp.where(lane, pair[0], pltpu.roll(pair[1], HD, 1))
        key = jnp.where(lane, pltpu.roll(pair[0], HD, 1), pair[1])
        for kind, part in ((0, query), (1, key)):
            part = part * cos_ref[...] - swap_halves(part) * sin_ref[...]
            grads_s[p, :, 2 * HD * kind : 2 * HD * (kind + 1)] = part.astype(BF16)
        value = [
            heads_s[2 * p + i, 8:12].reshape(mid_row, 2 * HD).astype(F32) for i in range(2)
        ]
        early = jnp.where(lane_half, value[0], pltpu.roll(value[1], HD, 1))
        late = jnp.where(lane_half, pltpu.roll(value[0], HD, 1), value[1])
        grads_s[p, 0:mid_row, 4 * HD : 6 * HD] = early.astype(BF16)
        grads_s[p, mid_row : z_.rows, 4 * HD : 6 * HD] = late.astype(BF16)
        return carried

    lax.fori_loop(0, z_.pairs, chunk_grads, 0)

    for g in range(z_.fsdp):
        columns = slice(g * z_.shard, (g + 1) * z_.shard)

        def back_tile(i, carried):
            rows = pl.ds(pl.multiple_of(i * tile, tile), tile)
            total = jnp.zeros((tile, z_.shard), F32)
            for p in range(z_.pairs):
                total = total + lax.dot_general(
                    grads_s[p, rows, :],
                    wq_s[p, g],
                    (((1,), (1,)), ((), ())),
                    preferred_element_type=F32,
                )
            back_s[rows, columns] = total.astype(BF16)
            return carried

        lax.fori_loop(0, z_.rows // tile, back_tile, 0)
    back_copy().start()

    half = z_.shard // 2

    def qkv_tile(p, carried):
        for g in range(z_.fsdp):
            for side in range(2):
                grad = jnp.dot(
                    entry_s[g, side * half : (side + 1) * half, :],
                    grads_s[p],
                    preferred_element_type=F32,
                )
                rows = pl.ds(pl.multiple_of(p * half, half), half)
                g_qkv[g, side, rows, :] = grad.astype(BF16)
        return carried

    lax.fori_loop(0, z_.pairs, qkv_tile, 0)
    red.core_copy(qkv).start()
    red.own_copy(qkv).start()
    red.peer_sum(wide)
    red.outermost_start(wide)
    red.own_copy(qkv).wait()
    red.core_sum(qkv)
    red.peer_start(qkv)
    red.peer_sum(attn)
    red.outermost_start(attn)

    parts = [(item, cut) for item in (down, wide, attn) for cut in range(len(item.cuts))]
    def input_part():
        back_copy().wait_recv()
        load_mgrad.wait()
        gain_acc[...] = jnp.zeros(gain_acc.shape, F32)

        def input_tile(i, carried):
            rows = pl.ds(pl.multiple_of(i * tile, tile), tile)
            normed, scaling = normalize(tok_ref[rows, :].astype(F32))
            back = back_s[rows, :].astype(F32) + back_in[rows, :].astype(F32)
            gain_acc[0:1, :] += jnp.sum(back * normed, axis=0, keepdims=True)
            gains = jnp.concatenate([gain_ref[g, 0:1, :] for g in range(z_.fsdp)], axis=1)
            igrad_ref[rows, :] = (
                mgrad_s[rows, :] + norm_back(back * gains, normed, scaling)
            ).astype(BF16)
            return carried

        lax.fori_loop(0, z_.rows // tile, input_tile, 0)
        top = lax.broadcasted_iota(jnp.int32, (16, z_.shard), 0) == 0
        for g in range(z_.fsdp):
            columns = slice(g * z_.shard, (g + 1) * z_.shard)
            for side, row in ((0, gain_acc[0:1, columns]), (1, gain2_ref[0:1, columns])):
                g_gain[g, side] = jnp.where(top, row, 0.0).astype(BF16)
        red.core_copy(gain).start()
        red.own_copy(gain).start()
        red.peer_sum(qkv)
        red.outermost_start(qkv)
        red.own_copy(gain).wait()
        red.core_sum(gain)
        red.peer_start(gain)

    def gain_part():
        red.peer_sum(gain)
        red.outermost_start(gain)

    def gain_update():
        red.done_copy(gain, 0).wait_recv()
        inner_in, mate_out = red.refs[4][5:7]
        own_row = inner_in[0:1, :].astype(F32)
        mate_row = mate_out[0:1, :].astype(F32)
        first = (red.core == 0).astype(F32)
        for row, gradient in (
            (0, own_row * first + mate_row * (1.0 - first)),
            (1, mate_row * first + own_row * (1.0 - first)),
        ):
            place = slice(row, row + 1)
            got = adam_step(gw_ref[place, :], gradient, gm_ref[place, :], gv_ref[place, :], RATE_GAIN)
            for n in range(3):
                gain_results[n][place, :] = got[n]

    finish.gain_update = gain_update
    parts += [(qkv, cut) for cut in range(len(qkv.cuts))]
    spot = len(parts) - 2
    parts.insert(spot, (gain, 0))
    red.line(parts, finish, {spot - 4: input_part, spot: gain_part})

    own_sends = [heads_copy(j) for j in range(1, count)] + [branch_copy(), back_copy()]
    for copy in own_sends:
        copy.wait_send()
    red.settle()
    finish.settle()


def reduce_all(
    z_,
    tokens,
    gains,
    cosine,
    sines,
    branch,
    middle,
    middle_grad,
    gain2,
    gain_states,
    heads,
    wq,
    g_down,
    g_wide,
    g_attn,
    states,
):
    items = (
        Item(0, z_.units // 2, z_.shard, 2),
        Item(1, z_.units, z_.shard, 4),
        Item(2, z_.head_width // 2, z_.shard, 1),
        Item(3, z_.pairs * (z_.shard // 2), 6 * HD, z_.pairs),
        Item(4, 16, z_.shard, 1),
    )
    dma = pltpu.SemaphoreType.DMA
    peers = max(1, z_.fsdp - 1)
    pieces = sum(len(item.cuts) for item in items)
    groups = []
    for item in items:
        groups += [
            pltpu.VMEM((z_.fsdp, item.rows, item.columns), BF16),
            pltpu.VMEM((z_.fsdp, item.rows, item.columns), BF16),
            pltpu.VMEM((peers, item.rows, item.columns), BF16),
            pltpu.VMEM((item.rows, item.columns), BF16),
            pltpu.VMEM((item.rows, item.columns), BF16),
            pltpu.VMEM((item.rows, item.columns), BF16),
        ]
    count = z_.ctx // z_.share
    number = len(items)
    largest = max(rows for item in items[:3] for first, rows in item.cuts)
    rows = (z_.rows, z_.width)
    flat = [array for group in states for array in group]
    return pl.pallas_call(
        functools.partial(reduce_kernel, z_, items),
        out_shape=tuple(
            [jax.ShapeDtypeStruct(rows, BF16)] * 2
            + [jax.ShapeDtypeStruct(array.shape, F32) for array in flat]
            + [jax.ShapeDtypeStruct(array.shape, F32) for array in gain_states]
        ),
        in_specs=[vmem()] * 4
        + [anywhere()] * 3
        + [vmem()] * 4
        + [anywhere()] * 5
        + [anywhere()] * 12,
        out_specs=tuple([vmem()] * 2 + [anywhere()] * 12 + [vmem()] * 3),
        scratch_shapes=[
            pltpu.VMEM((z_.heads, 12, z_.block, 2 * HD), BF16),
            pltpu.VMEM((z_.pairs, z_.fsdp, z_.shard, 6 * HD), BF16),
            pltpu.VMEM((z_.fsdp, z_.shard, z_.rows), BF16),
            pltpu.VMEM((z_.pairs, z_.rows, 6 * HD), BF16),
            pltpu.VMEM(rows, BF16),
            pltpu.VMEM(rows, BF16),
            pltpu.VMEM(rows, BF16),
            pltpu.VMEM(rows, BF16),
            pltpu.VMEM(rows, F32),
            pltpu.VMEM(rows, F32),
            pltpu.VMEM((z_.fsdp, 2, items[3].rows, items[3].columns), BF16),
            pltpu.VMEM((z_.fsdp, 2, 16, z_.shard), BF16),
            pltpu.VMEM((8, z_.width), F32),
            pltpu.VMEM((2, 3, largest, z_.shard), F32),
            pltpu.VMEM((2, 3, 3, z_.shard // 2, 2 * HD), F32),
        ]
        + groups
        + [dma((count,)), dma((count,)), dma((2,)), dma((2,)), dma((5,)), dma((2, 3)), dma((2, 3))]
        + [
            dma((number,)),
            dma((number,)),
            dma((number,)),
            dma((number, peers)),
            dma((number, peers)),
        ]
        + [dma((pieces,))] * 6,
        compiler_params=pltpu.CompilerParams(
            collective_id=1, has_side_effects=True, vmem_limit_bytes=VMEM_BYTES
        ),
        name="reduce",
    )(
        tokens,
        gains,
        cosine,
        sines,
        branch,
        middle,
        middle_grad,
        gain2,
        *gain_states,
        heads,
        wq,
        g_down,
        g_wide,
        g_attn,
        *flat,
    )


def on_device(
    tokens,
    cotangent,
    lengths,
    order,
    qkv_weight,
    attn_weight,
    wide_weight,
    down_weight,
    norm_gains,
    qkv_mean,
    attn_mean,
    wide_mean,
    down_mean,
    gains_mean,
    qkv_square,
    attn_square,
    wide_square,
    down_square,
    gains_square,
):
    z_ = Sizes(
        lax.axis_size("fsdp"),
        lax.axis_size("ctx"),
        tokens.shape[0],
        tokens.shape[1],
        qkv_weight.shape[2],
        wide_weight.shape[2],
    )
    ctx_index = lax.axis_index("ctx")
    in_order, endings = sequence_ends(lengths[0], order[0])
    local_ids = jnp.arange(z_.rows, dtype=jnp.int32)
    cosine, sines = rope_tables(
        positions(in_order, endings, packed_place(local_ids, ctx_index, z_.ctx, z_.block))
    )
    gain_rows = jnp.pad(norm_gains.astype(BF16).astype(F32), ((0, 6), (0, 0)))
    packed, wq_full, wo_full, wi_full, gains_full = project(
        z_,
        tokens,
        gain_rows,
        cosine,
        sines,
        qkv_weight.transpose(1, 0, 2),
        attn_weight,
        wide_weight.transpose(1, 2, 0),
    )
    attended_packed, attended_turned, lse = attend(z_, endings, packed)
    branch_low, middle, middle_grad, gain_second, grads_packed, down_grad, wide_grad, attn_grad = (
        middle_part(
            z_,
            tokens,
            cotangent,
            gains_full,
            attended_packed,
            wo_full,
            wi_full,
            wide_weight.transpose(1, 2, 0),
            down_weight,
        )
    )
    head_grads = attend_back(
        z_,
        endings,
        packed,
        grads_packed,
        attended_turned,
        lse,
    )
    output, input_grad, *updated = reduce_all(
        z_,
        tokens,
        gains_full,
        cosine,
        sines,
        branch_low,
        middle,
        middle_grad,
        gain_second,
        (norm_gains, gains_mean, gains_square),
        head_grads,
        wq_full,
        down_grad,
        wide_grad,
        attn_grad,
        (
            (down_weight, down_mean, down_square),
            [array.transpose(1, 2, 0) for array in (wide_weight, wide_mean, wide_square)],
            (attn_weight, attn_mean, attn_square),
            [array.transpose(1, 0, 2) for array in (qkv_weight, qkv_mean, qkv_square)],
        ),
    )
    down_new, wide_new, attn_new, qkv_new, gains_new = [updated[n : n + 3] for n in range(0, 15, 3)]
    return (
        output,
        input_grad,
        *[array.transpose(1, 0, 2) for array in qkv_new],
        *attn_new,
        *[array.transpose(2, 0, 1) for array in wide_new],
        *down_new,
        *gains_new,
    )


def solution(mesh):
    return jax.shard_map(
        on_device,
        mesh=mesh,
        in_specs=(
            P(("fsdp", "ctx"), None),
            P(("fsdp", "ctx"), None),
            P("fsdp", None),
            P("fsdp", None),
            P("fsdp", None, "tp"),
            P("tp", "fsdp"),
            P("fsdp", None, "tp"),
            P("tp", "fsdp"),
            P(None, "fsdp"),
            P("fsdp", None, "tp"),
            P("tp", "fsdp"),
            P("fsdp", None, "tp"),
            P("tp", "fsdp"),
            P(None, "fsdp"),
            P("fsdp", None, "tp"),
            P("tp", "fsdp"),
            P("fsdp", None, "tp"),
            P("tp", "fsdp"),
            P(None, "fsdp"),
        ),
        out_specs=(
            P(("fsdp", "ctx"), None),
            P(("fsdp", "ctx"), None),
            P("fsdp", None, "tp"),
            P("fsdp", None, "tp"),
            P("fsdp", None, "tp"),
            P("tp", "fsdp"),
            P("tp", "fsdp"),
            P("tp", "fsdp"),
            P("fsdp", None, "tp"),
            P("fsdp", None, "tp"),
            P("fsdp", None, "tp"),
            P("tp", "fsdp"),
            P("tp", "fsdp"),
            P("tp", "fsdp"),
            P(None, "fsdp"),
            P(None, "fsdp"),
            P(None, "fsdp"),
        ),
        check_vma=False,
    )
```

```python
import functools

import jax
import jax.numpy as jnp
from jax import lax
from jax.experimental import pallas as pl
from jax.experimental.pallas import tpu as pltpu
from jax.sharding import PartitionSpec as P

D = 1024
HD = 64
FF = 2624
STEP = 10


NORM_EPS = 1e-05
ROPE_BASE = 160000.0
BETA_FIRST = 0.9
BETA_SECOND = 0.98
ADAM_EPS = 1e-06
DECAY = 0.01
RATE_ATTN = 0.5
RATE_GAIN = 0.8
MASKED = -1e30

MESH = pl.DeviceIdType.MESH
BF16 = jnp.bfloat16
F32 = jnp.float32
VMEM_BYTES = 62 * 2**20
REDUCE_BYTES = 46 * 2**20


class Sizes:
    def __init__(self, fsdp, ctx, rows, width, head_width, units):
        self.fsdp = fsdp
        self.ctx = ctx
        self.chips = ctx // 2
        self.rows = rows
        self.block = rows // 8
        self.group = rows * ctx
        self.width = width
        self.shard = width // fsdp
        self.heads = head_width // HD
        self.head_width = head_width
        self.units = units
        self.share = max(1, ctx // self.heads)
        self.pairs = self.heads // 2
        self.ranks = ctx // self.pairs


def remote(src, dst, send, recv, device):
    return pltpu.make_async_remote_copy(
        src_ref=src,
        dst_ref=dst,
        send_sem=send,
        recv_sem=recv,
        device_id=device,
        device_id_type=MESH,
    )


def greet(devices):
    barrier = pltpu.get_barrier_semaphore()
    for device in devices:
        pl.semaphore_signal(barrier, inc=1, device_id=device, device_id_type=MESH)
    pl.semaphore_wait(barrier, len(devices))


def vmem():
    return pl.BlockSpec(memory_space=pltpu.VMEM)


def anywhere():
    return pl.BlockSpec(memory_space=pl.ANY)


def normalize(values):
    centered = values - jnp.mean(values, axis=1, keepdims=True)
    scaling = lax.rsqrt(jnp.mean(centered * centered, axis=1, keepdims=True) + NORM_EPS)
    return (centered * scaling, scaling)


def norm_back(grad_hat, normed, scaling):
    return scaling * (
        grad_hat
        - jnp.mean(grad_hat, axis=1, keepdims=True)
        - normed * jnp.mean(grad_hat * normed, axis=1, keepdims=True)
    )


def swap_halves(values):
    lane = lax.broadcasted_iota(jnp.int32, values.shape, 1)
    return jnp.where(
        lane % HD < HD // 2, pltpu.roll(values, 2 * HD - HD // 2, 1), pltpu.roll(values, HD // 2, 1)
    )


def packed_place(local_row, device, devices, block_size):
    return (local_row // block_size * devices + device) * block_size + local_row % block_size


def sequence_ends(lengths_row, order_row):
    count_seqs = lengths_row.shape[0]
    chosen = (order_row[:, None] == jnp.arange(count_seqs, dtype=jnp.int32)[None, :]).astype(
        jnp.int32
    )
    in_order = jnp.sum(chosen * lengths_row[None, :], axis=1)
    return (in_order, jnp.cumsum(in_order))


def positions(in_order, endings, places):
    passed = (endings[None, :] <= places[:, None]).astype(jnp.int32)
    return places - jnp.sum(passed * in_order[None, :], axis=1)


def rope_tables(position):
    half_size = HD // 2
    frequency = ROPE_BASE ** (-(2.0 * jnp.arange(half_size, dtype=jnp.float32)) / (2.0 * half_size))
    angles = position.astype(jnp.float32)[:, None] * frequency[None, :]
    cosine, sines = jnp.cos(angles), jnp.sin(angles)
    return (
        jnp.concatenate([cosine] * 4, axis=1),
        jnp.concatenate([-sines, sines, -sines, sines], axis=1),
    )


def cuts_of(rows, count):
    unit = rows // 16
    marks = [16 * (unit * i // count) for i in range(count + 1)]
    return [(a, b - a) for a, b in zip(marks, marks[1:]) if b > a]


def over_rows(start, rows, step, body):
    whole = rows // step

    def turn(i, carried):
        body(pl.multiple_of(start + i * step, 16), step)
        return carried

    if whole > 1:
        lax.fori_loop(0, whole, turn, 0)
    elif whole == 1:
        body(start, step)
    if rows % step:
        body(start + whole * step, rows % step)


def project_kernel(
    z_,
    tok_ref,
    gain_ref,
    cos_ref,
    sin_ref,
    wq_ref,
    wo_ref,
    wi_ref,
    packed_ref,
    wq_out,
    wo_out,
    wi_out,
    gain_out,
    entry_s,
    wq_f,
    wo_f,
    wi_f,
    wq_s,
    wo_s,
    wi_s,
    send_s,
    gain_s,
    gain_send,
    gain_recv,
    wq_send,
    wq_recv,
    wq_fsend,
    wq_frecv,
    w_send,
    w_recv,
    w_fsend,
    w_frecv,
    a_send,
    a_recv,
    local_sem,
):
    f, c, t = lax.axis_index("fsdp"), lax.axis_index("ctx"), lax.axis_index("tp")
    core = lax.rem(c, 2)
    mate = (f, c + 1 - 2 * core, t)
    others = range(1, z_.fsdp)
    mine = c // z_.ranks
    place_in = lax.rem(c, z_.ranks)
    last = z_.pairs - 1
    unit_half = z_.units // 2

    def ahead(k):
        return lax.rem(f + k, z_.fsdp)

    def behind(k):
        return lax.rem(f + z_.fsdp - k, z_.fsdp)

    def pair_of(s):
        return lax.rem(mine + 1 + s, z_.pairs)

    load_wq = pltpu.make_async_copy(wq_ref, wq_f, local_sem.at[0])
    load_wo = pltpu.make_async_copy(wo_ref, wo_f, local_sem.at[1])
    load_wi = pltpu.make_async_copy(wi_ref.at[:, 0:unit_half], wi_f, local_sem.at[2])
    load_wq.start()
    load_wo.start()
    load_wi.start()
    greet(
        [(ahead(k), c, t) for k in others]
        + [(f, lax.rem(c + j, z_.ctx), t) for j in range(1, z_.ctx)]
    )

    half = z_.shard // 2
    own_half = pl.ds(pl.multiple_of(core * half, half), half)
    mate_half = pl.ds(pl.multiple_of((1 - core) * half, half), half)

    def gain_copy(k, owner):
        return remote(
            gain_ref, gain_s.at[owner], gain_send.at[k - 1], gain_recv.at[k - 1], (ahead(k), c, t)
        )

    def wq_copy(s, k, owner):
        place = wq_s.at[pair_of(s), owner, own_half]
        return remote(
            place, place, wq_send.at[s, k - 1], wq_recv.at[s, k - 1], (ahead(k), c, t)
        )

    def wq_pass(s, k, rows):
        place = wq_s.at[pair_of(s), behind(k), rows]
        return remote(place, place, wq_fsend.at[s, k - 1], wq_frecv.at[s, k - 1], mate)

    attn_half = z_.head_width // 2

    def weight_places(side, owner):
        rows = pl.ds(pl.multiple_of(side * attn_half, attn_half), attn_half)
        return (
            (wo_s.at[rows], wo_out.at[owner, rows]),
            (wi_s.at[side], wi_out.at[side, owner]),
        )

    pieces = 2

    def w_copy(n, k, owner):
        source, place = weight_places(core, owner)[n]
        return remote(source, place, w_send.at[n, k - 1], w_recv.at[n, k - 1], (ahead(k), c, t))

    def w_pass(n, k, side):
        place = weight_places(side, behind(k))[n][1]
        return remote(place, place, w_fsend.at[n, k - 1], w_frecv.at[n, k - 1], mate)

    def head_copy(s, i):
        return remote(
            send_s.at[s, i // z_.share],
            packed_ref.at[:, c],
            a_send.at[s, i],
            a_recv.at[s, place_in],
            (f, pair_of(s) * z_.ranks + i, t),
        )

    def head_arrival(s, i):
        source = lax.rem(mine + 2 * z_.pairs - 1 - s, z_.pairs) * z_.ranks + i
        return remote(
            send_s.at[s, 0], packed_ref.at[:, source], a_send.at[s, 0], a_recv.at[s, i], mate
        )

    def near_copy(j):
        i = lax.rem(place_in + j, z_.ranks)
        return remote(
            send_s.at[last, i // z_.share],
            packed_ref.at[:, c],
            a_send.at[last, j],
            a_recv.at[last, j],
            (f, mine * z_.ranks + i, t),
        )

    def near_arrival(j):
        source = mine * z_.ranks + lax.rem(place_in + z_.ranks - j, z_.ranks)
        return remote(
            send_s.at[last, 0], packed_ref.at[:, source], a_send.at[last, j], a_recv.at[last, j], mate
        )

    for k in others:
        gain_copy(k, f).start()
    load_wq.wait()

    def round_pair(s):
        p = pair_of(s)
        columns = pl.ds(pl.multiple_of(p * 2 * HD, 2 * HD), 2 * HD)
        for kind in range(3):
            wq_s[p, f, :, kind * 2 * HD : (kind + 1) * 2 * HD] = wq_f[kind, :, columns].astype(BF16)

    for s in range(2):
        round_pair(s)
        for k in others:
            wq_copy(s, k, f).start()
    gain_s[f] = gain_ref[...]
    for k in others:
        gain_copy(k, behind(k)).wait()

    gain_out[...] = gain_s[...]
    tile = min(128, z_.rows)

    def norm_tile(i, carried):
        rows = pl.ds(pl.multiple_of(i * tile, tile), tile)
        normed, nothing = normalize(tok_ref[rows, :].astype(F32))
        for g in range(z_.fsdp):
            columns = slice(g * z_.shard, (g + 1) * z_.shard)
            entry_s[g, rows, :] = (normed[:, columns] * gain_s[g, 0:1, :]).astype(BF16)
        return carried

    lax.fori_loop(0, z_.rows // tile, norm_tile, 0)
    load_wo.wait()
    wo_s[...] = wo_f[...].astype(BF16)
    own_wo = pltpu.make_async_copy(wo_s, wo_out.at[f], local_sem.at[1])
    own_wo.start()
    load_wi.wait()
    own_wi = pltpu.make_async_copy(wi_s, wi_out.at[:, f], local_sem.at[2])

    def round_wide(side):
        def turn(first, rows):
            place = pl.ds(first, rows)
            wi_s[side, place, :] = wi_f[side, place, :].astype(BF16)

        over_rows(0, unit_half, 128, turn)

    lane = lax.broadcasted_iota(jnp.int32, (z_.rows, 2 * HD), 1) < HD
    lane_half = lax.broadcasted_iota(jnp.int32, (z_.rows // 2, 2 * HD), 1) < HD

    def chunk_step(s, carried):
        @pl.when(s + 2 < z_.pairs)
        def more():
            round_pair(s + 2)
            for k in others:
                wq_copy(s + 2, k, f).start()

        @pl.when(s + 2 == z_.pairs)
        def attn_part():
            for k in others:
                w_copy(0, k, f).start()
            round_wide(core)

        @pl.when(s + 1 == z_.pairs)
        def wide_part():
            for k in others:
                w_copy(1, k, f).start()

        for k in others:
            wq_copy(s, k, behind(k)).wait_recv()
            wq_pass(s, k, own_half).start()
        for k in others:
            wq_pass(s, k, mate_half).wait_recv()
        p = pair_of(s)
        total = jnp.zeros((z_.rows, 6 * HD), F32)
        for g in range(z_.fsdp):
            total = total + jnp.dot(entry_s[g], wq_s[p, g], preferred_element_type=F32)
        turned = []
        for kind in range(2):
            part = total[:, kind * 2 * HD : (kind + 1) * 2 * HD]
            turned.append(part * cos_ref[...] + swap_halves(part) * sin_ref[...])
        query, key = turned
        value = total[:, 4 * HD : 6 * HD]
        early, late = value[: z_.rows // 2], value[z_.rows // 2 :]
        both = (
            (
                jnp.where(lane, query, pltpu.roll(key, HD, 1)),
                jnp.where(lane_half, early, pltpu.roll(late, HD, 1)),
            ),
            (
                jnp.where(lane, pltpu.roll(query, HD, 1), key),
                jnp.where(lane_half, pltpu.roll(early, HD, 1), late),
            ),
        )
        for i in range(2):
            send_s[s, i, 0:8] = both[i][0].astype(BF16).reshape(8, z_.block, 2 * HD)
            send_s[s, i, 8:12] = both[i][1].astype(BF16).reshape(4, z_.block, 2 * HD)

        @pl.when(s < last)
        def away():
            for i in range(z_.ranks):
                head_copy(s, i).start()

        return carried

    lax.fori_loop(0, z_.pairs, chunk_step, 0)
    kept = pltpu.make_async_copy(
        send_s.at[last, place_in // z_.share], packed_ref.at[:, c], local_sem.at[3]
    )
    kept.start()
    for j in range(1, z_.ranks):
        near_copy(j).start()
    keep_wq = pltpu.make_async_copy(wq_s, wq_out, local_sem.at[4])
    keep_wq.start()
    round_wide(1 - core)
    own_wi.start()
    for n in range(pieces):
        for k in others:
            w_copy(n, k, behind(k)).wait_recv()
            w_pass(n, k, core).start()
    for s in range(last):
        for i in range(z_.ranks):
            head_arrival(s, i).wait_recv()
            head_copy(s, i).wait_send()
    for j in range(1, z_.ranks):
        near_arrival(j).wait_recv()
        near_copy(j).wait_send()
    for k in others:
        for s in range(z_.pairs):
            wq_copy(s, k, f).wait_send()
            wq_pass(s, k, own_half).wait_send()
        for n in range(pieces):
            w_copy(n, k, f).wait_send()
            w_pass(n, k, core).wait_send()
            w_pass(n, k, 1 - core).wait_recv()
    kept.wait()
    keep_wq.wait()
    own_wo.wait()
    own_wi.wait()


def project(z_, tokens, gains, cosine, sines, wq, wo, wi):
    peers = max(1, z_.fsdp - 1)
    dma = pltpu.SemaphoreType.DMA
    return pl.pallas_call(
        functools.partial(project_kernel, z_),
        out_shape=(
            jax.ShapeDtypeStruct((12, z_.ctx, z_.block, 2 * HD), BF16),
            jax.ShapeDtypeStruct((z_.pairs, z_.fsdp, z_.shard, 6 * HD), BF16),
            jax.ShapeDtypeStruct((z_.fsdp, z_.head_width, z_.shard), BF16),
            jax.ShapeDtypeStruct((2, z_.fsdp, z_.units // 2, z_.shard), BF16),
            jax.ShapeDtypeStruct((z_.fsdp, 8, z_.shard), F32),
        ),
        in_specs=[vmem()] * 4 + [anywhere()] * 3,
        out_specs=(anywhere(), anywhere(), anywhere(), anywhere(), vmem()),
        scratch_shapes=[
            pltpu.VMEM((z_.fsdp, z_.rows, z_.shard), BF16),
            pltpu.VMEM((3, z_.shard, z_.head_width), F32),
            pltpu.VMEM((z_.head_width, z_.shard), F32),
            pltpu.VMEM((2, z_.units // 2, z_.shard), F32),
            pltpu.VMEM((z_.pairs, z_.fsdp, z_.shard, 6 * HD), BF16),
            pltpu.VMEM((z_.head_width, z_.shard), BF16),
            pltpu.VMEM((2, z_.units // 2, z_.shard), BF16),
            pltpu.VMEM((z_.pairs, 2, 12, z_.block, 2 * HD), BF16),
            pltpu.VMEM((z_.fsdp, 8, z_.shard), F32),
            dma((peers,)),
            dma((peers,)),
            dma((z_.pairs, peers)),
            dma((z_.pairs, peers)),
            dma((z_.pairs, peers)),
            dma((z_.pairs, peers)),
            dma((2, peers)),
            dma((2, peers)),
            dma((2, peers)),
            dma((2, peers)),
            dma((z_.pairs, z_.ranks)),
            dma((z_.pairs, z_.ranks)),
            dma((5,)),
        ],
        compiler_params=pltpu.CompilerParams(
            collective_id=0, has_side_effects=True, vmem_limit_bytes=VMEM_BYTES
        ),
        name="project",
    )(tokens, gains, cosine, sines, wq, wo, wi)


def packing(lengths_ref, order_ref):
    count = order_ref.shape[1]
    lengths = [lengths_ref[0, order_ref[0, k]] for k in range(count)]
    longest, start, chosen = lengths[0], jnp.int32(0), jnp.int32(0)
    passed = lengths[0]
    for k in range(1, count):
        more = lengths[k] > longest
        longest = jnp.where(more, lengths[k], longest)
        start = jnp.where(more, passed, start)
        chosen = jnp.where(more, k, chosen)
        passed = passed + lengths[k]
    ends, total = [], jnp.int32(0)
    for j in range(count):
        length = lengths[j]
        for first in range(1, count):
            length = jnp.where(chosen == first, lengths[(first + j) % count], length)
        total = total + length
        ends.append(total)
    return (start, ends)


def sequence_at(ends, place):
    start, end = jnp.int32(0), ends[0]
    for k in range(len(ends) - 1):
        past = ends[k] <= place
        start = jnp.where(past, ends[k], start)
        end = jnp.where(past, ends[k + 1], end)
    return (start, end)


def segments_of(ends, places):
    segment = jnp.zeros(places.shape, jnp.int32)
    for end in ends:
        segment = segment + (end <= places).astype(jnp.int32)
    return segment


def turned_rows(stage, start, group, rows):
    return stage[pl.ds(lax.rem(start, group), rows), :]


def attend_kernel(
    z_,
    q_tile,
    k_tile,
    lengths_ref,
    order_ref,
    packed_ref,
    out_ref,
    outt_ref,
    lse_ref,
    swapped_ref,
    query_ref,
    key_ref,
    value_ref,
    value_s,
    top_s,
    total_s,
    stage_s,
):
    group = z_.group
    half = group // 2
    piece = min(512, half)
    scaling = HD ** (-0.5)
    sums = 16
    shift, ends = packing(lengths_ref, order_ref)
    packed_ref = packed_ref.reshape(group + half, 2 * HD)
    out_ref = out_ref.reshape(half, 2 * HD)
    query_ref[HD : 2 * HD, :] = jnp.zeros((HD, group), BF16)
    value_s[HD : HD + sums, :] = jnp.ones((sums, group), BF16)
    lane = lax.broadcasted_iota(jnp.int32, (piece, 2 * HD), 1) < HD

    def place(i, offset=0):
        return pl.ds(pl.multiple_of(offset + i * piece, piece), piece)

    def stage_pairs(i, carried):
        stage_s[place(i), :] = packed_ref[place(i), :].astype(F32)
        return carried

    lax.fori_loop(0, group // piece, stage_pairs, 0)
    stage_s[group : group + piece, :] = stage_s[0:piece, :]

    def pairs(i, carried):
        pair = turned_rows(stage_s, shift + i * piece, group, piece)
        swapped_ref[place(i), :] = pltpu.roll(pair, HD, 1).astype(BF16)
        turned = pair.astype(BF16).T
        query_ref[0:HD, place(i)] = (turned[0:HD].astype(F32) * scaling).astype(BF16)
        key_ref[:, place(i)] = turned[HD : 2 * HD]
        return carried

    lax.fori_loop(0, group // piece, pairs, 0)

    def stage_values(i, carried):
        both = packed_ref[place(i, group), :].astype(F32)
        stage_s[place(i), :] = both
        stage_s[place(i, half), :] = pltpu.roll(both, HD, 1)
        return carried

    lax.fori_loop(0, half // piece, stage_values, 0)
    stage_s[group : group + piece, :] = stage_s[0:piece, :]

    def values(i, carried):
        value = turned_rows(stage_s, shift + i * piece, group, piece)
        low = jnp.where(lane, value, 0.0).astype(BF16)
        value_ref[place(i), :] = low
        value_s[0:HD, place(i)] = low.T[0:HD]
        return carried

    lax.fori_loop(0, group // piece, values, 0)

    def one_tile(i, carried):
        first = pl.multiple_of(i * q_tile, q_tile)
        columns = pl.ds(first, q_tile)
        low, low_end = sequence_at(ends, first)
        high_start, high = sequence_at(ends, first + q_tile - 1)
        single = low == high_start
        top_s[...] = jnp.full(top_s.shape, MASKED, F32)
        total_s[...] = jnp.zeros(total_s.shape, F32)

        def one_step(j, masked):
            start = pl.multiple_of(j * k_tile, k_tile)
            rows = pl.ds(start, k_tile)
            scores = jnp.dot(swapped_ref[rows, :], query_ref[:, columns], preferred_element_type=F32)
            if masked:
                key_seg = segments_of(
                    ends, start + lax.broadcasted_iota(jnp.int32, (k_tile, 1), 0)
                )
                query_seg = segments_of(
                    ends, first + lax.broadcasted_iota(jnp.int32, (1, q_tile), 1)
                )
                scores = jnp.where(key_seg == query_seg, scores, MASKED)
            before = top_s[0:1, :]
            after = jnp.maximum(before, jnp.max(scores, axis=0, keepdims=True))
            weights = jnp.exp(scores - after).astype(BF16)
            top_s[0:1, :] = after
            total_s[...] = total_s[...] * jnp.exp(before - after) + jnp.dot(
                value_s[:, rows], weights, preferred_element_type=F32
            )

        def step(j, inner):
            start = j * k_tile
            whole = single & (start >= low) & (start + k_tile <= high)

            @pl.when(whole)
            def plain():
                one_step(j, False)

            @pl.when(jnp.logical_not(whole))
            def partial():
                one_step(j, True)

            return inner

        lax.fori_loop(low // k_tile, (high + k_tile - 1) // k_tile, step, 0)
        summed = total_s[HD : HD + 1, :]
        lse_ref[:, columns] = jnp.broadcast_to(top_s[0:1, :] + jnp.log(summed), (8, q_tile))
        outt_ref[:, columns] = total_s[0:HD, :] / summed
        return carried

    lax.fori_loop(0, group // q_tile, one_tile, 0)

    def stage_out(i, carried):
        both = jnp.concatenate([outt_ref[:, place(i)], jnp.zeros((HD, piece), F32)], axis=0)
        stage_s[place(i), :] = both.astype(BF16).T.astype(F32)
        return carried

    lax.fori_loop(0, group // piece, stage_out, 0)
    stage_s[group : group + piece, :] = stage_s[0:piece, :]

    def finish(i, carried):
        early = turned_rows(stage_s, group - shift + i * piece, group, piece)
        late = turned_rows(stage_s, group + half - shift + i * piece, group, piece)
        out_ref[place(i), :] = jnp.where(lane, early, pltpu.roll(late, HD, 1)).astype(BF16)
        return carried

    lax.fori_loop(0, half // piece, finish, 0)


def attend(z_, lengths, order, packed):
    group = z_.group
    half = group // 2
    q_tile, k_tile = min(1024, half), min(1024, half)
    scalars = pl.BlockSpec(memory_space=pltpu.SMEM)
    return pl.pallas_call(
        functools.partial(attend_kernel, z_, q_tile, k_tile),
        out_shape=(
            jax.ShapeDtypeStruct((4, z_.ctx, z_.block, 2 * HD), BF16),
            jax.ShapeDtypeStruct((HD, group), F32),
            jax.ShapeDtypeStruct((8, group), F32),
            jax.ShapeDtypeStruct((group, 2 * HD), BF16),
            jax.ShapeDtypeStruct((2 * HD, group), BF16),
            jax.ShapeDtypeStruct((HD, group), BF16),
            jax.ShapeDtypeStruct((group, 2 * HD), BF16),
        ),
        in_specs=[scalars, scalars, vmem()],
        out_specs=tuple([vmem()] * 7),
        scratch_shapes=[
            pltpu.VMEM((HD + 16, group), BF16),
            pltpu.VMEM((8, q_tile), F32),
            pltpu.VMEM((HD + 16, q_tile), F32),
            pltpu.VMEM((group + min(512, half), 2 * HD), F32),
        ],
        compiler_params=pltpu.CompilerParams(vmem_limit_bytes=VMEM_BYTES),
        name="attend",
    )(lengths, order, packed)


def attend_back_kernel(
    z_,
    lengths_ref,
    order_ref,
    lse_ref,
    packed_grad,
    outt_ref,
    swapped_ref,
    query_ref,
    key_ref,
    value_ref,
    out_ref,
    turned_s,
    grad_s,
    delta_s,
    stage_s,
    dquery_s,
    dvalue_s,
    key_acc,
    value_acc,
):
    group = z_.group
    half = group // 2
    tile = min(512, half)
    scaling = HD ** (-0.5)
    shift, ends = packing(lengths_ref, order_ref)
    lane = lax.broadcasted_iota(jnp.int32, (tile, 2 * HD), 1) < HD
    flat_grad = packed_grad.reshape(half, 2 * HD)
    flat_out = out_ref.reshape(group + half, 2 * HD)

    def place(i, offset=0):
        return pl.ds(pl.multiple_of(offset + i * tile, tile), tile)

    def stage_grads(i, carried):
        both = flat_grad[place(i), :].astype(F32)
        stage_s[place(i), :] = both
        stage_s[place(i, half), :] = pltpu.roll(both, HD, 1)
        return carried

    lax.fori_loop(0, half // tile, stage_grads, 0)
    stage_s[group : group + tile, :] = stage_s[0:tile, :]

    def order_grads(i, carried):
        rows = turned_rows(stage_s, shift + i * tile, group, tile)
        low = jnp.where(lane, rows, 0.0).astype(BF16)
        grad_s[place(i), :] = low
        turned = low.T[0:HD]
        turned_s[0:HD, place(i)] = turned
        turned_s[HD : 2 * HD, place(i)] = key_ref[:, place(i)]
        delta = jnp.sum(turned.astype(F32) * outt_ref[:, place(i)], axis=0, keepdims=True)
        delta_s[:, place(i)] = jnp.broadcast_to(delta, (8, tile))
        dquery_s[:, place(i)] = jnp.zeros((HD, tile), F32)
        return carried

    lax.fori_loop(0, group // tile, order_grads, 0)

    def one_step(rows, start, first, masked):
        columns = pl.ds(first, tile)
        scores = jnp.dot(swapped_ref[rows, :], query_ref[:, columns], preferred_element_type=F32)
        chances = jnp.exp(scores - lse_ref[0:1, columns])
        if masked:
            key_seg = segments_of(ends, start + lax.broadcasted_iota(jnp.int32, (tile, 1), 0))
            query_seg = segments_of(ends, first + lax.broadcasted_iota(jnp.int32, (1, tile), 1))
            chances = jnp.where(key_seg == query_seg, chances, 0.0)
        chance_grad = jnp.dot(
            value_ref[rows, :], turned_s[:, columns], preferred_element_type=F32
        )
        score_grad = (chances * (chance_grad - delta_s[0:1, columns])).astype(BF16)
        value_acc[...] += jnp.dot(
            chances.astype(BF16), grad_s[columns, :], preferred_element_type=F32
        )
        key_acc[...] += jnp.dot(score_grad, swapped_ref[columns, :], preferred_element_type=F32)
        dquery_s[:, columns] += jnp.dot(
            turned_s[HD : 2 * HD, rows], score_grad, preferred_element_type=F32
        )

    def one_tile(j, masked):
        start = pl.multiple_of(j * tile, tile)
        rows = pl.ds(start, tile)
        key_acc[...] = jnp.zeros(key_acc.shape, F32)
        value_acc[...] = jnp.zeros(value_acc.shape, F32)
        low, high = jnp.int32(0), jnp.int32(half)
        if masked:
            low, low_end = sequence_at(ends, start)
            high_start, high = sequence_at(ends, start + tile - 1)

        def step(i, inner):
            one_step(rows, start, pl.multiple_of(i * tile, tile), masked)
            return inner

        lax.fori_loop(low // tile, (high + tile - 1) // tile, step, 0)
        dvalue_s[rows, :] = value_acc[...].astype(BF16)
        stage_s[rows, :] = key_acc[...]

    def long_tile(j, carried):
        one_tile(j, False)
        return carried

    def other_tile(j, carried):
        one_tile(j, True)
        return carried

    lax.fori_loop(0, half // tile, long_tile, 0)
    lax.fori_loop(half // tile, group // tile, other_tile, 0)

    def join_pairs(i, carried):
        turned = jnp.concatenate([dquery_s[:, place(i)], jnp.zeros((HD, tile), F32)], axis=0)
        query_rows = (turned * scaling).astype(BF16).T.astype(F32)
        stage_s[place(i), :] = jnp.where(lane, query_rows, stage_s[place(i), :] * scaling)
        return carried

    lax.fori_loop(0, group // tile, join_pairs, 0)
    stage_s[group : group + tile, :] = stage_s[0:tile, :]

    def order_pairs(i, carried):
        rows = turned_rows(stage_s, group - shift + i * tile, group, tile)
        flat_out[place(i), :] = rows.astype(BF16)
        return carried

    lax.fori_loop(0, group // tile, order_pairs, 0)

    def stage_values(i, carried):
        stage_s[place(i), :] = dvalue_s[place(i), :].astype(F32)
        return carried

    lax.fori_loop(0, group // tile, stage_values, 0)
    stage_s[group : group + tile, :] = stage_s[0:tile, :]

    def order_values(i, carried):
        early = turned_rows(stage_s, group - shift + i * tile, group, tile)
        late = turned_rows(stage_s, group + half - shift + i * tile, group, tile)
        flat_out[place(i, group), :] = jnp.where(lane, early, pltpu.roll(late, HD, 1)).astype(BF16)
        return carried

    lax.fori_loop(0, half // tile, order_values, 0)


def attend_back(z_, lengths, order, lse, grads, turned_out, swapped, query, key, value):
    group = z_.group
    tile = min(512, group // 2)
    scalars = pl.BlockSpec(memory_space=pltpu.SMEM)
    return pl.pallas_call(
        functools.partial(attend_back_kernel, z_),
        out_shape=jax.ShapeDtypeStruct((12, z_.ctx, z_.block, 2 * HD), BF16),
        in_specs=[scalars, scalars] + [vmem()] * 7,
        out_specs=vmem(),
        scratch_shapes=[
            pltpu.VMEM((2 * HD, group), BF16),
            pltpu.VMEM((group, 2 * HD), BF16),
            pltpu.VMEM((8, group), F32),
            pltpu.VMEM((group + tile, 2 * HD), F32),
            pltpu.VMEM((HD, group), F32),
            pltpu.VMEM((group, 2 * HD), BF16),
            pltpu.VMEM((tile, 2 * HD), F32),
            pltpu.VMEM((tile, 2 * HD), F32),
        ],
        compiler_params=pltpu.CompilerParams(vmem_limit_bytes=VMEM_BYTES),
        name="attend_back",
    )(lengths, order, lse, grads, turned_out, swapped, query, key, value)


def middle_kernel(
    z_,
    tok_ref,
    cot_ref,
    gain_ref,
    heads_ref,
    wo_ref,
    wi_ref,
    wide_ref,
    down_ref,
    branch_ref,
    middle_ref,
    mgrad_ref,
    gain2_ref,
    grads_ref,
    g_down,
    g_wide,
    g_attn,
    heads_s,
    wo_s,
    wi_s,
    wide_f,
    down_f,
    wm_s,
    mixed_s,
    mixed_t,
    sum_s,
    sum_in,
    back_s,
    back_in,
    entry_s,
    branch_s,
    middle_s,
    grad_f,
    normed_s,
    scale_s,
    gate_s,
    hgrad_s,
    hidden_s,
    hidden_t,
    gated_s,
    gated_t,
    mgrad_s,
    dsend_s,
    down_s,
    wide_s,
    attn_s,
    a_send,
    a_recv,
    d_send,
    d_recv,
    y_send,
    y_recv,
    w_send,
    w_recv,
    f_send,
    f_recv,
    local_sem,
):
    f, c, t = lax.axis_index("fsdp"), lax.axis_index("ctx"), lax.axis_index("tp")
    core = lax.rem(c, 2)
    mate = (f, c + 1 - 2 * core, t)
    other = (f, c, 1 - t)
    count = z_.ctx // z_.share
    others = range(1, z_.fsdp)
    half = z_.rows // 2

    def ahead(k):
        return lax.rem(f + k, z_.fsdp)

    def behind(k):
        return lax.rem(f + z_.fsdp - k, z_.fsdp)

    def to_token(j):
        return lax.rem(c + z_.share * j, z_.ctx)

    def from_head(j):
        return lax.rem(c + z_.ctx - z_.share * j, z_.ctx)

    def heads_copy(j):
        return remote(
            heads_ref.at[:, to_token(j)],
            heads_s.at[c // z_.share],
            a_send.at[j],
            a_recv.at[j],
            (f, to_token(j), t),
        )

    def heads_arrival(j):
        return remote(
            heads_ref.at[:, c],
            heads_s.at[from_head(j) // z_.share],
            a_send.at[j],
            a_recv.at[j],
            mate,
        )

    def grads_copy(j):
        rank = lax.rem(c + j, z_.ctx)
        return remote(
            dsend_s.at[rank // z_.share],
            grads_ref.at[:, c],
            d_send.at[j],
            d_recv.at[j],
            (f, rank, t),
        )

    def grads_arrival(j):
        source = lax.rem(c + z_.ctx - j, z_.ctx)
        return remote(
            dsend_s.at[0], grads_ref.at[:, source], d_send.at[j], d_recv.at[j], mate
        )

    units_half = z_.units // 2

    def weight_place(n, side, owner):
        if n == 0:
            rows = pl.ds(pl.multiple_of(side * units_half, 16), units_half)
            return wm_s.at[owner, rows]
        return wi_s.at[side, owner, units_half : z_.units]

    def w_copy(n, k, owner):
        place = weight_place(n, core, owner)
        return remote(place, place, w_send.at[n, k - 1], w_recv.at[n, k - 1], (ahead(k), c, t))

    def w_pass(n, k, side):
        place = weight_place(n, side, behind(k))
        return remote(place, place, f_send.at[n, k - 1], f_recv.at[n, k - 1], mate)

    def sum_copy(r):
        rows = pl.ds(r * half, half)
        return remote(sum_s.at[rows], sum_in.at[rows], y_send.at[r], y_recv.at[r], other)

    def back_copy(r):
        rows = pl.ds(r * half, half)
        return remote(
            back_s.at[rows], back_in.at[rows], y_send.at[2 + r], y_recv.at[2 + r], other
        )

    load_down = pltpu.make_async_copy(down_ref, down_f, local_sem.at[3])
    load_down.start()
    load_wide = pltpu.make_async_copy(
        wide_ref.at[:, units_half : z_.units], wide_f, local_sem.at[8]
    )
    load_wide.start()
    load_wo = pltpu.make_async_copy(wo_ref, wo_s, local_sem.at[1])
    load_wi = pltpu.make_async_copy(
        wi_ref, wi_s.at[:, :, 0:units_half], local_sem.at[2]
    )
    load_wo.start()
    load_wi.start()
    greet(
        [(ahead(k), c, t) for k in others]
        + [(f, lax.rem(c + j, z_.ctx), t) for j in range(1, z_.ctx)]
        + [other]
    )
    for j in range(1, count):
        heads_copy(j).start()
    own_heads = pltpu.make_async_copy(
        heads_ref.at[:, c], heads_s.at[c // z_.share], local_sem.at[0]
    )
    own_heads.start()
    load_down.wait()

    def round_down(first, rows):
        place = pl.ds(first, rows)
        wm_s[f, place, :] = down_f[place, :].astype(BF16)

    over_rows(0, z_.units, 128, round_down)
    for k in others:
        w_copy(0, k, f).start()
    load_wide.wait()
    for side in range(2):

        def round_wide(first, rows, side=side):
            wi_s[side, f, pl.ds(units_half + first, rows), :] = wide_f[
                side, pl.ds(first, rows), :
            ].astype(BF16)

        over_rows(0, units_half, 128, round_wide)
    for k in others:
        w_copy(1, k, f).start()
    load_wo.wait()
    own_heads.wait()
    for j in range(1, count):
        heads_arrival(j).wait_recv()

    low_lane = lax.broadcasted_iota(jnp.int32, (half, 2 * HD), 1) < HD
    for h in range(0, z_.heads, 2):
        columns = slice(h * HD, (h + 2) * HD)
        one = heads_s[h].reshape(half, 2 * HD).astype(F32)
        two = heads_s[h + 1].reshape(half, 2 * HD).astype(F32)
        early = jnp.where(low_lane, one, pltpu.roll(two, HD, 1))
        late = jnp.where(low_lane, pltpu.roll(one, HD, 1), two)
        mixed_s[0:half, columns] = early.astype(BF16)
        mixed_s[half:, columns] = late.astype(BF16)
        mixed_t[columns, 0:half] = early.T.astype(BF16)
        mixed_t[columns, half:] = late.T.astype(BF16)

    for r in range(2):
        rows = slice(r * half, (r + 1) * half)
        for g in range(z_.fsdp):
            sum_s[rows, g * z_.shard : (g + 1) * z_.shard] = jnp.dot(
                mixed_s[rows, :], wo_s[g], preferred_element_type=F32
            ).astype(BF16)
        sum_copy(r).start()

    for k in others:
        w_copy(0, k, behind(k)).wait_recv()
        w_pass(0, k, core).start()
    for k in others:
        w_pass(0, k, 1 - core).wait_recv()

    tile = min(128, half)

    def hidden_grad(i, carried):
        rows = pl.ds(pl.multiple_of(i * tile, tile), tile)
        total = jnp.zeros((tile, z_.units), F32)
        for g in range(z_.fsdp):
            total = total + lax.dot_general(
                cot_ref[rows, g * z_.shard : (g + 1) * z_.shard],
                wm_s[g],
                (((1,), (1,)), ((), ())),
                preferred_element_type=F32,
            )
        hgrad_s[rows, :] = total
        return carried

    lax.fori_loop(0, z_.rows // tile, hidden_grad, 0)
    load_wi.wait()
    for k in others:
        w_copy(1, k, behind(k)).wait_recv()
        w_pass(1, k, core).start()
    for k in others:
        w_pass(1, k, 1 - core).wait_recv()
    full = z_.units // 128 * 128

    for r in range(2):
        sum_copy(r).wait_recv()

        def middle_tile(i, carried):
            rows = pl.ds(pl.multiple_of(r * half + i * tile, tile), tile)
            middle = tok_ref[rows, :].astype(F32) + (
                sum_s[rows, :].astype(F32) + sum_in[rows, :].astype(F32)
            )
            middle_s[rows, :] = middle
            normed, scaling = normalize(middle)
            normed_s[rows, :] = normed
            scale_s[rows, :] = jnp.broadcast_to(scaling, (tile, 128))
            gains = jnp.concatenate([gain_ref[g, 1:2, :] for g in range(z_.fsdp)], axis=1)
            entry_s[rows, :] = (normed * gains).astype(BF16)
            return carried

        lax.fori_loop(0, half // tile, middle_tile, 0)
        rows = pl.ds(r * half, half)

        def gate(k, carried):
            total = jnp.zeros((half, z_.units), F32)
            for g in range(z_.fsdp):
                total = total + lax.dot_general(
                    entry_s[rows, g * z_.shard : (g + 1) * z_.shard],
                    wi_s[k, g],
                    (((1,), (1,)), ((), ())),
                    preferred_element_type=F32,
                )
            gate_s[k] = total
            return carried

        lax.fori_loop(0, 2, gate, 0)

        def activate(i, carried):
            inner = pl.ds(pl.multiple_of(i * 16, 16), 16)
            outer = pl.ds(pl.multiple_of(r * half + i * 16, 16), 16)
            up, side = gate_s[0, inner, :], gate_s[1, inner, :]
            grad = hgrad_s[outer, :]
            chance = 0.5 + 0.5 * lax.erf(up * (0.5**0.5))
            slope = chance + up * (jnp.exp(-0.5 * up * up) * 0.3989422804014327)
            active = up * chance
            hidden_s[outer, :] = (active * side).astype(BF16)
            gated_s[0, outer, :] = (grad * side * slope).astype(BF16)
            gated_s[1, outer, :] = (grad * active).astype(BF16)
            return carried

        lax.fori_loop(0, half // 16, activate, 0)

        for g in range(z_.fsdp):
            place = slice(g * z_.shard, (g + 1) * z_.shard)
            total = jnp.zeros((half, z_.shard), F32)
            for k in range(2):
                total = total + jnp.dot(
                    gated_s[k, rows, :], wi_s[k, g], preferred_element_type=F32
                )
            back_s[rows, place] = total.astype(BF16)
        back_copy(r).start()

    keep_middle = pltpu.make_async_copy(middle_s, middle_ref, local_sem.at[9])
    keep_middle.start()

    def turn(source, target):
        def turn_tile(i, carried):
            rows = pl.ds(pl.multiple_of(i * tile, tile), tile)
            for first in range(0, full, 128):
                block = source[rows, first : first + 128].astype(F32)
                target[first : first + 128, rows] = block.T.astype(BF16)
            if full < z_.units:
                rest = z_.units - full
                block = source[rows, full : z_.units].astype(F32)
                block = jnp.concatenate([block, jnp.zeros((tile, 128 - rest), F32)], axis=1)
                target[full : z_.units, rows] = block.T[0:rest].astype(BF16)
            return carried

        lax.fori_loop(0, z_.rows // tile, turn_tile, 0)

    turn(hidden_s, hidden_t)
    for g in range(z_.fsdp):
        place = slice(g * z_.shard, (g + 1) * z_.shard)
        for side in range(2):
            rows = slice(side * units_half, (side + 1) * units_half)
            down_s[g, side] = jnp.dot(
                hidden_t[rows, :], cot_ref[:, place], preferred_element_type=F32
            ).astype(BF16)
    keep_down = pltpu.make_async_copy(down_s, g_down, local_sem.at[4])
    keep_down.start()

    for k in range(2):
        turn(gated_s.at[k], gated_t.at[k])
        for g in range(z_.fsdp):
            wide_s[g, k] = jnp.dot(
                gated_t[k],
                entry_s[:, g * z_.shard : (g + 1) * z_.shard],
                preferred_element_type=F32,
            ).astype(BF16)
    keep_wide = pltpu.make_async_copy(wide_s, g_wide, local_sem.at[5])
    keep_wide.start()
    for g in range(z_.fsdp):
        place = slice(g * z_.shard, (g + 1) * z_.shard)
        branch_s[:, place] = jnp.dot(
            hidden_s[...], wm_s[g], preferred_element_type=F32
        ).astype(BF16)
    keep_branch = pltpu.make_async_copy(branch_s, branch_ref, local_sem.at[10])
    keep_branch.start()

    gain2_ref[...] = jnp.zeros(gain2_ref.shape, F32)
    for r in range(2):
        back_copy(r).wait_recv()

        def back_tile(i, carried):
            rows = pl.ds(pl.multiple_of(r * half + i * tile, tile), tile)
            back = back_s[rows, :].astype(F32) + back_in[rows, :].astype(F32)
            normed = normed_s[rows, :]
            gain2_ref[0:1, :] += jnp.sum(back * normed, axis=0, keepdims=True)
            gains = jnp.concatenate([gain_ref[g, 1:2, :] for g in range(z_.fsdp)], axis=1)
            grad = cot_ref[rows, :].astype(F32) + norm_back(
                back * gains, normed, scale_s[rows, 0:1]
            )
            grad_f[rows, :] = grad
            mgrad_s[rows, :] = grad.astype(BF16)
            return carried

        lax.fori_loop(0, half // tile, back_tile, 0)

    keep_grad = pltpu.make_async_copy(grad_f, mgrad_ref, local_sem.at[11])
    keep_grad.start()

    def heads_grad(rows):
        total = jnp.zeros((half, z_.head_width), F32)
        for g in range(z_.fsdp):
            total = total + lax.dot_general(
                mgrad_s[rows, g * z_.shard : (g + 1) * z_.shard],
                wo_s[g],
                (((1,), (1,)), ((), ())),
                preferred_element_type=F32,
            )
        return total

    early = heads_grad(slice(0, half))
    late = heads_grad(slice(half, z_.rows))
    for h in range(0, z_.heads, 2):
        columns = slice(h * HD, (h + 2) * HD)
        one = jnp.where(low_lane, early[:, columns], pltpu.roll(late[:, columns], HD, 1))
        two = jnp.where(low_lane, pltpu.roll(early[:, columns], HD, 1), late[:, columns])
        dsend_s[h] = one.astype(BF16).reshape(4, z_.block, 2 * HD)
        dsend_s[h + 1] = two.astype(BF16).reshape(4, z_.block, 2 * HD)
    for j in range(1, z_.ctx):
        grads_copy(j).start()
    own_grads = pltpu.make_async_copy(
        dsend_s.at[c // z_.share], grads_ref.at[:, c], local_sem.at[6]
    )
    own_grads.start()
    attn_half = z_.head_width // 2
    for g in range(z_.fsdp):
        for side in range(2):
            attn_s[g, side] = jnp.dot(
                mixed_t[side * attn_half : (side + 1) * attn_half, :],
                mgrad_s[:, g * z_.shard : (g + 1) * z_.shard],
                preferred_element_type=F32,
            ).astype(BF16)
    keep_attn = pltpu.make_async_copy(attn_s, g_attn, local_sem.at[7])
    keep_attn.start()

    own_grads.wait()
    for j in range(1, z_.ctx):
        grads_arrival(j).wait_recv()
        grads_copy(j).wait_send()
    for j in range(1, count):
        heads_copy(j).wait_send()
    for k in others:
        for n in range(2):
            w_copy(n, k, f).wait_send()
            w_pass(n, k, core).wait_send()
    for r in range(2):
        sum_copy(r).wait_send()
        back_copy(r).wait_send()
    keep_down.wait()
    keep_wide.wait()
    keep_attn.wait()
    keep_middle.wait()
    keep_branch.wait()
    keep_grad.wait()


def middle_part(z_, tokens, cotangent, gains, heads, wo, wi, wide_weight, down_weight):
    dma = pltpu.SemaphoreType.DMA
    peers = max(1, z_.fsdp - 1)
    count = z_.ctx // z_.share
    rows, width, units = z_.rows, z_.width, z_.units
    down = (z_.fsdp, 2, units // 2, z_.shard)
    wide = (z_.fsdp, 2, units, z_.shard)
    attn = (z_.fsdp, 2, z_.head_width // 2, z_.shard)
    return pl.pallas_call(
        functools.partial(middle_kernel, z_),
        out_shape=(
            jax.ShapeDtypeStruct((rows, width), BF16),
            jax.ShapeDtypeStruct((rows, width), F32),
            jax.ShapeDtypeStruct((rows, width), F32),
            jax.ShapeDtypeStruct((8, width), F32),
            jax.ShapeDtypeStruct((4, z_.ctx, z_.block, 2 * HD), BF16),
            jax.ShapeDtypeStruct(down, BF16),
            jax.ShapeDtypeStruct(wide, BF16),
            jax.ShapeDtypeStruct(attn, BF16),
        ),
        in_specs=[vmem()] * 3 + [anywhere()] * 5,
        out_specs=tuple([anywhere()] * 3 + [vmem()] + [anywhere()] * 4),
        scratch_shapes=[
            pltpu.VMEM((z_.heads, 4, z_.block, 2 * HD), BF16),
            pltpu.VMEM((z_.fsdp, z_.head_width, z_.shard), BF16),
            pltpu.VMEM((2, z_.fsdp, units, z_.shard), BF16),
            pltpu.VMEM((2, units // 2, z_.shard), F32),
            pltpu.VMEM((units, z_.shard), F32),
            pltpu.VMEM((z_.fsdp, units, z_.shard), BF16),
            pltpu.VMEM((rows, z_.head_width), BF16),
            pltpu.VMEM((z_.head_width, rows), BF16),
            pltpu.VMEM((rows, width), BF16),
            pltpu.VMEM((rows, width), BF16),
            pltpu.VMEM((rows, width), BF16),
            pltpu.VMEM((rows, width), BF16),
            pltpu.VMEM((rows, width), BF16),
            pltpu.VMEM((rows, width), BF16),
            pltpu.VMEM((rows, width), F32),
            pltpu.VMEM((rows, width), F32),
            pltpu.VMEM((rows, width), F32),
            pltpu.VMEM((rows, 128), F32),
            pltpu.VMEM((2, rows // 2, units), F32),
            pltpu.VMEM((rows, units), F32),
            pltpu.VMEM((rows, units), BF16),
            pltpu.VMEM((units, rows), BF16),
            pltpu.VMEM((2, rows, units), BF16),
            pltpu.VMEM((2, units, rows), BF16),
            pltpu.VMEM((rows, width), BF16),
            pltpu.VMEM((z_.heads, 4, z_.block, 2 * HD), BF16),
            pltpu.VMEM(down, BF16),
            pltpu.VMEM(wide, BF16),
            pltpu.VMEM(attn, BF16),
            dma((count,)),
            dma((count,)),
            dma((z_.ctx,)),
            dma((z_.ctx,)),
            dma((4,)),
            dma((4,)),
            dma((2, peers)),
            dma((2, peers)),
            dma((2, peers)),
            dma((2, peers)),
            dma((12,)),
        ],
        compiler_params=pltpu.CompilerParams(
            collective_id=2, has_side_effects=True, vmem_limit_bytes=VMEM_BYTES
        ),
        name="middle",
    )(tokens, cotangent, gains, heads, wo, wi, wide_weight, down_weight)


class Item:
    def __init__(self, number, rows, columns, cuts):
        self.number = number
        self.rows = rows
        self.columns = columns
        self.cuts = cuts_of(rows, cuts)


class Reducer:
    def __init__(self, z_, items, refs, sems):
        self.z_ = z_
        self.items = items
        self.refs = refs
        self.sems = sems
        f, c, t = lax.axis_index("fsdp"), lax.axis_index("ctx"), lax.axis_index("tp")
        self.f, self.c, self.t = f, c, t
        self.core = lax.rem(c, 2)
        self.chip = c // 2
        self.mate = (f, c + 1 - 2 * self.core, t)
        middle = z_.chips // 2
        low = self.chip < middle
        self.is_mid = (self.chip == middle - 1) | (self.chip == middle)
        self.has_outer = (self.chip > 0) & (self.chip < z_.chips - 1)
        self.is_end = jnp.logical_not(self.is_mid | self.has_outer)
        towards = jnp.where(low, 2, -2)
        self.inner = (f, c + towards, t)
        self.outer = (f, c - towards, t)
        self.numbers = {}
        for item in items:
            for cut in range(len(item.cuts)):
                self.numbers[(item.number, cut)] = len(self.numbers)

    def ahead(self, k):
        return lax.rem(self.f + k, self.z_.fsdp)

    def behind(self, k):
        return lax.rem(self.f + self.z_.fsdp - k, self.z_.fsdp)

    def part(self, item, cut):
        first, rows = item.cuts[cut]
        return self.numbers[(item.number, cut)], pl.ds(first, rows)


    def core_copy(self, item, cut):
        source, own, mate_in = self.refs[item.number][:3]
        n, rows = self.part(item, cut)
        return remote(
            source.at[:, 1 - self.core, rows],
            mate_in.at[:, rows],
            self.sems["core_send"].at[n],
            self.sems["core_recv"].at[n],
            self.mate,
        )

    def own_copy(self, item, cut):
        source, own = self.refs[item.number][:2]
        n, rows = self.part(item, cut)
        return pltpu.make_async_copy(
            source.at[:, self.core, rows], own.at[:, rows], self.sems["own"].at[n]
        )

    def core_start(self, item, cut):
        self.core_copy(item, cut).start()
        self.own_copy(item, cut).start()

    def core_sum(self, item, cut):
        own, mate_in = self.refs[item.number][1:3]
        first, rows = item.cuts[cut]
        self.own_copy(item, cut).wait()
        self.core_copy(item, cut).wait_recv()
        for k in range(self.z_.fsdp - 1, -1, -1):
            g = self.ahead(k)

            def add(start, count):
                place = pl.ds(start, count)
                own[g, place, :] = (
                    own[g, place, :].astype(F32) + mate_in[g, place, :].astype(F32)
                ).astype(BF16)

            over_rows(first, rows, 128, add)
            if k:
                self.peer_copy(item, cut, k, g).start()


    def peer_copy(self, item, cut, k, owner):
        own, peer_in = self.refs[item.number][1], self.refs[item.number][3]
        n, rows = self.part(item, cut)
        return remote(
            own.at[owner, rows],
            peer_in.at[k - 1, rows],
            self.sems["peer_send"].at[n, k - 1],
            self.sems["peer_recv"].at[n, k - 1],
            (self.ahead(k), self.c, self.t),
        )

    def peer_sum(self, item, cut):
        own, peer_in = self.refs[item.number][1], self.refs[item.number][3]
        first, rows = item.cuts[cut]
        for k in range(1, self.z_.fsdp):
            self.peer_copy(item, cut, k, self.ahead(k)).wait_recv()

        def add(start, count):
            place = pl.ds(start, count)
            total = own[self.f, place, :].astype(F32)
            for k in range(1, self.z_.fsdp):
                total = total + peer_in[k - 1, place, :].astype(F32)
            own[self.f, place, :] = total.astype(BF16)

        over_rows(first, rows, 128, add)

        @pl.when(jnp.logical_not(self.has_outer))
        def outermost():
            self.inward_start(item, cut)


    def in_copy(self, item, cut, middle):
        own, peer_in, outer_in, inner_in = self.refs[item.number][1:2] + self.refs[item.number][3:6]
        rows = pl.ds(*item.cuts[cut])
        n = self.numbers[(item.number, cut)]
        if middle:
            target, name = inner_in, "inner_recv"
        else:
            target, name = outer_in, "outer_recv"
        return remote(
            own.at[self.f, rows],
            target.at[rows],
            self.sems["in_send"].at[n],
            self.sems[name].at[n],
            self.inner,
        )

    def out_copy(self, item, cut):
        inner_in = self.refs[item.number][5]
        rows = pl.ds(*item.cuts[cut])
        n = self.numbers[(item.number, cut)]
        return remote(
            inner_in.at[rows],
            inner_in.at[rows],
            self.sems["out_send"].at[n],
            self.sems["inner_recv"].at[n],
            self.outer,
        )

    def done_copy(self, item, cut):
        inner_in, mate_out = self.refs[item.number][5:7]
        rows = pl.ds(*item.cuts[cut])
        n = self.numbers[(item.number, cut)]
        return remote(
            inner_in.at[rows],
            mate_out.at[rows],
            self.sems["done_send"].at[n],
            self.sems["done_recv"].at[n],
            self.mate,
        )

    def inward_start(self, item, cut):
        @pl.when(self.is_mid)
        def cross():
            self.in_copy(item, cut, True).start()

        @pl.when(jnp.logical_not(self.is_mid))
        def along():
            self.in_copy(item, cut, False).start()

    def inward(self, item, cut):
        own, outer_in = self.refs[item.number][1], self.refs[item.number][4]
        first, rows = item.cuts[cut]

        @pl.when(self.has_outer)
        def passed():
            self.in_copy(item, cut, False).wait_recv()

            def add(start, count):
                place = pl.ds(start, count)
                own[self.f, place, :] = (
                    own[self.f, place, :].astype(F32) + outer_in[place, :].astype(F32)
                ).astype(BF16)

            over_rows(first, rows, 128, add)
            self.inward_start(item, cut)

    def outward(self, item, cut):
        own, inner_in = self.refs[item.number][1], self.refs[item.number][5]
        first, rows = item.cuts[cut]

        @pl.when(jnp.logical_not(self.is_end))
        def onwards():
            self.out_copy(item, cut).wait_recv()

            @pl.when(self.is_mid)
            def total():
                def add(start, count):
                    place = pl.ds(start, count)
                    inner_in[place, :] = (
                        own[self.f, place, :].astype(F32) + inner_in[place, :].astype(F32)
                    ).astype(BF16)

                over_rows(first, rows, 128, add)

            @pl.when(self.has_outer)
            def onward():
                self.out_copy(item, cut).start()

            self.done_copy(item, cut).start()

    def arrive(self, item, cut):
        @pl.when(self.is_end)
        def ended():
            self.out_copy(item, cut).wait_recv()
            self.done_copy(item, cut).start()

    def settle(self):
        for item in self.items:
            for cut in range(len(item.cuts)):
                self.core_copy(item, cut).wait_send()
                for k in range(1, self.z_.fsdp):
                    self.peer_copy(item, cut, k, self.ahead(k)).wait_send()
                self.in_copy(item, cut, False).wait_send()

                @pl.when(self.has_outer)
                def outwards(item=item, cut=cut):
                    self.out_copy(item, cut).wait_send()

                self.done_copy(item, cut).wait_send()


class Finisher:
    def __init__(self, z_, reducer, results, store_sem):
        self.z_ = z_
        self.red = reducer
        self.results = results
        self.store_sem = store_sem

    def copies(self, item, cut, which):
        first, rows = item.cuts[cut]
        number = item.number
        red = self.red
        side = red.core if which == 0 else 1 - red.core
        sums = red.refs[number][5 + which]
        result = self.results[number]
        sem = self.store_sem.at[which]
        index = red.numbers[(number, cut)]
        if number == 3:
            half = self.z_.shard // 2
            place = pl.ds(pl.multiple_of(side * half, half), half)
            columns = slice(2 * HD * cut, 2 * HD * (cut + 1))
            return [
                pltpu.make_async_copy(
                    sums.at[first : first + rows, 2 * HD * kind : 2 * HD * (kind + 1)],
                    result.at[kind, place, columns],
                    sem.at[index, kind],
                )
                for kind in range(3)
            ]
        if number in (1, 4):
            target = result.at[side, first : first + rows]
        else:
            target = result.at[pl.ds(pl.multiple_of(side * item.rows + first, 16), rows)]
        return [pltpu.make_async_copy(sums.at[first : first + rows], target, sem.at[index, 0])]

    def update(self, item, cut):
        for copy in self.copies(item, cut, 0):
            copy.start()
        self.red.done_copy(item, cut).wait_recv()
        for copy in self.copies(item, cut, 1):
            copy.start()

    def settle(self):
        for item in self.red.items:
            for cut in range(len(item.cuts)):
                for which in range(2):
                    for copy in self.copies(item, cut, which):
                        copy.wait()


def reduce_kernel(
    z_,
    items,
    tok_ref,
    gain_ref,
    cos_ref,
    sin_ref,
    branch_ref,
    middle_ref,
    mgrad_ref,
    gain2_ref,
    heads_ref,
    wq_ref,
    g_down,
    g_wide,
    g_attn,
    *others,
):
    down, wide, attn, qkv, gain = items
    scratch = list(others)

    def take(count):
        taken = scratch[:count]
        del scratch[:count]
        return taken

    out_ref, igrad_ref = take(2)
    results = take(5)
    heads_s, wq_s, entry_s, grads_s, branch_own, branch_s, back_s, back_in = take(8)
    middle_s, mgrad_s = take(2)
    g_qkv, g_gain, gain_in, gain_acc = take(4)
    groups = [take(6) for item in items]
    (a_send, a_recv, y_send, y_recv, local_sem, store_sem) = take(6)
    names = (
        "peer_send",
        "peer_recv",
        "core_send",
        "core_recv",
        "own",
        "in_send",
        "outer_recv",
        "inner_recv",
        "out_send",
        "done_send",
        "done_recv",
    )
    sems = dict(zip(names, take(len(names))))
    sources = (g_down, g_wide, g_attn, g_qkv, g_gain)
    refs = [(source, *group) for source, group in zip(sources, groups)]
    red = Reducer(z_, items, refs, sems)
    finish = Finisher(z_, red, results, store_sem)
    f, c, t = red.f, red.c, red.t
    other = (f, c, 1 - t)
    count = z_.ctx // z_.share

    def to_token(j):
        return lax.rem(c + z_.share * j, z_.ctx)

    def from_head(j):
        return lax.rem(c + z_.ctx - z_.share * j, z_.ctx)

    def heads_copy(j):
        return remote(
            heads_ref.at[:, to_token(j)],
            heads_s.at[c // z_.share],
            a_send.at[j],
            a_recv.at[j],
            (f, to_token(j), t),
        )

    def branch_copy():
        return remote(branch_ref, branch_s, y_send.at[0], y_recv.at[0], other)

    def back_copy(r):
        rows = pl.ds(r * (z_.rows // 2), z_.rows // 2)
        return remote(back_s.at[rows], back_in.at[rows], y_send.at[2 + r], y_recv.at[2 + r], other)

    load_wq = pltpu.make_async_copy(wq_ref, wq_s, local_sem.at[1])
    load_branch = pltpu.make_async_copy(branch_ref, branch_own, local_sem.at[2])
    load_middle = pltpu.make_async_copy(middle_ref, middle_s, local_sem.at[3])
    load_mgrad = pltpu.make_async_copy(mgrad_ref, mgrad_s, local_sem.at[4])
    load_wq.start()
    load_branch.start()
    load_middle.start()
    load_mgrad.start()
    greet(
        [(red.ahead(k), c, t) for k in range(1, z_.fsdp)]
        + [(f, lax.rem(c + j, z_.ctx), t) for j in range(1, z_.ctx)]
        + [other]
    )
    for j in range(1, count):
        heads_copy(j).start()
    branch_copy().start()
    own_heads = pltpu.make_async_copy(heads_ref.at[:, c], heads_s.at[c // z_.share], local_sem.at[0])
    own_heads.start()
    ready = [(item, cut) for item in (down, wide, attn) for cut in range(len(item.cuts))]
    for part in ready:
        red.core_start(*part)

    for part in ready:
        red.core_sum(*part)

    def run(*steps):
        for step in steps:
            item = {"d": down, "w": wide, "a": attn, "q": qkv, "g": gain}[step[1]]
            part = (item, int(step[2]))
            if step[0] == "x":
                red.peer_sum(*part)
            elif step[0] == "i":
                red.inward(*part)
            elif step[0] == "o":
                red.outward(*part)
            elif step[0] == "e":
                red.arrive(*part)
            else:
                finish.update(*part)

    tile = min(128, z_.rows)

    def entry_tile(i, carried):
        rows = pl.ds(pl.multiple_of(i * tile, tile), tile)
        normed, nothing = normalize(tok_ref[rows, :].astype(F32))
        for g in range(z_.fsdp):
            columns = slice(g * z_.shard, (g + 1) * z_.shard)
            entry_s[g, :, rows] = (normed[:, columns] * gain_ref[g, 0:1, :]).T.astype(BF16)
        return carried

    lax.fori_loop(0, z_.rows // tile, entry_tile, 0)

    run("xd0", "xd1")
    branch_copy().wait_recv()
    load_branch.wait()
    load_middle.wait()

    def output_tile(i, carried):
        rows = pl.ds(pl.multiple_of(i * tile, tile), tile)
        branch = branch_own[rows, :].astype(F32) + branch_s[rows, :].astype(F32)
        out_ref[rows, :] = (middle_s[rows, :] + branch).astype(BF16)
        return carried

    lax.fori_loop(0, z_.rows // tile, output_tile, 0)

    run("id0", "xw0", "id1", "od0", "xw1", "iw0", "od1")

    own_heads.wait()
    for j in range(1, count):
        remote(
            heads_ref.at[:, c],
            heads_s.at[from_head(j) // z_.share],
            a_send.at[j],
            a_recv.at[j],
            red.mate,
        ).wait_recv()
    load_wq.wait()

    lane = lax.broadcasted_iota(jnp.int32, (z_.rows, 2 * HD), 1) < HD
    lane_half = lax.broadcasted_iota(jnp.int32, (z_.rows // 2, 2 * HD), 1) < HD
    mid_row = z_.rows // 2

    def chunk_grads(p, carried):
        pair = [
            heads_s[2 * p + i, 0:8].reshape(z_.rows, 2 * HD).astype(F32) for i in range(2)
        ]
        query = jnp.where(lane, pair[0], pltpu.roll(pair[1], HD, 1))
        key = jnp.where(lane, pltpu.roll(pair[0], HD, 1), pair[1])
        for kind, part in ((0, query), (1, key)):
            part = part * cos_ref[...] - swap_halves(part) * sin_ref[...]
            grads_s[p, :, 2 * HD * kind : 2 * HD * (kind + 1)] = part.astype(BF16)
        value = [
            heads_s[2 * p + i, 8:12].reshape(mid_row, 2 * HD).astype(F32) for i in range(2)
        ]
        early = jnp.where(lane_half, value[0], pltpu.roll(value[1], HD, 1))
        late = jnp.where(lane_half, pltpu.roll(value[0], HD, 1), value[1])
        grads_s[p, 0:mid_row, 4 * HD : 6 * HD] = early.astype(BF16)
        grads_s[p, mid_row : z_.rows, 4 * HD : 6 * HD] = late.astype(BF16)
        return carried

    lax.fori_loop(0, z_.pairs, chunk_grads, 0)

    gain_acc[...] = jnp.zeros(gain_acc.shape, F32)

    def back_tile(i, carried):
        rows = pl.ds(pl.multiple_of(i * tile, tile), tile)
        normed, nothing = normalize(tok_ref[rows, :].astype(F32))
        for g in range(z_.fsdp):
            columns = slice(g * z_.shard, (g + 1) * z_.shard)
            total = jnp.zeros((tile, z_.shard), F32)
            for p in range(z_.pairs):
                total = total + lax.dot_general(
                    grads_s[p, rows, :],
                    wq_s[p, g],
                    (((1,), (1,)), ((), ())),
                    preferred_element_type=F32,
                )
            back_s[rows, columns] = total.astype(BF16)
            gain_acc[0:1, columns] += jnp.sum(total * normed[:, columns], axis=0, keepdims=True)
        return carried

    for r in range(2):
        tiles = z_.rows // tile
        lax.fori_loop(r * tiles // 2, (r + 1) * tiles // 2, back_tile, 0)
        back_copy(r).start()
    top = lax.broadcasted_iota(jnp.int32, (16, z_.shard), 0) == 0
    for g in range(z_.fsdp):
        columns = slice(g * z_.shard, (g + 1) * z_.shard)
        for side, row in ((0, gain_acc[0:1, columns]), (1, gain2_ref[0:1, columns])):
            g_gain[g, side] = jnp.where(top, row, 0.0).astype(BF16)

    def gain_copy():
        return remote(g_gain.at[:, 0], gain_in, y_send.at[1], y_recv.at[1], other)

    gain_copy().start()
    run("xw2", "iw1", "ow0")
    half = z_.shard // 2

    def qkv_pair(p):
        for g in range(z_.fsdp):
            for side in range(2):
                grad = jnp.dot(
                    entry_s[g, side * half : (side + 1) * half, :],
                    grads_s[p],
                    preferred_element_type=F32,
                )
                g_qkv[g, side, p * half : (p + 1) * half, :] = grad.astype(BF16)

    for p in range(z_.pairs):
        qkv_pair(p)
        red.core_start(qkv, p)
    run("xw3", "iw2", "ow1", "ed0")
    for p in range(z_.pairs):
        red.core_sum(qkv, p)
    run("xa0", "iw3", "ow2", "ed1", "ud0", "xq0", "ia0", "ow3", "ew0", "ud1")
    gain_copy().wait()
    for g in range(z_.fsdp):
        g_gain[g, 0] = (g_gain[g, 0].astype(F32) + gain_in[g].astype(F32)).astype(BF16)
    red.core_start(gain, 0)
    run("xq1", "iq0", "oa0", "ew1", "uw0")
    red.core_sum(gain, 0)
    run("xq2", "iq1", "oq0", "ew2", "uw1", "xg0", "xq3", "iq2", "oq1", "ew3", "uw2", "ig0", "iq3")
    run("oq2", "og0", "oq3", "ea0", "uw3", "eq0", "ua0")

    for r in range(2):
        back_copy(r).wait_recv()
    load_mgrad.wait()

    def input_tile(i, carried):
        rows = pl.ds(pl.multiple_of(i * tile, tile), tile)
        normed, scaling = normalize(tok_ref[rows, :].astype(F32))
        back = back_s[rows, :].astype(F32) + back_in[rows, :].astype(F32)
        gains = jnp.concatenate([gain_ref[g, 0:1, :] for g in range(z_.fsdp)], axis=1)
        igrad_ref[rows, :] = (
            mgrad_s[rows, :] + norm_back(back * gains, normed, scaling)
        ).astype(BF16)
        return carried

    lax.fori_loop(0, z_.rows // tile, input_tile, 0)
    run("eq1", "uq0", "eq2", "uq1", "eg0", "uq2", "eq3", "ug0", "uq3")

    own_sends = [heads_copy(j) for j in range(1, count)] + [branch_copy(), back_copy(0), back_copy(1)]
    for copy in own_sends:
        copy.wait_send()
    red.settle()
    finish.settle()


def reduce_all(
    z_,
    tokens,
    gains,
    cosine,
    sines,
    branch,
    middle,
    middle_grad,
    gain2,
    heads,
    wq,
    g_down,
    g_wide,
    g_attn,
):
    items = (
        Item(0, z_.units // 2, z_.shard, 2),
        Item(1, z_.units, z_.shard, 4),
        Item(2, z_.head_width // 2, z_.shard, 1),
        Item(3, z_.pairs * (z_.shard // 2), 6 * HD, z_.pairs),
        Item(4, 16, z_.shard, 1),
    )
    dma = pltpu.SemaphoreType.DMA
    peers = max(1, z_.fsdp - 1)
    pieces = sum(len(item.cuts) for item in items)
    groups = []
    for item in items:
        groups += [
            pltpu.VMEM((z_.fsdp, item.rows, item.columns), BF16),
            pltpu.VMEM((z_.fsdp, item.rows, item.columns), BF16),
            pltpu.VMEM((peers, item.rows, item.columns), BF16),
            pltpu.VMEM((item.rows, item.columns), BF16),
            pltpu.VMEM((item.rows, item.columns), BF16),
            pltpu.VMEM((item.rows, item.columns), BF16),
        ]
    count = z_.ctx // z_.share
    rows = (z_.rows, z_.width)
    return pl.pallas_call(
        functools.partial(reduce_kernel, z_, items),
        out_shape=tuple(
            [jax.ShapeDtypeStruct(rows, BF16)] * 2
            + [
                jax.ShapeDtypeStruct(shape, BF16)
                for shape in (
                    (z_.units, z_.shard),
                    (2, z_.units, z_.shard),
                    (z_.head_width, z_.shard),
                    (3, z_.shard, z_.head_width),
                    (2, 16, z_.shard),
                )
            ]
        ),
        in_specs=[vmem()] * 4
        + [anywhere()] * 3
        + [vmem()]
        + [anywhere()] * 5,
        out_specs=tuple([vmem()] * 2 + [anywhere()] * 5),
        scratch_shapes=[
            pltpu.VMEM((z_.heads, 12, z_.block, 2 * HD), BF16),
            pltpu.VMEM((z_.pairs, z_.fsdp, z_.shard, 6 * HD), BF16),
            pltpu.VMEM((z_.fsdp, z_.shard, z_.rows), BF16),
            pltpu.VMEM((z_.pairs, z_.rows, 6 * HD), BF16),
            pltpu.VMEM(rows, BF16),
            pltpu.VMEM(rows, BF16),
            pltpu.VMEM(rows, BF16),
            pltpu.VMEM(rows, BF16),
            pltpu.VMEM(rows, F32),
            pltpu.VMEM(rows, F32),
            pltpu.VMEM((z_.fsdp, 2, items[3].rows, items[3].columns), BF16),
            pltpu.VMEM((z_.fsdp, 2, 16, z_.shard), BF16),
            pltpu.VMEM((z_.fsdp, 16, z_.shard), BF16),
            pltpu.VMEM((8, z_.width), F32),
        ]
        + groups
        + [dma((count,)), dma((count,)), dma((4,)), dma((4,)), dma((5,)), dma((2, pieces, 3))]
        + [
            dma((pieces, peers)),
            dma((pieces, peers)),
        ]
        + [dma((pieces,))] * 9,
        compiler_params=pltpu.CompilerParams(
            collective_id=1, has_side_effects=True, vmem_limit_bytes=REDUCE_BYTES
        ),
        name="reduce",
    )(
        tokens,
        gains,
        cosine,
        sines,
        branch,
        middle,
        middle_grad,
        gain2,
        heads,
        wq,
        g_down,
        g_wide,
        g_attn,
    )


def adam_step(weight, gradient, moment, squared, rate_now):
    first = BETA_FIRST * moment + (1.0 - BETA_FIRST) * gradient
    second = BETA_SECOND * squared + (1.0 - BETA_SECOND) * gradient * gradient
    corrected = first / (1.0 - BETA_FIRST**STEP)
    spread = jnp.sqrt(second / (1.0 - BETA_SECOND**STEP))
    return (weight - rate_now * (corrected / (spread + ADAM_EPS) + DECAY * weight), first, second)


def on_device(
    tokens,
    cotangent,
    lengths,
    order,
    qkv_weight,
    attn_weight,
    wide_weight,
    down_weight,
    norm_gains,
    qkv_mean,
    attn_mean,
    wide_mean,
    down_mean,
    gains_mean,
    qkv_square,
    attn_square,
    wide_square,
    down_square,
    gains_square,
):
    z_ = Sizes(
        lax.axis_size("fsdp"),
        lax.axis_size("ctx"),
        tokens.shape[0],
        tokens.shape[1],
        qkv_weight.shape[2],
        wide_weight.shape[2],
    )
    ctx_index = lax.axis_index("ctx")
    in_order, endings = sequence_ends(lengths[0], order[0])
    local_ids = jnp.arange(z_.rows, dtype=jnp.int32)
    cosine, sines = rope_tables(
        positions(in_order, endings, packed_place(local_ids, ctx_index, z_.ctx, z_.block))
    )
    gain_rows = jnp.pad(norm_gains.astype(BF16).astype(F32), ((0, 6), (0, 0)))
    packed, wq_full, wo_full, wi_full, gains_full = project(
        z_,
        tokens,
        gain_rows,
        cosine,
        sines,
        qkv_weight.transpose(1, 0, 2),
        attn_weight,
        wide_weight.transpose(1, 2, 0),
    )
    attended_packed, attended_turned, lse, swapped, query, key, value = attend(
        z_, lengths, order, packed
    )
    branch_low, middle, middle_grad, gain_second, grads_packed, down_grad, wide_grad, attn_grad = (
        middle_part(
            z_,
            tokens,
            cotangent,
            gains_full,
            attended_packed,
            wo_full,
            wi_full,
            wide_weight.transpose(1, 2, 0),
            down_weight,
        )
    )
    head_grads = attend_back(
        z_, lengths, order, lse, grads_packed, attended_turned, swapped, query, key, value
    )
    output, input_grad, down_sum, wide_sum, attn_sum, qkv_sum, gain_sum = reduce_all(
        z_,
        tokens,
        gains_full,
        cosine,
        sines,
        branch_low,
        middle,
        middle_grad,
        gain_second,
        head_grads,
        wq_full,
        down_grad,
        wide_grad,
        attn_grad,
    )
    updated = []
    for weight, gradient, moment, squared, rate_now in (
        (qkv_weight, qkv_sum.transpose(1, 0, 2), qkv_mean, qkv_square, D ** (-0.5)),
        (attn_weight, attn_sum, attn_mean, attn_square, RATE_ATTN),
        (wide_weight, wide_sum.transpose(2, 0, 1), wide_mean, wide_square, D ** (-0.5)),
        (down_weight, down_sum, down_mean, down_square, FF ** (-0.5)),
        (norm_gains, gain_sum[:, 0, :], gains_mean, gains_square, RATE_GAIN),
    ):
        updated += adam_step(weight, gradient.astype(F32), moment, squared, rate_now)
    return (output, input_grad, *updated)


def solution(mesh):
    return jax.shard_map(
        on_device,
        mesh=mesh,
        in_specs=(
            P(("fsdp", "ctx"), None),
            P(("fsdp", "ctx"), None),
            P("fsdp", None),
            P("fsdp", None),
            P("fsdp", None, "tp"),
            P("tp", "fsdp"),
            P("fsdp", None, "tp"),
            P("tp", "fsdp"),
            P(None, "fsdp"),
            P("fsdp", None, "tp"),
            P("tp", "fsdp"),
            P("fsdp", None, "tp"),
            P("tp", "fsdp"),
            P(None, "fsdp"),
            P("fsdp", None, "tp"),
            P("tp", "fsdp"),
            P("fsdp", None, "tp"),
            P("tp", "fsdp"),
            P(None, "fsdp"),
        ),
        out_specs=(
            P(("fsdp", "ctx"), None),
            P(("fsdp", "ctx"), None),
            P("fsdp", None, "tp"),
            P("fsdp", None, "tp"),
            P("fsdp", None, "tp"),
            P("tp", "fsdp"),
            P("tp", "fsdp"),
            P("tp", "fsdp"),
            P("fsdp", None, "tp"),
            P("fsdp", None, "tp"),
            P("fsdp", None, "tp"),
            P("tp", "fsdp"),
            P("tp", "fsdp"),
            P("tp", "fsdp"),
            P(None, "fsdp"),
            P(None, "fsdp"),
            P(None, "fsdp"),
        ),
        check_vma=False,
    )
```

```python
import functools

import jax
import jax.numpy as jnp
from jax import lax
from jax.experimental import pallas as pl
from jax.experimental.pallas import tpu as pltpu
from jax.sharding import PartitionSpec as P

D = 1024
HD = 64
FF = 2624
STEP = 10


NORM_EPS = 1e-05
ROPE_BASE = 160000.0
BETA_FIRST = 0.9
BETA_SECOND = 0.98
ADAM_EPS = 1e-06
DECAY = 0.01
RATE_ATTN = 0.5
RATE_GAIN = 0.8
MASKED = -1e30

MESH = pl.DeviceIdType.MESH
BF16 = jnp.bfloat16
F32 = jnp.float32
VMEM_BYTES = 62 * 2**20
REDUCE_BYTES = 46 * 2**20


class Sizes:
    def __init__(self, fsdp, ctx, rows, width, head_width, units):
        self.fsdp = fsdp
        self.ctx = ctx
        self.chips = ctx // 2
        self.rows = rows
        self.block = rows // 8
        self.group = rows * ctx
        self.width = width
        self.shard = width // fsdp
        self.heads = head_width // HD
        self.head_width = head_width
        self.units = units
        self.units_first = 16 * (units // 16 * 5 // 8)
        self.share = max(1, ctx // self.heads)
        self.pairs = self.heads // 2
        self.ranks = ctx // self.pairs


def remote(src, dst, send, recv, device):
    return pltpu.make_async_remote_copy(
        src_ref=src,
        dst_ref=dst,
        send_sem=send,
        recv_sem=recv,
        device_id=device,
        device_id_type=MESH,
    )


def greet(devices):
    barrier = pltpu.get_barrier_semaphore()
    for device in devices:
        pl.semaphore_signal(barrier, inc=1, device_id=device, device_id_type=MESH)
    pl.semaphore_wait(barrier, len(devices))


def vmem():
    return pl.BlockSpec(memory_space=pltpu.VMEM)


def anywhere():
    return pl.BlockSpec(memory_space=pl.ANY)


def normalize(values):
    centered = values - jnp.mean(values, axis=1, keepdims=True)
    scaling = lax.rsqrt(jnp.mean(centered * centered, axis=1, keepdims=True) + NORM_EPS)
    return (centered * scaling, scaling)


def norm_back(grad_hat, normed, scaling):
    return scaling * (
        grad_hat
        - jnp.mean(grad_hat, axis=1, keepdims=True)
        - normed * jnp.mean(grad_hat * normed, axis=1, keepdims=True)
    )


def swap_halves(values):
    lane = lax.broadcasted_iota(jnp.int32, values.shape, 1)
    return jnp.where(
        lane % HD < HD // 2, pltpu.roll(values, 2 * HD - HD // 2, 1), pltpu.roll(values, HD // 2, 1)
    )


def packed_place(local_row, device, devices, block_size):
    return (local_row // block_size * devices + device) * block_size + local_row % block_size


def sequence_ends(lengths_row, order_row):
    count_seqs = lengths_row.shape[0]
    chosen = (order_row[:, None] == jnp.arange(count_seqs, dtype=jnp.int32)[None, :]).astype(
        jnp.int32
    )
    in_order = jnp.sum(chosen * lengths_row[None, :], axis=1)
    return (in_order, jnp.cumsum(in_order))


def positions(in_order, endings, places):
    passed = (endings[None, :] <= places[:, None]).astype(jnp.int32)
    return places - jnp.sum(passed * in_order[None, :], axis=1)


def rope_tables(position):
    half_size = HD // 2
    lane = jnp.arange(2 * HD, dtype=jnp.int32)
    index = (lane % half_size).astype(jnp.float32)
    frequency = ROPE_BASE ** (-(2.0 * index) / (2.0 * half_size))
    angles = position.astype(jnp.float32)[:, None] * frequency[None, :]
    sign = jnp.where(lane % HD < half_size, -1.0, 1.0)
    return (jnp.cos(angles), jnp.sin(angles) * sign[None, :])


def cuts_of(rows, count):
    unit = rows // 16
    marks = [16 * (unit * i // count) for i in range(count + 1)]
    return [(a, b - a) for a, b in zip(marks, marks[1:]) if b > a]


def over_rows(start, rows, step, body):
    whole = rows // step

    def turn(i, carried):
        body(pl.multiple_of(start + i * step, 16), step)
        return carried

    if whole > 1:
        lax.fori_loop(0, whole, turn, 0)
    elif whole == 1:
        body(start, step)
    if rows % step:
        body(start + whole * step, rows % step)


def project_kernel(
    z_,
    tok_ref,
    gain_ref,
    cos_ref,
    sin_ref,
    wq_ref,
    wo_ref,
    wi_ref,
    packed_ref,
    wq_out,
    wo_out,
    wi_out,
    gain_out,
    entry_s,
    wq_f,
    wo_f,
    wi_f,
    wq_s,
    wo_s,
    wi_s,
    send_s,
    gain_s,
    gain_send,
    gain_recv,
    wq_send,
    wq_recv,
    wq_fsend,
    wq_frecv,
    w_send,
    w_recv,
    w_fsend,
    w_frecv,
    a_send,
    a_recv,
    local_sem,
):
    f, c, t = lax.axis_index("fsdp"), lax.axis_index("ctx"), lax.axis_index("tp")
    core = lax.rem(c, 2)
    mate = (f, c + 1 - 2 * core, t)
    others = range(1, z_.fsdp)
    mine = c // z_.ranks
    place_in = lax.rem(c, z_.ranks)
    last = z_.pairs - 1
    unit_half = z_.units_first

    def ahead(k):
        return lax.rem(f + k, z_.fsdp)

    def behind(k):
        return lax.rem(f + z_.fsdp - k, z_.fsdp)

    def pair_of(s):
        return lax.rem(mine + 1 + s, z_.pairs)

    load_wq = pltpu.make_async_copy(wq_ref, wq_f, local_sem.at[0])
    load_wo = pltpu.make_async_copy(wo_ref, wo_f, local_sem.at[1])
    load_wi = pltpu.make_async_copy(wi_ref.at[:, 0:unit_half], wi_f, local_sem.at[2])
    load_wq.start()
    load_wo.start()
    load_wi.start()
    greet(
        [(ahead(k), c, t) for k in others]
        + [(f, lax.rem(c + j, z_.ctx), t) for j in range(1, z_.ctx)]
    )

    half = z_.shard // 2
    own_half = pl.ds(pl.multiple_of(core * half, half), half)
    mate_half = pl.ds(pl.multiple_of((1 - core) * half, half), half)

    def gain_copy(k, owner):
        return remote(
            gain_s.at[f], gain_s.at[owner], gain_send.at[k - 1], gain_recv.at[k - 1], (ahead(k), c, t)
        )

    def wq_copy(s, k, owner):
        place = wq_s.at[pair_of(s), owner, own_half]
        return remote(
            place, place, wq_send.at[s, k - 1], wq_recv.at[s, k - 1], (ahead(k), c, t)
        )

    def wq_pass(s, k, rows):
        place = wq_s.at[pair_of(s), behind(k), rows]
        return remote(place, place, wq_fsend.at[s, k - 1], wq_frecv.at[s, k - 1], mate)

    attn_half = z_.head_width // 2

    def weight_places(side, owner):
        rows = pl.ds(pl.multiple_of(side * attn_half, attn_half), attn_half)
        return (
            (wo_s.at[rows], wo_out.at[owner, rows]),
            (wi_s.at[side], wi_out.at[side, owner]),
        )

    pieces = 2

    def w_copy(n, k, owner):
        source, place = weight_places(core, owner)[n]
        return remote(source, place, w_send.at[n, k - 1], w_recv.at[n, k - 1], (ahead(k), c, t))

    def w_pass(n, k, side):
        place = weight_places(side, behind(k))[n][1]
        return remote(place, place, w_fsend.at[n, k - 1], w_frecv.at[n, k - 1], mate)

    def head_copy(s, i):
        return remote(
            send_s.at[s, i // z_.share],
            packed_ref.at[:, c],
            a_send.at[s, i],
            a_recv.at[s, place_in],
            (f, pair_of(s) * z_.ranks + i, t),
        )

    def head_arrival(s, i):
        source = lax.rem(mine + 2 * z_.pairs - 1 - s, z_.pairs) * z_.ranks + i
        return remote(
            send_s.at[s, 0], packed_ref.at[:, source], a_send.at[s, 0], a_recv.at[s, i], mate
        )

    def near_copy(j):
        i = lax.rem(place_in + j, z_.ranks)
        return remote(
            send_s.at[last, i // z_.share],
            packed_ref.at[:, c],
            a_send.at[last, j],
            a_recv.at[last, j],
            (f, mine * z_.ranks + i, t),
        )

    def near_arrival(j):
        source = mine * z_.ranks + lax.rem(place_in + z_.ranks - j, z_.ranks)
        return remote(
            send_s.at[last, 0], packed_ref.at[:, source], a_send.at[last, j], a_recv.at[last, j], mate
        )

    gain_s[f] = jnp.zeros((8, z_.shard), F32)
    gain_s[f, 0:2, :] = gain_ref[...].astype(BF16).astype(F32)
    for k in others:
        gain_copy(k, f).start()
    load_wq.wait()

    def round_pair(s):
        p = pair_of(s)
        columns = pl.ds(pl.multiple_of(p * 2 * HD, 2 * HD), 2 * HD)
        for kind in range(3):
            wq_s[p, f, :, kind * 2 * HD : (kind + 1) * 2 * HD] = wq_f[kind, :, columns].astype(BF16)

    for s in range(2):
        round_pair(s)
        for k in others:
            wq_copy(s, k, f).start()
    for k in others:
        gain_copy(k, behind(k)).wait()

    gain_out[...] = gain_s[...]
    tile = min(128, z_.rows)

    def norm_tile(i, carried):
        rows = pl.ds(pl.multiple_of(i * tile, tile), tile)
        normed, nothing = normalize(tok_ref[rows, :].astype(F32))
        for g in range(z_.fsdp):
            columns = slice(g * z_.shard, (g + 1) * z_.shard)
            entry_s[g, rows, :] = (normed[:, columns] * gain_s[g, 0:1, :]).astype(BF16)
        return carried

    lax.fori_loop(0, z_.rows // tile, norm_tile, 0)
    load_wo.wait()
    wo_s[...] = wo_f[...].astype(BF16)
    own_wo = pltpu.make_async_copy(wo_s, wo_out.at[f], local_sem.at[1])
    own_wo.start()
    load_wi.wait()
    own_wi = pltpu.make_async_copy(wi_s, wi_out.at[:, f], local_sem.at[2])

    def round_wide(side):
        def turn(first, rows):
            place = pl.ds(first, rows)
            wi_s[side, place, :] = wi_f[side, place, :].astype(BF16)

        over_rows(0, unit_half, 128, turn)

    lane = lax.broadcasted_iota(jnp.int32, (z_.rows, 2 * HD), 1) < HD
    lane_half = lax.broadcasted_iota(jnp.int32, (z_.rows // 2, 2 * HD), 1) < HD

    def chunk_step(s, carried):
        @pl.when(s + 2 < z_.pairs)
        def more():
            round_pair(s + 2)
            for k in others:
                wq_copy(s + 2, k, f).start()

        @pl.when(s + 2 == z_.pairs)
        def attn_part():
            for k in others:
                w_copy(0, k, f).start()
            round_wide(core)

        @pl.when(s + 1 == z_.pairs)
        def wide_part():
            for k in others:
                w_copy(1, k, f).start()

        for k in others:
            wq_copy(s, k, behind(k)).wait_recv()
            wq_pass(s, k, own_half).start()
        for k in others:
            wq_pass(s, k, mate_half).wait_recv()
        p = pair_of(s)
        total = jnp.zeros((z_.rows, 6 * HD), F32)
        for g in range(z_.fsdp):
            total = total + jnp.dot(entry_s[g], wq_s[p, g], preferred_element_type=F32)
        turned = []
        for kind in range(2):
            part = total[:, kind * 2 * HD : (kind + 1) * 2 * HD]
            turned.append(part * cos_ref[...] + swap_halves(part) * sin_ref[...])
        query, key = turned
        value = total[:, 4 * HD : 6 * HD]
        early, late = value[: z_.rows // 2], value[z_.rows // 2 :]
        both = (
            (
                jnp.where(lane, query, pltpu.roll(key, HD, 1)),
                jnp.where(lane_half, early, pltpu.roll(late, HD, 1)),
            ),
            (
                jnp.where(lane, pltpu.roll(query, HD, 1), key),
                jnp.where(lane_half, pltpu.roll(early, HD, 1), late),
            ),
        )
        for i in range(2):
            send_s[s, i, 0:8] = both[i][0].astype(BF16).reshape(8, z_.block, 2 * HD)
            send_s[s, i, 8:12] = both[i][1].astype(BF16).reshape(4, z_.block, 2 * HD)

        @pl.when(s < last)
        def away():
            for i in range(z_.ranks):
                head_copy(s, i).start()

        return carried

    lax.fori_loop(0, z_.pairs, chunk_step, 0)
    kept = pltpu.make_async_copy(
        send_s.at[last, place_in // z_.share], packed_ref.at[:, c], local_sem.at[3]
    )
    kept.start()
    for j in range(1, z_.ranks):
        near_copy(j).start()
    keep_wq = pltpu.make_async_copy(wq_s, wq_out, local_sem.at[4])
    keep_wq.start()
    round_wide(1 - core)
    own_wi.start()
    for n in range(pieces):
        for k in others:
            w_copy(n, k, behind(k)).wait_recv()
            w_pass(n, k, core).start()
    for s in range(last):
        for i in range(z_.ranks):
            head_arrival(s, i).wait_recv()
            head_copy(s, i).wait_send()
    for j in range(1, z_.ranks):
        near_arrival(j).wait_recv()
        near_copy(j).wait_send()
    for k in others:
        for s in range(z_.pairs):
            wq_copy(s, k, f).wait_send()
            wq_pass(s, k, own_half).wait_send()
        for n in range(pieces):
            w_copy(n, k, f).wait_send()
            w_pass(n, k, core).wait_send()
            w_pass(n, k, 1 - core).wait_recv()
    kept.wait()
    keep_wq.wait()
    own_wo.wait()
    own_wi.wait()


def project(z_, tokens, gains, cosine, sines, wq, wo, wi):
    peers = max(1, z_.fsdp - 1)
    dma = pltpu.SemaphoreType.DMA
    return pl.pallas_call(
        functools.partial(project_kernel, z_),
        out_shape=(
            jax.ShapeDtypeStruct((12, z_.ctx, z_.block, 2 * HD), BF16),
            jax.ShapeDtypeStruct((z_.pairs, z_.fsdp, z_.shard, 6 * HD), BF16),
            jax.ShapeDtypeStruct((z_.fsdp, z_.head_width, z_.shard), BF16),
            jax.ShapeDtypeStruct((2, z_.fsdp, z_.units_first, z_.shard), BF16),
            jax.ShapeDtypeStruct((z_.fsdp, 8, z_.shard), F32),
        ),
        in_specs=[vmem()] * 4 + [anywhere()] * 3,
        out_specs=(anywhere(), anywhere(), anywhere(), anywhere(), vmem()),
        scratch_shapes=[
            pltpu.VMEM((z_.fsdp, z_.rows, z_.shard), BF16),
            pltpu.VMEM((3, z_.shard, z_.head_width), F32),
            pltpu.VMEM((z_.head_width, z_.shard), F32),
            pltpu.VMEM((2, z_.units_first, z_.shard), F32),
            pltpu.VMEM((z_.pairs, z_.fsdp, z_.shard, 6 * HD), BF16),
            pltpu.VMEM((z_.head_width, z_.shard), BF16),
            pltpu.VMEM((2, z_.units_first, z_.shard), BF16),
            pltpu.VMEM((z_.pairs, 2, 12, z_.block, 2 * HD), BF16),
            pltpu.VMEM((z_.fsdp, 8, z_.shard), F32),
            dma((peers,)),
            dma((peers,)),
            dma((z_.pairs, peers)),
            dma((z_.pairs, peers)),
            dma((z_.pairs, peers)),
            dma((z_.pairs, peers)),
            dma((2, peers)),
            dma((2, peers)),
            dma((2, peers)),
            dma((2, peers)),
            dma((z_.pairs, z_.ranks)),
            dma((z_.pairs, z_.ranks)),
            dma((5,)),
        ],
        compiler_params=pltpu.CompilerParams(
            collective_id=0, has_side_effects=True, vmem_limit_bytes=VMEM_BYTES
        ),
        name="project",
    )(tokens, gains, cosine, sines, wq, wo, wi)


def packing(lengths_ref, order_ref):
    count = order_ref.shape[1]
    lengths = [lengths_ref[0, order_ref[0, k]] for k in range(count)]
    longest, start, chosen = lengths[0], jnp.int32(0), jnp.int32(0)
    passed = lengths[0]
    for k in range(1, count):
        more = lengths[k] > longest
        longest = jnp.where(more, lengths[k], longest)
        start = jnp.where(more, passed, start)
        chosen = jnp.where(more, k, chosen)
        passed = passed + lengths[k]
    ends, total = [], jnp.int32(0)
    for j in range(count):
        length = lengths[j]
        for first in range(1, count):
            length = jnp.where(chosen == first, lengths[(first + j) % count], length)
        total = total + length
        ends.append(total)
    return (start, ends)


def sequence_at(ends, place):
    start, end = jnp.int32(0), ends[0]
    for k in range(len(ends) - 1):
        past = ends[k] <= place
        start = jnp.where(past, ends[k], start)
        end = jnp.where(past, ends[k + 1], end)
    return (start, end)


def segments_of(ends, places):
    segment = jnp.zeros(places.shape, jnp.int32)
    for end in ends:
        segment = segment + (end <= places).astype(jnp.int32)
    return segment


def turned_rows(stage, start, group, rows):
    return stage[pl.ds(lax.rem(start, group), rows), :]


def attend_kernel(
    z_,
    q_tile,
    k_tile,
    lengths_ref,
    order_ref,
    packed_ref,
    out_ref,
    outt_ref,
    lse_ref,
    swapped_ref,
    query_ref,
    key_ref,
    value_ref,
    value_s,
    top_s,
    total_s,
    stage_s,
):
    group = z_.group
    half = group // 2
    piece = min(512, half)
    scaling = HD ** (-0.5)
    sums = 16
    shift, ends = packing(lengths_ref, order_ref)
    packed_ref = packed_ref.reshape(group + half, 2 * HD)
    out_ref = out_ref.reshape(half, 2 * HD)
    query_ref[HD : 2 * HD, :] = jnp.zeros((HD, group), BF16)
    value_s[HD : HD + sums, :] = jnp.ones((sums, group), BF16)
    lane = lax.broadcasted_iota(jnp.int32, (piece, 2 * HD), 1) < HD

    def place(i, offset=0):
        return pl.ds(pl.multiple_of(offset + i * piece, piece), piece)

    def stage_pairs(i, carried):
        stage_s[place(i), :] = packed_ref[place(i), :].astype(F32)
        return carried

    lax.fori_loop(0, group // piece, stage_pairs, 0)
    stage_s[group : group + piece, :] = stage_s[0:piece, :]

    def pairs(i, carried):
        pair = turned_rows(stage_s, shift + i * piece, group, piece)
        swapped_ref[place(i), :] = pltpu.roll(pair, HD, 1).astype(BF16)
        turned = pair.astype(BF16).T
        query_ref[0:HD, place(i)] = (turned[0:HD].astype(F32) * scaling).astype(BF16)
        key_ref[:, place(i)] = turned[HD : 2 * HD]
        return carried

    lax.fori_loop(0, group // piece, pairs, 0)

    def stage_values(i, carried):
        both = packed_ref[place(i, group), :].astype(F32)
        stage_s[place(i), :] = both
        stage_s[place(i, half), :] = pltpu.roll(both, HD, 1)
        return carried

    lax.fori_loop(0, half // piece, stage_values, 0)
    stage_s[group : group + piece, :] = stage_s[0:piece, :]

    def values(i, carried):
        value = turned_rows(stage_s, shift + i * piece, group, piece)
        low = jnp.where(lane, value, 0.0).astype(BF16)
        value_ref[place(i), :] = low
        value_s[0:HD, place(i)] = low.T[0:HD]
        return carried

    lax.fori_loop(0, group // piece, values, 0)

    def one_tile(i, carried):
        first = pl.multiple_of(i * q_tile, q_tile)
        columns = pl.ds(first, q_tile)
        low, low_end = sequence_at(ends, first)
        high_start, high = sequence_at(ends, first + q_tile - 1)
        single = low == high_start
        top_s[...] = jnp.full(top_s.shape, MASKED, F32)
        total_s[...] = jnp.zeros(total_s.shape, F32)

        def one_step(j, masked):
            start = pl.multiple_of(j * k_tile, k_tile)
            rows = pl.ds(start, k_tile)
            scores = jnp.dot(swapped_ref[rows, :], query_ref[:, columns], preferred_element_type=F32)
            if masked:
                key_seg = segments_of(
                    ends, start + lax.broadcasted_iota(jnp.int32, (k_tile, 1), 0)
                )
                query_seg = segments_of(
                    ends, first + lax.broadcasted_iota(jnp.int32, (1, q_tile), 1)
                )
                scores = jnp.where(key_seg == query_seg, scores, MASKED)
            before = top_s[0:1, :]
            after = jnp.maximum(before, jnp.max(scores, axis=0, keepdims=True))
            weights = jnp.exp(scores - after).astype(BF16)
            top_s[0:1, :] = after
            total_s[...] = total_s[...] * jnp.exp(before - after) + jnp.dot(
                value_s[:, rows], weights, preferred_element_type=F32
            )

        def step(j, inner):
            start = j * k_tile
            whole = single & (start >= low) & (start + k_tile <= high)

            @pl.when(whole)
            def plain():
                one_step(j, False)

            @pl.when(jnp.logical_not(whole))
            def partial():
                one_step(j, True)

            return inner

        lax.fori_loop(low // k_tile, (high + k_tile - 1) // k_tile, step, 0)
        summed = total_s[HD : HD + 1, :]
        lse_ref[:, columns] = jnp.broadcast_to(top_s[0:1, :] + jnp.log(summed), (8, q_tile))
        outt_ref[:, columns] = total_s[0:HD, :] / summed
        return carried

    lax.fori_loop(0, group // q_tile, one_tile, 0)

    def stage_out(i, carried):
        both = jnp.concatenate([outt_ref[:, place(i)], jnp.zeros((HD, piece), F32)], axis=0)
        stage_s[place(i), :] = both.astype(BF16).T.astype(F32)
        return carried

    lax.fori_loop(0, group // piece, stage_out, 0)
    stage_s[group : group + piece, :] = stage_s[0:piece, :]

    def finish(i, carried):
        early = turned_rows(stage_s, group - shift + i * piece, group, piece)
        late = turned_rows(stage_s, group + half - shift + i * piece, group, piece)
        out_ref[place(i), :] = jnp.where(lane, early, pltpu.roll(late, HD, 1)).astype(BF16)
        return carried

    lax.fori_loop(0, half // piece, finish, 0)


def attend(z_, lengths, order, packed):
    group = z_.group
    half = group // 2
    q_tile, k_tile = min(1024, half), min(1024, half)
    scalars = pl.BlockSpec(memory_space=pltpu.SMEM)
    return pl.pallas_call(
        functools.partial(attend_kernel, z_, q_tile, k_tile),
        out_shape=(
            jax.ShapeDtypeStruct((4, z_.ctx, z_.block, 2 * HD), BF16),
            jax.ShapeDtypeStruct((HD, group), F32),
            jax.ShapeDtypeStruct((8, group), F32),
            jax.ShapeDtypeStruct((group, 2 * HD), BF16),
            jax.ShapeDtypeStruct((2 * HD, group), BF16),
            jax.ShapeDtypeStruct((HD, group), BF16),
            jax.ShapeDtypeStruct((group, 2 * HD), BF16),
        ),
        in_specs=[scalars, scalars, vmem()],
        out_specs=tuple([vmem()] * 7),
        scratch_shapes=[
            pltpu.VMEM((HD + 16, group), BF16),
            pltpu.VMEM((8, q_tile), F32),
            pltpu.VMEM((HD + 16, q_tile), F32),
            pltpu.VMEM((group + min(512, half), 2 * HD), F32),
        ],
        compiler_params=pltpu.CompilerParams(vmem_limit_bytes=VMEM_BYTES),
        name="attend",
    )(lengths, order, packed)


def attend_back_kernel(
    z_,
    lengths_ref,
    order_ref,
    lse_ref,
    packed_grad,
    outt_ref,
    swapped_ref,
    query_ref,
    key_ref,
    value_ref,
    out_ref,
    turned_s,
    grad_s,
    delta_s,
    stage_s,
    dquery_s,
    dvalue_s,
    key_acc,
    value_acc,
):
    group = z_.group
    half = group // 2
    tile = min(512, half)
    scaling = HD ** (-0.5)
    shift, ends = packing(lengths_ref, order_ref)
    lane = lax.broadcasted_iota(jnp.int32, (tile, 2 * HD), 1) < HD
    flat_grad = packed_grad.reshape(half, 2 * HD)
    flat_out = out_ref.reshape(group + half, 2 * HD)

    def place(i, offset=0):
        return pl.ds(pl.multiple_of(offset + i * tile, tile), tile)

    def stage_grads(i, carried):
        both = flat_grad[place(i), :].astype(F32)
        stage_s[place(i), :] = both
        stage_s[place(i, half), :] = pltpu.roll(both, HD, 1)
        return carried

    lax.fori_loop(0, half // tile, stage_grads, 0)
    stage_s[group : group + tile, :] = stage_s[0:tile, :]

    def order_grads(i, carried):
        rows = turned_rows(stage_s, shift + i * tile, group, tile)
        low = jnp.where(lane, rows, 0.0).astype(BF16)
        grad_s[place(i), :] = low
        turned = low.T[0:HD]
        turned_s[0:HD, place(i)] = turned
        turned_s[HD : 2 * HD, place(i)] = key_ref[:, place(i)]
        delta = jnp.sum(turned.astype(F32) * outt_ref[:, place(i)], axis=0, keepdims=True)
        delta_s[:, place(i)] = jnp.broadcast_to(delta, (8, tile))
        dquery_s[:, place(i)] = jnp.zeros((HD, tile), F32)
        return carried

    lax.fori_loop(0, group // tile, order_grads, 0)

    def one_step(rows, start, first, masked):
        columns = pl.ds(first, tile)
        scores = jnp.dot(swapped_ref[rows, :], query_ref[:, columns], preferred_element_type=F32)
        chances = jnp.exp(scores - lse_ref[0:1, columns])
        if masked:
            key_seg = segments_of(ends, start + lax.broadcasted_iota(jnp.int32, (tile, 1), 0))
            query_seg = segments_of(ends, first + lax.broadcasted_iota(jnp.int32, (1, tile), 1))
            chances = jnp.where(key_seg == query_seg, chances, 0.0)
        chance_grad = jnp.dot(
            value_ref[rows, :], turned_s[:, columns], preferred_element_type=F32
        )
        score_grad = (chances * (chance_grad - delta_s[0:1, columns])).astype(BF16)
        value_acc[...] += jnp.dot(
            chances.astype(BF16), grad_s[columns, :], preferred_element_type=F32
        )
        key_acc[...] += jnp.dot(score_grad, swapped_ref[columns, :], preferred_element_type=F32)
        dquery_s[:, columns] += jnp.dot(
            turned_s[HD : 2 * HD, rows], score_grad, preferred_element_type=F32
        )

    def one_tile(j, masked):
        start = pl.multiple_of(j * tile, tile)
        rows = pl.ds(start, tile)
        key_acc[...] = jnp.zeros(key_acc.shape, F32)
        value_acc[...] = jnp.zeros(value_acc.shape, F32)
        low, high = jnp.int32(0), jnp.int32(half)
        if masked:
            low, low_end = sequence_at(ends, start)
            high_start, high = sequence_at(ends, start + tile - 1)

        def step(i, inner):
            one_step(rows, start, pl.multiple_of(i * tile, tile), masked)
            return inner

        lax.fori_loop(low // tile, (high + tile - 1) // tile, step, 0)
        dvalue_s[rows, :] = value_acc[...].astype(BF16)
        stage_s[rows, :] = key_acc[...]

    def long_tile(j, carried):
        one_tile(j, False)
        return carried

    def other_tile(j, carried):
        one_tile(j, True)
        return carried

    lax.fori_loop(0, half // tile, long_tile, 0)
    lax.fori_loop(half // tile, group // tile, other_tile, 0)

    def join_pairs(i, carried):
        turned = jnp.concatenate([dquery_s[:, place(i)], jnp.zeros((HD, tile), F32)], axis=0)
        query_rows = (turned * scaling).astype(BF16).T.astype(F32)
        stage_s[place(i), :] = jnp.where(lane, query_rows, stage_s[place(i), :] * scaling)
        return carried

    lax.fori_loop(0, group // tile, join_pairs, 0)
    stage_s[group : group + tile, :] = stage_s[0:tile, :]

    def order_pairs(i, carried):
        rows = turned_rows(stage_s, group - shift + i * tile, group, tile)
        flat_out[place(i), :] = rows.astype(BF16)
        return carried

    lax.fori_loop(0, group // tile, order_pairs, 0)

    def stage_values(i, carried):
        stage_s[place(i), :] = dvalue_s[place(i), :].astype(F32)
        return carried

    lax.fori_loop(0, group // tile, stage_values, 0)
    stage_s[group : group + tile, :] = stage_s[0:tile, :]

    def order_values(i, carried):
        early = turned_rows(stage_s, group - shift + i * tile, group, tile)
        late = turned_rows(stage_s, group + half - shift + i * tile, group, tile)
        flat_out[place(i, group), :] = jnp.where(lane, early, pltpu.roll(late, HD, 1)).astype(BF16)
        return carried

    lax.fori_loop(0, half // tile, order_values, 0)


def attend_back(z_, lengths, order, lse, grads, turned_out, swapped, query, key, value):
    group = z_.group
    tile = min(512, group // 2)
    scalars = pl.BlockSpec(memory_space=pltpu.SMEM)
    return pl.pallas_call(
        functools.partial(attend_back_kernel, z_),
        out_shape=jax.ShapeDtypeStruct((12, z_.ctx, z_.block, 2 * HD), BF16),
        in_specs=[scalars, scalars] + [vmem()] * 7,
        out_specs=vmem(),
        scratch_shapes=[
            pltpu.VMEM((2 * HD, group), BF16),
            pltpu.VMEM((group, 2 * HD), BF16),
            pltpu.VMEM((8, group), F32),
            pltpu.VMEM((group + tile, 2 * HD), F32),
            pltpu.VMEM((HD, group), F32),
            pltpu.VMEM((group, 2 * HD), BF16),
            pltpu.VMEM((tile, 2 * HD), F32),
            pltpu.VMEM((tile, 2 * HD), F32),
        ],
        compiler_params=pltpu.CompilerParams(vmem_limit_bytes=VMEM_BYTES),
        name="attend_back",
    )(lengths, order, lse, grads, turned_out, swapped, query, key, value)


def middle_kernel(
    z_,
    tok_ref,
    cot_ref,
    gain_ref,
    heads_ref,
    wo_ref,
    wi_ref,
    wide_ref,
    down_ref,
    branch_ref,
    middle_ref,
    mgrad_ref,
    gain2_ref,
    grads_ref,
    g_down,
    g_wide,
    g_attn,
    heads_s,
    wo_s,
    wi_s,
    wide_f,
    down_f,
    wm_s,
    mixed_s,
    mixed_t,
    sum_s,
    sum_in,
    back_s,
    back_in,
    entry_s,
    branch_s,
    middle_s,
    grad_f,
    normed_s,
    scale_s,
    gate_s,
    hgrad_s,
    hidden_s,
    hidden_t,
    gated_s,
    gated_t,
    mgrad_s,
    dsend_s,
    down_s,
    wide_s,
    attn_s,
    a_send,
    a_recv,
    d_send,
    d_recv,
    y_send,
    y_recv,
    w_send,
    w_recv,
    f_send,
    f_recv,
    local_sem,
):
    f, c, t = lax.axis_index("fsdp"), lax.axis_index("ctx"), lax.axis_index("tp")
    core = lax.rem(c, 2)
    mate = (f, c + 1 - 2 * core, t)
    other = (f, c, 1 - t)
    count = z_.ctx // z_.share
    others = range(1, z_.fsdp)
    half = z_.rows // 2

    def ahead(k):
        return lax.rem(f + k, z_.fsdp)

    def behind(k):
        return lax.rem(f + z_.fsdp - k, z_.fsdp)

    def to_token(j):
        return lax.rem(c + z_.share * j, z_.ctx)

    def from_head(j):
        return lax.rem(c + z_.ctx - z_.share * j, z_.ctx)

    def heads_copy(j):
        return remote(
            heads_ref.at[:, to_token(j)],
            heads_s.at[c // z_.share],
            a_send.at[j],
            a_recv.at[j],
            (f, to_token(j), t),
        )

    def heads_arrival(j):
        return remote(
            heads_ref.at[:, c],
            heads_s.at[from_head(j) // z_.share],
            a_send.at[j],
            a_recv.at[j],
            mate,
        )

    def grads_copy(j):
        rank = lax.rem(c + j, z_.ctx)
        return remote(
            dsend_s.at[rank // z_.share],
            grads_ref.at[:, c],
            d_send.at[j],
            d_recv.at[j],
            (f, rank, t),
        )

    def grads_arrival(j):
        source = lax.rem(c + z_.ctx - j, z_.ctx)
        return remote(
            dsend_s.at[0], grads_ref.at[:, source], d_send.at[j], d_recv.at[j], mate
        )

    units_half = z_.units // 2

    def weight_place(n, side, owner):
        if n == 0:
            rows = pl.ds(pl.multiple_of(side * units_half, 16), units_half)
            return wm_s.at[owner, rows]
        return wi_s.at[side, owner, z_.units_first : z_.units]

    def w_copy(n, k, owner):
        place = weight_place(n, core, owner)
        return remote(place, place, w_send.at[n, k - 1], w_recv.at[n, k - 1], (ahead(k), c, t))

    def w_pass(n, k, side):
        place = weight_place(n, side, behind(k))
        return remote(place, place, f_send.at[n, k - 1], f_recv.at[n, k - 1], mate)

    def sum_copy(r):
        rows = pl.ds(r * half, half)
        return remote(sum_s.at[rows], sum_in.at[rows], y_send.at[r], y_recv.at[r], other)

    def back_copy(r):
        rows = pl.ds(r * half, half)
        return remote(
            back_s.at[rows], back_in.at[rows], y_send.at[2 + r], y_recv.at[2 + r], other
        )

    load_wide = pltpu.make_async_copy(
        wide_ref.at[:, z_.units_first : z_.units], wide_f, local_sem.at[8]
    )
    load_wide.start()
    load_down = pltpu.make_async_copy(down_ref, down_f, local_sem.at[3])
    load_down.start()
    load_wo = pltpu.make_async_copy(wo_ref, wo_s, local_sem.at[1])
    load_wi = pltpu.make_async_copy(
        wi_ref, wi_s.at[:, :, 0 : z_.units_first], local_sem.at[2]
    )
    load_wo.start()
    load_wi.start()
    greet(
        [(ahead(k), c, t) for k in others]
        + [(f, lax.rem(c + j, z_.ctx), t) for j in range(1, z_.ctx)]
        + [other]
    )
    for j in range(1, count):
        heads_copy(j).start()
    own_heads = pltpu.make_async_copy(
        heads_ref.at[:, c], heads_s.at[c // z_.share], local_sem.at[0]
    )
    own_heads.start()
    load_wide.wait()
    for side in range(2):

        def round_wide(first, rows, side=side):
            wi_s[side, f, pl.ds(z_.units_first + first, rows), :] = wide_f[
                side, pl.ds(first, rows), :
            ].astype(BF16)

        over_rows(0, z_.units - z_.units_first, 128, round_wide)
    for k in others:
        w_copy(1, k, f).start()
    load_down.wait()

    def round_down(first, rows):
        place = pl.ds(first, rows)
        wm_s[f, place, :] = down_f[place, :].astype(BF16)

    over_rows(0, z_.units, 128, round_down)
    for k in others:
        w_copy(0, k, f).start()
    load_wo.wait()
    own_heads.wait()
    for j in range(1, count):
        heads_arrival(j).wait_recv()

    low_lane = lax.broadcasted_iota(jnp.int32, (half, 2 * HD), 1) < HD
    for h in range(0, z_.heads, 2):
        columns = slice(h * HD, (h + 2) * HD)
        one = heads_s[h].reshape(half, 2 * HD).astype(F32)
        two = heads_s[h + 1].reshape(half, 2 * HD).astype(F32)
        early = jnp.where(low_lane, one, pltpu.roll(two, HD, 1))
        late = jnp.where(low_lane, pltpu.roll(one, HD, 1), two)
        mixed_s[0:half, columns] = early.astype(BF16)
        mixed_s[half:, columns] = late.astype(BF16)
        mixed_t[columns, 0:half] = early.T.astype(BF16)
        mixed_t[columns, half:] = late.T.astype(BF16)

    for r in range(2):
        rows = slice(r * half, (r + 1) * half)
        for g in range(z_.fsdp):
            sum_s[rows, g * z_.shard : (g + 1) * z_.shard] = jnp.dot(
                mixed_s[rows, :], wo_s[g], preferred_element_type=F32
            ).astype(BF16)
        sum_copy(r).start()

    tile = min(128, half)

    def hidden_grad(i, carried):
        rows = pl.ds(pl.multiple_of(i * tile, tile), tile)
        total = jnp.zeros((tile, z_.units), F32)
        for g in range(z_.fsdp):
            total = total + lax.dot_general(
                cot_ref[rows, g * z_.shard : (g + 1) * z_.shard],
                wm_s[g],
                (((1,), (1,)), ((), ())),
                preferred_element_type=F32,
            )
        hgrad_s[rows, :] = total
        return carried

    load_wi.wait()
    for k in others:
        w_copy(1, k, behind(k)).wait_recv()
        w_pass(1, k, core).start()
    for k in others:
        w_pass(1, k, 1 - core).wait_recv()
    full = z_.units // 128 * 128

    for r in range(2):
        sum_copy(r).wait_recv()

        def middle_tile(i, carried):
            rows = pl.ds(pl.multiple_of(r * half + i * tile, tile), tile)
            middle = tok_ref[rows, :].astype(F32) + (
                sum_s[rows, :].astype(F32) + sum_in[rows, :].astype(F32)
            )
            middle_s[rows, :] = middle
            normed, scaling = normalize(middle)
            normed_s[rows, :] = normed
            scale_s[rows, :] = jnp.broadcast_to(scaling, (tile, 128))
            gains = jnp.concatenate([gain_ref[g, 1:2, :] for g in range(z_.fsdp)], axis=1)
            entry_s[rows, :] = (normed * gains).astype(BF16)
            return carried

        lax.fori_loop(0, half // tile, middle_tile, 0)
        rows = pl.ds(r * half, half)

        def gate(k, carried):
            total = jnp.zeros((half, z_.units), F32)
            for g in range(z_.fsdp):
                total = total + lax.dot_general(
                    entry_s[rows, g * z_.shard : (g + 1) * z_.shard],
                    wi_s[k, g],
                    (((1,), (1,)), ((), ())),
                    preferred_element_type=F32,
                )
            gate_s[k] = total
            return carried

        lax.fori_loop(0, 2, gate, 0)

        if r == 0:
            for k in others:
                w_copy(0, k, behind(k)).wait_recv()
                w_pass(0, k, core).start()
            for k in others:
                w_pass(0, k, 1 - core).wait_recv()
        tiles = half // tile
        lax.fori_loop(r * tiles, (r + 1) * tiles, hidden_grad, 0)

        def activate(i, carried):
            inner = pl.ds(pl.multiple_of(i * 16, 16), 16)
            outer = pl.ds(pl.multiple_of(r * half + i * 16, 16), 16)
            up, side = gate_s[0, inner, :], gate_s[1, inner, :]
            grad = hgrad_s[outer, :]
            chance = 0.5 + 0.5 * lax.erf(up * (0.5**0.5))
            slope = chance + up * (jnp.exp(-0.5 * up * up) * 0.3989422804014327)
            active = up * chance
            hidden_s[outer, :] = (active * side).astype(BF16)
            gated_s[0, outer, :] = (grad * side * slope).astype(BF16)
            gated_s[1, outer, :] = (grad * active).astype(BF16)
            return carried

        lax.fori_loop(0, half // 16, activate, 0)

        for g in range(z_.fsdp):
            place = slice(g * z_.shard, (g + 1) * z_.shard)
            total = jnp.zeros((half, z_.shard), F32)
            for k in range(2):
                total = total + jnp.dot(
                    gated_s[k, rows, :], wi_s[k, g], preferred_element_type=F32
                )
            back_s[rows, place] = total.astype(BF16)
        back_copy(r).start()

    keep_middle = pltpu.make_async_copy(middle_s, middle_ref, local_sem.at[9])
    keep_middle.start()

    def turn(source, target):
        def turn_tile(i, carried):
            rows = pl.ds(pl.multiple_of(i * tile, tile), tile)
            for first in range(0, full, 128):
                block = source[rows, first : first + 128].astype(F32)
                target[first : first + 128, rows] = block.T.astype(BF16)
            if full < z_.units:
                rest = z_.units - full
                block = source[rows, full : z_.units].astype(F32)
                block = jnp.concatenate([block, jnp.zeros((tile, 128 - rest), F32)], axis=1)
                target[full : z_.units, rows] = block.T[0:rest].astype(BF16)
            return carried

        lax.fori_loop(0, z_.rows // tile, turn_tile, 0)

    turn(hidden_s, hidden_t)
    for g in range(z_.fsdp):
        place = slice(g * z_.shard, (g + 1) * z_.shard)
        for side in range(2):
            rows = slice(side * units_half, (side + 1) * units_half)
            down_s[g, side] = jnp.dot(
                hidden_t[rows, :], cot_ref[:, place], preferred_element_type=F32
            ).astype(BF16)
    keep_down = pltpu.make_async_copy(down_s, g_down, local_sem.at[4])
    keep_down.start()

    for k in range(2):
        turn(gated_s.at[k], gated_t.at[k])
        for g in range(z_.fsdp):
            wide_s[g, k] = jnp.dot(
                gated_t[k],
                entry_s[:, g * z_.shard : (g + 1) * z_.shard],
                preferred_element_type=F32,
            ).astype(BF16)
    keep_wide = pltpu.make_async_copy(wide_s, g_wide, local_sem.at[5])
    keep_wide.start()
    for g in range(z_.fsdp):
        place = slice(g * z_.shard, (g + 1) * z_.shard)
        branch_s[:, place] = jnp.dot(
            hidden_s[...], wm_s[g], preferred_element_type=F32
        ).astype(BF16)
    keep_branch = pltpu.make_async_copy(branch_s, branch_ref, local_sem.at[10])
    keep_branch.start()

    gain2_ref[...] = jnp.zeros(gain2_ref.shape, F32)
    for r in range(2):
        back_copy(r).wait_recv()

        def back_tile(i, carried):
            rows = pl.ds(pl.multiple_of(r * half + i * tile, tile), tile)
            back = back_s[rows, :].astype(F32) + back_in[rows, :].astype(F32)
            normed = normed_s[rows, :]
            gain2_ref[0:1, :] += jnp.sum(back * normed, axis=0, keepdims=True)
            gains = jnp.concatenate([gain_ref[g, 1:2, :] for g in range(z_.fsdp)], axis=1)
            grad = cot_ref[rows, :].astype(F32) + norm_back(
                back * gains, normed, scale_s[rows, 0:1]
            )
            grad_f[rows, :] = grad
            mgrad_s[rows, :] = grad.astype(BF16)
            return carried

        lax.fori_loop(0, half // tile, back_tile, 0)

    keep_grad = pltpu.make_async_copy(grad_f, mgrad_ref, local_sem.at[11])
    keep_grad.start()

    def heads_grad(rows):
        total = jnp.zeros((half, z_.head_width), F32)
        for g in range(z_.fsdp):
            total = total + lax.dot_general(
                mgrad_s[rows, g * z_.shard : (g + 1) * z_.shard],
                wo_s[g],
                (((1,), (1,)), ((), ())),
                preferred_element_type=F32,
            )
        return total

    early = heads_grad(slice(0, half))
    late = heads_grad(slice(half, z_.rows))
    for h in range(0, z_.heads, 2):
        columns = slice(h * HD, (h + 2) * HD)
        one = jnp.where(low_lane, early[:, columns], pltpu.roll(late[:, columns], HD, 1))
        two = jnp.where(low_lane, pltpu.roll(early[:, columns], HD, 1), late[:, columns])
        dsend_s[h] = one.astype(BF16).reshape(4, z_.block, 2 * HD)
        dsend_s[h + 1] = two.astype(BF16).reshape(4, z_.block, 2 * HD)
    for j in range(1, z_.ctx):
        grads_copy(j).start()
    own_grads = pltpu.make_async_copy(
        dsend_s.at[c // z_.share], grads_ref.at[:, c], local_sem.at[6]
    )
    own_grads.start()
    attn_half = z_.head_width // 2
    for g in range(z_.fsdp):
        for side in range(2):
            attn_s[g, side] = jnp.dot(
                mixed_t[side * attn_half : (side + 1) * attn_half, :],
                mgrad_s[:, g * z_.shard : (g + 1) * z_.shard],
                preferred_element_type=F32,
            ).astype(BF16)
    keep_attn = pltpu.make_async_copy(attn_s, g_attn, local_sem.at[7])
    keep_attn.start()

    own_grads.wait()
    for j in range(1, z_.ctx):
        grads_arrival(j).wait_recv()
        grads_copy(j).wait_send()
    for j in range(1, count):
        heads_copy(j).wait_send()
    for k in others:
        for n in range(2):
            w_copy(n, k, f).wait_send()
            w_pass(n, k, core).wait_send()
    for r in range(2):
        sum_copy(r).wait_send()
        back_copy(r).wait_send()
    keep_down.wait()
    keep_wide.wait()
    keep_attn.wait()
    keep_middle.wait()
    keep_branch.wait()
    keep_grad.wait()


def middle_part(z_, tokens, cotangent, gains, heads, wo, wi, wide_weight, down_weight):
    dma = pltpu.SemaphoreType.DMA
    peers = max(1, z_.fsdp - 1)
    count = z_.ctx // z_.share
    rows, width, units = z_.rows, z_.width, z_.units
    down = (z_.fsdp, 2, units // 2, z_.shard)
    wide = (z_.fsdp, 2, units, z_.shard)
    attn = (z_.fsdp, 2, z_.head_width // 2, z_.shard)
    return pl.pallas_call(
        functools.partial(middle_kernel, z_),
        out_shape=(
            jax.ShapeDtypeStruct((rows, width), BF16),
            jax.ShapeDtypeStruct((rows, width), F32),
            jax.ShapeDtypeStruct((rows, width), F32),
            jax.ShapeDtypeStruct((8, width), F32),
            jax.ShapeDtypeStruct((4, z_.ctx, z_.block, 2 * HD), BF16),
            jax.ShapeDtypeStruct(down, BF16),
            jax.ShapeDtypeStruct(wide, BF16),
            jax.ShapeDtypeStruct(attn, BF16),
        ),
        in_specs=[vmem()] * 3 + [anywhere()] * 5,
        out_specs=tuple([anywhere()] * 3 + [vmem()] + [anywhere()] * 4),
        scratch_shapes=[
            pltpu.VMEM((z_.heads, 4, z_.block, 2 * HD), BF16),
            pltpu.VMEM((z_.fsdp, z_.head_width, z_.shard), BF16),
            pltpu.VMEM((2, z_.fsdp, units, z_.shard), BF16),
            pltpu.VMEM((2, units - z_.units_first, z_.shard), F32),
            pltpu.VMEM((units, z_.shard), F32),
            pltpu.VMEM((z_.fsdp, units, z_.shard), BF16),
            pltpu.VMEM((rows, z_.head_width), BF16),
            pltpu.VMEM((z_.head_width, rows), BF16),
            pltpu.VMEM((rows, width), BF16),
            pltpu.VMEM((rows, width), BF16),
            pltpu.VMEM((rows, width), BF16),
            pltpu.VMEM((rows, width), BF16),
            pltpu.VMEM((rows, width), BF16),
            pltpu.VMEM((rows, width), BF16),
            pltpu.VMEM((rows, width), F32),
            pltpu.VMEM((rows, width), F32),
            pltpu.VMEM((rows, width), F32),
            pltpu.VMEM((rows, 128), F32),
            pltpu.VMEM((2, rows // 2, units), F32),
            pltpu.VMEM((rows, units), F32),
            pltpu.VMEM((rows, units), BF16),
            pltpu.VMEM((units, rows), BF16),
            pltpu.VMEM((2, rows, units), BF16),
            pltpu.VMEM((2, units, rows), BF16),
            pltpu.VMEM((rows, width), BF16),
            pltpu.VMEM((z_.heads, 4, z_.block, 2 * HD), BF16),
            pltpu.VMEM(down, BF16),
            pltpu.VMEM(wide, BF16),
            pltpu.VMEM(attn, BF16),
            dma((count,)),
            dma((count,)),
            dma((z_.ctx,)),
            dma((z_.ctx,)),
            dma((4,)),
            dma((4,)),
            dma((2, peers)),
            dma((2, peers)),
            dma((2, peers)),
            dma((2, peers)),
            dma((12,)),
        ],
        compiler_params=pltpu.CompilerParams(
            collective_id=2, has_side_effects=True, vmem_limit_bytes=VMEM_BYTES
        ),
        name="middle",
    )(tokens, cotangent, gains, heads, wo, wi, wide_weight, down_weight)


class Item:
    def __init__(self, number, rows, columns, cuts):
        self.number = number
        self.rows = rows
        self.columns = columns
        self.cuts = cuts_of(rows, cuts)


class Reducer:
    def __init__(self, z_, items, refs, sems):
        self.z_ = z_
        self.items = items
        self.refs = refs
        self.sems = sems
        f, c, t = lax.axis_index("fsdp"), lax.axis_index("ctx"), lax.axis_index("tp")
        self.f, self.c, self.t = f, c, t
        self.core = lax.rem(c, 2)
        self.chip = c // 2
        self.mate = (f, c + 1 - 2 * self.core, t)
        middle = z_.chips // 2
        low = self.chip < middle
        self.is_mid = (self.chip == middle - 1) | (self.chip == middle)
        self.has_outer = (self.chip > 0) & (self.chip < z_.chips - 1)
        self.is_end = jnp.logical_not(self.is_mid | self.has_outer)
        towards = jnp.where(low, 2, -2)
        self.inner = (f, c + towards, t)
        self.outer = (f, c - towards, t)
        self.numbers = {}
        for item in items:
            for cut in range(len(item.cuts)):
                self.numbers[(item.number, cut)] = len(self.numbers)

    def ahead(self, k):
        return lax.rem(self.f + k, self.z_.fsdp)

    def behind(self, k):
        return lax.rem(self.f + self.z_.fsdp - k, self.z_.fsdp)

    def part(self, item, cut):
        first, rows = item.cuts[cut]
        return self.numbers[(item.number, cut)], pl.ds(first, rows)


    def core_copy(self, item, cut):
        source, own, mate_in = self.refs[item.number][:3]
        n, rows = self.part(item, cut)
        return remote(
            source.at[:, 1 - self.core, rows],
            mate_in.at[:, rows],
            self.sems["core_send"].at[n],
            self.sems["core_recv"].at[n],
            self.mate,
        )

    def own_copy(self, item, cut):
        source, own = self.refs[item.number][:2]
        n, rows = self.part(item, cut)
        return pltpu.make_async_copy(
            source.at[:, self.core, rows], own.at[:, rows], self.sems["own"].at[n]
        )

    def core_start(self, item, cut):
        self.core_copy(item, cut).start()
        self.own_copy(item, cut).start()

    def core_sum(self, item, cut):
        own, mate_in = self.refs[item.number][1:3]
        first, rows = item.cuts[cut]
        self.own_copy(item, cut).wait()
        self.core_copy(item, cut).wait_recv()
        for k in range(self.z_.fsdp - 1, -1, -1):
            g = self.ahead(k)

            def add(start, count):
                place = pl.ds(start, count)
                own[g, place, :] = (
                    own[g, place, :].astype(F32) + mate_in[g, place, :].astype(F32)
                ).astype(BF16)

            over_rows(first, rows, 128, add)
            if k:
                self.peer_copy(item, cut, k, g).start()


    def peer_copy(self, item, cut, k, owner):
        own, peer_in = self.refs[item.number][1], self.refs[item.number][3]
        n, rows = self.part(item, cut)
        return remote(
            own.at[owner, rows],
            peer_in.at[k - 1, rows],
            self.sems["peer_send"].at[n, k - 1],
            self.sems["peer_recv"].at[n, k - 1],
            (self.ahead(k), self.c, self.t),
        )

    def peer_sum(self, item, cut):
        own, peer_in = self.refs[item.number][1], self.refs[item.number][3]
        first, rows = item.cuts[cut]
        for k in range(1, self.z_.fsdp):
            self.peer_copy(item, cut, k, self.ahead(k)).wait_recv()

        def add(start, count):
            place = pl.ds(start, count)
            total = own[self.f, place, :].astype(F32)
            for k in range(1, self.z_.fsdp):
                total = total + peer_in[k - 1, place, :].astype(F32)
            own[self.f, place, :] = total.astype(BF16)

        over_rows(first, rows, 128, add)

        @pl.when(jnp.logical_not(self.has_outer))
        def outermost():
            self.inward_start(item, cut)


    def in_copy(self, item, cut, middle):
        own, peer_in, outer_in, inner_in = self.refs[item.number][1:2] + self.refs[item.number][3:6]
        rows = pl.ds(*item.cuts[cut])
        n = self.numbers[(item.number, cut)]
        if middle:
            target, name = inner_in, "inner_recv"
        else:
            target, name = outer_in, "outer_recv"
        return remote(
            own.at[self.f, rows],
            target.at[rows],
            self.sems["in_send"].at[n],
            self.sems[name].at[n],
            self.inner,
        )

    def out_copy(self, item, cut):
        inner_in = self.refs[item.number][5]
        rows = pl.ds(*item.cuts[cut])
        n = self.numbers[(item.number, cut)]
        return remote(
            inner_in.at[rows],
            inner_in.at[rows],
            self.sems["out_send"].at[n],
            self.sems["inner_recv"].at[n],
            self.outer,
        )

    def done_copy(self, item, cut):
        inner_in, mate_out = self.refs[item.number][5:7]
        rows = pl.ds(*item.cuts[cut])
        n = self.numbers[(item.number, cut)]
        return remote(
            inner_in.at[rows],
            mate_out.at[rows],
            self.sems["done_send"].at[n],
            self.sems["done_recv"].at[n],
            self.mate,
        )

    def inward_start(self, item, cut):
        @pl.when(self.is_mid)
        def cross():
            self.in_copy(item, cut, True).start()

        @pl.when(jnp.logical_not(self.is_mid))
        def along():
            self.in_copy(item, cut, False).start()

    def inward(self, item, cut):
        own, outer_in = self.refs[item.number][1], self.refs[item.number][4]
        first, rows = item.cuts[cut]

        @pl.when(self.has_outer)
        def passed():
            self.in_copy(item, cut, False).wait_recv()

            def add(start, count):
                place = pl.ds(start, count)
                own[self.f, place, :] = (
                    own[self.f, place, :].astype(F32) + outer_in[place, :].astype(F32)
                ).astype(BF16)

            over_rows(first, rows, 128, add)
            self.inward_start(item, cut)

    def outward(self, item, cut):
        own, inner_in = self.refs[item.number][1], self.refs[item.number][5]
        first, rows = item.cuts[cut]

        @pl.when(jnp.logical_not(self.is_end))
        def onwards():
            self.out_copy(item, cut).wait_recv()

            @pl.when(self.is_mid)
            def total():
                def add(start, count):
                    place = pl.ds(start, count)
                    inner_in[place, :] = (
                        own[self.f, place, :].astype(F32) + inner_in[place, :].astype(F32)
                    ).astype(BF16)

                over_rows(first, rows, 128, add)

            @pl.when(self.has_outer)
            def onward():
                self.out_copy(item, cut).start()

            self.done_copy(item, cut).start()

    def arrive(self, item, cut):
        @pl.when(self.is_end)
        def ended():
            self.out_copy(item, cut).wait_recv()
            self.done_copy(item, cut).start()

    def settle(self):
        for item in self.items:
            for cut in range(len(item.cuts)):
                self.core_copy(item, cut).wait_send()
                for k in range(1, self.z_.fsdp):
                    self.peer_copy(item, cut, k, self.ahead(k)).wait_send()
                self.in_copy(item, cut, False).wait_send()

                @pl.when(self.has_outer)
                def outwards(item=item, cut=cut):
                    self.out_copy(item, cut).wait_send()

                self.done_copy(item, cut).wait_send()


class Finisher:
    def __init__(self, z_, reducer, results, store_sem):
        self.z_ = z_
        self.red = reducer
        self.results = results
        self.store_sem = store_sem

    def copies(self, item, cut, which):
        first, rows = item.cuts[cut]
        number = item.number
        red = self.red
        side = red.core if which == 0 else 1 - red.core
        sums = red.refs[number][5 + which]
        result = self.results[number]
        sem = self.store_sem.at[which]
        index = red.numbers[(number, cut)]
        if number == 3:
            half = self.z_.shard // 2
            place = pl.ds(pl.multiple_of(side * half, half), half)
            columns = slice(2 * HD * cut, 2 * HD * (cut + 1))
            return [
                pltpu.make_async_copy(
                    sums.at[first : first + rows, 2 * HD * kind : 2 * HD * (kind + 1)],
                    result.at[kind, place, columns],
                    sem.at[index, kind],
                )
                for kind in range(3)
            ]
        if number in (1, 4):
            target = result.at[side, first : first + rows]
        else:
            target = result.at[pl.ds(pl.multiple_of(side * item.rows + first, 16), rows)]
        return [pltpu.make_async_copy(sums.at[first : first + rows], target, sem.at[index, 0])]

    def update(self, item, cut):
        for copy in self.copies(item, cut, 0):
            copy.start()
        self.red.done_copy(item, cut).wait_recv()
        for copy in self.copies(item, cut, 1):
            copy.start()

    def settle(self):
        for item in self.red.items:
            for cut in range(len(item.cuts)):
                for which in range(2):
                    for copy in self.copies(item, cut, which):
                        copy.wait()


def reduce_kernel(
    z_,
    items,
    tok_ref,
    gain_ref,
    cos_ref,
    sin_ref,
    branch_ref,
    middle_ref,
    mgrad_ref,
    gain2_ref,
    heads_ref,
    wq_ref,
    g_down,
    g_wide,
    g_attn,
    *others,
):
    down, wide, attn, qkv, gain = items
    scratch = list(others)

    def take(count):
        taken = scratch[:count]
        del scratch[:count]
        return taken

    out_ref, igrad_ref = take(2)
    results = take(5)
    heads_s, wq_s, entry_s, grads_s, branch_own, branch_s, back_s, back_in = take(8)
    middle_s, mgrad_s = take(2)
    g_qkv, g_gain, gain_in, gain_acc = take(4)
    groups = [take(6) for item in items]
    (a_send, a_recv, y_send, y_recv, local_sem, store_sem) = take(6)
    names = (
        "peer_send",
        "peer_recv",
        "core_send",
        "core_recv",
        "own",
        "in_send",
        "outer_recv",
        "inner_recv",
        "out_send",
        "done_send",
        "done_recv",
    )
    sems = dict(zip(names, take(len(names))))
    sources = (g_down, g_wide, g_attn, g_qkv, g_gain)
    refs = [(source, *group) for source, group in zip(sources, groups)]
    red = Reducer(z_, items, refs, sems)
    finish = Finisher(z_, red, results, store_sem)
    f, c, t = red.f, red.c, red.t
    other = (f, c, 1 - t)
    count = z_.ctx // z_.share

    def to_token(j):
        return lax.rem(c + z_.share * j, z_.ctx)

    def from_head(j):
        return lax.rem(c + z_.ctx - z_.share * j, z_.ctx)

    def heads_copy(j):
        return remote(
            heads_ref.at[:, to_token(j)],
            heads_s.at[c // z_.share],
            a_send.at[j],
            a_recv.at[j],
            (f, to_token(j), t),
        )

    def branch_copy():
        return remote(branch_ref, branch_s, y_send.at[0], y_recv.at[0], other)

    def back_copy(r):
        rows = pl.ds(r * (z_.rows // 2), z_.rows // 2)
        return remote(back_s.at[rows], back_in.at[rows], y_send.at[2 + r], y_recv.at[2 + r], other)

    load_wq = pltpu.make_async_copy(wq_ref, wq_s, local_sem.at[1])
    load_branch = pltpu.make_async_copy(branch_ref, branch_own, local_sem.at[2])
    load_middle = pltpu.make_async_copy(middle_ref, middle_s, local_sem.at[3])
    load_mgrad = pltpu.make_async_copy(mgrad_ref, mgrad_s, local_sem.at[4])
    load_wq.start()
    load_branch.start()
    load_middle.start()
    load_mgrad.start()
    greet(
        [(red.ahead(k), c, t) for k in range(1, z_.fsdp)]
        + [(f, lax.rem(c + j, z_.ctx), t) for j in range(1, z_.ctx)]
        + [other]
    )
    for j in range(1, count):
        heads_copy(j).start()
    branch_copy().start()
    own_heads = pltpu.make_async_copy(heads_ref.at[:, c], heads_s.at[c // z_.share], local_sem.at[0])
    own_heads.start()
    ready = [(item, cut) for item in (down, wide, attn) for cut in range(len(item.cuts))]
    for part in ready:
        red.core_start(*part)

    for part in ready:
        red.core_sum(*part)

    def run(*steps):
        for step in steps:
            item = {"d": down, "w": wide, "a": attn, "q": qkv, "g": gain}[step[1]]
            part = (item, int(step[2]))
            if step[0] == "x":
                red.peer_sum(*part)
            elif step[0] == "i":
                red.inward(*part)
            elif step[0] == "o":
                red.outward(*part)
            elif step[0] == "e":
                red.arrive(*part)
            else:
                finish.update(*part)

    tile = min(128, z_.rows)

    def entry_tile(i, carried):
        rows = pl.ds(pl.multiple_of(i * tile, tile), tile)
        normed, nothing = normalize(tok_ref[rows, :].astype(F32))
        for g in range(z_.fsdp):
            columns = slice(g * z_.shard, (g + 1) * z_.shard)
            entry_s[g, :, rows] = (normed[:, columns] * gain_ref[g, 0:1, :]).T.astype(BF16)
        return carried

    lax.fori_loop(0, z_.rows // tile, entry_tile, 0)

    run("xd0", "xd1")
    branch_copy().wait_recv()
    load_branch.wait()
    load_middle.wait()

    def output_tile(i, carried):
        rows = pl.ds(pl.multiple_of(i * tile, tile), tile)
        branch = branch_own[rows, :].astype(F32) + branch_s[rows, :].astype(F32)
        out_ref[rows, :] = (middle_s[rows, :] + branch).astype(BF16)
        return carried

    lax.fori_loop(0, z_.rows // tile, output_tile, 0)

    run("id0", "xw0", "id1", "od0", "xw1", "iw0", "od1")

    own_heads.wait()
    for j in range(1, count):
        remote(
            heads_ref.at[:, c],
            heads_s.at[from_head(j) // z_.share],
            a_send.at[j],
            a_recv.at[j],
            red.mate,
        ).wait_recv()
    load_wq.wait()

    lane = lax.broadcasted_iota(jnp.int32, (z_.rows, 2 * HD), 1) < HD
    lane_half = lax.broadcasted_iota(jnp.int32, (z_.rows // 2, 2 * HD), 1) < HD
    mid_row = z_.rows // 2

    def chunk_grads(p, carried):
        pair = [
            heads_s[2 * p + i, 0:8].reshape(z_.rows, 2 * HD).astype(F32) for i in range(2)
        ]
        query = jnp.where(lane, pair[0], pltpu.roll(pair[1], HD, 1))
        key = jnp.where(lane, pltpu.roll(pair[0], HD, 1), pair[1])
        for kind, part in ((0, query), (1, key)):
            part = part * cos_ref[...] - swap_halves(part) * sin_ref[...]
            grads_s[p, :, 2 * HD * kind : 2 * HD * (kind + 1)] = part.astype(BF16)
        value = [
            heads_s[2 * p + i, 8:12].reshape(mid_row, 2 * HD).astype(F32) for i in range(2)
        ]
        early = jnp.where(lane_half, value[0], pltpu.roll(value[1], HD, 1))
        late = jnp.where(lane_half, pltpu.roll(value[0], HD, 1), value[1])
        grads_s[p, 0:mid_row, 4 * HD : 6 * HD] = early.astype(BF16)
        grads_s[p, mid_row : z_.rows, 4 * HD : 6 * HD] = late.astype(BF16)
        return carried

    lax.fori_loop(0, z_.pairs, chunk_grads, 0)

    gain_acc[...] = jnp.zeros(gain_acc.shape, F32)

    def back_tile(i, carried):
        rows = pl.ds(pl.multiple_of(i * tile, tile), tile)
        normed, nothing = normalize(tok_ref[rows, :].astype(F32))
        for g in range(z_.fsdp):
            columns = slice(g * z_.shard, (g + 1) * z_.shard)
            total = jnp.zeros((tile, z_.shard), F32)
            for p in range(z_.pairs):
                total = total + lax.dot_general(
                    grads_s[p, rows, :],
                    wq_s[p, g],
                    (((1,), (1,)), ((), ())),
                    preferred_element_type=F32,
                )
            back_s[rows, columns] = total.astype(BF16)
            gain_acc[0:1, columns] += jnp.sum(total * normed[:, columns], axis=0, keepdims=True)
        return carried

    for r in range(2):
        tiles = z_.rows // tile
        lax.fori_loop(r * tiles // 2, (r + 1) * tiles // 2, back_tile, 0)
        back_copy(r).start()
    top = lax.broadcasted_iota(jnp.int32, (16, z_.shard), 0) == 0
    for g in range(z_.fsdp):
        columns = slice(g * z_.shard, (g + 1) * z_.shard)
        for side, row in ((0, gain_acc[0:1, columns]), (1, gain2_ref[0:1, columns])):
            g_gain[g, side] = jnp.where(top, row, 0.0).astype(BF16)

    def gain_copy():
        return remote(g_gain.at[:, 0], gain_in, y_send.at[1], y_recv.at[1], other)

    gain_copy().start()
    run("xw2", "iw1", "ow0")
    half = z_.shard // 2

    def qkv_pair(p):
        for g in range(z_.fsdp):
            for side in range(2):
                grad = jnp.dot(
                    entry_s[g, side * half : (side + 1) * half, :],
                    grads_s[p],
                    preferred_element_type=F32,
                )
                g_qkv[g, side, p * half : (p + 1) * half, :] = grad.astype(BF16)

    for p in range(z_.pairs):
        qkv_pair(p)
        red.core_start(qkv, p)
    run("xw3", "iw2", "ow1", "ed0")
    for p in range(z_.pairs):
        red.core_sum(qkv, p)
    run("xa0", "iw3", "ow2", "ed1", "ud0", "xq0", "ia0", "ow3", "ew0", "ud1")
    gain_copy().wait()
    for g in range(z_.fsdp):
        g_gain[g, 0] = (g_gain[g, 0].astype(F32) + gain_in[g].astype(F32)).astype(BF16)
    red.core_start(gain, 0)
    run("xq1", "iq0", "oa0", "ew1", "uw0")
    red.core_sum(gain, 0)
    run("xq2", "iq1", "oq0", "ew2", "uw1", "xg0", "xq3", "iq2", "oq1", "ew3", "uw2", "ig0", "iq3")
    run("oq2", "og0", "oq3", "ea0", "uw3", "eq0", "ua0")

    for r in range(2):
        back_copy(r).wait_recv()
    load_mgrad.wait()

    def input_tile(i, carried):
        rows = pl.ds(pl.multiple_of(i * tile, tile), tile)
        normed, scaling = normalize(tok_ref[rows, :].astype(F32))
        back = back_s[rows, :].astype(F32) + back_in[rows, :].astype(F32)
        gains = jnp.concatenate([gain_ref[g, 0:1, :] for g in range(z_.fsdp)], axis=1)
        igrad_ref[rows, :] = (
            mgrad_s[rows, :] + norm_back(back * gains, normed, scaling)
        ).astype(BF16)
        return carried

    lax.fori_loop(0, z_.rows // tile, input_tile, 0)
    run("eq1", "uq0", "eq2", "uq1", "eg0", "uq2", "eq3", "ug0", "uq3")

    own_sends = [heads_copy(j) for j in range(1, count)] + [branch_copy(), back_copy(0), back_copy(1)]
    for copy in own_sends:
        copy.wait_send()
    red.settle()
    finish.settle()


def reduce_all(
    z_,
    tokens,
    gains,
    cosine,
    sines,
    branch,
    middle,
    middle_grad,
    gain2,
    heads,
    wq,
    g_down,
    g_wide,
    g_attn,
):
    items = (
        Item(0, z_.units // 2, z_.shard, 2),
        Item(1, z_.units, z_.shard, 4),
        Item(2, z_.head_width // 2, z_.shard, 1),
        Item(3, z_.pairs * (z_.shard // 2), 6 * HD, z_.pairs),
        Item(4, 16, z_.shard, 1),
    )
    dma = pltpu.SemaphoreType.DMA
    peers = max(1, z_.fsdp - 1)
    pieces = sum(len(item.cuts) for item in items)
    groups = []
    for item in items:
        groups += [
            pltpu.VMEM((z_.fsdp, item.rows, item.columns), BF16),
            pltpu.VMEM((z_.fsdp, item.rows, item.columns), BF16),
            pltpu.VMEM((peers, item.rows, item.columns), BF16),
            pltpu.VMEM((item.rows, item.columns), BF16),
            pltpu.VMEM((item.rows, item.columns), BF16),
            pltpu.VMEM((item.rows, item.columns), BF16),
        ]
    count = z_.ctx // z_.share
    rows = (z_.rows, z_.width)
    return pl.pallas_call(
        functools.partial(reduce_kernel, z_, items),
        out_shape=tuple(
            [jax.ShapeDtypeStruct(rows, BF16)] * 2
            + [
                jax.ShapeDtypeStruct(shape, BF16)
                for shape in (
                    (z_.units, z_.shard),
                    (2, z_.units, z_.shard),
                    (z_.head_width, z_.shard),
                    (3, z_.shard, z_.head_width),
                    (2, 16, z_.shard),
                )
            ]
        ),
        in_specs=[vmem()] * 4
        + [anywhere()] * 3
        + [vmem()]
        + [anywhere()] * 5,
        out_specs=tuple([vmem()] * 2 + [anywhere()] * 5),
        scratch_shapes=[
            pltpu.VMEM((z_.heads, 12, z_.block, 2 * HD), BF16),
            pltpu.VMEM((z_.pairs, z_.fsdp, z_.shard, 6 * HD), BF16),
            pltpu.VMEM((z_.fsdp, z_.shard, z_.rows), BF16),
            pltpu.VMEM((z_.pairs, z_.rows, 6 * HD), BF16),
            pltpu.VMEM(rows, BF16),
            pltpu.VMEM(rows, BF16),
            pltpu.VMEM(rows, BF16),
            pltpu.VMEM(rows, BF16),
            pltpu.VMEM(rows, F32),
            pltpu.VMEM(rows, F32),
            pltpu.VMEM((z_.fsdp, 2, items[3].rows, items[3].columns), BF16),
            pltpu.VMEM((z_.fsdp, 2, 16, z_.shard), BF16),
            pltpu.VMEM((z_.fsdp, 16, z_.shard), BF16),
            pltpu.VMEM((8, z_.width), F32),
        ]
        + groups
        + [dma((count,)), dma((count,)), dma((4,)), dma((4,)), dma((5,)), dma((2, pieces, 3))]
        + [
            dma((pieces, peers)),
            dma((pieces, peers)),
        ]
        + [dma((pieces,))] * 9,
        compiler_params=pltpu.CompilerParams(
            collective_id=1, has_side_effects=True, vmem_limit_bytes=REDUCE_BYTES
        ),
        name="reduce",
    )(
        tokens,
        gains,
        cosine,
        sines,
        branch,
        middle,
        middle_grad,
        gain2,
        heads,
        wq,
        g_down,
        g_wide,
        g_attn,
    )


def adam_step(weight, gradient, moment, squared, rate_now):
    first = BETA_FIRST * moment + (1.0 - BETA_FIRST) * gradient
    second = BETA_SECOND * squared + (1.0 - BETA_SECOND) * gradient * gradient
    corrected = first / (1.0 - BETA_FIRST**STEP)
    spread = jnp.sqrt(second / (1.0 - BETA_SECOND**STEP))
    return (weight - rate_now * (corrected / (spread + ADAM_EPS) + DECAY * weight), first, second)


def on_device(
    tokens,
    cotangent,
    lengths,
    order,
    qkv_weight,
    attn_weight,
    wide_weight,
    down_weight,
    norm_gains,
    qkv_mean,
    attn_mean,
    wide_mean,
    down_mean,
    gains_mean,
    qkv_square,
    attn_square,
    wide_square,
    down_square,
    gains_square,
):
    z_ = Sizes(
        lax.axis_size("fsdp"),
        lax.axis_size("ctx"),
        tokens.shape[0],
        tokens.shape[1],
        qkv_weight.shape[2],
        wide_weight.shape[2],
    )
    ctx_index = lax.axis_index("ctx")
    in_order, endings = sequence_ends(lengths[0], order[0])
    local_ids = jnp.arange(z_.rows, dtype=jnp.int32)
    cosine, sines = rope_tables(
        positions(in_order, endings, packed_place(local_ids, ctx_index, z_.ctx, z_.block))
    )
    packed, wq_full, wo_full, wi_full, gains_full = project(
        z_,
        tokens,
        norm_gains,
        cosine,
        sines,
        qkv_weight.transpose(1, 0, 2),
        attn_weight,
        wide_weight.transpose(1, 2, 0),
    )
    attended_packed, attended_turned, lse, swapped, query, key, value = attend(
        z_, lengths, order, packed
    )
    branch_low, middle, middle_grad, gain_second, grads_packed, down_grad, wide_grad, attn_grad = (
        middle_part(
            z_,
            tokens,
            cotangent,
            gains_full,
            attended_packed,
            wo_full,
            wi_full,
            wide_weight.transpose(1, 2, 0),
            down_weight,
        )
    )
    head_grads = attend_back(
        z_, lengths, order, lse, grads_packed, attended_turned, swapped, query, key, value
    )
    output, input_grad, down_sum, wide_sum, attn_sum, qkv_sum, gain_sum = reduce_all(
        z_,
        tokens,
        gains_full,
        cosine,
        sines,
        branch_low,
        middle,
        middle_grad,
        gain_second,
        head_grads,
        wq_full,
        down_grad,
        wide_grad,
        attn_grad,
    )
    updated = []
    for weight, gradient, moment, squared, rate_now in (
        (qkv_weight, qkv_sum.transpose(1, 0, 2), qkv_mean, qkv_square, D ** (-0.5)),
        (attn_weight, attn_sum, attn_mean, attn_square, RATE_ATTN),
        (wide_weight, wide_sum.transpose(2, 0, 1), wide_mean, wide_square, D ** (-0.5)),
        (down_weight, down_sum, down_mean, down_square, FF ** (-0.5)),
        (norm_gains, gain_sum[:, 0, :], gains_mean, gains_square, RATE_GAIN),
    ):
        updated += adam_step(weight, gradient.astype(F32), moment, squared, rate_now)
    return (output, input_grad, *updated)


def solution(mesh):
    return jax.shard_map(
        on_device,
        mesh=mesh,
        in_specs=(
            P(("fsdp", "ctx"), None),
            P(("fsdp", "ctx"), None),
            P("fsdp", None),
            P("fsdp", None),
            P("fsdp", None, "tp"),
            P("tp", "fsdp"),
            P("fsdp", None, "tp"),
            P("tp", "fsdp"),
            P(None, "fsdp"),
            P("fsdp", None, "tp"),
            P("tp", "fsdp"),
            P("fsdp", None, "tp"),
            P("tp", "fsdp"),
            P(None, "fsdp"),
            P("fsdp", None, "tp"),
            P("tp", "fsdp"),
            P("fsdp", None, "tp"),
            P("tp", "fsdp"),
            P(None, "fsdp"),
        ),
        out_specs=(
            P(("fsdp", "ctx"), None),
            P(("fsdp", "ctx"), None),
            P("fsdp", None, "tp"),
            P("fsdp", None, "tp"),
            P("fsdp", None, "tp"),
            P("tp", "fsdp"),
            P("tp", "fsdp"),
            P("tp", "fsdp"),
            P("fsdp", None, "tp"),
            P("fsdp", None, "tp"),
            P("fsdp", None, "tp"),
            P("tp", "fsdp"),
            P("tp", "fsdp"),
            P("tp", "fsdp"),
            P(None, "fsdp"),
            P(None, "fsdp"),
            P(None, "fsdp"),
        ),
        check_vma=False,
    )
```

```python
import functools

import jax
import jax.numpy as jnp
from jax import lax
from jax.experimental import pallas as pl
from jax.experimental.pallas import tpu as pltpu
from jax.sharding import PartitionSpec as P

D = 1024
HD = 64
FF = 2624
STEP = 10


NORM_EPS = 1e-05
ROPE_BASE = 160000.0
BETA_FIRST = 0.9
BETA_SECOND = 0.98
ADAM_EPS = 1e-06
DECAY = 0.01
RATE_ATTN = 0.5
RATE_GAIN = 0.8
MASKED = -1e30

MESH = pl.DeviceIdType.MESH
BF16 = jnp.bfloat16
F32 = jnp.float32
VMEM_BYTES = 62 * 2**20
REDUCE_BYTES = 62 * 2**20


class Sizes:
    def __init__(self, fsdp, ctx, rows, width, head_width, units):
        self.fsdp = fsdp
        self.ctx = ctx
        self.chips = ctx // 2
        self.rows = rows
        self.block = rows // 8
        self.group = rows * ctx
        self.width = width
        self.shard = width // fsdp
        self.heads = head_width // HD
        self.head_width = head_width
        self.units = units
        self.units_first = 16 * (units // 16 * 5 // 8)
        self.share = max(1, ctx // self.heads)
        self.pairs = self.heads // 2
        self.ranks = ctx // self.pairs


def remote(src, dst, send, recv, device):
    return pltpu.make_async_remote_copy(
        src_ref=src,
        dst_ref=dst,
        send_sem=send,
        recv_sem=recv,
        device_id=device,
        device_id_type=MESH,
    )


def greet(devices):
    barrier = pltpu.get_barrier_semaphore()
    for device in devices:
        pl.semaphore_signal(barrier, inc=1, device_id=device, device_id_type=MESH)
    pl.semaphore_wait(barrier, len(devices))


def vmem():
    return pl.BlockSpec(memory_space=pltpu.VMEM)


def anywhere():
    return pl.BlockSpec(memory_space=pl.ANY)


def normalize(values):
    centered = values - jnp.mean(values, axis=1, keepdims=True)
    scaling = lax.rsqrt(jnp.mean(centered * centered, axis=1, keepdims=True) + NORM_EPS)
    return (centered * scaling, scaling)


def norm_back(grad_hat, normed, scaling):
    return scaling * (
        grad_hat
        - jnp.mean(grad_hat, axis=1, keepdims=True)
        - normed * jnp.mean(grad_hat * normed, axis=1, keepdims=True)
    )


def swap_halves(values):
    lane = lax.broadcasted_iota(jnp.int32, values.shape, 1)
    return jnp.where(
        lane % HD < HD // 2, pltpu.roll(values, 2 * HD - HD // 2, 1), pltpu.roll(values, HD // 2, 1)
    )


def packed_place(local_row, device, devices, block_size):
    return (local_row // block_size * devices + device) * block_size + local_row % block_size


def sequence_ends(lengths_row, order_row):
    count_seqs = lengths_row.shape[0]
    chosen = (order_row[:, None] == jnp.arange(count_seqs, dtype=jnp.int32)[None, :]).astype(
        jnp.int32
    )
    in_order = jnp.sum(chosen * lengths_row[None, :], axis=1)
    return (in_order, jnp.cumsum(in_order))


def positions(in_order, endings, places):
    passed = (endings[None, :] <= places[:, None]).astype(jnp.int32)
    return places - jnp.sum(passed * in_order[None, :], axis=1)


def rope_tables(position):
    half_size = HD // 2
    lane = jnp.arange(2 * HD, dtype=jnp.int32)
    index = (lane % half_size).astype(jnp.float32)
    frequency = ROPE_BASE ** (-(2.0 * index) / (2.0 * half_size))
    angles = position.astype(jnp.float32)[:, None] * frequency[None, :]
    sign = jnp.where(lane % HD < half_size, -1.0, 1.0)
    return (jnp.cos(angles), jnp.sin(angles) * sign[None, :])


def cuts_of(rows, count):
    unit = rows // 16
    marks = [16 * (unit * i // count) for i in range(count + 1)]
    return [(a, b - a) for a, b in zip(marks, marks[1:]) if b > a]


def over_rows(start, rows, step, body):
    whole = rows // step

    def turn(i, carried):
        body(pl.multiple_of(start + i * step, 16), step)
        return carried

    if whole > 1:
        lax.fori_loop(0, whole, turn, 0)
    elif whole == 1:
        body(start, step)
    if rows % step:
        body(start + whole * step, rows % step)


def project_kernel(
    z_,
    tok_ref,
    gain_ref,
    cos_ref,
    sin_ref,
    wq_ref,
    wo_ref,
    wi_ref,
    packed_ref,
    wq_out,
    wo_out,
    wi_out,
    gain_out,
    entry_s,
    wq_f,
    wo_f,
    wi_f,
    wq_s,
    wo_s,
    wi_s,
    send_s,
    gain_s,
    gain_send,
    gain_recv,
    wq_send,
    wq_recv,
    wq_fsend,
    wq_frecv,
    w_send,
    w_recv,
    w_fsend,
    w_frecv,
    a_send,
    a_recv,
    local_sem,
):
    f, c, t = lax.axis_index("fsdp"), lax.axis_index("ctx"), lax.axis_index("tp")
    core = lax.rem(c, 2)
    mate = (f, c + 1 - 2 * core, t)
    others = range(1, z_.fsdp)
    mine = c // z_.ranks
    place_in = lax.rem(c, z_.ranks)
    last = z_.pairs - 1
    unit_half = z_.units_first

    def ahead(k):
        return lax.rem(f + k, z_.fsdp)

    def behind(k):
        return lax.rem(f + z_.fsdp - k, z_.fsdp)

    def pair_of(s):
        return lax.rem(mine + 1 + s, z_.pairs)

    load_wq = pltpu.make_async_copy(wq_ref, wq_f, local_sem.at[0])
    load_wo = pltpu.make_async_copy(wo_ref, wo_f, local_sem.at[1])
    load_wi = pltpu.make_async_copy(wi_ref.at[:, 0:unit_half], wi_f, local_sem.at[2])
    load_wq.start()
    load_wo.start()
    load_wi.start()
    greet(
        [(ahead(k), c, t) for k in others]
        + [(f, lax.rem(c + j, z_.ctx), t) for j in range(1, z_.ctx)]
    )

    half = z_.shard // 2
    own_half = pl.ds(pl.multiple_of(core * half, half), half)
    mate_half = pl.ds(pl.multiple_of((1 - core) * half, half), half)

    def gain_copy(k, owner):
        return remote(
            gain_s.at[f], gain_s.at[owner], gain_send.at[k - 1], gain_recv.at[k - 1], (ahead(k), c, t)
        )

    def wq_copy(s, k, owner):
        place = wq_s.at[pair_of(s), owner, own_half]
        return remote(
            place, place, wq_send.at[s, k - 1], wq_recv.at[s, k - 1], (ahead(k), c, t)
        )

    def wq_pass(s, k, rows):
        place = wq_s.at[pair_of(s), behind(k), rows]
        return remote(place, place, wq_fsend.at[s, k - 1], wq_frecv.at[s, k - 1], mate)

    attn_half = z_.head_width // 2

    def weight_places(side, owner):
        rows = pl.ds(pl.multiple_of(side * attn_half, attn_half), attn_half)
        return (
            (wo_s.at[rows], wo_out.at[owner, rows]),
            (wi_s.at[side], wi_out.at[side, owner]),
        )

    pieces = 2

    def w_copy(n, k, owner):
        source, place = weight_places(core, owner)[n]
        return remote(source, place, w_send.at[n, k - 1], w_recv.at[n, k - 1], (ahead(k), c, t))

    def w_pass(n, k, side):
        place = weight_places(side, behind(k))[n][1]
        return remote(place, place, w_fsend.at[n, k - 1], w_frecv.at[n, k - 1], mate)

    def head_copy(s, i):
        return remote(
            send_s.at[s, i // z_.share],
            packed_ref.at[:, c],
            a_send.at[s, i],
            a_recv.at[s, place_in],
            (f, pair_of(s) * z_.ranks + i, t),
        )

    def head_arrival(s, i):
        source = lax.rem(mine + 2 * z_.pairs - 1 - s, z_.pairs) * z_.ranks + i
        return remote(
            send_s.at[s, 0], packed_ref.at[:, source], a_send.at[s, 0], a_recv.at[s, i], mate
        )

    def near_copy(j):
        i = lax.rem(place_in + j, z_.ranks)
        return remote(
            send_s.at[last, i // z_.share],
            packed_ref.at[:, c],
            a_send.at[last, j],
            a_recv.at[last, j],
            (f, mine * z_.ranks + i, t),
        )

    def near_arrival(j):
        source = mine * z_.ranks + lax.rem(place_in + z_.ranks - j, z_.ranks)
        return remote(
            send_s.at[last, 0], packed_ref.at[:, source], a_send.at[last, j], a_recv.at[last, j], mate
        )

    gain_s[f] = jnp.zeros((8, z_.shard), F32)
    gain_s[f, 0:2, :] = gain_ref[...].astype(BF16).astype(F32)
    for k in others:
        gain_copy(k, f).start()
    load_wq.wait()

    def round_pair(s):
        p = pair_of(s)
        columns = pl.ds(pl.multiple_of(p * 2 * HD, 2 * HD), 2 * HD)
        for kind in range(3):
            wq_s[p, f, :, kind * 2 * HD : (kind + 1) * 2 * HD] = wq_f[kind, :, columns].astype(BF16)

    for s in range(2):
        round_pair(s)
        for k in others:
            wq_copy(s, k, f).start()
    for k in others:
        gain_copy(k, behind(k)).wait()

    gain_out[...] = gain_s[...]
    tile = min(128, z_.rows)

    def norm_tile(i, carried):
        rows = pl.ds(pl.multiple_of(i * tile, tile), tile)
        normed, nothing = normalize(tok_ref[rows, :].astype(F32))
        for g in range(z_.fsdp):
            columns = slice(g * z_.shard, (g + 1) * z_.shard)
            entry_s[g, rows, :] = (normed[:, columns] * gain_s[g, 0:1, :]).astype(BF16)
        return carried

    lax.fori_loop(0, z_.rows // tile, norm_tile, 0)
    load_wo.wait()
    wo_s[...] = wo_f[...].astype(BF16)
    own_wo = pltpu.make_async_copy(wo_s, wo_out.at[f], local_sem.at[1])
    own_wo.start()
    load_wi.wait()
    own_wi = pltpu.make_async_copy(wi_s, wi_out.at[:, f], local_sem.at[2])

    def round_wide(side):
        def turn(first, rows):
            place = pl.ds(first, rows)
            wi_s[side, place, :] = wi_f[side, place, :].astype(BF16)

        over_rows(0, unit_half, 128, turn)

    lane = lax.broadcasted_iota(jnp.int32, (z_.rows, 2 * HD), 1) < HD
    lane_half = lax.broadcasted_iota(jnp.int32, (z_.rows // 2, 2 * HD), 1) < HD

    def chunk_step(s, carried):
        @pl.when(s + 2 < z_.pairs)
        def more():
            round_pair(s + 2)
            for k in others:
                wq_copy(s + 2, k, f).start()

        @pl.when(s + 2 == z_.pairs)
        def attn_part():
            for k in others:
                w_copy(0, k, f).start()
            round_wide(core)

        @pl.when(s + 1 == z_.pairs)
        def wide_part():
            for k in others:
                w_copy(1, k, f).start()

        for k in others:
            wq_copy(s, k, behind(k)).wait_recv()
            wq_pass(s, k, own_half).start()
        for k in others:
            wq_pass(s, k, mate_half).wait_recv()
        p = pair_of(s)
        total = jnp.zeros((z_.rows, 6 * HD), F32)
        for g in range(z_.fsdp):
            total = total + jnp.dot(entry_s[g], wq_s[p, g], preferred_element_type=F32)
        turned = []
        for kind in range(2):
            part = total[:, kind * 2 * HD : (kind + 1) * 2 * HD]
            turned.append(part * cos_ref[...] + swap_halves(part) * sin_ref[...])
        query, key = turned
        value = total[:, 4 * HD : 6 * HD]
        early, late = value[: z_.rows // 2], value[z_.rows // 2 :]
        both = (
            (
                jnp.where(lane, query, pltpu.roll(key, HD, 1)),
                jnp.where(lane_half, early, pltpu.roll(late, HD, 1)),
            ),
            (
                jnp.where(lane, pltpu.roll(query, HD, 1), key),
                jnp.where(lane_half, pltpu.roll(early, HD, 1), late),
            ),
        )
        for i in range(2):
            send_s[s, i, 0:8] = both[i][0].astype(BF16).reshape(8, z_.block, 2 * HD)
            send_s[s, i, 8:12] = both[i][1].astype(BF16).reshape(4, z_.block, 2 * HD)

        @pl.when(s < last)
        def away():
            for i in range(z_.ranks):
                head_copy(s, i).start()

        return carried

    lax.fori_loop(0, z_.pairs, chunk_step, 0)
    kept = pltpu.make_async_copy(
        send_s.at[last, place_in // z_.share], packed_ref.at[:, c], local_sem.at[3]
    )
    kept.start()
    for j in range(1, z_.ranks):
        near_copy(j).start()
    keep_wq = pltpu.make_async_copy(wq_s, wq_out, local_sem.at[4])
    keep_wq.start()
    round_wide(1 - core)
    own_wi.start()
    for n in range(pieces):
        for k in others:
            w_copy(n, k, behind(k)).wait_recv()
            w_pass(n, k, core).start()
    for s in range(last):
        for i in range(z_.ranks):
            head_arrival(s, i).wait_recv()
            head_copy(s, i).wait_send()
    for j in range(1, z_.ranks):
        near_arrival(j).wait_recv()
        near_copy(j).wait_send()
    for k in others:
        for s in range(z_.pairs):
            wq_copy(s, k, f).wait_send()
            wq_pass(s, k, own_half).wait_send()
        for n in range(pieces):
            w_copy(n, k, f).wait_send()
            w_pass(n, k, core).wait_send()
            w_pass(n, k, 1 - core).wait_recv()
    kept.wait()
    keep_wq.wait()
    own_wo.wait()
    own_wi.wait()


def project(z_, tokens, gains, cosine, sines, wq, wo, wi):
    peers = max(1, z_.fsdp - 1)
    dma = pltpu.SemaphoreType.DMA
    return pl.pallas_call(
        functools.partial(project_kernel, z_),
        out_shape=(
            jax.ShapeDtypeStruct((12, z_.ctx, z_.block, 2 * HD), BF16),
            jax.ShapeDtypeStruct((z_.pairs, z_.fsdp, z_.shard, 6 * HD), BF16),
            jax.ShapeDtypeStruct((z_.fsdp, z_.head_width, z_.shard), BF16),
            jax.ShapeDtypeStruct((2, z_.fsdp, z_.units_first, z_.shard), BF16),
            jax.ShapeDtypeStruct((z_.fsdp, 8, z_.shard), F32),
        ),
        in_specs=[vmem()] * 4 + [anywhere()] * 3,
        out_specs=(anywhere(), anywhere(), anywhere(), anywhere(), vmem()),
        scratch_shapes=[
            pltpu.VMEM((z_.fsdp, z_.rows, z_.shard), BF16),
            pltpu.VMEM((3, z_.shard, z_.head_width), F32),
            pltpu.VMEM((z_.head_width, z_.shard), F32),
            pltpu.VMEM((2, z_.units_first, z_.shard), F32),
            pltpu.VMEM((z_.pairs, z_.fsdp, z_.shard, 6 * HD), BF16),
            pltpu.VMEM((z_.head_width, z_.shard), BF16),
            pltpu.VMEM((2, z_.units_first, z_.shard), BF16),
            pltpu.VMEM((z_.pairs, 2, 12, z_.block, 2 * HD), BF16),
            pltpu.VMEM((z_.fsdp, 8, z_.shard), F32),
            dma((peers,)),
            dma((peers,)),
            dma((z_.pairs, peers)),
            dma((z_.pairs, peers)),
            dma((z_.pairs, peers)),
            dma((z_.pairs, peers)),
            dma((2, peers)),
            dma((2, peers)),
            dma((2, peers)),
            dma((2, peers)),
            dma((z_.pairs, z_.ranks)),
            dma((z_.pairs, z_.ranks)),
            dma((5,)),
        ],
        compiler_params=pltpu.CompilerParams(
            collective_id=0, has_side_effects=True, vmem_limit_bytes=VMEM_BYTES
        ),
        name="project",
    )(tokens, gains, cosine, sines, wq, wo, wi)


def packing(lengths_ref, order_ref):
    count = order_ref.shape[1]
    lengths = [lengths_ref[0, order_ref[0, k]] for k in range(count)]
    longest, start, chosen = lengths[0], jnp.int32(0), jnp.int32(0)
    passed = lengths[0]
    for k in range(1, count):
        more = lengths[k] > longest
        longest = jnp.where(more, lengths[k], longest)
        start = jnp.where(more, passed, start)
        chosen = jnp.where(more, k, chosen)
        passed = passed + lengths[k]
    ends, total = [], jnp.int32(0)
    for j in range(count):
        length = lengths[j]
        for first in range(1, count):
            length = jnp.where(chosen == first, lengths[(first + j) % count], length)
        total = total + length
        ends.append(total)
    return (start, ends)


def sequence_at(ends, place):
    start, end = jnp.int32(0), ends[0]
    for k in range(len(ends) - 1):
        past = ends[k] <= place
        start = jnp.where(past, ends[k], start)
        end = jnp.where(past, ends[k + 1], end)
    return (start, end)


def segments_of(ends, places):
    segment = jnp.zeros(places.shape, jnp.int32)
    for end in ends:
        segment = segment + (end <= places).astype(jnp.int32)
    return segment


def turned_rows(stage, start, group, rows):
    return stage[pl.ds(lax.rem(start, group), rows), :]


def attend_kernel(
    z_,
    q_tile,
    k_tile,
    lengths_ref,
    order_ref,
    packed_ref,
    out_ref,
    outt_ref,
    lse_ref,
    swapped_ref,
    query_ref,
    key_ref,
    value_ref,
    value_s,
    top_s,
    total_s,
    stage_s,
):
    group = z_.group
    half = group // 2
    piece = min(512, half)
    scaling = HD ** (-0.5)
    sums = 16
    shift, ends = packing(lengths_ref, order_ref)
    packed_ref = packed_ref.reshape(group + half, 2 * HD)
    out_ref = out_ref.reshape(half, 2 * HD)
    query_ref[HD : 2 * HD, :] = jnp.zeros((HD, group), BF16)
    value_s[HD : HD + sums, :] = jnp.ones((sums, group), BF16)
    lane = lax.broadcasted_iota(jnp.int32, (piece, 2 * HD), 1) < HD

    def place(i, offset=0):
        return pl.ds(pl.multiple_of(offset + i * piece, piece), piece)

    def stage_pairs(i, carried):
        stage_s[place(i), :] = packed_ref[place(i), :].astype(F32)
        return carried

    lax.fori_loop(0, group // piece, stage_pairs, 0)
    stage_s[group : group + piece, :] = stage_s[0:piece, :]

    def pairs(i, carried):
        pair = turned_rows(stage_s, shift + i * piece, group, piece)
        swapped_ref[place(i), :] = pltpu.roll(pair, HD, 1).astype(BF16)
        turned = pair.astype(BF16).T
        query_ref[0:HD, place(i)] = (turned[0:HD].astype(F32) * scaling).astype(BF16)
        key_ref[:, place(i)] = turned[HD : 2 * HD]
        return carried

    lax.fori_loop(0, group // piece, pairs, 0)

    def stage_values(i, carried):
        both = packed_ref[place(i, group), :].astype(F32)
        stage_s[place(i), :] = both
        stage_s[place(i, half), :] = pltpu.roll(both, HD, 1)
        return carried

    lax.fori_loop(0, half // piece, stage_values, 0)
    stage_s[group : group + piece, :] = stage_s[0:piece, :]

    def values(i, carried):
        value = turned_rows(stage_s, shift + i * piece, group, piece)
        low = jnp.where(lane, value, 0.0).astype(BF16)
        value_ref[place(i), :] = low
        value_s[0:HD, place(i)] = low.T[0:HD]
        return carried

    lax.fori_loop(0, group // piece, values, 0)

    def one_tile(i, carried):
        first = pl.multiple_of(i * q_tile, q_tile)
        columns = pl.ds(first, q_tile)
        low, low_end = sequence_at(ends, first)
        high_start, high = sequence_at(ends, first + q_tile - 1)
        single = low == high_start
        top_s[...] = jnp.full(top_s.shape, MASKED, F32)
        total_s[...] = jnp.zeros(total_s.shape, F32)

        def one_step(j, masked):
            start = pl.multiple_of(j * k_tile, k_tile)
            rows = pl.ds(start, k_tile)
            scores = jnp.dot(swapped_ref[rows, :], query_ref[:, columns], preferred_element_type=F32)
            if masked:
                key_seg = segments_of(
                    ends, start + lax.broadcasted_iota(jnp.int32, (k_tile, 1), 0)
                )
                query_seg = segments_of(
                    ends, first + lax.broadcasted_iota(jnp.int32, (1, q_tile), 1)
                )
                scores = jnp.where(key_seg == query_seg, scores, MASKED)
            before = top_s[0:1, :]
            after = jnp.maximum(before, jnp.max(scores, axis=0, keepdims=True))
            weights = jnp.exp(scores - after).astype(BF16)
            top_s[0:1, :] = after
            total_s[...] = total_s[...] * jnp.exp(before - after) + jnp.dot(
                value_s[:, rows], weights, preferred_element_type=F32
            )

        def step(j, inner):
            start = j * k_tile
            whole = single & (start >= low) & (start + k_tile <= high)

            @pl.when(whole)
            def plain():
                one_step(j, False)

            @pl.when(jnp.logical_not(whole))
            def partial():
                one_step(j, True)

            return inner

        lax.fori_loop(low // k_tile, (high + k_tile - 1) // k_tile, step, 0)
        summed = total_s[HD : HD + 1, :]
        lse_ref[:, columns] = jnp.broadcast_to(top_s[0:1, :] + jnp.log(summed), (8, q_tile))
        outt_ref[:, columns] = total_s[0:HD, :] / summed
        return carried

    lax.fori_loop(0, group // q_tile, one_tile, 0)

    def stage_out(i, carried):
        both = jnp.concatenate([outt_ref[:, place(i)], jnp.zeros((HD, piece), F32)], axis=0)
        stage_s[place(i), :] = both.astype(BF16).T.astype(F32)
        return carried

    lax.fori_loop(0, group // piece, stage_out, 0)
    stage_s[group : group + piece, :] = stage_s[0:piece, :]

    def finish(i, carried):
        early = turned_rows(stage_s, group - shift + i * piece, group, piece)
        late = turned_rows(stage_s, group + half - shift + i * piece, group, piece)
        out_ref[place(i), :] = jnp.where(lane, early, pltpu.roll(late, HD, 1)).astype(BF16)
        return carried

    lax.fori_loop(0, half // piece, finish, 0)


def attend(z_, lengths, order, packed):
    group = z_.group
    half = group // 2
    q_tile, k_tile = min(1024, half), min(1024, half)
    scalars = pl.BlockSpec(memory_space=pltpu.SMEM)
    return pl.pallas_call(
        functools.partial(attend_kernel, z_, q_tile, k_tile),
        out_shape=(
            jax.ShapeDtypeStruct((4, z_.ctx, z_.block, 2 * HD), BF16),
            jax.ShapeDtypeStruct((HD, group), F32),
            jax.ShapeDtypeStruct((8, group), F32),
            jax.ShapeDtypeStruct((group, 2 * HD), BF16),
            jax.ShapeDtypeStruct((2 * HD, group), BF16),
            jax.ShapeDtypeStruct((HD, group), BF16),
            jax.ShapeDtypeStruct((group, 2 * HD), BF16),
        ),
        in_specs=[scalars, scalars, vmem()],
        out_specs=tuple([vmem()] * 7),
        scratch_shapes=[
            pltpu.VMEM((HD + 16, group), BF16),
            pltpu.VMEM((8, q_tile), F32),
            pltpu.VMEM((HD + 16, q_tile), F32),
            pltpu.VMEM((group + min(512, half), 2 * HD), F32),
        ],
        compiler_params=pltpu.CompilerParams(vmem_limit_bytes=VMEM_BYTES),
        name="attend",
    )(lengths, order, packed)


def attend_back_kernel(
    z_,
    lengths_ref,
    order_ref,
    lse_ref,
    packed_grad,
    outt_ref,
    swapped_ref,
    query_ref,
    key_ref,
    value_ref,
    out_ref,
    turned_s,
    grad_s,
    delta_s,
    stage_s,
    dquery_s,
    dvalue_s,
    key_acc,
    value_acc,
):
    group = z_.group
    half = group // 2
    tile = min(512, half)
    scaling = HD ** (-0.5)
    shift, ends = packing(lengths_ref, order_ref)
    lane = lax.broadcasted_iota(jnp.int32, (tile, 2 * HD), 1) < HD
    flat_grad = packed_grad.reshape(half, 2 * HD)
    flat_out = out_ref.reshape(group + half, 2 * HD)

    def place(i, offset=0):
        return pl.ds(pl.multiple_of(offset + i * tile, tile), tile)

    def stage_grads(i, carried):
        both = flat_grad[place(i), :].astype(F32)
        stage_s[place(i), :] = both
        stage_s[place(i, half), :] = pltpu.roll(both, HD, 1)
        return carried

    lax.fori_loop(0, half // tile, stage_grads, 0)
    stage_s[group : group + tile, :] = stage_s[0:tile, :]

    def order_grads(i, carried):
        rows = turned_rows(stage_s, shift + i * tile, group, tile)
        low = jnp.where(lane, rows, 0.0).astype(BF16)
        grad_s[place(i), :] = low
        turned = low.T[0:HD]
        turned_s[0:HD, place(i)] = turned
        turned_s[HD : 2 * HD, place(i)] = key_ref[:, place(i)]
        delta = jnp.sum(turned.astype(F32) * outt_ref[:, place(i)], axis=0, keepdims=True)
        delta_s[:, place(i)] = jnp.broadcast_to(delta, (8, tile))
        dquery_s[:, place(i)] = jnp.zeros((HD, tile), F32)
        return carried

    lax.fori_loop(0, group // tile, order_grads, 0)

    def one_step(rows, start, first, masked):
        columns = pl.ds(first, tile)
        scores = jnp.dot(swapped_ref[rows, :], query_ref[:, columns], preferred_element_type=F32)
        chances = jnp.exp(scores - lse_ref[0:1, columns])
        if masked:
            key_seg = segments_of(ends, start + lax.broadcasted_iota(jnp.int32, (tile, 1), 0))
            query_seg = segments_of(ends, first + lax.broadcasted_iota(jnp.int32, (1, tile), 1))
            chances = jnp.where(key_seg == query_seg, chances, 0.0)
        chance_grad = jnp.dot(
            value_ref[rows, :], turned_s[:, columns], preferred_element_type=F32
        )
        score_grad = (chances * (chance_grad - delta_s[0:1, columns])).astype(BF16)
        value_acc[...] += jnp.dot(
            chances.astype(BF16), grad_s[columns, :], preferred_element_type=F32
        )
        key_acc[...] += jnp.dot(score_grad, swapped_ref[columns, :], preferred_element_type=F32)
        dquery_s[:, columns] += jnp.dot(
            turned_s[HD : 2 * HD, rows], score_grad, preferred_element_type=F32
        )

    def one_tile(j, masked):
        start = pl.multiple_of(j * tile, tile)
        rows = pl.ds(start, tile)
        key_acc[...] = jnp.zeros(key_acc.shape, F32)
        value_acc[...] = jnp.zeros(value_acc.shape, F32)
        low, high = jnp.int32(0), jnp.int32(half)
        if masked:
            low, low_end = sequence_at(ends, start)
            high_start, high = sequence_at(ends, start + tile - 1)

        def step(i, inner):
            one_step(rows, start, pl.multiple_of(i * tile, tile), masked)
            return inner

        lax.fori_loop(low // tile, (high + tile - 1) // tile, step, 0)
        dvalue_s[rows, :] = value_acc[...].astype(BF16)
        stage_s[rows, :] = key_acc[...]

    def long_tile(j, carried):
        one_tile(j, False)
        return carried

    def other_tile(j, carried):
        one_tile(j, True)
        return carried

    lax.fori_loop(0, half // tile, long_tile, 0)
    lax.fori_loop(half // tile, group // tile, other_tile, 0)

    def join_pairs(i, carried):
        turned = jnp.concatenate([dquery_s[:, place(i)], jnp.zeros((HD, tile), F32)], axis=0)
        query_rows = (turned * scaling).astype(BF16).T.astype(F32)
        stage_s[place(i), :] = jnp.where(lane, query_rows, stage_s[place(i), :] * scaling)
        return carried

    lax.fori_loop(0, group // tile, join_pairs, 0)
    stage_s[group : group + tile, :] = stage_s[0:tile, :]

    def order_pairs(i, carried):
        rows = turned_rows(stage_s, group - shift + i * tile, group, tile)
        flat_out[place(i), :] = rows.astype(BF16)
        return carried

    lax.fori_loop(0, group // tile, order_pairs, 0)

    def stage_values(i, carried):
        stage_s[place(i), :] = dvalue_s[place(i), :].astype(F32)
        return carried

    lax.fori_loop(0, group // tile, stage_values, 0)
    stage_s[group : group + tile, :] = stage_s[0:tile, :]

    def order_values(i, carried):
        early = turned_rows(stage_s, group - shift + i * tile, group, tile)
        late = turned_rows(stage_s, group + half - shift + i * tile, group, tile)
        flat_out[place(i, group), :] = jnp.where(lane, early, pltpu.roll(late, HD, 1)).astype(BF16)
        return carried

    lax.fori_loop(0, half // tile, order_values, 0)


def attend_back(z_, lengths, order, lse, grads, turned_out, swapped, query, key, value):
    group = z_.group
    tile = min(512, group // 2)
    scalars = pl.BlockSpec(memory_space=pltpu.SMEM)
    return pl.pallas_call(
        functools.partial(attend_back_kernel, z_),
        out_shape=jax.ShapeDtypeStruct((12, z_.ctx, z_.block, 2 * HD), BF16),
        in_specs=[scalars, scalars] + [vmem()] * 7,
        out_specs=vmem(),
        scratch_shapes=[
            pltpu.VMEM((2 * HD, group), BF16),
            pltpu.VMEM((group, 2 * HD), BF16),
            pltpu.VMEM((8, group), F32),
            pltpu.VMEM((group + tile, 2 * HD), F32),
            pltpu.VMEM((HD, group), F32),
            pltpu.VMEM((group, 2 * HD), BF16),
            pltpu.VMEM((tile, 2 * HD), F32),
            pltpu.VMEM((tile, 2 * HD), F32),
        ],
        compiler_params=pltpu.CompilerParams(vmem_limit_bytes=VMEM_BYTES),
        name="attend_back",
    )(lengths, order, lse, grads, turned_out, swapped, query, key, value)


def middle_kernel(
    z_,
    tok_ref,
    cot_ref,
    gain_ref,
    heads_ref,
    wo_ref,
    wi_ref,
    wide_ref,
    down_ref,
    branch_ref,
    middle_ref,
    mgrad_ref,
    gain2_ref,
    grads_ref,
    g_down,
    g_wide,
    g_attn,
    heads_s,
    wo_s,
    wi_s,
    wide_f,
    down_f,
    wm_s,
    mixed_s,
    mixed_t,
    sum_s,
    sum_in,
    back_s,
    back_in,
    entry_s,
    branch_s,
    middle_s,
    grad_f,
    normed_s,
    scale_s,
    gate_s,
    hgrad_s,
    hidden_s,
    hidden_t,
    gated_s,
    gated_t,
    mgrad_s,
    dsend_s,
    down_s,
    wide_s,
    attn_s,
    a_send,
    a_recv,
    d_send,
    d_recv,
    y_send,
    y_recv,
    w_send,
    w_recv,
    f_send,
    f_recv,
    local_sem,
):
    f, c, t = lax.axis_index("fsdp"), lax.axis_index("ctx"), lax.axis_index("tp")
    core = lax.rem(c, 2)
    mate = (f, c + 1 - 2 * core, t)
    other = (f, c, 1 - t)
    count = z_.ctx // z_.share
    others = range(1, z_.fsdp)
    half = z_.rows // 2

    def ahead(k):
        return lax.rem(f + k, z_.fsdp)

    def behind(k):
        return lax.rem(f + z_.fsdp - k, z_.fsdp)

    def to_token(j):
        return lax.rem(c + z_.share * j, z_.ctx)

    def from_head(j):
        return lax.rem(c + z_.ctx - z_.share * j, z_.ctx)

    def heads_copy(j):
        return remote(
            heads_ref.at[:, to_token(j)],
            heads_s.at[c // z_.share],
            a_send.at[j],
            a_recv.at[j],
            (f, to_token(j), t),
        )

    def heads_arrival(j):
        return remote(
            heads_ref.at[:, c],
            heads_s.at[from_head(j) // z_.share],
            a_send.at[j],
            a_recv.at[j],
            mate,
        )

    def grads_copy(j):
        rank = lax.rem(c + j, z_.ctx)
        return remote(
            dsend_s.at[rank // z_.share],
            grads_ref.at[:, c],
            d_send.at[j],
            d_recv.at[j],
            (f, rank, t),
        )

    def grads_arrival(j):
        source = lax.rem(c + z_.ctx - j, z_.ctx)
        return remote(
            dsend_s.at[0], grads_ref.at[:, source], d_send.at[j], d_recv.at[j], mate
        )

    units_half = z_.units // 2

    def weight_place(n, side, owner):
        if n == 0:
            rows = pl.ds(pl.multiple_of(side * units_half, 16), units_half)
            return wm_s.at[owner, rows]
        return wi_s.at[side, owner, z_.units_first : z_.units]

    def w_copy(n, k, owner):
        place = weight_place(n, core, owner)
        return remote(place, place, w_send.at[n, k - 1], w_recv.at[n, k - 1], (ahead(k), c, t))

    def w_pass(n, k, side):
        place = weight_place(n, side, behind(k))
        return remote(place, place, f_send.at[n, k - 1], f_recv.at[n, k - 1], mate)

    def sum_copy(r):
        rows = pl.ds(r * half, half)
        return remote(sum_s.at[rows], sum_in.at[rows], y_send.at[r], y_recv.at[r], other)

    def back_copy(r):
        rows = pl.ds(r * half, half)
        return remote(
            back_s.at[rows], back_in.at[rows], y_send.at[2 + r], y_recv.at[2 + r], other
        )

    load_wide = pltpu.make_async_copy(
        wide_ref.at[:, z_.units_first : z_.units], wide_f, local_sem.at[8]
    )
    load_wide.start()
    load_down = pltpu.make_async_copy(down_ref, down_f, local_sem.at[3])
    load_down.start()
    load_wo = pltpu.make_async_copy(wo_ref, wo_s, local_sem.at[1])
    load_wi = pltpu.make_async_copy(
        wi_ref, wi_s.at[:, :, 0 : z_.units_first], local_sem.at[2]
    )
    load_wo.start()
    load_wi.start()
    greet(
        [(ahead(k), c, t) for k in others]
        + [(f, lax.rem(c + j, z_.ctx), t) for j in range(1, z_.ctx)]
        + [other]
    )
    for j in range(1, count):
        heads_copy(j).start()
    own_heads = pltpu.make_async_copy(
        heads_ref.at[:, c], heads_s.at[c // z_.share], local_sem.at[0]
    )
    own_heads.start()
    load_wide.wait()
    for side in range(2):

        def round_wide(first, rows, side=side):
            wi_s[side, f, pl.ds(z_.units_first + first, rows), :] = wide_f[
                side, pl.ds(first, rows), :
            ].astype(BF16)

        over_rows(0, z_.units - z_.units_first, 128, round_wide)
    for k in others:
        w_copy(1, k, f).start()
    load_down.wait()

    def round_down(first, rows):
        place = pl.ds(first, rows)
        wm_s[f, place, :] = down_f[place, :].astype(BF16)

    over_rows(0, z_.units, 128, round_down)
    for k in others:
        w_copy(0, k, f).start()
    load_wo.wait()
    own_heads.wait()
    for j in range(1, count):
        heads_arrival(j).wait_recv()

    low_lane = lax.broadcasted_iota(jnp.int32, (half, 2 * HD), 1) < HD
    for h in range(0, z_.heads, 2):
        columns = slice(h * HD, (h + 2) * HD)
        one = heads_s[h].reshape(half, 2 * HD).astype(F32)
        two = heads_s[h + 1].reshape(half, 2 * HD).astype(F32)
        early = jnp.where(low_lane, one, pltpu.roll(two, HD, 1))
        late = jnp.where(low_lane, pltpu.roll(one, HD, 1), two)
        mixed_s[0:half, columns] = early.astype(BF16)
        mixed_s[half:, columns] = late.astype(BF16)
        mixed_t[columns, 0:half] = early.T.astype(BF16)
        mixed_t[columns, half:] = late.T.astype(BF16)

    for r in range(2):
        rows = slice(r * half, (r + 1) * half)
        for g in range(z_.fsdp):
            sum_s[rows, g * z_.shard : (g + 1) * z_.shard] = jnp.dot(
                mixed_s[rows, :], wo_s[g], preferred_element_type=F32
            ).astype(BF16)
        sum_copy(r).start()

    tile = min(128, half)

    def hidden_grad(i, carried):
        rows = pl.ds(pl.multiple_of(i * tile, tile), tile)
        total = jnp.zeros((tile, z_.units), F32)
        for g in range(z_.fsdp):
            total = total + lax.dot_general(
                cot_ref[rows, g * z_.shard : (g + 1) * z_.shard],
                wm_s[g],
                (((1,), (1,)), ((), ())),
                preferred_element_type=F32,
            )
        hgrad_s[rows, :] = total
        return carried

    load_wi.wait()
    for k in others:
        w_copy(1, k, behind(k)).wait_recv()
        w_pass(1, k, core).start()
    for k in others:
        w_pass(1, k, 1 - core).wait_recv()
    full = z_.units // 128 * 128

    for r in range(2):
        sum_copy(r).wait_recv()

        def middle_tile(i, carried):
            rows = pl.ds(pl.multiple_of(r * half + i * tile, tile), tile)
            middle = tok_ref[rows, :].astype(F32) + (
                sum_s[rows, :].astype(F32) + sum_in[rows, :].astype(F32)
            )
            middle_s[rows, :] = middle
            normed, scaling = normalize(middle)
            normed_s[rows, :] = normed
            scale_s[rows, :] = jnp.broadcast_to(scaling, (tile, 128))
            gains = jnp.concatenate([gain_ref[g, 1:2, :] for g in range(z_.fsdp)], axis=1)
            entry_s[rows, :] = (normed * gains).astype(BF16)
            return carried

        lax.fori_loop(0, half // tile, middle_tile, 0)
        rows = pl.ds(r * half, half)

        def gate(k, carried):
            total = jnp.zeros((half, z_.units), F32)
            for g in range(z_.fsdp):
                total = total + lax.dot_general(
                    entry_s[rows, g * z_.shard : (g + 1) * z_.shard],
                    wi_s[k, g],
                    (((1,), (1,)), ((), ())),
                    preferred_element_type=F32,
                )
            gate_s[k] = total
            return carried

        lax.fori_loop(0, 2, gate, 0)

        if r == 0:
            for k in others:
                w_copy(0, k, behind(k)).wait_recv()
                w_pass(0, k, core).start()
            for k in others:
                w_pass(0, k, 1 - core).wait_recv()
        tiles = half // tile
        lax.fori_loop(r * tiles, (r + 1) * tiles, hidden_grad, 0)

        def activate(i, carried):
            inner = pl.ds(pl.multiple_of(i * 16, 16), 16)
            outer = pl.ds(pl.multiple_of(r * half + i * 16, 16), 16)
            up, side = gate_s[0, inner, :], gate_s[1, inner, :]
            grad = hgrad_s[outer, :]
            chance = 0.5 + 0.5 * lax.erf(up * (0.5**0.5))
            slope = chance + up * (jnp.exp(-0.5 * up * up) * 0.3989422804014327)
            active = up * chance
            hidden_s[outer, :] = (active * side).astype(BF16)
            gated_s[0, outer, :] = (grad * side * slope).astype(BF16)
            gated_s[1, outer, :] = (grad * active).astype(BF16)
            return carried

        lax.fori_loop(0, half // 16, activate, 0)

        for g in range(z_.fsdp):
            place = slice(g * z_.shard, (g + 1) * z_.shard)
            total = jnp.zeros((half, z_.shard), F32)
            for k in range(2):
                total = total + jnp.dot(
                    gated_s[k, rows, :], wi_s[k, g], preferred_element_type=F32
                )
            back_s[rows, place] = total.astype(BF16)
        back_copy(r).start()

    keep_middle = pltpu.make_async_copy(middle_s, middle_ref, local_sem.at[9])
    keep_middle.start()

    def turn(source, target):
        def turn_tile(i, carried):
            rows = pl.ds(pl.multiple_of(i * tile, tile), tile)
            for first in range(0, full, 128):
                block = source[rows, first : first + 128].astype(F32)
                target[first : first + 128, rows] = block.T.astype(BF16)
            if full < z_.units:
                rest = z_.units - full
                block = source[rows, full : z_.units].astype(F32)
                block = jnp.concatenate([block, jnp.zeros((tile, 128 - rest), F32)], axis=1)
                target[full : z_.units, rows] = block.T[0:rest].astype(BF16)
            return carried

        lax.fori_loop(0, z_.rows // tile, turn_tile, 0)

    turn(hidden_s, hidden_t)
    for g in range(z_.fsdp):
        place = slice(g * z_.shard, (g + 1) * z_.shard)
        for side in range(2):
            rows = slice(side * units_half, (side + 1) * units_half)
            down_s[g, side] = jnp.dot(
                hidden_t[rows, :], cot_ref[:, place], preferred_element_type=F32
            ).astype(BF16)
    keep_down = pltpu.make_async_copy(down_s, g_down, local_sem.at[4])
    keep_down.start()

    for k in range(2):
        turn(gated_s.at[k], gated_t.at[k])
        for g in range(z_.fsdp):
            wide_s[g, k] = jnp.dot(
                gated_t[k],
                entry_s[:, g * z_.shard : (g + 1) * z_.shard],
                preferred_element_type=F32,
            ).astype(BF16)
    keep_wide = pltpu.make_async_copy(wide_s, g_wide, local_sem.at[5])
    keep_wide.start()
    for g in range(z_.fsdp):
        place = slice(g * z_.shard, (g + 1) * z_.shard)
        branch_s[:, place] = jnp.dot(
            hidden_s[...], wm_s[g], preferred_element_type=F32
        ).astype(BF16)
    keep_branch = pltpu.make_async_copy(branch_s, branch_ref, local_sem.at[10])
    keep_branch.start()

    gain2_ref[...] = jnp.zeros(gain2_ref.shape, F32)
    for r in range(2):
        back_copy(r).wait_recv()

        def back_tile(i, carried):
            rows = pl.ds(pl.multiple_of(r * half + i * tile, tile), tile)
            back = back_s[rows, :].astype(F32) + back_in[rows, :].astype(F32)
            normed = normed_s[rows, :]
            gain2_ref[0:1, :] += jnp.sum(back * normed, axis=0, keepdims=True)
            gains = jnp.concatenate([gain_ref[g, 1:2, :] for g in range(z_.fsdp)], axis=1)
            grad = cot_ref[rows, :].astype(F32) + norm_back(
                back * gains, normed, scale_s[rows, 0:1]
            )
            grad_f[rows, :] = grad
            mgrad_s[rows, :] = grad.astype(BF16)
            return carried

        lax.fori_loop(0, half // tile, back_tile, 0)

    keep_grad = pltpu.make_async_copy(grad_f, mgrad_ref, local_sem.at[11])
    keep_grad.start()

    def heads_grad(rows):
        total = jnp.zeros((half, z_.head_width), F32)
        for g in range(z_.fsdp):
            total = total + lax.dot_general(
                mgrad_s[rows, g * z_.shard : (g + 1) * z_.shard],
                wo_s[g],
                (((1,), (1,)), ((), ())),
                preferred_element_type=F32,
            )
        return total

    early = heads_grad(slice(0, half))
    late = heads_grad(slice(half, z_.rows))
    for h in range(0, z_.heads, 2):
        columns = slice(h * HD, (h + 2) * HD)
        one = jnp.where(low_lane, early[:, columns], pltpu.roll(late[:, columns], HD, 1))
        two = jnp.where(low_lane, pltpu.roll(early[:, columns], HD, 1), late[:, columns])
        dsend_s[h] = one.astype(BF16).reshape(4, z_.block, 2 * HD)
        dsend_s[h + 1] = two.astype(BF16).reshape(4, z_.block, 2 * HD)
    for j in range(1, z_.ctx):
        grads_copy(j).start()
    own_grads = pltpu.make_async_copy(
        dsend_s.at[c // z_.share], grads_ref.at[:, c], local_sem.at[6]
    )
    own_grads.start()
    attn_half = z_.head_width // 2
    for g in range(z_.fsdp):
        for side in range(2):
            attn_s[g, side] = jnp.dot(
                mixed_t[side * attn_half : (side + 1) * attn_half, :],
                mgrad_s[:, g * z_.shard : (g + 1) * z_.shard],
                preferred_element_type=F32,
            ).astype(BF16)
    keep_attn = pltpu.make_async_copy(attn_s, g_attn, local_sem.at[7])
    keep_attn.start()

    own_grads.wait()
    for j in range(1, z_.ctx):
        grads_arrival(j).wait_recv()
        grads_copy(j).wait_send()
    for j in range(1, count):
        heads_copy(j).wait_send()
    for k in others:
        for n in range(2):
            w_copy(n, k, f).wait_send()
            w_pass(n, k, core).wait_send()
    for r in range(2):
        sum_copy(r).wait_send()
        back_copy(r).wait_send()
    keep_down.wait()
    keep_wide.wait()
    keep_attn.wait()
    keep_middle.wait()
    keep_branch.wait()
    keep_grad.wait()


def middle_part(z_, tokens, cotangent, gains, heads, wo, wi, wide_weight, down_weight):
    dma = pltpu.SemaphoreType.DMA
    peers = max(1, z_.fsdp - 1)
    count = z_.ctx // z_.share
    rows, width, units = z_.rows, z_.width, z_.units
    down = (z_.fsdp, 2, units // 2, z_.shard)
    wide = (z_.fsdp, 2, units, z_.shard)
    attn = (z_.fsdp, 2, z_.head_width // 2, z_.shard)
    return pl.pallas_call(
        functools.partial(middle_kernel, z_),
        out_shape=(
            jax.ShapeDtypeStruct((rows, width), BF16),
            jax.ShapeDtypeStruct((rows, width), F32),
            jax.ShapeDtypeStruct((rows, width), F32),
            jax.ShapeDtypeStruct((8, width), F32),
            jax.ShapeDtypeStruct((4, z_.ctx, z_.block, 2 * HD), BF16),
            jax.ShapeDtypeStruct(down, BF16),
            jax.ShapeDtypeStruct(wide, BF16),
            jax.ShapeDtypeStruct(attn, BF16),
        ),
        in_specs=[vmem()] * 3 + [anywhere()] * 5,
        out_specs=tuple([anywhere()] * 3 + [vmem()] + [anywhere()] * 4),
        scratch_shapes=[
            pltpu.VMEM((z_.heads, 4, z_.block, 2 * HD), BF16),
            pltpu.VMEM((z_.fsdp, z_.head_width, z_.shard), BF16),
            pltpu.VMEM((2, z_.fsdp, units, z_.shard), BF16),
            pltpu.VMEM((2, units - z_.units_first, z_.shard), F32),
            pltpu.VMEM((units, z_.shard), F32),
            pltpu.VMEM((z_.fsdp, units, z_.shard), BF16),
            pltpu.VMEM((rows, z_.head_width), BF16),
            pltpu.VMEM((z_.head_width, rows), BF16),
            pltpu.VMEM((rows, width), BF16),
            pltpu.VMEM((rows, width), BF16),
            pltpu.VMEM((rows, width), BF16),
            pltpu.VMEM((rows, width), BF16),
            pltpu.VMEM((rows, width), BF16),
            pltpu.VMEM((rows, width), BF16),
            pltpu.VMEM((rows, width), F32),
            pltpu.VMEM((rows, width), F32),
            pltpu.VMEM((rows, width), F32),
            pltpu.VMEM((rows, 128), F32),
            pltpu.VMEM((2, rows // 2, units), F32),
            pltpu.VMEM((rows, units), F32),
            pltpu.VMEM((rows, units), BF16),
            pltpu.VMEM((units, rows), BF16),
            pltpu.VMEM((2, rows, units), BF16),
            pltpu.VMEM((2, units, rows), BF16),
            pltpu.VMEM((rows, width), BF16),
            pltpu.VMEM((z_.heads, 4, z_.block, 2 * HD), BF16),
            pltpu.VMEM(down, BF16),
            pltpu.VMEM(wide, BF16),
            pltpu.VMEM(attn, BF16),
            dma((count,)),
            dma((count,)),
            dma((z_.ctx,)),
            dma((z_.ctx,)),
            dma((4,)),
            dma((4,)),
            dma((2, peers)),
            dma((2, peers)),
            dma((2, peers)),
            dma((2, peers)),
            dma((12,)),
        ],
        compiler_params=pltpu.CompilerParams(
            collective_id=2, has_side_effects=True, vmem_limit_bytes=VMEM_BYTES
        ),
        name="middle",
    )(tokens, cotangent, gains, heads, wo, wi, wide_weight, down_weight)


class Item:
    def __init__(self, number, rows, columns, cuts):
        self.number = number
        self.rows = rows
        self.columns = columns
        self.cuts = cuts_of(rows, cuts)


class Reducer:
    def __init__(self, z_, items, refs, sems):
        self.z_ = z_
        self.items = items
        self.refs = refs
        self.sems = sems
        f, c, t = lax.axis_index("fsdp"), lax.axis_index("ctx"), lax.axis_index("tp")
        self.f, self.c, self.t = f, c, t
        self.core = lax.rem(c, 2)
        self.chip = c // 2
        self.mate = (f, c + 1 - 2 * self.core, t)
        middle = z_.chips // 2
        low = self.chip < middle
        self.is_mid = (self.chip == middle - 1) | (self.chip == middle)
        self.has_outer = (self.chip > 0) & (self.chip < z_.chips - 1)
        self.is_end = jnp.logical_not(self.is_mid | self.has_outer)
        towards = jnp.where(low, 2, -2)
        self.inner = (f, c + towards, t)
        self.outer = (f, c - towards, t)
        self.numbers = {}
        for item in items:
            for cut in range(len(item.cuts)):
                self.numbers[(item.number, cut)] = len(self.numbers)

    def ahead(self, k):
        return lax.rem(self.f + k, self.z_.fsdp)

    def behind(self, k):
        return lax.rem(self.f + self.z_.fsdp - k, self.z_.fsdp)

    def part(self, item, cut):
        first, rows = item.cuts[cut]
        return self.numbers[(item.number, cut)], pl.ds(first, rows)


    def core_copy(self, item, cut):
        source, own, mate_in = self.refs[item.number][:3]
        n, rows = self.part(item, cut)
        return remote(
            source.at[:, 1 - self.core, rows],
            mate_in.at[:, rows],
            self.sems["core_send"].at[n],
            self.sems["core_recv"].at[n],
            self.mate,
        )

    def own_copy(self, item, cut):
        source, own = self.refs[item.number][:2]
        n, rows = self.part(item, cut)
        return pltpu.make_async_copy(
            source.at[:, self.core, rows], own.at[:, rows], self.sems["own"].at[n]
        )

    def core_start(self, item, cut):
        self.core_copy(item, cut).start()
        self.own_copy(item, cut).start()

    def core_sum(self, item, cut):
        own, mate_in = self.refs[item.number][1:3]
        first, rows = item.cuts[cut]
        self.own_copy(item, cut).wait()
        self.core_copy(item, cut).wait_recv()
        for k in range(self.z_.fsdp - 1, -1, -1):
            g = self.ahead(k)

            def add(start, count):
                place = pl.ds(start, count)
                own[g, place, :] = (
                    own[g, place, :].astype(F32) + mate_in[g, place, :].astype(F32)
                ).astype(BF16)

            over_rows(first, rows, 128, add)
            if k:
                self.peer_copy(item, cut, k, g).start()


    def peer_copy(self, item, cut, k, owner):
        own, peer_in = self.refs[item.number][1], self.refs[item.number][3]
        n, rows = self.part(item, cut)
        return remote(
            own.at[owner, rows],
            peer_in.at[k - 1, rows],
            self.sems["peer_send"].at[n, k - 1],
            self.sems["peer_recv"].at[n, k - 1],
            (self.ahead(k), self.c, self.t),
        )

    def peer_sum(self, item, cut):
        own, peer_in = self.refs[item.number][1], self.refs[item.number][3]
        first, rows = item.cuts[cut]
        for k in range(1, self.z_.fsdp):
            self.peer_copy(item, cut, k, self.ahead(k)).wait_recv()

        def add(start, count):
            place = pl.ds(start, count)
            total = own[self.f, place, :].astype(F32)
            for k in range(1, self.z_.fsdp):
                total = total + peer_in[k - 1, place, :].astype(F32)
            own[self.f, place, :] = total.astype(BF16)

        over_rows(first, rows, 128, add)

        @pl.when(jnp.logical_not(self.has_outer))
        def outermost():
            self.inward_start(item, cut)


    def in_copy(self, item, cut, middle):
        own, peer_in, outer_in, inner_in = self.refs[item.number][1:2] + self.refs[item.number][3:6]
        rows = pl.ds(*item.cuts[cut])
        n = self.numbers[(item.number, cut)]
        if middle:
            target, name = inner_in, "inner_recv"
        else:
            target, name = outer_in, "outer_recv"
        return remote(
            own.at[self.f, rows],
            target.at[rows],
            self.sems["in_send"].at[n],
            self.sems[name].at[n],
            self.inner,
        )

    def out_copy(self, item, cut):
        inner_in = self.refs[item.number][5]
        rows = pl.ds(*item.cuts[cut])
        n = self.numbers[(item.number, cut)]
        return remote(
            inner_in.at[rows],
            inner_in.at[rows],
            self.sems["out_send"].at[n],
            self.sems["inner_recv"].at[n],
            self.outer,
        )

    def done_copy(self, item, cut):
        inner_in, mate_out = self.refs[item.number][5:7]
        rows = pl.ds(*item.cuts[cut])
        n = self.numbers[(item.number, cut)]
        return remote(
            inner_in.at[rows],
            mate_out.at[rows],
            self.sems["done_send"].at[n],
            self.sems["done_recv"].at[n],
            self.mate,
        )

    def inward_start(self, item, cut):
        @pl.when(self.is_mid)
        def cross():
            self.in_copy(item, cut, True).start()

        @pl.when(jnp.logical_not(self.is_mid))
        def along():
            self.in_copy(item, cut, False).start()

    def inward(self, item, cut):
        own, outer_in = self.refs[item.number][1], self.refs[item.number][4]
        first, rows = item.cuts[cut]

        @pl.when(self.has_outer)
        def passed():
            self.in_copy(item, cut, False).wait_recv()

            def add(start, count):
                place = pl.ds(start, count)
                own[self.f, place, :] = (
                    own[self.f, place, :].astype(F32) + outer_in[place, :].astype(F32)
                ).astype(BF16)

            over_rows(first, rows, 128, add)
            self.inward_start(item, cut)

    def outward(self, item, cut):
        own, inner_in = self.refs[item.number][1], self.refs[item.number][5]
        first, rows = item.cuts[cut]

        @pl.when(jnp.logical_not(self.is_end))
        def onwards():
            self.out_copy(item, cut).wait_recv()

            @pl.when(self.is_mid)
            def total():
                def add(start, count):
                    place = pl.ds(start, count)
                    inner_in[place, :] = (
                        own[self.f, place, :].astype(F32) + inner_in[place, :].astype(F32)
                    ).astype(BF16)

                over_rows(first, rows, 128, add)

            @pl.when(self.has_outer)
            def onward():
                self.out_copy(item, cut).start()

            self.done_copy(item, cut).start()

    def arrive(self, item, cut):
        @pl.when(self.is_end)
        def ended():
            self.out_copy(item, cut).wait_recv()
            self.done_copy(item, cut).start()

    def settle(self):
        for item in self.items:
            for cut in range(len(item.cuts)):
                self.core_copy(item, cut).wait_send()
                for k in range(1, self.z_.fsdp):
                    self.peer_copy(item, cut, k, self.ahead(k)).wait_send()
                self.in_copy(item, cut, False).wait_send()

                @pl.when(self.has_outer)
                def outwards(item=item, cut=cut):
                    self.out_copy(item, cut).wait_send()

                self.done_copy(item, cut).wait_send()


class Finisher:
    def __init__(self, z_, reducer, results, store_sem):
        self.z_ = z_
        self.red = reducer
        self.results = results
        self.store_sem = store_sem

    def copies(self, item, cut, which):
        first, rows = item.cuts[cut]
        number = item.number
        red = self.red
        side = red.core if which == 0 else 1 - red.core
        sums = red.refs[number][5 + which]
        result = self.results[number]
        sem = self.store_sem.at[which]
        index = red.numbers[(number, cut)]
        if number == 3:
            half = self.z_.shard // 2
            place = pl.ds(pl.multiple_of(side * half, half), half)
            columns = slice(2 * HD * cut, 2 * HD * (cut + 1))
            return [
                pltpu.make_async_copy(
                    sums.at[first : first + rows, 2 * HD * kind : 2 * HD * (kind + 1)],
                    result.at[kind, place, columns],
                    sem.at[index, kind],
                )
                for kind in range(3)
            ]
        if number in (1, 4):
            target = result.at[side, first : first + rows]
        else:
            target = result.at[pl.ds(pl.multiple_of(side * item.rows + first, 16), rows)]
        return [pltpu.make_async_copy(sums.at[first : first + rows], target, sem.at[index, 0])]

    def update(self, item, cut):
        for copy in self.copies(item, cut, 0):
            copy.start()
        self.red.done_copy(item, cut).wait_recv()
        for copy in self.copies(item, cut, 1):
            copy.start()

    def settle(self):
        for item in self.red.items:
            for cut in range(len(item.cuts)):
                for which in range(2):
                    for copy in self.copies(item, cut, which):
                        copy.wait()


def reduce_kernel(
    z_,
    items,
    tok_ref,
    gain_ref,
    cos_ref,
    sin_ref,
    branch_ref,
    middle_ref,
    mgrad_ref,
    gain2_ref,
    heads_ref,
    wq_ref,
    g_down,
    g_wide,
    g_attn,
    *others,
):
    down, wide, attn, qkv, gain = items
    scratch = list(others)

    def take(count):
        taken = scratch[:count]
        del scratch[:count]
        return taken

    out_ref, igrad_ref = take(2)
    results = take(5)
    heads_s, wq_s, entry_s, grads_s, branch_own, branch_s, back_s, back_in = take(8)
    middle_s, mgrad_s = take(2)
    g_qkv, g_gain, gain_in, gain_acc = take(4)
    groups = [take(6) for item in items]
    (a_send, a_recv, y_send, y_recv, local_sem, store_sem) = take(6)
    names = (
        "peer_send",
        "peer_recv",
        "core_send",
        "core_recv",
        "own",
        "in_send",
        "outer_recv",
        "inner_recv",
        "out_send",
        "done_send",
        "done_recv",
    )
    sems = dict(zip(names, take(len(names))))
    sources = (g_down, g_wide, g_attn, g_qkv, g_gain)
    refs = [(source, *group) for source, group in zip(sources, groups)]
    red = Reducer(z_, items, refs, sems)
    finish = Finisher(z_, red, results, store_sem)
    f, c, t = red.f, red.c, red.t
    other = (f, c, 1 - t)
    count = z_.ctx // z_.share

    def to_token(j):
        return lax.rem(c + z_.share * j, z_.ctx)

    def from_head(j):
        return lax.rem(c + z_.ctx - z_.share * j, z_.ctx)

    def heads_copy(j):
        return remote(
            heads_ref.at[:, to_token(j)],
            heads_s.at[c // z_.share],
            a_send.at[j],
            a_recv.at[j],
            (f, to_token(j), t),
        )

    def branch_copy():
        return remote(branch_ref, branch_s, y_send.at[0], y_recv.at[0], other)

    def back_copy(r):
        rows = pl.ds(r * (z_.rows // 2), z_.rows // 2)
        return remote(back_s.at[rows], back_in.at[rows], y_send.at[2 + r], y_recv.at[2 + r], other)

    load_wq = pltpu.make_async_copy(wq_ref, wq_s, local_sem.at[1])
    load_branch = pltpu.make_async_copy(branch_ref, branch_own, local_sem.at[2])
    load_middle = pltpu.make_async_copy(middle_ref, middle_s, local_sem.at[3])
    load_mgrad = pltpu.make_async_copy(mgrad_ref, mgrad_s, local_sem.at[4])
    load_wq.start()
    load_branch.start()
    load_middle.start()
    load_mgrad.start()
    greet(
        [(red.ahead(k), c, t) for k in range(1, z_.fsdp)]
        + [(f, lax.rem(c + j, z_.ctx), t) for j in range(1, z_.ctx)]
        + [other]
    )
    for j in range(1, count):
        heads_copy(j).start()
    branch_copy().start()
    own_heads = pltpu.make_async_copy(heads_ref.at[:, c], heads_s.at[c // z_.share], local_sem.at[0])
    own_heads.start()
    ready = [(item, cut) for item in (down, wide, attn) for cut in range(len(item.cuts))]
    for part in ready:
        red.core_start(*part)

    for part in ready:
        red.core_sum(*part)

    def run(*steps):
        for step in steps:
            item = {"d": down, "w": wide, "a": attn, "q": qkv, "g": gain}[step[1]]
            part = (item, int(step[2]))
            if step[0] == "x":
                red.peer_sum(*part)
            elif step[0] == "i":
                red.inward(*part)
            elif step[0] == "o":
                red.outward(*part)
            elif step[0] == "e":
                red.arrive(*part)
            else:
                finish.update(*part)

    tile = min(128, z_.rows)

    def entry_tile(i, carried):
        rows = pl.ds(pl.multiple_of(i * tile, tile), tile)
        normed, nothing = normalize(tok_ref[rows, :].astype(F32))
        for g in range(z_.fsdp):
            columns = slice(g * z_.shard, (g + 1) * z_.shard)
            entry_s[g, :, rows] = (normed[:, columns] * gain_ref[g, 0:1, :]).T.astype(BF16)
        return carried

    lax.fori_loop(0, z_.rows // tile, entry_tile, 0)

    run("xd0", "xd1")
    branch_copy().wait_recv()
    load_branch.wait()
    load_middle.wait()

    def output_tile(i, carried):
        rows = pl.ds(pl.multiple_of(i * tile, tile), tile)
        branch = branch_own[rows, :].astype(F32) + branch_s[rows, :].astype(F32)
        out_ref[rows, :] = (middle_s[rows, :] + branch).astype(BF16)
        return carried

    lax.fori_loop(0, z_.rows // tile, output_tile, 0)

    run("id0", "xw0", "id1", "od0", "xw1", "iw0", "od1")

    own_heads.wait()
    for j in range(1, count):
        remote(
            heads_ref.at[:, c],
            heads_s.at[from_head(j) // z_.share],
            a_send.at[j],
            a_recv.at[j],
            red.mate,
        ).wait_recv()
    load_wq.wait()

    lane = lax.broadcasted_iota(jnp.int32, (z_.rows, 2 * HD), 1) < HD
    lane_half = lax.broadcasted_iota(jnp.int32, (z_.rows // 2, 2 * HD), 1) < HD
    mid_row = z_.rows // 2

    def chunk_grads(p, carried):
        pair = [
            heads_s[2 * p + i, 0:8].reshape(z_.rows, 2 * HD).astype(F32) for i in range(2)
        ]
        query = jnp.where(lane, pair[0], pltpu.roll(pair[1], HD, 1))
        key = jnp.where(lane, pltpu.roll(pair[0], HD, 1), pair[1])
        for kind, part in ((0, query), (1, key)):
            part = part * cos_ref[...] - swap_halves(part) * sin_ref[...]
            grads_s[p, :, 2 * HD * kind : 2 * HD * (kind + 1)] = part.astype(BF16)
        value = [
            heads_s[2 * p + i, 8:12].reshape(mid_row, 2 * HD).astype(F32) for i in range(2)
        ]
        early = jnp.where(lane_half, value[0], pltpu.roll(value[1], HD, 1))
        late = jnp.where(lane_half, pltpu.roll(value[0], HD, 1), value[1])
        grads_s[p, 0:mid_row, 4 * HD : 6 * HD] = early.astype(BF16)
        grads_s[p, mid_row : z_.rows, 4 * HD : 6 * HD] = late.astype(BF16)
        return carried

    lax.fori_loop(0, z_.pairs, chunk_grads, 0)

    gain_acc[...] = jnp.zeros(gain_acc.shape, F32)

    def back_tile(i, carried):
        rows = pl.ds(pl.multiple_of(i * tile, tile), tile)
        normed, nothing = normalize(tok_ref[rows, :].astype(F32))
        for g in range(z_.fsdp):
            columns = slice(g * z_.shard, (g + 1) * z_.shard)
            total = jnp.zeros((tile, z_.shard), F32)
            for p in range(z_.pairs):
                total = total + lax.dot_general(
                    grads_s[p, rows, :],
                    wq_s[p, g],
                    (((1,), (1,)), ((), ())),
                    preferred_element_type=F32,
                )
            back_s[rows, columns] = total.astype(BF16)
            gain_acc[0:1, columns] += jnp.sum(total * normed[:, columns], axis=0, keepdims=True)
        return carried

    for r in range(2):
        tiles = z_.rows // tile
        lax.fori_loop(r * tiles // 2, (r + 1) * tiles // 2, back_tile, 0)
        back_copy(r).start()
    top = lax.broadcasted_iota(jnp.int32, (16, z_.shard), 0) == 0
    for g in range(z_.fsdp):
        columns = slice(g * z_.shard, (g + 1) * z_.shard)
        for side, row in ((0, gain_acc[0:1, columns]), (1, gain2_ref[0:1, columns])):
            g_gain[g, side] = jnp.where(top, row, 0.0).astype(BF16)

    def gain_copy():
        return remote(g_gain.at[:, 0], gain_in, y_send.at[1], y_recv.at[1], other)

    gain_copy().start()
    run("xw2", "iw1", "ow0")
    half = z_.shard // 2

    def qkv_pair(p):
        for g in range(z_.fsdp):
            for side in range(2):
                grad = jnp.dot(
                    entry_s[g, side * half : (side + 1) * half, :],
                    grads_s[p],
                    preferred_element_type=F32,
                )
                g_qkv[g, side, p * half : (p + 1) * half, :] = grad.astype(BF16)

    for p in range(z_.pairs):
        qkv_pair(p)
        red.core_start(qkv, p)
    run("xw3", "iw2", "ow1", "ed0")
    for p in range(z_.pairs):
        red.core_sum(qkv, p)
    run("xa0", "iw3", "ow2", "ed1", "ud0", "xq0", "ia0", "ow3", "ew0", "ud1")
    gain_copy().wait()
    for g in range(z_.fsdp):
        g_gain[g, 0] = (g_gain[g, 0].astype(F32) + gain_in[g].astype(F32)).astype(BF16)
    red.core_start(gain, 0)
    run("xq1", "iq0", "oa0", "ew1", "uw0")
    red.core_sum(gain, 0)
    run("xq2", "iq1", "oq0", "ew2", "uw1", "xg0", "xq3", "iq2", "oq1", "ew3", "uw2", "ig0", "iq3")
    run("oq2", "og0", "oq3", "ea0", "uw3", "eq0", "ua0")

    for r in range(2):
        back_copy(r).wait_recv()
    load_mgrad.wait()

    def input_tile(i, carried):
        rows = pl.ds(pl.multiple_of(i * tile, tile), tile)
        normed, scaling = normalize(tok_ref[rows, :].astype(F32))
        back = back_s[rows, :].astype(F32) + back_in[rows, :].astype(F32)
        gains = jnp.concatenate([gain_ref[g, 0:1, :] for g in range(z_.fsdp)], axis=1)
        igrad_ref[rows, :] = (
            mgrad_s[rows, :] + norm_back(back * gains, normed, scaling)
        ).astype(BF16)
        return carried

    lax.fori_loop(0, z_.rows // tile, input_tile, 0)
    run("eq1", "uq0", "eq2", "uq1", "eg0", "uq2", "eq3", "ug0", "uq3")

    own_sends = [heads_copy(j) for j in range(1, count)] + [branch_copy(), back_copy(0), back_copy(1)]
    for copy in own_sends:
        copy.wait_send()
    red.settle()
    finish.settle()


def reduce_all(
    z_,
    tokens,
    gains,
    cosine,
    sines,
    branch,
    middle,
    middle_grad,
    gain2,
    heads,
    wq,
    g_down,
    g_wide,
    g_attn,
):
    items = (
        Item(0, z_.units // 2, z_.shard, 2),
        Item(1, z_.units, z_.shard, 4),
        Item(2, z_.head_width // 2, z_.shard, 1),
        Item(3, z_.pairs * (z_.shard // 2), 6 * HD, z_.pairs),
        Item(4, 16, z_.shard, 1),
    )
    dma = pltpu.SemaphoreType.DMA
    peers = max(1, z_.fsdp - 1)
    pieces = sum(len(item.cuts) for item in items)
    groups = []
    for item in items:
        groups += [
            pltpu.VMEM((z_.fsdp, item.rows, item.columns), BF16),
            pltpu.VMEM((z_.fsdp, item.rows, item.columns), BF16),
            pltpu.VMEM((peers, item.rows, item.columns), BF16),
            pltpu.VMEM((item.rows, item.columns), BF16),
            pltpu.VMEM((item.rows, item.columns), BF16),
            pltpu.VMEM((item.rows, item.columns), BF16),
        ]
    count = z_.ctx // z_.share
    rows = (z_.rows, z_.width)
    return pl.pallas_call(
        functools.partial(reduce_kernel, z_, items),
        out_shape=tuple(
            [jax.ShapeDtypeStruct(rows, BF16)] * 2
            + [
                jax.ShapeDtypeStruct(shape, BF16)
                for shape in (
                    (z_.units, z_.shard),
                    (2, z_.units, z_.shard),
                    (z_.head_width, z_.shard),
                    (3, z_.shard, z_.head_width),
                    (2, 16, z_.shard),
                )
            ]
        ),
        in_specs=[vmem()] * 4
        + [anywhere()] * 3
        + [vmem()]
        + [anywhere()] * 5,
        out_specs=tuple([vmem()] * 2 + [anywhere()] * 5),
        scratch_shapes=[
            pltpu.VMEM((z_.heads, 12, z_.block, 2 * HD), BF16),
            pltpu.VMEM((z_.pairs, z_.fsdp, z_.shard, 6 * HD), BF16),
            pltpu.VMEM((z_.fsdp, z_.shard, z_.rows), BF16),
            pltpu.VMEM((z_.pairs, z_.rows, 6 * HD), BF16),
            pltpu.VMEM(rows, BF16),
            pltpu.VMEM(rows, BF16),
            pltpu.VMEM(rows, BF16),
            pltpu.VMEM(rows, BF16),
            pltpu.VMEM(rows, F32),
            pltpu.VMEM(rows, F32),
            pltpu.VMEM((z_.fsdp, 2, items[3].rows, items[3].columns), BF16),
            pltpu.VMEM((z_.fsdp, 2, 16, z_.shard), BF16),
            pltpu.VMEM((z_.fsdp, 16, z_.shard), BF16),
            pltpu.VMEM((8, z_.width), F32),
        ]
        + groups
        + [dma((count,)), dma((count,)), dma((4,)), dma((4,)), dma((5,)), dma((2, pieces, 3))]
        + [
            dma((pieces, peers)),
            dma((pieces, peers)),
        ]
        + [dma((pieces,))] * 9,
        compiler_params=pltpu.CompilerParams(
            collective_id=1, has_side_effects=True, vmem_limit_bytes=REDUCE_BYTES
        ),
        name="reduce",
    )(
        tokens,
        gains,
        cosine,
        sines,
        branch,
        middle,
        middle_grad,
        gain2,
        heads,
        wq,
        g_down,
        g_wide,
        g_attn,
    )


def adam_step(weight, gradient, moment, squared, rate_now):
    first = BETA_FIRST * moment + (1.0 - BETA_FIRST) * gradient
    second = BETA_SECOND * squared + (1.0 - BETA_SECOND) * gradient * gradient
    corrected = first * (1.0 / (1.0 - BETA_FIRST**STEP))
    spread = jnp.sqrt(second * (1.0 / (1.0 - BETA_SECOND**STEP)))
    return (weight - rate_now * (corrected / (spread + ADAM_EPS) + DECAY * weight), first, second)


SLOTS = 4


def update_kernel(pieces, *refs):
    groups = (len(refs) - 4 - 7) // 7
    arrays = [refs[4 * n : 4 * n + 4] for n in range(groups)]
    gains = refs[4 * groups : 4 * groups + 4]
    after = refs[4 * groups + 4 :]
    results = [after[3 * n : 3 * n + 3] for n in range(groups)]
    gain_results = after[3 * groups : 3 * groups + 3]
    state_s, grad_s, out_s, load_sem, store_sem = after[3 * groups + 3 :]

    def loads(i):
        n, first, rows, columns, rate = pieces[i]
        slot = i % SLOTS
        place = slice(first, first + rows)
        made = [
            pltpu.make_async_copy(
                arrays[n][k].at[place], state_s.at[slot, k, 0:rows, 0:columns], load_sem.at[slot, k]
            )
            for k in range(3)
        ]
        made.append(
            pltpu.make_async_copy(
                arrays[n][3].at[place], grad_s.at[slot, 0:rows, 0:columns], load_sem.at[slot, 3]
            )
        )
        return made

    def stores(i):
        n, first, rows, columns, rate = pieces[i]
        slot = i % SLOTS
        return [
            pltpu.make_async_copy(
                out_s.at[slot, k, 0:rows, 0:columns],
                results[n][k].at[first : first + rows],
                store_sem.at[slot, k],
            )
            for k in range(3)
        ]

    for i in range(SLOTS - 1):
        for copy in loads(i):
            copy.start()
    weight, moment, squared, gradient = gains
    got = adam_step(
        weight[...], gradient[:, 0, :].astype(F32), moment[...], squared[...], RATE_GAIN
    )
    for k in range(3):
        gain_results[k][...] = got[k]
    for i, (n, first, rows, columns, rate) in enumerate(pieces):
        if i + SLOTS - 1 < len(pieces):
            for copy in loads(i + SLOTS - 1):
                copy.start()
        for copy in loads(i):
            copy.wait()
        if i >= SLOTS:
            for copy in stores(i - SLOTS):
                copy.wait()
        slot = i % SLOTS

        def step(start, count, slot=slot, rate=rate, across=slice(0, columns)):
            place = pl.ds(start, count)
            got = adam_step(
                state_s[slot, 0, place, across],
                grad_s[slot, place, across].astype(F32),
                state_s[slot, 1, place, across],
                state_s[slot, 2, place, across],
                rate,
            )
            for k in range(3):
                out_s[slot, k, place, across] = got[k]

        over_rows(0, rows, 64, step)
        for copy in stores(i):
            copy.start()
    for i in range(len(pieces) - SLOTS, len(pieces)):
        for copy in stores(i):
            copy.wait()


def update_all(groups, gains):
    pieces = []
    for n, (weight, moment, squared, gradient, rate) in enumerate(groups):
        rows, columns = weight.shape
        for first, count in cuts_of(rows, max(1, rows // 320)):
            pieces.append((n, first, count, columns, rate))
    largest = max(piece[2] for piece in pieces)
    columns = max(piece[3] for piece in pieces)
    flat = [array for group in groups for array in group[:4]]
    shapes = [jax.ShapeDtypeStruct(group[0].shape, F32) for group in groups for k in range(3)]
    shapes += [jax.ShapeDtypeStruct(gains[0].shape, F32)] * 3
    return pl.pallas_call(
        functools.partial(update_kernel, pieces),
        out_shape=tuple(shapes),
        in_specs=[anywhere()] * len(flat) + [vmem()] * 4,
        out_specs=tuple([anywhere()] * (3 * len(groups)) + [vmem()] * 3),
        scratch_shapes=[
            pltpu.VMEM((SLOTS, 3, largest, columns), F32),
            pltpu.VMEM((SLOTS, largest, columns), BF16),
            pltpu.VMEM((SLOTS, 3, largest, columns), F32),
            pltpu.SemaphoreType.DMA((SLOTS, 4)),
            pltpu.SemaphoreType.DMA((SLOTS, 3)),
        ],
        compiler_params=pltpu.CompilerParams(vmem_limit_bytes=VMEM_BYTES),
        name="update",
    )(*flat, *gains)


def on_device(
    tokens,
    cotangent,
    lengths,
    order,
    qkv_weight,
    attn_weight,
    wide_weight,
    down_weight,
    norm_gains,
    qkv_mean,
    attn_mean,
    wide_mean,
    down_mean,
    gains_mean,
    qkv_square,
    attn_square,
    wide_square,
    down_square,
    gains_square,
):
    z_ = Sizes(
        lax.axis_size("fsdp"),
        lax.axis_size("ctx"),
        tokens.shape[0],
        tokens.shape[1],
        qkv_weight.shape[2],
        wide_weight.shape[2],
    )
    ctx_index = lax.axis_index("ctx")
    in_order, endings = sequence_ends(lengths[0], order[0])
    local_ids = jnp.arange(z_.rows, dtype=jnp.int32)
    cosine, sines = rope_tables(
        positions(in_order, endings, packed_place(local_ids, ctx_index, z_.ctx, z_.block))
    )
    packed, wq_full, wo_full, wi_full, gains_full = project(
        z_,
        tokens,
        norm_gains,
        cosine,
        sines,
        qkv_weight.transpose(1, 0, 2),
        attn_weight,
        wide_weight.transpose(1, 2, 0),
    )
    attended_packed, attended_turned, lse, swapped, query, key, value = attend(
        z_, lengths, order, packed
    )
    branch_low, middle, middle_grad, gain_second, grads_packed, down_grad, wide_grad, attn_grad = (
        middle_part(
            z_,
            tokens,
            cotangent,
            gains_full,
            attended_packed,
            wo_full,
            wi_full,
            wide_weight.transpose(1, 2, 0),
            down_weight,
        )
    )
    head_grads = attend_back(
        z_, lengths, order, lse, grads_packed, attended_turned, swapped, query, key, value
    )
    output, input_grad, down_sum, wide_sum, attn_sum, qkv_sum, gain_sum = reduce_all(
        z_,
        tokens,
        gains_full,
        cosine,
        sines,
        branch_low,
        middle,
        middle_grad,
        gain_second,
        head_grads,
        wq_full,
        down_grad,
        wide_grad,
        attn_grad,
    )
    wide_rows, qkv_rows = (2 * z_.units, z_.shard), (3 * z_.shard, z_.head_width)
    wide_group = [
        array.transpose(1, 2, 0).reshape(wide_rows)
        for array in (wide_weight, wide_mean, wide_square)
    ]
    qkv_group = [
        array.transpose(1, 0, 2).reshape(qkv_rows) for array in (qkv_weight, qkv_mean, qkv_square)
    ]
    updated = update_all(
        (
            (*wide_group, wide_sum.reshape(wide_rows), D ** (-0.5)),
            (*qkv_group, qkv_sum.reshape(qkv_rows), D ** (-0.5)),
            (down_weight, down_mean, down_square, down_sum, FF ** (-0.5)),
            (attn_weight, attn_mean, attn_square, attn_sum, RATE_ATTN),
        ),
        (norm_gains, gains_mean, gains_square, gain_sum),
    )
    wide_new = [
        array.reshape(2, z_.units, z_.shard).transpose(2, 0, 1) for array in updated[0:3]
    ]
    qkv_new = [
        array.reshape(3, z_.shard, z_.head_width).transpose(1, 0, 2) for array in updated[3:6]
    ]
    return (
        output,
        input_grad,
        *qkv_new,
        *updated[9:12],
        *wide_new,
        *updated[6:9],
        *updated[12:15],
    )


def solution(mesh):
    return jax.shard_map(
        on_device,
        mesh=mesh,
        in_specs=(
            P(("fsdp", "ctx"), None),
            P(("fsdp", "ctx"), None),
            P("fsdp", None),
            P("fsdp", None),
            P("fsdp", None, "tp"),
            P("tp", "fsdp"),
            P("fsdp", None, "tp"),
            P("tp", "fsdp"),
            P(None, "fsdp"),
            P("fsdp", None, "tp"),
            P("tp", "fsdp"),
            P("fsdp", None, "tp"),
            P("tp", "fsdp"),
            P(None, "fsdp"),
            P("fsdp", None, "tp"),
            P("tp", "fsdp"),
            P("fsdp", None, "tp"),
            P("tp", "fsdp"),
            P(None, "fsdp"),
        ),
        out_specs=(
            P(("fsdp", "ctx"), None),
            P(("fsdp", "ctx"), None),
            P("fsdp", None, "tp"),
            P("fsdp", None, "tp"),
            P("fsdp", None, "tp"),
            P("tp", "fsdp"),
            P("tp", "fsdp"),
            P("tp", "fsdp"),
            P("fsdp", None, "tp"),
            P("fsdp", None, "tp"),
            P("fsdp", None, "tp"),
            P("tp", "fsdp"),
            P("tp", "fsdp"),
            P("tp", "fsdp"),
            P(None, "fsdp"),
            P(None, "fsdp"),
            P(None, "fsdp"),
        ),
        check_vma=False,
    )
```
